32 devices in a mesh: pipe: 2 (over core), rows: 16 (over z, y, x).
Axes of the slice: x: 2, y: 2, z: 4, core: 2. Of those that a mesh axis runs over, the one named last changes fastest.
Arguments:
- section_in: bfloat16 [2, 4, 64, 24, 2048], P('pipe', None, 'rows'), may hold values from -12 to 12
- image_start: int32 [4, 64], replicated, may hold values from 0 to 1, as said below
- pool_choice: int32 [4, 32, 12], P(None, 'rows'), may hold values from 0 to 3
- conv_shared: bfloat16 [2, 2, 4608, 512], P('pipe'), may hold values from -0.09375 to 0.09375
- task_in: bfloat16 [2, 3, 1024, 512], P('pipe'), may hold values from -0.1875 to 0.1875
- task_mid: bfloat16 [2, 3, 512, 512], P('pipe'), may hold values from -0.25 to 0.25
- task_conv: bfloat16 [2, 3, 4608, 512], P('pipe'), may hold values from -0.09375 to 0.09375
- bn_gain: float32 [2, 11, 512], P('pipe'), may hold values from 0.25 to 1.75
- bn_bias: float32 [2, 11, 512], P('pipe'), may hold values from -2 to 2
Outputs:
- section_out: bfloat16 [2, 4, 64, 24, 2048], P('pipe', None, 'rows')
- conv_shared_grad: float32 [2, 2, 2359296], P('pipe', None, 'rows')
- task_in_grad: float32 [2, 3, 524288], P('pipe', None, 'rows')
- task_mid_grad: float32 [2, 3, 262144], P('pipe', None, 'rows')
- task_conv_grad: float32 [2, 3, 2359296], P('pipe', None, 'rows')
- bn_gain_grad: float32 [2, 11, 512], P('pipe')
- bn_bias_grad: float32 [2, 11, 512], P('pipe')
The draws below stay inside these ranges and needn't reach their ends.
Inputs may be any that keep to these rules, and one draw needn't show every extreme that they name: `image_start`: in each micro-batch, 1 on every 18-th row, from an even first row below 18 drawn from the seed; in one micro-batch, drawn from the seed, every row is 0.
All inputs are finite; a program needn't handle non-finite values.
Results may differ from the reference program's by a relative error of at most 0.023.
Values may be sent and summed in bfloat16 or wider, within the bound.
A program may use at most 320 MiB of HBM per device.

```python
import jax
import jax.numpy as jnp
from jax import lax

C = 512
TASKS = 3
WID = 24
IMAGE_ROWS = 18
M = 4
SHARED = 2
NORMS = 11
ROWS = 64
N_PIPE = 2


def draw_image_start(key, part):
    key = jax.random.fold_in(key, 11)
    phase = 2 * jax.random.randint(key, (M, 1), 0, IMAGE_ROWS // 2)
    places = jnp.arange(ROWS, dtype=jnp.int32)[None, :]
    starts = (places - phase) % IMAGE_ROWS == 0
    whole_batch = jax.random.randint(jax.random.fold_in(key, 1), (), 0, M)
    keeper = jnp.arange(M, dtype=jnp.int32)[:, None] != whole_batch
    return (starts & keeper).astype(jnp.int32)


def draw_section_in(key, part):
    key = jax.random.fold_in(key, 5)
    layout = (2, M, ROWS, WID, (1 + TASKS) * C)
    row_place = jnp.arange(ROWS, dtype=jnp.float32) / max(ROWS - 1, 1)
    lane_scale = 10.0 ** (jax.random.uniform(jax.random.fold_in(key, 2), ((1 + TASKS) * C,)) - 0.5)
    base = jax.random.truncated_normal(key, -3.0, 3.0, layout)
    row_scale = 10.0 ** (row_place - 0.5)
    scaled = base * row_scale[None, None, :, None, None] * lane_scale
    return jnp.clip(scaled, -12.0, 12.0).astype(jnp.bfloat16)


def touch_ends(result, stream_key, smallest, top_value):
    longest = result.shape.index(max(result.shape))
    spots = []
    for shift in (0, 1):
        where = [jax.random.randint(jax.random.fold_in(stream_key, axis), (), 0, length) for axis, length in enumerate(result.shape)]
        where[longest] = (where[longest] + shift) % result.shape[longest]
        spots.append(tuple(where))
    return result.at[spots[0]].set(smallest).at[spots[1]].set(top_value)


def level_of(own_key, extent, cuts, smallest, largest):
    loudness, own = 1.0, jax.random.fold_in(own_key, 6)
    for dim, shards_of in cuts:
        heights = jnp.exp(jax.random.uniform(jax.random.fold_in(own, dim), (shards_of,), jnp.float32, smallest / len(cuts), largest / len(cuts)))
        loudness = loudness * jnp.repeat(heights, extent[dim] // shards_of).reshape([-1 if axis == dim else 1 for axis in range(len(extent))])
    return loudness


def centred(rng, extent, width, limit, cuts=(), kind=jnp.bfloat16):
    level = level_of(rng, extent, cuts, -0.22, 0.18) if cuts else 1.0
    values = jax.random.normal(rng, extent, jnp.float32) * width * level
    return jnp.minimum(jnp.maximum(values, -limit), limit).astype(kind)


def setup_inputs(seed: int = 0) -> dict:
    splits = jax.random.split(jax.random.key(seed), 10)
    section_in = draw_section_in(jax.random.fold_in(splits[9], 71), 0)
    image_start = draw_image_start(jax.random.fold_in(splits[9], 71), 0)
    pool_choice = touch_ends(jax.random.randint(splits[2], (M, ROWS // 2, WID // 2), 0, 4), jax.random.fold_in(splits[2], 1), 0, 3).astype(jnp.int32)
    conv_shared = centred(splits[3], (N_PIPE, SHARED, 9 * C, C), (9 * C) ** -0.5, 0.09375, ((0, 2),))
    task_in = centred(splits[4], (N_PIPE, TASKS, 2 * C, C), (2 * C) ** -0.5, 0.1875, ((0, 2),))
    task_mid = centred(splits[5], (N_PIPE, TASKS, C, C), C ** -0.5, 0.25, ((0, 2),))
    task_conv = centred(splits[6], (N_PIPE, TASKS, 9 * C, C), (9 * C) ** -0.5, 0.09375, ((0, 2),))
    bn_gain = jnp.clip(1.0 + 0.15 * jax.random.normal(splits[7], (N_PIPE, NORMS, C), jnp.float32), 0.25, 1.75)
    bn_bias = centred(splits[8], (N_PIPE, NORMS, C), 0.5, 2.0, ((0, 2),), jnp.float32)
    return dict(section_in=section_in, image_start=image_start, pool_choice=pool_choice, conv_shared=conv_shared, task_in=task_in, task_mid=task_mid, task_conv=task_conv, bn_gain=bn_gain, bn_bias=bn_bias)


@jax.custom_vjp
def low(v):
    return lax.optimization_barrier(v.astype(jnp.bfloat16)).astype(jnp.float32)

@jax.custom_vjp
def low_back(v):
    return v

def low_keep(v):
    return (low(v), None)

def low_pass(kept, grad):
    return (grad,)

def back_keep(v):
    return (v, None)

def back_low(kept, grad):
    return (low(grad),)
low.defvjp(low_keep, low_pass)
low_back.defvjp(back_keep, back_low)
HIGHEST_PRECISION = lax.Precision.HIGHEST
epsilon = 1e-05

def masks_of(starts):
    upper_ok = 1.0 - starts.astype(jnp.float32)
    lower_ok = jnp.concatenate([upper_ok[1:], jnp.ones((1,), jnp.float32)])
    return (upper_ok, lower_ok)

def conv_three(feature, kernel, upper_ok, lower_ok):
    zero_row = jnp.zeros_like(feature[:1])
    above_rows = jnp.concatenate([zero_row, feature[:-1]], 0) * upper_ok[:, None, None]
    below_rows = jnp.concatenate([feature[1:], zero_row], 0) * lower_ok[:, None, None]
    columns = feature.shape[1]
    pieces = []
    for shifted in (above_rows, feature, below_rows):
        widened = jnp.pad(shifted, ((0, 0), (1, 1), (0, 0)))
        for offset in range(3):
            pieces.append(widened[:, offset:offset + columns])
    stacked = jnp.concatenate(pieces, -1)
    return jnp.einsum('rwk,ko->rwo', stacked, kernel, precision=HIGHEST_PRECISION)

def batch_norm(tensor, gain_row, bias_row):
    average = lax.optimization_barrier(jnp.mean(tensor, (0, 1)))
    spread = lax.optimization_barrier(jnp.mean(tensor * tensor, (0, 1))) - average * average
    return (tensor - average) * lax.rsqrt(spread + epsilon) * gain_row + bias_row

def section_pass(shared, branches, upper_ok, lower_ok, params):
    conv_kernels, joint_kernels, middle_kernels, branch_kernels, gain_rows, biases = params
    pre_one = low_back(conv_three(shared, conv_kernels[0], upper_ok, lower_ok))
    hidden_one = low(jax.nn.silu(batch_norm(pre_one, gain_rows[0], biases[0])))
    pre_two = low_back(conv_three(hidden_one, conv_kernels[1], upper_ok, lower_ok))
    hidden_two = low(jax.nn.silu(batch_norm(pre_two, gain_rows[1], biases[1])))
    results = [hidden_two]
    for task in range(TASKS):
        base = 2 + 3 * task
        joined = jnp.concatenate([hidden_one, branches[..., task * C:(task + 1) * C]], -1)
        pre_three = low_back(jnp.einsum('rwc,co->rwo', joined, joint_kernels[task], precision=HIGHEST_PRECISION))
        branch_act = low(jax.nn.silu(batch_norm(pre_three, gain_rows[base], biases[base])))
        pre_four = low_back(jnp.einsum('rwc,co->rwo', branch_act, middle_kernels[task], precision=HIGHEST_PRECISION))
        gating = jax.nn.sigmoid(batch_norm(pre_four, gain_rows[base + 1], biases[base + 1]))
        product = low(gating * hidden_two)
        pre_five = low_back(conv_three(product, branch_kernels[task], upper_ok, lower_ok))
        results.append(low(jax.nn.silu(batch_norm(pre_five, gain_rows[base + 2], biases[base + 2]))))
    return jnp.concatenate(results, -1)

def pool_mean(tensor):
    height, across, channels = tensor.shape
    return lax.optimization_barrier(jnp.mean(tensor.reshape(height // 2, 2, across // 2, 2, channels), (1, 3)))

def unpool(pooled, selector):
    height, across, channels = pooled.shape
    onehot = (selector[:, :, None] == jnp.arange(4, dtype=jnp.int32)).astype(pooled.dtype)
    onehot = onehot.reshape(height, across, 2, 2).transpose(0, 2, 1, 3)
    return (pooled[:, None, :, None, :] * onehot[..., None]).reshape(2 * height, 2 * across, channels)

def reference(section_in, image_start, pool_choice, conv_shared, task_in, task_mid, task_conv, bn_gain, bn_bias):
    floats = section_in.astype(jnp.float32)
    inputs = floats[0]
    cotangent = floats[1]
    weights = (conv_shared.astype(jnp.float32), task_in.astype(jnp.float32), task_mid.astype(jnp.float32), task_conv.astype(jnp.float32), bn_gain, bn_bias)

    def micro_batch(weights, batch_in):
        feature, starts, selector = batch_in
        upper_ok, lower_ok = masks_of(starts)
        encoder = tuple((member[0] for member in weights))
        decoder = tuple((member[1] for member in weights))
        encoded = section_pass(feature[..., :C], feature[..., C:], upper_ok, lower_ok, encoder)
        pooled = low_back(low(pool_mean(encoded)))
        opened = unpool(pooled, selector)
        return section_pass(opened[..., :C], opened[..., C:], upper_ok, lower_ok, decoder)
    stepper = jax.checkpoint(micro_batch)

    def forward(inputs, weights):
        return lax.map(lambda batch_in: stepper(weights, batch_in), (inputs, image_start, pool_choice))
    features, pullback = jax.vjp(forward, inputs, weights)
    grad_in, grad_w = pullback(cotangent)
    stacked_out = jnp.stack([grad_in, features]).astype(jnp.bfloat16)
    return (stacked_out, grad_w[0].reshape(N_PIPE, SHARED, 9 * C * C), grad_w[1].reshape(N_PIPE, TASKS, 2 * C * C), grad_w[2].reshape(N_PIPE, TASKS, C * C), grad_w[3].reshape(N_PIPE, TASKS, 9 * C * C), grad_w[4], grad_w[5])
```

```python
import functools

import jax
import jax.numpy as jnp
import numpy as np
from jax import lax
from jax.experimental import pallas as pl
from jax.experimental.pallas import tpu as pltpu
from jax.sharding import PartitionSpec as P

MESH = pl.DeviceIdType.MESH
half = jnp.bfloat16
f32 = jnp.float32
epsilon = 1e-05
TEAM = 4

ANY = pl.BlockSpec(memory_space=pl.ANY)
VMEM = pl.BlockSpec(memory_space=pltpu.VMEM)


def sigmoid(x):
    return 0.5 * jnp.tanh(0.5 * x) + 0.5


def dot(a, b):
    return jnp.dot(a, b, preferred_element_type=f32)


def dot_nt(a, b):
    return lax.dot_general(a, b, (((1,), (1,)), ((), ())), preferred_element_type=f32)


def dot_tn(a, b):
    return lax.dot_general(a, b, (((0,), (0,)), ((), ())), preferred_element_type=f32)


class Remote:
    def __init__(self, src, dst, send, recv, to):
        self.src, self.dst, self.send, self.recv, self.to = src, dst, send, recv, to
        self.local = to == lax.axis_index("rows")

    def remote(self):
        return pltpu.make_async_remote_copy(
            src_ref=self.src,
            dst_ref=self.dst,
            send_sem=self.send,
            recv_sem=self.recv,
            device_id=(lax.axis_index("pipe"), self.to),
            device_id_type=MESH,
        )

    def start(self):
        @pl.when(self.local)
        def _():
            pltpu.make_async_copy(self.src, self.dst, self.recv).start()

        @pl.when(jnp.logical_not(self.local))
        def _():
            self.remote().start()

    def sent(self):
        @pl.when(jnp.logical_not(self.local))
        def _():
            self.remote().wait_send()


def arrived(dst, sem):
    pltpu.make_async_copy(dst, dst, sem).wait()


EDGES = 13


def section_kernel(cfg, *refs):
    M, G, H, W, C, T = cfg["M"], cfg["G"], cfg["H"], cfg["W"], cfg["C"], cfg["T"]
    R = M * G
    pix = H * W
    part = pix // M
    count = float(pix * G)
    norms = 2 + 3 * T
    (sec, sel, msk, perm, perm_t, spread, spread_edge, pool, gain, bias, wc, wi, wm, wt) = refs[:14]
    (out, bng, xu, xh, xp, xt, xv, xd5, xd5e, xd4, xd3, xd1, xd1e) = refs[14:27]
    (
        kc, ki, km, kt, rin, field, selin, chosen, uh, selh, uedge, px, ps, rb, ys, esend, erecv, ssend, srecv,
        h1, h2, h2e, t1, pr, res, dz, dh, dy5, dy5e, dy2, dy2e, dy4, dy3, dy1, dy1e, bn, bnr,
        w_sem, in_s, in_r, ed_s, ed_r, st_s, st_r, pp_s, pp_r, out_s, out_r, bn_s, bn_r, x_s, x_r,
    ) = refs[27:]
    p = lax.axis_index("pipe")
    r = lax.axis_index("rows")
    b, m = r // M, r % M
    e, e0 = m, r - m
    first, last = b == 0, b == G - 1
    CW = C * (1 + T)

    loads = {}

    def load(name, src, dst, i):
        loads[name] = pltpu.make_async_copy(src, dst, w_sem.at[i])
        loads[name].start()

    load("c0", wc.at[0], kc.at[0], 0)
    load("i", wi, ki, 1)
    load("c1", wc.at[1], kc.at[1], 2)
    load("m", wm, km, 3)
    for t in range(T):
        load("t%d" % t, wt.at[t], kt.at[t], 4 + t)

    zero_col = jnp.zeros((H, C), half)
    for a in range(3):
        rb[a, 0:H, :] = zero_col
        rb[a, H * (W + 1) : H * (W + 2), :] = zero_col
    px[pix // 4 :, :] = jnp.zeros((px.shape[0] - pix // 4, CW), half)

    @pl.when(first)
    def _():
        for s in range(EDGES):
            erecv[s, 0] = jnp.zeros((W, 1, C), f32)
        uh[0] = jnp.zeros((32, C), half)
        selh[0] = jnp.zeros((32, 128), half)

    @pl.when(last)
    def _():
        for s in range(EDGES):
            erecv[s, 1] = jnp.zeros((W, 1, C), f32)
        uh[1] = jnp.zeros((32, C), half)
        selh[1] = jnp.zeros((32, 128), half)

    bar = pltpu.get_barrier_semaphore()

    def hello(side, row):
        pl.semaphore_signal(bar, inc=1, device_id=(side, row), device_id_type=MESH)

    for d in range(1, M):
        hello(p, e0 + lax.rem(m + d, M))
    for d in range(1, G):
        hello(p, M * lax.rem(b + d, G) + m)
    hello(1 - p, r)
    tops = jnp.logical_and(m == M - 1, jnp.logical_not(last))
    bottoms = jnp.logical_and(m == 0, jnp.logical_not(first))

    @pl.when(jnp.logical_not(first))
    def _():
        hello(1 - p, r - M)
        hello(p, e0 - 1)

    @pl.when(jnp.logical_not(last))
    def _():
        hello(1 - p, r + M)
        hello(p, e0 + M)

    @pl.when(tops)
    def _():
        for j in range(M):
            hello(p, e0 + M + j)

    @pl.when(bottoms)
    def _():
        for j in range(M):
            hello(p, e0 - M + j)

    below_me, above_me = 1 - (b + 1) // G, (b + G - 1) // G
    top_member, bottom_member = (m + 1) // M, 1 - (m + M - 1) // M
    pl.semaphore_wait(
        bar, M + G - 1 + 2 * (below_me + above_me) + M * (top_member * below_me + bottom_member * above_me)
    )

    mine = pl.ds(pl.multiple_of(part * m, 16), part)
    field_moves, rest_moves, sel_moves, edge_moves = [], [], [], ([], [])
    for d in range(M):
        j = lax.rem(m + d, M)
        to = e0 + j
        field_moves.append(Remote(sec.at[j, :, 0:C], rin.at[mine, 0:C], in_s.at[0, d], in_r.at[0, m], to))
        sel_moves.append(Remote(sel.at[j], selin.at[mine], in_s.at[2, d], in_r.at[2, m], to))
        rest_moves.append(Remote(sec.at[j, :, C:CW], rin.at[mine, C:CW], in_s.at[1, d], in_r.at[1, m], to))
    for j in range(M):
        to = e0 + j
        edge_moves[0].append(
            Remote(sec.at[j, pl.ds(part - 32, 32), 0:C], uh.at[0], in_s.at[3, j], in_r.at[3, 0], to + M)
        )
        edge_moves[0].append(Remote(sel.at[j, pl.ds(part - 32, 32)], selh.at[0], in_s.at[4, j], in_r.at[3, 1], to + M))
        edge_moves[1].append(Remote(sec.at[j, pl.ds(0, 32), 0:C], uh.at[1], in_s.at[5, j], in_r.at[4, 0], to - M))
        edge_moves[1].append(Remote(sel.at[j, pl.ds(0, 32)], selh.at[1], in_s.at[6, j], in_r.at[4, 1], to - M))

    def start_field():
        for move in field_moves:
            move.start()
        for move in rest_moves:
            move.start()

    @pl.when(tops)
    def _():
        for move in edge_moves[0]:
            move.start()

    @pl.when(bottoms)
    def _():
        for move in edge_moves[1]:
            move.start()

    @pl.when(p == 0)
    def _():
        start_field()

    for move in sel_moves:
        move.start()

    row_of = lax.broadcasted_iota(jnp.int32, (H, C), 0)
    at_top, at_bottom = row_of == 0, row_of == H - 1

    def column(j):
        return pl.ds(pl.multiple_of(j * H, H), H)

    def over_columns(body, start=0, step=2):
        def several(c, carry):
            for u in range(step):
                carry = body(c * step + u, carry)
            return carry

        return lax.fori_loop(0, W // step, several, start)

    def build(j, value, above, below, up, down):
        here = pl.ds(pl.multiple_of(H + j * H, H), H)
        rb[1, here, :] = value.astype(half)
        rb[0, here, :] = (jnp.where(at_top, above, pltpu.roll(value, 1, 0)) * up).astype(half)
        rb[2, here, :] = (jnp.where(at_bottom, below, pltpu.roll(value, H - 1, 0)) * down).astype(half)

    def conv(kernel):
        total = None
        for tap in range(9):
            a, c = tap // 3, tap % 3
            term = dot(rb[a, H * c : H * c + pix, :], kernel[tap * C : (tap + 1) * C, :])
            total = term if total is None else total + term
        return total

    def conv_t(kernel):
        total = None
        for tap in range(9):
            a, c = tap // 3, tap % 3
            term = dot_nt(rb[a, H * c : H * c + pix, :], kernel[(8 - tap) * C : (9 - tap) * C, :])
            total = term if total is None else total + term
        return total

    def folded(total):
        return jnp.sum(total, 0, keepdims=True)

    def fold(x):
        return jnp.sum(x.reshape(H // 8, 8, C), 0)

    zero8 = jnp.zeros((8, C), f32)

    def edge_copy(slot, side):
        to = r - M if side == 0 else r + M
        return pltpu.make_async_remote_copy(
            src_ref=esend.at[slot, side],
            dst_ref=erecv.at[slot, 1 - side],
            send_sem=ed_s.at[slot, side],
            recv_sem=ed_r.at[slot, 1 - side],
            device_id=(p, to),
            device_id_type=MESH,
        )

    def send_edges(slot):
        @pl.when(jnp.logical_not(first))
        def _():
            edge_copy(slot, 0).start()

        @pl.when(jnp.logical_not(last))
        def _():
            edge_copy(slot, 1).start()

    def get_edges(slot):
        @pl.when(jnp.logical_not(first))
        def _():
            arrived(erecv.at[slot, 0], ed_r.at[slot, 0])

        @pl.when(jnp.logical_not(last))
        def _():
            arrived(erecv.at[slot, 1], ed_r.at[slot, 1])

    def finish_edges(slot):
        @pl.when(jnp.logical_not(first))
        def _():
            edge_copy(slot, 0).wait_send()

        @pl.when(jnp.logical_not(last))
        def _():
            edge_copy(slot, 1).wait_send()

    def stat_copy(slot, n, d):
        to = M * lax.rem(b + d, G) + m
        return pltpu.make_async_remote_copy(
            src_ref=ssend.at[pl.ds(slot, n)],
            dst_ref=srecv.at[b, pl.ds(slot, n)],
            send_sem=st_s.at[slot, d],
            recv_sem=st_r.at[slot, b],
            device_id=(p, to),
            device_id_type=MESH,
        )

    def send_sums(slot, n):
        srecv[b, slot : slot + n] = ssend[slot : slot + n]
        for d in range(1, G):
            stat_copy(slot, n, d).start()

    sums_sent = []

    def get_sums(slot, n):
        sums_sent.append((slot, n))
        for d in range(1, G):
            s = lax.rem(b + d, G)
            arrived(srecv.at[s, pl.ds(slot, n)], st_r.at[slot, s])

    def total(slot):
        acc = srecv[0, slot]
        for g in range(1, G):
            acc = acc + srecv[g, slot]
        return acc

    def put_sums(slot, s, q):
        ssend[slot] = jnp.concatenate([folded(s), folded(q)], 0)

    x_moves = []

    def post(index, src, dst, target):
        move = Remote(src, dst.at[e], x_s.at[index], x_r.at[index - (target if index in cfg["to_all"] else 0), e], e0 + target)
        move.start()
        x_moves.append(move)

    def moments(k, slot, edge=None):
        def body(j, carry):
            s, q = carry
            y = ys[k, column(j), :]
            if edge is not None:
                esend[edge, 0, j] = y[0:1]
                esend[edge, 1, j] = y[H - 1 : H]
            return s + fold(y), q + fold(y * y)

        s, q = over_columns(body, (zero8, zero8))
        put_sums(slot, s, q)

    norm = {}

    def norm_rows(k, slot):
        acc = total(slot)
        mean = acc[0:1] / count
        rs = lax.rsqrt(acc[1:2] / count - mean * mean + epsilon)
        scale = gain[k : k + 1, :] * rs
        norm[k] = (mean, rs, scale, bias[k : k + 1, :])

    def normed(k, y):
        mean, rs, scale, shift = norm[k]
        return (y - mean) * scale + shift

    def silu(x):
        return x * sigmoid(x)

    def silu_slope(x):
        s = sigmoid(x)
        return s * (1.0 + x * (1.0 - s))

    def pair(slot, j):
        return jnp.concatenate([erecv[slot, 0, j], erecv[slot, 1, j]], 0)

    nt = 2 + 3 * T
    F3, F4, F5 = 2, 2 + T, 2 + 2 * T

    def wait_field(kind, buffer):
        for k in range(M):
            arrived(buffer(k), in_r.at[kind, k])

    @pl.when(jnp.logical_not(first))
    def _():
        arrived(uh.at[0], in_r.at[3, 0])
        arrived(selh.at[0], in_r.at[3, 1])

    @pl.when(jnp.logical_not(last))
    def _():
        arrived(uh.at[1], in_r.at[4, 0])
        arrived(selh.at[1], in_r.at[4, 1])

    def start_of_field():
        wait_field(0, lambda k: rin.at[pl.ds(part * k, part), 0:C])
        field[p, :, 0:C] = dot(perm[...], rin[:, 0:C]).astype(half)

    def rest_of_field():
        wait_field(1, lambda k: rin.at[pl.ds(part * k, part), C:CW])
        for t in range(T):
            cols = slice((t + 1) * C, (t + 2) * C)
            field[p, :, cols] = dot(perm[...], rin[:, cols]).astype(half)

    @pl.when(p == 0)
    def _():
        start_of_field()

    wait_field(2, lambda k: selin.at[pl.ds(part * k, part)])
    chosen[...] = spread[...] * dot(perm[...], selin[...]).astype(half)

    def halo_copies():
        return (
            pltpu.make_async_remote_copy(
                src_ref=ps.at[pl.ds(pix // 4, 16), 0:C], dst_ref=px.at[pl.ds(pix // 4, 16), 0:C],
                send_sem=pp_s.at[1], recv_sem=pp_r.at[1], device_id=(1 - p, r + M), device_id_type=MESH),
            pltpu.make_async_remote_copy(
                src_ref=ps.at[pl.ds(pix // 4 + 16, 16), 0:C], dst_ref=px.at[pl.ds(pix // 4 + 16, 16), 0:C],
                send_sem=pp_s.at[2], recv_sem=pp_r.at[2], device_id=(1 - p, M * (b - 1) + m), device_id_type=MESH),
        )

    def pool_copy():
        return pltpu.make_async_remote_copy(
            src_ref=ps.at[pl.ds(0, pix // 4)], dst_ref=px.at[pl.ds(0, pix // 4)],
            send_sem=pp_s.at[0], recv_sem=pp_r.at[0], device_id=(1 - p, r), device_id_type=MESH)

    @pl.when(p == 1)
    def _():
        arrived(px.at[pl.ds(0, pix // 4)], pp_r.at[0])
        start_field()

        @pl.when(jnp.logical_not(first))
        def _():
            arrived(px.at[pl.ds(pix // 4, 16), 0:C], pp_r.at[1])

        @pl.when(jnp.logical_not(last))
        def _():
            arrived(px.at[pl.ds(pix // 4 + 16, 16), 0:C], pp_r.at[2])

        for t in range(1 + T):
            cols = slice(t * C, (t + 1) * C)
            field[0, :, cols] = dot(chosen[...], px[:, cols]).astype(half)
        edges = spread_edge[...] * jnp.concatenate([selh[0], selh[1]], 0)
        both = dot(edges, px[:, 0:C]).astype(half)
        uh[0] = both[0:32]
        uh[1] = both[32:64]

    above = uh[0].astype(f32)
    below = uh[1].astype(f32)
    for j in range(W):
        uedge[0, j] = above[32 - W + j : 33 - W + j]
        uedge[1, j] = below[j : j + 1]

    up = msk[0]
    down = msk[1]

    def body_u(j, carry):
        build(j, field[0, column(j), 0:C].astype(f32), uedge[0, j], uedge[1, j], up, down)
        return carry

    over_columns(body_u)
    loads["c0"].wait()
    ys[0] = conv(kc.at[0])
    moments(0, 0, 0)
    send_sums(0, 1)
    send_edges(0)

    @pl.when(p == 0)
    def _():
        rest_of_field()

    for q in range(TEAM):
        post(q, field.at[0, :, 0:C], xu, q)
    for t in range(T):
        post(8 + t, field.at[0, :, (t + 1) * C : (t + 2) * C], xv, t)
    get_sums(0, 1)
    get_edges(0)
    norm_rows(0, 0)

    def body_h1(j, carry):
        value = silu(normed(0, ys[0, column(j), :]))
        side = silu(normed(0, pair(0, j)))
        h1[column(j), :] = value.astype(half)
        build(j, value, side[0:1], side[1:2], up, down)
        return carry

    over_columns(body_h1)
    for q in range(TEAM):
        post(4 + q, h1, xh, q)

    loads["i"].wait()
    for t in range(T):
        k = 2 + 3 * t
        ys[k] = dot(h1[...], ki[t, 0:C, :]) + dot(field[0, :, (t + 1) * C : (t + 2) * C], ki[t, C : 2 * C, :])
        moments(k, F3 + t)
    send_sums(F3, T)
    loads["c1"].wait()
    ys[1] = conv(kc.at[1])
    moments(1, 1, 1)
    send_sums(1, 1)
    send_edges(1)

    get_sums(F3, T)
    loads["m"].wait()
    for t in range(T):
        k = 2 + 3 * t
        norm_rows(k, F3 + t)

        def body_t1(j, carry):
            t1[t, column(j), :] = silu(normed(k, ys[k, column(j), :])).astype(half)
            return carry

        over_columns(body_t1)
        post(11 + t, t1.at[t], xt, t)
        ys[k + 1] = dot(t1[t], km[t])
        moments(k + 1, F4 + t, 2 + t)
    send_sums(F4, T)
    for t in range(T):
        send_edges(2 + t)

    get_sums(1, 1)
    get_edges(1)
    norm_rows(1, 1)

    def body_h2(j, carry):
        value = silu(normed(1, ys[1, column(j), :])).astype(half)
        h2[column(j), :] = value
        res[column(j), 0:C] = value
        side = silu(normed(1, pair(1, j))).astype(half).astype(f32)
        h2e[j] = side
        return carry

    over_columns(body_h2)
    get_sums(F4, T)
    for t in range(T):
        k = 3 + 3 * t
        get_edges(2 + t)
        norm_rows(k, F4 + t)

        def body_p(j, carry):
            gate = sigmoid(normed(k, ys[k, column(j), :]))
            value = gate * h2[column(j), :].astype(f32)
            side = sigmoid(normed(k, pair(2 + t, j))) * h2e[j]
            pr[t, column(j), :] = value.astype(half)
            build(j, value, side[0:1], side[1:2], up, down)
            return carry

        over_columns(body_p)
        post(14 + t, pr.at[t], xp, t)
        loads["t%d" % t].wait()
        ys[k + 1] = conv(kt.at[t])
        moments(k + 1, F5 + t, 5 + t)
    send_sums(F5, T)
    for t in range(T):
        send_edges(5 + t)
    get_sums(F5, T)
    for t in range(T):
        k = 4 + 3 * t
        get_edges(5 + t)
        norm_rows(k, F5 + t)

        def body_q(j, carry):
            res[column(j), (t + 1) * C : (t + 2) * C] = silu(normed(k, ys[k, column(j), :])).astype(half)
            return carry

        over_columns(body_q)

    def out_moves(which):
        cols = slice(0, C) if which == 0 else slice(C, CW)
        moves = []
        for d in range(M):
            k = lax.rem(m + d, M)
            rows = pl.ds(pl.multiple_of(part * k, 16), part)
            moves.append(
                Remote(rin.at[rows, cols], out.at[m, :, cols], out_s.at[which, d], out_r.at[which, m], e0 + k)
            )
        return moves

    def send_result(which):
        for t in range(0, 1) if which == 0 else range(1, 1 + T):
            cols = slice(t * C, (t + 1) * C)
            rin[:, cols] = dot(perm_t[...], res[:, cols]).astype(half)
        for move in out_moves(which):
            move.start()

    @pl.when(p == 0)
    def _():
        for t in range(1 + T):
            cols = slice(t * C, (t + 1) * C)
            ps[:, cols] = dot(pool[...], res[:, cols]).astype(half)
        pool_copy().start()

        @pl.when(jnp.logical_not(last))
        def _():
            halo_copies()[0].start()

        @pl.when(jnp.logical_not(first))
        def _():
            halo_copies()[1].start()

        pool_copy().wait_send()

        @pl.when(jnp.logical_not(last))
        def _():
            halo_copies()[0].wait_send()

        @pl.when(jnp.logical_not(first))
        def _():
            halo_copies()[1].wait_send()

        arrived(px.at[pl.ds(0, pix // 4)], pp_r.at[0])
        for t in range(1 + T):
            cols = slice(t * C, (t + 1) * C)
            field[1, :, cols] = (dot(spread[...], px[:, cols]) * 0.25).astype(half)

    @pl.when(p == 1)
    def _():
        start_of_field()
        rest_of_field()
        send_result(0)
        send_result(1)

    B3, B4, B5 = nt + F3, nt + F4, nt + F5
    back = {}

    def back_rows(k, slot):
        acc = total(slot)
        mean, rs, scale, shift = norm[k]
        slope = -scale * rs * acc[1:2] / count
        back[k] = (scale, slope, -scale * acc[0:1] / count - slope * mean)
        bn[k : k + 1, :] = acc[1:2]
        bn[norms + k : norms + k + 1, :] = acc[0:1]

    def grad_pre(k, dzv, y):
        scale, slope, rest = back[k]
        return scale * dzv + slope * y + rest

    def hat(k, y):
        mean, rs, scale, shift = norm[k]
        return (y - mean) * rs

    for t in range(T):
        k = 4 + 3 * t

        def body_dz5(j, carry):
            s, q = carry
            y = ys[k, column(j), :]
            g = field[1, column(j), (t + 1) * C : (t + 2) * C].astype(f32)
            v = g * silu_slope(normed(k, y))
            dz[t, column(j), :] = v
            esend[8 + t, 0, j] = v[0:1]
            esend[8 + t, 1, j] = v[H - 1 : H]
            return s + fold(v), q + fold(v * hat(k, y))

        s, q = over_columns(body_dz5, (zero8, zero8))
        put_sums(B5 + t, s, q)
    send_sums(B5, T)
    for t in range(T):
        send_edges(8 + t)
    get_sums(B5, T)

    for t in range(T):
        k = 4 + 3 * t
        get_edges(8 + t)
        back_rows(k, B5 + t)

        def body_dy5(j, carry):
            v = grad_pre(k, dz[t, column(j), :], ys[k, column(j), :])
            side = grad_pre(k, pair(8 + t, j), pair(5 + t, j))
            dy5[t, column(j), :] = v.astype(half)
            dy5e[t, 0, j] = side[0:1]
            dy5e[t, 1, j] = side[1:2]
            build(j, v, side[0:1], side[1:2], up, down)
            return carry

        over_columns(body_dy5)
        post(17 + t, dy5.at[t], xd5, t)
        post(21 + t, dy5e.at[t], xd5e, t)
        ys[k] = conv_t(kt.at[t])

        def body_dz4(j, carry):
            s, q = carry
            dp = ys[k, column(j), :]
            y = ys[k - 1, column(j), :]
            gate = sigmoid(normed(k - 1, y))
            dgate = dp * h2[column(j), :].astype(f32)
            base = field[1, column(j), 0:C].astype(f32) if t == 0 else dh[column(j), :]
            dh[column(j), :] = base + dp * gate
            v = dgate * gate * (1.0 - gate)
            ys[k, column(j), :] = v
            return s + fold(v), q + fold(v * hat(k - 1, y))

        s, q = over_columns(body_dz4, (zero8, zero8))
        put_sums(B4 + t, s, q)
    send_sums(B4, T)

    def body_dz2(j, carry):
        s, q = carry
        y = ys[1, column(j), :]
        v = dh[column(j), :] * silu_slope(normed(1, y))
        dh[column(j), :] = v
        esend[11, 0, j] = v[0:1]
        esend[11, 1, j] = v[H - 1 : H]
        return s + fold(v), q + fold(v * hat(1, y))

    s, q = over_columns(body_dz2, (zero8, zero8))
    put_sums(nt + 1, s, q)
    send_sums(nt + 1, 1)
    send_edges(11)

    get_sums(B4, T)
    for t in range(T):
        k = 3 + 3 * t
        back_rows(k, B4 + t)

        def body_dy4(j, carry):
            dy4[t, column(j), :] = grad_pre(k, ys[k + 1, column(j), :], ys[k, column(j), :]).astype(half)
            return carry

        over_columns(body_dy4)
        post(25 + t, dy4.at[t], xd4, t)
        dz[t] = dot_nt(dy4[t], km[t])

        def body_dz3(j, carry):
            s, q = carry
            y = ys[k - 1, column(j), :]
            v = dz[t, column(j), :] * silu_slope(normed(k - 1, y))
            dz[t, column(j), :] = v
            return s + fold(v), q + fold(v * hat(k - 1, y))

        s, q = over_columns(body_dz3, (zero8, zero8))
        put_sums(B3 + t, s, q)
    send_sums(B3, T)

    get_sums(nt + 1, 1)
    get_edges(11)
    back_rows(1, nt + 1)

    def body_dy2(j, carry):
        v = grad_pre(1, dh[column(j), :], ys[1, column(j), :])
        side = grad_pre(1, pair(11, j), pair(1, j))
        dy2[column(j), :] = v.astype(half)
        dy2e[0, j] = side[0:1]
        dy2e[1, j] = side[1:2]
        build(j, v, side[0:1], side[1:2], up, down)
        return carry

    over_columns(body_dy2)
    post(20, dy2, xd5, TEAM - 1)
    post(24, dy2e, xd5e, TEAM - 1)
    dh[...] = conv_t(kc.at[1])

    get_sums(B3, T)
    for t in range(T):
        k = 2 + 3 * t
        back_rows(k, B3 + t)

        def body_dy3(j, carry):
            dy3[t, column(j), :] = grad_pre(k, dz[t, column(j), :], ys[k, column(j), :]).astype(half)
            return carry

        over_columns(body_dy3)
        post(28 + t, dy3.at[t], xd3, t)
        dh[...] += dot_nt(dy3[t], ki[t, 0:C, :])
        res[:, (t + 1) * C : (t + 2) * C] = dot_nt(dy3[t], ki[t, C : 2 * C, :]).astype(half)

    @pl.when(p == 0)
    def _():
        send_result(1)

    def body_dz1(j, carry):
        s, q = carry
        y = ys[0, column(j), :]
        v = dh[column(j), :] * silu_slope(normed(0, y))
        dh[column(j), :] = v
        esend[12, 0, j] = v[0:1]
        esend[12, 1, j] = v[H - 1 : H]
        return s + fold(v), q + fold(v * hat(0, y))

    s, q = over_columns(body_dz1, (zero8, zero8))
    put_sums(nt, s, q)
    send_sums(nt, 1)
    send_edges(12)
    get_sums(nt, 1)
    get_edges(12)
    back_rows(0, nt)

    def bn_moves():
        return [Remote(bn, bnr.at[m], bn_s.at[d], bn_r.at[m], e0 + lax.rem(m + d, M)) for d in range(M)]

    for move in bn_moves():
        move.start()

    quarter = C // TEAM

    def body_dy1(j, carry):
        v = grad_pre(0, dh[column(j), :], ys[0, column(j), :])
        side = grad_pre(0, pair(12, j), pair(0, j))
        low = v.astype(half)
        for o in range(TEAM):
            cols = slice(o * quarter, (o + 1) * quarter)
            dy1[o, column(j), :] = low[:, cols]
            dy1e[o, 0, j] = side[0:1, cols]
            dy1e[o, 1, j] = side[1:2, cols]
        build(j, v, side[0:1], side[1:2], up, down)
        return carry

    over_columns(body_dy1)
    for o in range(TEAM):
        post(31 + o, dy1.at[o], xd1, o)
        post(35 + o, dy1e.at[o], xd1e, o)
    res[:, 0:C] = conv_t(kc.at[0]).astype(half)

    @pl.when(p == 1)
    def _():
        for t in range(1 + T):
            cols = slice(t * C, (t + 1) * C)
            ps[0 : pix // 4, cols] = dot_tn(chosen[...], res[:, cols])[0 : pix // 4].astype(half)
        pool_copy().start()
        pool_copy().wait_send()

    @pl.when(p == 0)
    def _():
        send_result(0)

    for k in range(M):
        arrived(bnr.at[k], bn_r.at[k])
    acc = bnr[0]
    for k in range(1, M):
        acc = acc + bnr[k]
    bng[...] = acc
    for k in range(M):
        arrived(out.at[k, :, 0:C], out_r.at[0, k])
        arrived(out.at[k, :, C:CW], out_r.at[1, k])
    for move in out_moves(0) + out_moves(1) + bn_moves() + field_moves + rest_moves + sel_moves:
        move.sent()

    @pl.when(tops)
    def _():
        for move in edge_moves[0]:
            move.sent()

    @pl.when(bottoms)
    def _():
        for move in edge_moves[1]:
            move.sent()

    for s in range(EDGES):
        finish_edges(s)
    for slot, n in sums_sent:
        for d in range(1, G):
            stat_copy(slot, n, d).wait_send()
    for move in x_moves:
        move.sent()
    for j in range(TEAM):
        for index, dst in ((0, xu), (4, xh), (31, xd1), (35, xd1e)):
            arrived(dst.at[j], x_r.at[index, j])
    for t in range(T):

        @pl.when(e == t)
        def _():
            for j in range(TEAM):
                for index, dst in ((8, xv), (11, xt), (14, xp), (17, xd5), (21, xd5e), (25, xd4), (28, xd3)):
                    arrived(dst.at[j], x_r.at[index + t, j])

    @pl.when(e == TEAM - 1)
    def _():
        for j in range(TEAM):
            arrived(xd5.at[j], x_r.at[20, j])
            arrived(xd5e.at[j], x_r.at[24, j])


def tables(M, G, H, W):
    pix = H * W
    cm = np.zeros((pix, pix), np.float32)
    spread = np.zeros((pix, 128), np.float32)
    pool = np.zeros((128, pix), np.float32)
    edge = np.zeros((64, 128), np.float32)
    wide = W // 2
    own = pix // 4
    for i in range(H):
        for j in range(W):
            q = j * H + i
            cm[q, i * W + j] = 1
            w = (i // 2) * wide + j // 2
            spread[q, w] = 1
            pool[w, q] = 0.25
            if i >= H - 2:
                pool[own + j // 2, q] = 0.25
            if i < 2:
                pool[own + 16 + j // 2, q] = 0.25
    for j in range(W):
        edge[32 - W + j, own + j // 2] = 1
        edge[32 + j, own + 16 + j // 2] = 1
    return [jnp.asarray(v, half) for v in (cm, cm.T, spread, edge, pool)]


def gradient_kernel(cfg, *refs):
    M, G, H, W, C, T, n = cfg["M"], cfg["G"], cfg["H"], cfg["W"], cfg["C"], cfg["T"], cfg["n"]
    R = M * G
    pix = H * W
    q4 = C // TEAM
    (msk, xu, xh, xp, xt, xv, xd5, xd5e, xd4, xd3, xd1, xd1e) = refs[:12]
    (gm, g1, gi, gt) = refs[12:16]
    (va, vb, vc, vd, d5, d5e, rb, r1, d1, d1e, d3, pm, p1, pi_, pt, am, a1, ai, at, in_sem, s_sem, r_sem) = refs[16:]
    p = lax.axis_index("pipe")
    r = lax.axis_index("rows")
    e = r % TEAM
    z = r // TEAM
    task = e < T

    loads = {}

    def load(name, src, dst, i):
        loads[name] = pltpu.make_async_copy(src, dst, in_sem.at[i])
        loads[name].start()

    load("d5", xd5, d5, 0)
    load("d5e", xd5e, d5e, 1)
    load("h", xh, va, 2)

    @pl.when(task)
    def _():
        pltpu.make_async_copy(xp, vb, in_sem.at[3]).start()
        pltpu.make_async_copy(xv, vc, in_sem.at[4]).start()
        pltpu.make_async_copy(xt, vd, in_sem.at[5]).start()
        pltpu.make_async_copy(xd3, d3.at[0], in_sem.at[6]).start()
        pltpu.make_async_copy(xd4, d3.at[1], in_sem.at[7]).start()

    bar = pltpu.get_barrier_semaphore()

    def greet(i, _):
        pl.semaphore_signal(bar, inc=1, device_id=(p, lax.rem(r + TEAM * i, R)), device_id_type=MESH)
        return 0

    lax.fori_loop(1, n, greet, 0)
    pl.semaphore_wait(bar, n - 1)

    row_of = lax.broadcasted_iota(jnp.int32, (H, C), 0)
    row_of1 = lax.broadcasted_iota(jnp.int32, (H, q4), 0)

    def column(j):
        return pl.ds(pl.multiple_of(j * H, H), H)

    for j in range(TEAM):
        for a in range(3):
            rb[j, a, 0:H, :] = jnp.zeros((H, C), half)
            rb[j, a, H * (W + 1) : H * (W + 2), :] = jnp.zeros((H, C), half)
            r1[j, a, 0:H, :] = jnp.zeros((H, 3 * q4), half)
            r1[j, a, H * (W - 1) :, :] = jnp.zeros((H, 3 * q4), half)

    loads["d5"].wait()
    loads["d5e"].wait()
    for j in range(TEAM):

        def body(c, carry):
            for u in range(2):
                i = c * 2 + u
                here = pl.ds(pl.multiple_of(H + i * H, H), H)
                v = d5[j, column(i), :].astype(f32)
                rb[j, 1, here, :] = v.astype(half)
                rb[j, 0, here, :] = (jnp.where(row_of == 0, d5e[j, 0, i], pltpu.roll(v, 1, 0)) * msk[j, 0]).astype(half)
                rb[j, 2, here, :] = (
                    jnp.where(row_of == H - 1, d5e[j, 1, i], pltpu.roll(v, H - 1, 0)) * msk[j, 1]
                ).astype(half)
            return carry

        lax.fori_loop(0, W // 2, body, 0)
    loads["h"].wait()

    @pl.when(task)
    def _():
        pltpu.make_async_copy(xp, vb, in_sem.at[3]).wait()
        pltpu.make_async_copy(xv, vc, in_sem.at[4]).wait()
        pltpu.make_async_copy(xt, vd, in_sem.at[5]).wait()
        pltpu.make_async_copy(xd3, d3.at[0], in_sem.at[6]).wait()
        pltpu.make_async_copy(xd4, d3.at[1], in_sem.at[7]).wait()

    @pl.when(jnp.logical_not(task))
    def _():
        vb[...] = va[...]

    for tap in range(9):
        a, c = 2 - tap // 3, 2 - tap % 3
        acc = None
        for j in range(TEAM):
            term = dot_tn(vb[j], rb[j, a, H * c : H * c + pix, :])
            acc = term if acc is None else acc + term
        pm[tap * C : (tap + 1) * C, :] = acc.astype(half)

    pltpu.make_async_copy(xu, vb, in_sem.at[8]).start()
    pltpu.make_async_copy(xd1, d1, in_sem.at[9]).start()
    pltpu.make_async_copy(xd1e, d1e, in_sem.at[10]).start()

    def group(index, src, mine, rows):
        moves = []
        for d in range(1, n):
            to = lax.rem(z + d, n)
            moves.append(
                pltpu.make_async_remote_copy(
                    src_ref=src.at[pl.ds(pl.multiple_of(to * rows, 16), rows)],
                    dst_ref=mine.at[z],
                    send_sem=s_sem.at[index, d],
                    recv_sem=r_sem.at[index, z],
                    device_id=(p, TEAM * to + e),
                    device_id_type=MESH,
                )
            )
        return moves

    rows_m, rows_i, rows_t = 9 * C // n, 2 * C // n, C // n
    main = group(0, pm, am, rows_m)
    for move in main:
        move.start()

    @pl.when(task)
    def _():
        for part, value in ((0, va), (1, vc)):
            acc = None
            for j in range(TEAM):
                term = dot_tn(value[j], d3[0, j])
                acc = term if acc is None else acc + term
            pi_[part * C : (part + 1) * C, :] = acc.astype(half)
        acc = None
        for j in range(TEAM):
            term = dot_tn(vd[j], d3[1, j])
            acc = term if acc is None else acc + term
        pt[...] = acc.astype(half)
        for move in group(1, pi_, ai, rows_i) + group(2, pt, at, rows_t):
            move.start()

    pltpu.make_async_copy(xu, vb, in_sem.at[8]).wait()
    pltpu.make_async_copy(xd1, d1, in_sem.at[9]).wait()
    pltpu.make_async_copy(xd1e, d1e, in_sem.at[10]).wait()
    for j in range(TEAM):

        def body1(i, carry):
            v = d1[j, column(i), :].astype(f32)
            three = (
                (jnp.where(row_of1 == 0, d1e[j, 0, i], pltpu.roll(v, 1, 0)) * msk[j, 0][:, 0:q4]).astype(half),
                v.astype(half),
                (jnp.where(row_of1 == H - 1, d1e[j, 1, i], pltpu.roll(v, H - 1, 0)) * msk[j, 1][:, 0:q4]).astype(half),
            )
            for a in range(3):
                r1[j, a, column(i), q4 : 2 * q4] = three[a]
            return carry

        lax.fori_loop(0, W, body1, 0)
        for a in range(3):
            r1[j, a, H : W * H, 0:q4] = r1[j, a, 0 : (W - 1) * H, q4 : 2 * q4]
            r1[j, a, 0 : (W - 1) * H, 2 * q4 : 3 * q4] = r1[j, a, H : W * H, q4 : 2 * q4]
    for a in range(3):
        acc = None
        for j in range(TEAM):
            term = dot_tn(vb[j], r1[j, 2 - a])
            acc = term if acc is None else acc + term
        for c in range(3):
            p1[(3 * a + c) * C : (3 * a + c + 1) * C, :] = acc[:, (2 - c) * q4 : (3 - c) * q4].astype(half)
    one = group(3, p1, a1, rows_m)
    for move in one:
        move.start()

    def reduce(index, src, mine, rows, dst):
        for d in range(1, n):
            s = lax.rem(z + d, n)
            arrived(mine.at[s], r_sem.at[index, s])
        mine[z] = src[pl.ds(pl.multiple_of(z * rows, 16), rows), :]
        acc = mine[0].astype(f32)
        for s in range(1, n):
            acc = acc + mine[s].astype(f32)
        dst[...] = acc.astype(dst.dtype)

    reduce(0, pm, am, rows_m, gm)

    @pl.when(task)
    def _():
        reduce(1, pi_, ai, rows_i, gi)
        reduce(2, pt, at, rows_t, gt)

    @pl.when(jnp.logical_not(task))
    def _():
        gi[...] = jnp.zeros(gi.shape, gi.dtype)
        gt[...] = jnp.zeros(gt.shape, gt.dtype)

    reduce(3, p1, a1, rows_m, g1)
    for move in main + one:
        move.wait_send()

    @pl.when(task)
    def _():
        for move in group(1, pi_, ai, rows_i) + group(2, pt, at, rows_t):
            move.wait_send()


def per_device(cfg, section_in, image_start, pool_choice, conv_shared, task_in, task_mid, task_conv, bn_gain, bn_bias):
    M, G, H, W, C, T, n = cfg["M"], cfg["G"], cfg["H"], cfg["W"], cfg["C"], cfg["T"], cfg["n"]
    R = M * G
    pix = H * W
    part = pix // M
    rows_total = H * G
    norms = 2 + 3 * T
    CW = C * (1 + T)
    p = lax.axis_index("pipe")
    r = lax.axis_index("rows")
    b, m = r // M, r % M
    sec = section_in[0].reshape(M, part, CW)
    hp = pool_choice.shape[1]
    place = jnp.arange(4, dtype=jnp.int32).reshape(2, 1, 2)
    picked = pool_choice[:, :, None, :, None] == place[None, None]
    sel = jnp.broadcast_to(picked.reshape(M, part, 1), (M, part, 128)).astype(half)

    ones = jnp.ones((M, 1), jnp.int32)
    padded = jnp.concatenate([ones, image_start[:, 1:], ones], 1)
    links = 1.0 - lax.dynamic_slice_in_dim(padded, b * H, H + 1, 1).astype(f32)
    both = jnp.stack([links[:, :-1], links[:, 1:]], 1)
    team_masks = jnp.broadcast_to(both[..., None], (M, 2, H, C))
    own_masks = lax.dynamic_index_in_dim(team_masks, m, 0, keepdims=False)

    cm, cm_t, spread, edge, pool = tables(M, G, H, W)
    sds = jax.ShapeDtypeStruct
    exchange = [
        sds((TEAM, pix, C), half),
        sds((TEAM, pix, C), half),
        sds((TEAM, pix, C), half),
        sds((TEAM, pix, C), half),
        sds((TEAM, pix, C), half),
        sds((TEAM, pix, C), half),
        sds((TEAM, 2, W, 1, C), f32),
        sds((TEAM, pix, C), half),
        sds((TEAM, pix, C), half),
        sds((TEAM, pix, C // TEAM), half),
        sds((TEAM, 2, W, 1, C // TEAM), f32),
    ]
    dma = pltpu.SemaphoreType.DMA
    vm = pltpu.VMEM
    win = pix // 4 + 32
    outs = pl.pallas_call(
        functools.partial(section_kernel, cfg),
        name="sections",
        out_shape=[sds((M, part, CW), half), sds((2 * norms, C), f32)] + exchange,
        in_specs=[ANY, ANY] + [VMEM] * 8 + [ANY] * 4,
        out_specs=[ANY, VMEM] + [ANY] * len(exchange),
        scratch_shapes=[
            vm((2, 9 * C, C), half),
            vm((T, 2 * C, C), half),
            vm((T, C, C), half),
            vm((T, 9 * C, C), half),
            vm((pix, CW), half),
            vm((2, pix, CW), half),
            vm((pix, 128), half),
            vm((pix, 128), half),
            vm((2, 32, C), half),
            vm((2, 32, 128), half),
            vm((2, W, 1, C), f32),
            vm((win, CW), half),
            vm((win, CW), half),
            vm((3, pix + 2 * H, C), half),
            vm((norms, pix, C), f32),
            vm((EDGES, 2, W, 1, C), f32),
            vm((EDGES, 2, W, 1, C), f32),
            vm((2 * norms, 2, C), f32),
            vm((G, 2 * norms, 2, C), f32),
            vm((pix, C), half),
            vm((pix, C), half),
            vm((W, 2, C), f32),
            vm((T, pix, C), half),
            vm((T, pix, C), half),
            vm((pix, CW), half),
            vm((T, pix, C), f32),
            vm((pix, C), f32),
            vm((T, pix, C), half),
            vm((T, 2, W, 1, C), f32),
            vm((pix, C), half),
            vm((2, W, 1, C), f32),
            vm((T, pix, C), half),
            vm((T, pix, C), half),
            vm((TEAM, pix, C // TEAM), half),
            vm((TEAM, 2, W, 1, C // TEAM), f32),
            vm((2 * norms, C), f32),
            vm((M, 2 * norms, C), f32),
            dma((4 + T,)),
            dma((7, M)),
            dma((5, M)),
            dma((EDGES, 2)),
            dma((EDGES, 2)),
            dma((2 * norms, G)),
            dma((2 * norms, G)),
            dma((3,)),
            dma((3,)),
            dma((2, M)),
            dma((2, M)),
            dma((M,)),
            dma((M,)),
            dma((39,)),
            dma((39, TEAM)),
        ],
        compiler_params=pltpu.CompilerParams(
            collective_id=0, has_side_effects=True, vmem_limit_bytes=63 * 2**20
        ),
    )(sec, sel, own_masks, cm, cm_t, spread, edge, pool, bn_gain[0], bn_bias[0], conv_shared[0], task_in[0], task_mid[0], task_conv[0])
    result, bn_grads = outs[:2]

    rows_m, rows_i, rows_t = 9 * C // n, 2 * C // n, C // n
    q4 = C // TEAM
    grads = pl.pallas_call(
        functools.partial(gradient_kernel, cfg),
        name="kernel_gradients",
        out_shape=[sds((rows_m, C), half), sds((rows_m, q4), half), sds((rows_i, C), half), sds((rows_t, C), half)],
        in_specs=[VMEM] + [ANY] * 11,
        out_specs=[VMEM] * 4,
        scratch_shapes=[
            vm((TEAM, pix, C), half),
            vm((TEAM, pix, C), half),
            vm((TEAM, pix, C), half),
            vm((TEAM, pix, C), half),
            vm((TEAM, pix, C), half),
            vm((TEAM, 2, W, 1, C), f32),
            vm((TEAM, 3, pix + 2 * H, C), half),
            vm((TEAM, 3, pix, 3 * q4), half),
            vm((TEAM, pix, q4), half),
            vm((TEAM, 2, W, 1, q4), f32),
            vm((2, TEAM, pix, C), half),
            vm((9 * C, C), half),
            vm((9 * C, q4), half),
            vm((2 * C, C), half),
            vm((C, C), half),
            vm((n, rows_m, C), half),
            vm((n, rows_m, q4), half),
            vm((n, rows_i, C), half),
            vm((n, rows_t, C), half),
            dma((11,)),
            dma((4, n)),
            dma((4, n)),
        ],
        compiler_params=pltpu.CompilerParams(
            collective_id=1, has_side_effects=True, vmem_limit_bytes=60 * 2**20
        ),
    )(team_masks, *outs[2:])

    gm, g1, gi, gt = grads
    pieces = [
        gm.reshape(TEAM, -1),
        g1.reshape(TEAM, -1),
        gi.reshape(TEAM, -1),
        gt.reshape(TEAM, -1),
    ]
    packed = jnp.concatenate(pieces, 1)
    teams = [[TEAM * i + j for j in range(TEAM)] for i in range(R // TEAM)]
    swapped = lax.all_to_all(packed, "rows", 0, 0, axis_index_groups=teams, tiled=False).astype(f32)
    sizes = [v.shape[1] for v in pieces]
    o = [0, sizes[0], sizes[0] + sizes[1], sizes[0] + sizes[1] + sizes[2], sum(sizes)]
    mains = swapped[:, o[0] : o[1]]
    firsts = swapped[:, o[1] : o[2]].reshape(TEAM, -1, q4).transpose(1, 0, 2).reshape(-1)
    conv_grad = jnp.stack([firsts, mains[T]])
    return (
        result.reshape(1, M, part // W, W, CW),
        conv_grad[None],
        swapped[:T, o[2] : o[3]][None],
        swapped[:T, o[3] : o[4]][None],
        mains[:T][None],
        bn_grads[None, :norms],
        bn_grads[None, norms:],
    )


def solution(mesh):
    in_specs = (
        P("pipe", None, "rows", None, None),
        P(),
        P(None, "rows", None),
        P("pipe", None, None, None),
        P("pipe", None, None, None),
        P("pipe", None, None, None),
        P("pipe", None, None, None),
        P("pipe", None, None),
        P("pipe", None, None),
    )
    out_specs = (
        P("pipe", None, "rows", None, None),
        P("pipe", None, "rows"),
        P("pipe", None, "rows"),
        P("pipe", None, "rows"),
        P("pipe", None, "rows"),
        P("pipe", None, None),
        P("pipe", None, None),
    )
    bands = mesh.shape["rows"]

    def step(section_in, image_start, pool_choice, conv_shared, task_in, task_mid, task_conv, bn_gain, bn_bias):
        M = section_in.shape[1]
        G = bands // M
        cfg = dict(
            M=M,
            G=G,
            H=section_in.shape[2] // G,
            W=section_in.shape[3],
            C=conv_shared.shape[3],
            T=task_in.shape[1],
            n=bands // TEAM,
            to_all=frozenset(range(0, 8)) | frozenset(range(31, 39)),
        )
        return jax.shard_map(
            functools.partial(per_device, cfg), mesh=mesh, in_specs=in_specs, out_specs=out_specs, check_vma=False
        )(section_in, image_start, pool_choice, conv_shared, task_in, task_mid, task_conv, bn_gain, bn_bias)

    return step
```

```python
import functools

import jax
import jax.numpy as jnp
import numpy as np
from jax import lax
from jax.experimental import pallas as pl
from jax.experimental.pallas import tpu as pltpu
from jax.sharding import PartitionSpec as P

MESH = pl.DeviceIdType.MESH
half = jnp.bfloat16
f32 = jnp.float32
epsilon = 1e-05
TEAM = 4

ANY = pl.BlockSpec(memory_space=pl.ANY)
VMEM = pl.BlockSpec(memory_space=pltpu.VMEM)


def sigmoid(x):
    return 0.5 * jnp.tanh(0.5 * x) + 0.5


def dot(a, b):
    return jnp.dot(a, b, preferred_element_type=f32)


def dot_nt(a, b):
    return lax.dot_general(a, b, (((1,), (1,)), ((), ())), preferred_element_type=f32)


def dot_tn(a, b):
    return lax.dot_general(a, b, (((0,), (0,)), ((), ())), preferred_element_type=f32)


class Remote:
    def __init__(self, src, dst, send, recv, to):
        self.src, self.dst, self.send, self.recv, self.to = src, dst, send, recv, to
        self.local = to == lax.axis_index("rows")

    def remote(self):
        return pltpu.make_async_remote_copy(
            src_ref=self.src,
            dst_ref=self.dst,
            send_sem=self.send,
            recv_sem=self.recv,
            device_id=(lax.axis_index("pipe"), self.to),
            device_id_type=MESH,
        )

    def start(self):
        @pl.when(self.local)
        def _():
            pltpu.make_async_copy(self.src, self.dst, self.recv).start()

        @pl.when(jnp.logical_not(self.local))
        def _():
            self.remote().start()

    def sent(self):
        @pl.when(jnp.logical_not(self.local))
        def _():
            self.remote().wait_send()


def arrived(dst, sem):
    pltpu.make_async_copy(dst, dst, sem).wait()


EDGES = 13


def section_kernel(cfg, *refs):
    M, G, H, W, C, T = cfg["M"], cfg["G"], cfg["H"], cfg["W"], cfg["C"], cfg["T"]
    R = M * G
    pix = H * W
    part = pix // M
    count = float(pix * G)
    norms = 2 + 3 * T
    direct = cfg["direct"]
    (sec, sel, msks, perm, perm_t, spread, spread_edge, pool, gain, bias, wc, wi, wm, wt) = refs[:14]
    (out, bng, xu, xh, xp, xt, xv, xd5, xd5e, xd4, xd3, xd1, xd1e) = refs[14:27]
    refs = refs[27:]
    if direct:
        (gm, g1, gi, gt, am, a1, ai, at) = refs[:8]
        (d4, d5e, d1e, l_sem, rs_s, rs_r, o_sem) = refs[-7:]
        refs = refs[8:-7]
    (
        kc, ki, km, kt, rin, field, selin, chosen, uh, selh, uedge, px, ps, rb, ys, esend, erecv, ssend, srecv,
        h1, h2, h2e, t1, pr, res, dz, dh, dy5, dy5e, dy2, dy2e, dy4, dy3, dy1, dy1e, bn, bnr,
        go, w_sem, in_s, in_r, ed_s, ed_r, st_s, st_r, pp_s, pp_r, out_s, out_r, bn_s, bn_r, x_s, x_r,
    ) = refs
    p = lax.axis_index("pipe")
    r = lax.axis_index("rows")
    b, m = r // M, r % M
    e, e0 = m, r - m
    first, last = b == 0, b == G - 1
    CW = C * (1 + T)

    loads = {}

    def load(name, src, dst, i):
        loads[name] = pltpu.make_async_copy(src, dst, w_sem.at[i])
        loads[name].start()

    load("c0", wc.at[0], kc.at[0], 0)
    load("i", wi, ki, 1)
    load("c1", wc.at[1], kc.at[1], 2)
    load("m", wm, km, 3)
    for t in range(T):
        load("t%d" % t, wt.at[t], kt.at[t], 4 + t)

    zero_col = jnp.zeros((H, C), half)
    for a in range(3):
        rb[a, 0:H, :] = zero_col
        rb[a, H * (W + 1) : H * (W + 2), :] = zero_col
    px[pix // 4 :, :] = jnp.zeros((px.shape[0] - pix // 4, CW), half)

    @pl.when(first)
    def _():
        for s in range(EDGES):
            erecv[s, 0] = jnp.zeros((W, 1, C), f32)
        uh[0] = jnp.zeros((32, C), half)
        selh[0] = jnp.zeros((32, 128), half)

    @pl.when(last)
    def _():
        for s in range(EDGES):
            erecv[s, 1] = jnp.zeros((W, 1, C), f32)
        uh[1] = jnp.zeros((32, C), half)
        selh[1] = jnp.zeros((32, 128), half)

    bar = pltpu.get_barrier_semaphore()

    def hello(side, row):
        pl.semaphore_signal(bar, inc=1, device_id=(side, row), device_id_type=MESH)

    if direct:

        def greet(i, _):
            hello(p, lax.rem(r + i, R))
            return 0

        lax.fori_loop(1, R, greet, 0)
    else:
        for d in range(1, M):
            hello(p, e0 + lax.rem(m + d, M))
        for d in range(1, G):
            hello(p, M * lax.rem(b + d, G) + m)
    hello(1 - p, r)
    tops = jnp.logical_and(m == M - 1, jnp.logical_not(last))
    bottoms = jnp.logical_and(m == 0, jnp.logical_not(first))

    @pl.when(jnp.logical_not(first))
    def _():
        hello(1 - p, r - M)
        if not direct:
            hello(p, e0 - 1)

    @pl.when(jnp.logical_not(last))
    def _():
        hello(1 - p, r + M)
        if not direct:
            hello(p, e0 + M)

    if not direct:

        @pl.when(tops)
        def _():
            for j in range(M):
                hello(p, e0 + M + j)

        @pl.when(bottoms)
        def _():
            for j in range(M):
                hello(p, e0 - M + j)

    below_me, above_me = 1 - (b + 1) // G, (b + G - 1) // G
    top_member, bottom_member = (m + 1) // M, 1 - (m + M - 1) // M
    if direct:
        pl.semaphore_wait(bar, R + below_me + above_me)
    else:
        pl.semaphore_wait(
            bar, M + G - 1 + 2 * (below_me + above_me) + M * (top_member * below_me + bottom_member * above_me)
        )

    mine = pl.ds(pl.multiple_of(part * m, 16), part)
    field_moves, rest_moves, sel_moves, edge_moves = [], [], [], ([], [])
    for d in range(M):
        j = lax.rem(m + d, M)
        to = e0 + j
        field_moves.append(Remote(sec.at[j, :, 0:C], rin.at[mine, 0:C], in_s.at[0, d], in_r.at[0, m], to))
        sel_moves.append(Remote(sel.at[j], selin.at[mine], in_s.at[2, d], in_r.at[2, m], to))
        rest_moves.append(Remote(sec.at[j, :, C:CW], rin.at[mine, C:CW], in_s.at[1, d], in_r.at[1, m], to))
    for j in range(M):
        to = e0 + j
        edge_moves[0].append(
            Remote(sec.at[j, pl.ds(part - 32, 32), 0:C], uh.at[0], in_s.at[3, j], in_r.at[3, 0], to + M)
        )
        edge_moves[0].append(Remote(sel.at[j, pl.ds(part - 32, 32)], selh.at[0], in_s.at[4, j], in_r.at[3, 1], to + M))
        edge_moves[1].append(Remote(sec.at[j, pl.ds(0, 32), 0:C], uh.at[1], in_s.at[5, j], in_r.at[4, 0], to - M))
        edge_moves[1].append(Remote(sel.at[j, pl.ds(0, 32)], selh.at[1], in_s.at[6, j], in_r.at[4, 1], to - M))

    def start_field():
        for move in field_moves:
            move.start()
        for move in rest_moves:
            move.start()

    @pl.when(tops)
    def _():
        for move in edge_moves[0]:
            move.start()

    @pl.when(bottoms)
    def _():
        for move in edge_moves[1]:
            move.start()

    @pl.when(p == 0)
    def _():
        start_field()

    for move in sel_moves:
        move.start()

    row_of = lax.broadcasted_iota(jnp.int32, (H, C), 0)
    at_top, at_bottom = row_of == 0, row_of == H - 1

    def column(j):
        return pl.ds(pl.multiple_of(j * H, H), H)

    def over_columns(body, start=0, step=2):
        def several(c, carry):
            for u in range(step):
                carry = body(c * step + u, carry)
            return carry

        return lax.fori_loop(0, W // step, several, start)

    def build(j, value, above, below, up, down):
        here = pl.ds(pl.multiple_of(H + j * H, H), H)
        rb[1, here, :] = value.astype(half)
        rb[0, here, :] = (jnp.where(at_top, above, pltpu.roll(value, 1, 0)) * up).astype(half)
        rb[2, here, :] = (jnp.where(at_bottom, below, pltpu.roll(value, H - 1, 0)) * down).astype(half)

    def conv(kernel):
        total = None
        for tap in range(9):
            a, c = tap // 3, tap % 3
            term = dot(rb[a, H * c : H * c + pix, :], kernel[tap * C : (tap + 1) * C, :])
            total = term if total is None else total + term
        return total

    def conv_t(kernel):
        total = None
        for tap in range(9):
            a, c = tap // 3, tap % 3
            term = dot_nt(rb[a, H * c : H * c + pix, :], kernel[(8 - tap) * C : (9 - tap) * C, :])
            total = term if total is None else total + term
        return total

    def folded(total):
        return jnp.sum(total, 0, keepdims=True)

    def fold(x):
        return jnp.sum(x.reshape(H // 8, 8, C), 0)

    zero8 = jnp.zeros((8, C), f32)

    def edge_copy(slot, side):
        to = r - M if side == 0 else r + M
        return pltpu.make_async_remote_copy(
            src_ref=esend.at[slot, side],
            dst_ref=erecv.at[slot, 1 - side],
            send_sem=ed_s.at[slot, side],
            recv_sem=ed_r.at[slot, 1 - side],
            device_id=(p, to),
            device_id_type=MESH,
        )

    def send_edges(slot):
        @pl.when(jnp.logical_not(first))
        def _():
            edge_copy(slot, 0).start()

        @pl.when(jnp.logical_not(last))
        def _():
            edge_copy(slot, 1).start()

    def get_edges(slot):
        @pl.when(jnp.logical_not(first))
        def _():
            arrived(erecv.at[slot, 0], ed_r.at[slot, 0])

        @pl.when(jnp.logical_not(last))
        def _():
            arrived(erecv.at[slot, 1], ed_r.at[slot, 1])

    def finish_edges(slot):
        @pl.when(jnp.logical_not(first))
        def _():
            edge_copy(slot, 0).wait_send()

        @pl.when(jnp.logical_not(last))
        def _():
            edge_copy(slot, 1).wait_send()

    def stat_copy(slot, n, d):
        to = M * lax.rem(b + d, G) + m
        return pltpu.make_async_remote_copy(
            src_ref=ssend.at[pl.ds(slot, n)],
            dst_ref=srecv.at[b, pl.ds(slot, n)],
            send_sem=st_s.at[slot, d],
            recv_sem=st_r.at[slot, b],
            device_id=(p, to),
            device_id_type=MESH,
        )

    def send_sums(slot, n):
        srecv[b, slot : slot + n] = ssend[slot : slot + n]
        for d in range(1, G):
            stat_copy(slot, n, d).start()

    sums_sent = []

    def get_sums(slot, n):
        sums_sent.append((slot, n))
        for d in range(1, G):
            s = lax.rem(b + d, G)
            arrived(srecv.at[s, pl.ds(slot, n)], st_r.at[slot, s])

    def total(slot):
        acc = srecv[0, slot]
        for g in range(1, G):
            acc = acc + srecv[g, slot]
        return acc

    def put_sums(slot, s, q):
        ssend[slot] = jnp.concatenate([folded(s), folded(q)], 0)

    x_moves = []
    kept = {0: [], 1: []}

    def post(index, src, dst, target, keep=None):
        move = Remote(src, dst.at[e], x_s.at[index], x_r.at[index - (target if index in cfg["to_all"] else 0), e], e0 + target)
        x_moves.append(move)
        if keep is None:
            move.start()
        else:
            kept[keep].append(move)

            @pl.when(p == 1)
            def _():
                move.start()

    def send_kept(group):
        for move in kept[group]:
            move.start()


    def moments(k, slot, edge=None):
        def body(j, carry):
            s, q = carry
            y = ys[k, column(j), :]
            if edge is not None:
                esend[edge, 0, j] = y[0:1]
                esend[edge, 1, j] = y[H - 1 : H]
            return s + fold(y), q + fold(y * y)

        s, q = over_columns(body, (zero8, zero8))
        put_sums(slot, s, q)

    norm = {}

    def norm_rows(k, slot):
        acc = total(slot)
        mean = acc[0:1] / count
        rs = lax.rsqrt(acc[1:2] / count - mean * mean + epsilon)
        scale = gain[k : k + 1, :] * rs
        norm[k] = (mean, rs, scale, bias[k : k + 1, :])

    def normed(k, y):
        mean, rs, scale, shift = norm[k]
        return (y - mean) * scale + shift

    def silu(x):
        return x * sigmoid(x)

    def silu_slope(x):
        s = sigmoid(x)
        return s * (1.0 + x * (1.0 - s))

    def pair(slot, j):
        return jnp.concatenate([erecv[slot, 0, j], erecv[slot, 1, j]], 0)

    nt = 2 + 3 * T
    F3, F4, F5 = 2, 2 + T, 2 + 2 * T

    def wait_field(kind, buffer):
        for k in range(M):
            arrived(buffer(k), in_r.at[kind, k])

    @pl.when(jnp.logical_not(first))
    def _():
        arrived(uh.at[0], in_r.at[3, 0])
        arrived(selh.at[0], in_r.at[3, 1])

    @pl.when(jnp.logical_not(last))
    def _():
        arrived(uh.at[1], in_r.at[4, 0])
        arrived(selh.at[1], in_r.at[4, 1])

    def start_of_field():
        wait_field(0, lambda k: rin.at[pl.ds(part * k, part), 0:C])
        field[p, :, 0:C] = dot(perm[...], rin[:, 0:C]).astype(half)

    def rest_of_field():
        wait_field(1, lambda k: rin.at[pl.ds(part * k, part), C:CW])
        for t in range(T):
            cols = slice((t + 1) * C, (t + 2) * C)
            field[p, :, cols] = dot(perm[...], rin[:, cols]).astype(half)

    @pl.when(p == 0)
    def _():
        start_of_field()

    wait_field(2, lambda k: selin.at[pl.ds(part * k, part)])
    chosen[...] = spread[...] * dot(perm[...], selin[...]).astype(half)

    def halo_copies():
        return (
            pltpu.make_async_remote_copy(
                src_ref=ps.at[pl.ds(pix // 4, 16), 0:C], dst_ref=px.at[pl.ds(pix // 4, 16), 0:C],
                send_sem=pp_s.at[1], recv_sem=pp_r.at[1], device_id=(1 - p, r + M), device_id_type=MESH),
            pltpu.make_async_remote_copy(
                src_ref=ps.at[pl.ds(pix // 4 + 16, 16), 0:C], dst_ref=px.at[pl.ds(pix // 4 + 16, 16), 0:C],
                send_sem=pp_s.at[2], recv_sem=pp_r.at[2], device_id=(1 - p, M * (b - 1) + m), device_id_type=MESH),
        )

    def pool_copy():
        return pltpu.make_async_remote_copy(
            src_ref=ps.at[pl.ds(0, pix // 4)], dst_ref=px.at[pl.ds(0, pix // 4)],
            send_sem=pp_s.at[0], recv_sem=pp_r.at[0], device_id=(1 - p, r), device_id_type=MESH)

    @pl.when(p == 1)
    def _():
        pl.semaphore_wait(go, 1)
        start_field()
        start_of_field()
        rest_of_field()
        arrived(px.at[pl.ds(0, pix // 4)], pp_r.at[0])

        @pl.when(jnp.logical_not(first))
        def _():
            arrived(px.at[pl.ds(pix // 4, 16), 0:C], pp_r.at[1])

        @pl.when(jnp.logical_not(last))
        def _():
            arrived(px.at[pl.ds(pix // 4 + 16, 16), 0:C], pp_r.at[2])

        for t in range(1 + T):
            cols = slice(t * C, (t + 1) * C)
            field[0, :, cols] = dot(chosen[...], px[:, cols]).astype(half)
        edges = spread_edge[...] * jnp.concatenate([selh[0], selh[1]], 0)
        both = dot(edges, px[:, 0:C]).astype(half)
        uh[0] = both[0:32]
        uh[1] = both[32:64]

    above = uh[0].astype(f32)
    below = uh[1].astype(f32)
    for j in range(W):
        uedge[0, j] = above[32 - W + j : 33 - W + j]
        uedge[1, j] = below[j : j + 1]

    up = msks[m, 0]
    down = msks[m, 1]

    def body_u(j, carry):
        build(j, field[0, column(j), 0:C].astype(f32), uedge[0, j], uedge[1, j], up, down)
        return carry

    over_columns(body_u)
    loads["c0"].wait()
    ys[0] = conv(kc.at[0])
    moments(0, 0, 0)
    send_sums(0, 1)
    send_edges(0)

    @pl.when(p == 0)
    def _():
        rest_of_field()
        pl.semaphore_signal(go, inc=1, device_id=(1 - p, r), device_id_type=MESH)

    for q in range(TEAM):
        post(q, field.at[0, :, 0:C], xu, q)
    for t in range(T):
        post(8 + t, field.at[0, :, (t + 1) * C : (t + 2) * C], xv, t)
    get_sums(0, 1)
    get_edges(0)
    norm_rows(0, 0)

    def body_h1(j, carry):
        value = silu(normed(0, ys[0, column(j), :]))
        side = silu(normed(0, pair(0, j)))
        h1[column(j), :] = value.astype(half)
        build(j, value, side[0:1], side[1:2], up, down)
        return carry

    over_columns(body_h1)
    for q in range(TEAM):
        post(4 + q, h1, xh, q)

    loads["i"].wait()
    for t in range(T):
        k = 2 + 3 * t
        ys[k] = dot(h1[...], ki[t, 0:C, :]) + dot(field[0, :, (t + 1) * C : (t + 2) * C], ki[t, C : 2 * C, :])
        moments(k, F3 + t)
    send_sums(F3, T)
    loads["c1"].wait()
    ys[1] = conv(kc.at[1])
    moments(1, 1, 1)
    send_sums(1, 1)
    send_edges(1)

    get_sums(F3, T)
    loads["m"].wait()
    for t in range(T):
        k = 2 + 3 * t
        norm_rows(k, F3 + t)

        def body_t1(j, carry):
            t1[t, column(j), :] = silu(normed(k, ys[k, column(j), :])).astype(half)
            return carry

        over_columns(body_t1)
        post(11 + t, t1.at[t], xt, t, 0)
        ys[k + 1] = dot(t1[t], km[t])
        moments(k + 1, F4 + t, 2 + t)
    send_sums(F4, T)
    for t in range(T):
        send_edges(2 + t)

    get_sums(1, 1)
    get_edges(1)
    norm_rows(1, 1)

    def body_h2(j, carry):
        value = silu(normed(1, ys[1, column(j), :])).astype(half)
        h2[column(j), :] = value
        res[column(j), 0:C] = value
        side = silu(normed(1, pair(1, j))).astype(half).astype(f32)
        h2e[j] = side
        return carry

    over_columns(body_h2)
    get_sums(F4, T)
    for t in range(T):
        k = 3 + 3 * t
        get_edges(2 + t)
        norm_rows(k, F4 + t)

        def body_p(j, carry):
            gate = sigmoid(normed(k, ys[k, column(j), :]))
            value = gate * h2[column(j), :].astype(f32)
            side = sigmoid(normed(k, pair(2 + t, j))) * h2e[j]
            pr[t, column(j), :] = value.astype(half)
            build(j, value, side[0:1], side[1:2], up, down)
            return carry

        over_columns(body_p)
        post(14 + t, pr.at[t], xp, t, 0)
        loads["t%d" % t].wait()
        ys[k + 1] = conv(kt.at[t])
        moments(k + 1, F5 + t, 5 + t)
    send_sums(F5, T)
    for t in range(T):
        send_edges(5 + t)
    get_sums(F5, T)
    for t in range(T):
        k = 4 + 3 * t
        get_edges(5 + t)
        norm_rows(k, F5 + t)

        def body_q(j, carry):
            res[column(j), (t + 1) * C : (t + 2) * C] = silu(normed(k, ys[k, column(j), :])).astype(half)
            return carry

        over_columns(body_q)

    def out_moves(which):
        cols = slice(0, C) if which == 0 else slice(C, CW)
        moves = []
        for d in range(M):
            k = lax.rem(m + d, M)
            rows = pl.ds(pl.multiple_of(part * k, 16), part)
            moves.append(
                Remote(rin.at[rows, cols], out.at[m, :, cols], out_s.at[which, d], out_r.at[which, m], e0 + k)
            )
        return moves

    def send_result(which):
        for t in range(0, 1) if which == 0 else range(1, 1 + T):
            cols = slice(t * C, (t + 1) * C)
            rin[:, cols] = dot(perm_t[...], res[:, cols]).astype(half)
        for move in out_moves(which):
            move.start()

    @pl.when(p == 0)
    def _():
        for t in range(1 + T):
            cols = slice(t * C, (t + 1) * C)
            ps[:, cols] = dot(pool[...], res[:, cols]).astype(half)
        pool_copy().start()

        @pl.when(jnp.logical_not(last))
        def _():
            halo_copies()[0].start()

        @pl.when(jnp.logical_not(first))
        def _():
            halo_copies()[1].start()

        send_kept(0)
        pool_copy().wait_send()

        @pl.when(jnp.logical_not(last))
        def _():
            halo_copies()[0].wait_send()

        @pl.when(jnp.logical_not(first))
        def _():
            halo_copies()[1].wait_send()

        arrived(px.at[pl.ds(0, pix // 4)], pp_r.at[0])
        for t in range(1 + T):
            cols = slice(t * C, (t + 1) * C)
            field[1, :, cols] = (dot(spread[...], px[:, cols]) * 0.25).astype(half)
        send_kept(1)

    @pl.when(p == 1)
    def _():
        send_result(0)
        send_result(1)

    B3, B4, B5 = nt + F3, nt + F4, nt + F5
    back = {}

    def back_rows(k, slot):
        acc = total(slot)
        mean, rs, scale, shift = norm[k]
        slope = -scale * rs * acc[1:2] / count
        back[k] = (scale, slope, -scale * acc[0:1] / count - slope * mean)
        bn[k : k + 1, :] = acc[1:2]
        bn[norms + k : norms + k + 1, :] = acc[0:1]

    def grad_pre(k, dzv, y):
        scale, slope, rest = back[k]
        return scale * dzv + slope * y + rest

    def hat(k, y):
        mean, rs, scale, shift = norm[k]
        return (y - mean) * rs

    for t in range(T):
        k = 4 + 3 * t

        def body_dz5(j, carry):
            s, q = carry
            y = ys[k, column(j), :]
            g = field[1, column(j), (t + 1) * C : (t + 2) * C].astype(f32)
            v = g * silu_slope(normed(k, y))
            dz[t, column(j), :] = v
            esend[8 + t, 0, j] = v[0:1]
            esend[8 + t, 1, j] = v[H - 1 : H]
            return s + fold(v), q + fold(v * hat(k, y))

        s, q = over_columns(body_dz5, (zero8, zero8))
        put_sums(B5 + t, s, q)
    send_sums(B5, T)
    for t in range(T):
        send_edges(8 + t)
    get_sums(B5, T)

    for t in range(T):
        k = 4 + 3 * t
        get_edges(8 + t)
        back_rows(k, B5 + t)

        def body_dy5(j, carry):
            v = grad_pre(k, dz[t, column(j), :], ys[k, column(j), :])
            side = grad_pre(k, pair(8 + t, j), pair(5 + t, j))
            dy5[t, column(j), :] = v.astype(half)
            dy5e[t, 0, j] = side[0:1]
            dy5e[t, 1, j] = side[1:2]
            build(j, v, side[0:1], side[1:2], up, down)
            return carry

        over_columns(body_dy5)
        post(17 + t, dy5.at[t], xd5, t)
        post(21 + t, dy5e.at[t], xd5e, t)
        ys[k] = conv_t(kt.at[t])

        def body_dz4(j, carry):
            s, q = carry
            dp = ys[k, column(j), :]
            y = ys[k - 1, column(j), :]
            gate = sigmoid(normed(k - 1, y))
            dgate = dp * h2[column(j), :].astype(f32)
            base = field[1, column(j), 0:C].astype(f32) if t == 0 else dh[column(j), :]
            dh[column(j), :] = base + dp * gate
            v = dgate * gate * (1.0 - gate)
            ys[k, column(j), :] = v
            return s + fold(v), q + fold(v * hat(k - 1, y))

        s, q = over_columns(body_dz4, (zero8, zero8))
        put_sums(B4 + t, s, q)
    send_sums(B4, T)

    def body_dz2(j, carry):
        s, q = carry
        y = ys[1, column(j), :]
        v = dh[column(j), :] * silu_slope(normed(1, y))
        dh[column(j), :] = v
        esend[11, 0, j] = v[0:1]
        esend[11, 1, j] = v[H - 1 : H]
        return s + fold(v), q + fold(v * hat(1, y))

    s, q = over_columns(body_dz2, (zero8, zero8))
    put_sums(nt + 1, s, q)
    send_sums(nt + 1, 1)
    send_edges(11)

    get_sums(B4, T)
    for t in range(T):
        k = 3 + 3 * t
        back_rows(k, B4 + t)

        def body_dy4(j, carry):
            dy4[t, column(j), :] = grad_pre(k, ys[k + 1, column(j), :], ys[k, column(j), :]).astype(half)
            return carry

        over_columns(body_dy4)
        post(25 + t, dy4.at[t], xd4, t)
        dz[t] = dot_nt(dy4[t], km[t])

        def body_dz3(j, carry):
            s, q = carry
            y = ys[k - 1, column(j), :]
            v = dz[t, column(j), :] * silu_slope(normed(k - 1, y))
            dz[t, column(j), :] = v
            return s + fold(v), q + fold(v * hat(k - 1, y))

        s, q = over_columns(body_dz3, (zero8, zero8))
        put_sums(B3 + t, s, q)
    send_sums(B3, T)

    get_sums(nt + 1, 1)
    get_edges(11)
    back_rows(1, nt + 1)

    def body_dy2(j, carry):
        v = grad_pre(1, dh[column(j), :], ys[1, column(j), :])
        side = grad_pre(1, pair(11, j), pair(1, j))
        dy2[column(j), :] = v.astype(half)
        dy2e[0, j] = side[0:1]
        dy2e[1, j] = side[1:2]
        build(j, v, side[0:1], side[1:2], up, down)
        return carry

    over_columns(body_dy2)
    post(20, dy2, xd5, TEAM - 1)
    post(24, dy2e, xd5e, TEAM - 1)
    dh[...] = conv_t(kc.at[1])

    get_sums(B3, T)
    for t in range(T):
        k = 2 + 3 * t
        back_rows(k, B3 + t)

        def body_dy3(j, carry):
            dy3[t, column(j), :] = grad_pre(k, dz[t, column(j), :], ys[k, column(j), :]).astype(half)
            return carry

        over_columns(body_dy3)
        post(28 + t, dy3.at[t], xd3, t)
        dh[...] += dot_nt(dy3[t], ki[t, 0:C, :])
        res[:, (t + 1) * C : (t + 2) * C] = dot_nt(dy3[t], ki[t, C : 2 * C, :]).astype(half)

    @pl.when(p == 0)
    def _():
        send_result(1)

    def body_dz1(j, carry):
        s, q = carry
        y = ys[0, column(j), :]
        v = dh[column(j), :] * silu_slope(normed(0, y))
        dh[column(j), :] = v
        esend[12, 0, j] = v[0:1]
        esend[12, 1, j] = v[H - 1 : H]
        return s + fold(v), q + fold(v * hat(0, y))

    s, q = over_columns(body_dz1, (zero8, zero8))
    put_sums(nt, s, q)
    send_sums(nt, 1)
    send_edges(12)
    get_sums(nt, 1)
    get_edges(12)
    back_rows(0, nt)

    def bn_moves():
        return [Remote(bn, bnr.at[m], bn_s.at[d], bn_r.at[m], e0 + lax.rem(m + d, M)) for d in range(M)]

    for move in bn_moves():
        move.start()

    quarter = C // TEAM

    def body_dy1(j, carry):
        v = grad_pre(0, dh[column(j), :], ys[0, column(j), :])
        side = grad_pre(0, pair(12, j), pair(0, j))
        low = v.astype(half)
        for o in range(TEAM):
            cols = slice(o * quarter, (o + 1) * quarter)
            dy1[o, column(j), :] = low[:, cols]
            dy1e[o, 0, j] = side[0:1, cols]
            dy1e[o, 1, j] = side[1:2, cols]
        build(j, v, side[0:1], side[1:2], up, down)
        return carry

    over_columns(body_dy1)
    for o in range(TEAM):
        post(31 + o, dy1.at[o], xd1, o)
        post(35 + o, dy1e.at[o], xd1e, o)
    res[:, 0:C] = conv_t(kc.at[0]).astype(half)

    @pl.when(p == 1)
    def _():
        for t in range(1 + T):
            cols = slice(t * C, (t + 1) * C)
            ps[0 : pix // 4, cols] = dot_tn(chosen[...], res[:, cols])[0 : pix // 4].astype(half)
        pool_copy().start()
        pool_copy().wait_send()

    @pl.when(p == 0)
    def _():
        send_result(0)

    if direct:
        z, n = b, R // TEAM
        q4 = quarter
        all_rows = TEAM * pix
        wide = pix + 2 * H
        task = e < T
        vb, va, vc = (kt.at[2, i * all_rows : (i + 1) * all_rows, :] for i in range(3))
        vd, d5, d3 = (kc.at[0, i * all_rows : (i + 1) * all_rows, :] for i in range(3))
        pm, p1, pi_, pt = kt.at[0], kc.at[0, :, 0:q4], ki.at[0], km.at[0]
        d1 = kt.at[1, 0:all_rows, 3 * q4 : 4 * q4]
        rows_m, rows_i, rows_t = 9 * C // R, 2 * C // R, C // R

        def band(ref, j):
            return ref.at[j * pix : (j + 1) * pix]

        def fetch(index, src, j, dst, sem):
            arrived(src.at[j], sem)
            copy = pltpu.make_async_copy(src.at[j], dst, l_sem.at[index, j])
            copy.start()
            return copy

        def rows_shifted(j, a, lo):
            if j < TEAM - 1:
                start = (3 * j + a) * wide + lo
                return kc.at[1, start : start + pix, :]
            return rb.at[a, lo : lo + pix, :]

        for j in range(TEAM - 1):
            for a in range(3):
                start = (3 * j + a) * wide
                kc[1, start : start + H, :] = zero_col
                kc[1, start + H + pix : start + wide, :] = zero_col
        got = {}
        for j in range(TEAM):
            got["d5", j] = fetch(0, xd5, j, band(d5, j), x_r.at[17 + e, j])
            got["d5e", j] = fetch(1, xd5e, j, d5e.at[j], x_r.at[21 + e, j])

        @pl.when(task)
        def _():
            for j in range(TEAM):
                fetch(3, xp, j, band(vb, j), x_r.at[14 + e, j])

        for j in range(TEAM):
            got["h", j] = fetch(2, xh, j, band(va, j), x_r.at[4, j])
        for j in range(TEAM):
            got["d5", j].wait()
            got["d5e", j].wait()

            def body_r(i, carry):
                v = kc[0, pl.ds(pl.multiple_of(all_rows + j * pix + i * H, H), H), :].astype(f32)
                three = (
                    (jnp.where(at_top, d5e[j, 0, i], pltpu.roll(v, 1, 0)) * msks[j, 0]).astype(half),
                    v.astype(half),
                    (jnp.where(at_bottom, d5e[j, 1, i], pltpu.roll(v, H - 1, 0)) * msks[j, 1]).astype(half),
                )
                for a in range(3):
                    if j < TEAM - 1:
                        here = pl.ds(pl.multiple_of((3 * j + a) * wide + H + i * H, H), H)
                        kc[1, here, :] = three[a]
                    else:
                        rb[a, pl.ds(pl.multiple_of(H + i * H, H), H), :] = three[a]
                return carry

            over_columns(body_r)
        for j in range(TEAM):
            got["h", j].wait()

        @pl.when(task)
        def _():
            for j in range(TEAM):
                pltpu.make_async_copy(xp.at[j], band(vb, j), l_sem.at[3, j]).wait()

        @pl.when(jnp.logical_not(task))
        def _():
            vb[...] = va[...]

        for tap in range(9):
            a, c = 2 - tap // 3, 2 - tap % 3
            acc = None
            for j in range(TEAM):
                term = dot_tn(band(vb, j)[...], rows_shifted(j, a, H * c)[...])
                acc = term if acc is None else acc + term
            pm[tap * C : (tap + 1) * C, :] = acc.astype(half)

        def shares(index, src, slots, rows):
            moves = []
            for d in range(R):
                to = lax.rem(r + d, R)
                moves.append(
                    Remote(
                        src.at[pl.ds(pl.multiple_of(to * rows, 16), rows)],
                        slots.at[e, z],
                        rs_s.at[index, d],
                        rs_r.at[index, n * e + z],
                        to,
                    )
                )
            return moves

        main = shares(0, pm, am, rows_m)
        for move in main:
            move.start()
        first_u = []
        for j in range(TEAM):
            first_u.append(fetch(4, xu, j, band(vb, j), x_r.at[0, j]))

        @pl.when(task)
        def _():
            copies = []
            for j in range(TEAM):
                copies.append(fetch(5, xv, j, band(vc, j), x_r.at[8 + e, j]))
                copies.append(fetch(6, xt, j, band(vd, j), x_r.at[11 + e, j]))
                copies.append(fetch(7, xd4, j, band(d4, j), x_r.at[25 + e, j]))
                copies.append(fetch(8, xd3, j, band(d3, j), x_r.at[28 + e, j]))
            for copy in copies:
                copy.wait()
            pi_[0:C, :] = dot_tn(va[...], d3[...]).astype(half)
            pi_[C : 2 * C, :] = dot_tn(vc[...], d3[...]).astype(half)
            pt[...] = dot_tn(vd[...], d4[...]).astype(half)
            for move in shares(1, pi_, ai, rows_i) + shares(2, pt, at, rows_t):
                move.start()

        for j in range(TEAM):
            got["d1", j] = fetch(9, xd1, j, band(d1, j), x_r.at[31, j])
            got["d1e", j] = fetch(10, xd1e, j, d1e.at[j], x_r.at[35, j])
        row_of1 = lax.broadcasted_iota(jnp.int32, (H, q4), 0)

        def near(j, a, lo, size, cols):
            start = (3 * j + a) * pix + lo
            return kt.at[1, start : start + size, cols * q4 : (cols + 1) * q4]

        for j in range(TEAM):
            got["d1", j].wait()
            got["d1e", j].wait()

        for j in range(TEAM):

            def body_r1(i, carry):
                v = kt[1, pl.ds(pl.multiple_of(j * pix + i * H, H), H), 3 * q4 : 4 * q4].astype(f32)
                three = (
                    (jnp.where(row_of1 == 0, d1e[j, 0, i], pltpu.roll(v, 1, 0)) * msks[j, 0][:, 0:q4]).astype(half),
                    v.astype(half),
                    (jnp.where(row_of1 == H - 1, d1e[j, 1, i], pltpu.roll(v, H - 1, 0)) * msks[j, 1][:, 0:q4]).astype(
                        half
                    ),
                )
                for a in range(3):
                    kt[1, pl.ds(pl.multiple_of((3 * j + a) * pix + i * H, H), H), q4 : 2 * q4] = three[a]
                return carry

            over_columns(body_r1)
            for a in range(3):
                near(j, a, 0, H, 0)[...] = jnp.zeros((H, q4), half)
                near(j, a, H, pix - H, 0)[...] = near(j, a, 0, pix - H, 1)[...]
                near(j, a, 0, pix - H, 2)[...] = near(j, a, H, pix - H, 1)[...]
                near(j, a, pix - H, H, 2)[...] = jnp.zeros((H, q4), half)
        for copy in first_u:
            copy.wait()
        for a in range(3):
            acc = None
            for j in range(TEAM):
                start = (3 * j + 2 - a) * pix
                term = dot_tn(band(vb, j)[...], kt[1, start : start + pix, 0 : 3 * q4])
                acc = term if acc is None else acc + term
            for c in range(3):
                kc[0, (3 * a + c) * C : (3 * a + c + 1) * C, 0:q4] = acc[:, (2 - c) * q4 : (3 - c) * q4].astype(half)
        one = shares(3, p1, a1, rows_m)
        for move in one:
            move.start()

        def summed(index, slots, members, rows, buffer, put, base):
            copies = []
            for q in range(members):
                for k in range(n):
                    arrived(slots.at[q, k], rs_r.at[index, n * q + k])
                    start = (n * q + k) * rows
                    copy = pltpu.make_async_copy(
                        slots.at[q, k], buffer.at[start : start + rows], l_sem.at[base + q, k]
                    )
                    copy.start()
                    copies.append(copy)
            for copy in copies:
                copy.wait()
            for q in range(members):
                acc = None
                for k in range(n):
                    start = (n * q + k) * rows
                    term = buffer[start : start + rows, :].astype(f32)
                    acc = term if acc is None else acc + term
                put(q, acc)

        stores = []

        def store(src, dst, i):
            copy = pltpu.make_async_copy(src, dst, o_sem.at[i])
            copy.start()
            stores.append(copy)

        def put_m(q, value):
            ys[q, 0:rows_m, :] = value
            store(ys.at[q, 0:rows_m, :], gm.at[q], q)

        def put_i(q, value):
            ys[TEAM + 1, q * rows_i : (q + 1) * rows_i, :] = value

        def put_t(q, value):
            ys[TEAM + 2, q * rows_t : (q + 1) * rows_t, :] = value

        def put_1(q, value):
            ys[TEAM, 0:rows_m, q * q4 : (q + 1) * q4] = value

        summed(0, am, TEAM, rows_m, kc.at[1], put_m, 11)
        summed(1, ai, T, rows_i, ki.at[1], put_i, 15)
        store(ys.at[TEAM + 1, 0 : T * rows_i, :], gi, TEAM)
        summed(2, at, T, rows_t, km.at[1], put_t, 18)
        store(ys.at[TEAM + 2, 0 : T * rows_t, :], gt, TEAM + 1)
        summed(3, a1, TEAM, rows_m, kt.at[2, :, 0:q4], put_1, 21)
        store(ys.at[TEAM, 0:rows_m, :], g1, TEAM + 2)
        for move in main + one:
            move.sent()

        @pl.when(task)
        def _():
            for move in shares(1, pi_, ai, rows_i) + shares(2, pt, at, rows_t):
                move.sent()

        for copy in stores:
            copy.wait()

    for k in range(M):
        arrived(bnr.at[k], bn_r.at[k])
    acc = bnr[0]
    for k in range(1, M):
        acc = acc + bnr[k]
    bng[...] = acc
    for k in range(M):
        arrived(out.at[k, :, 0:C], out_r.at[0, k])
        arrived(out.at[k, :, C:CW], out_r.at[1, k])
    for move in out_moves(0) + out_moves(1) + bn_moves() + field_moves + rest_moves + sel_moves:
        move.sent()

    @pl.when(tops)
    def _():
        for move in edge_moves[0]:
            move.sent()

    @pl.when(bottoms)
    def _():
        for move in edge_moves[1]:
            move.sent()

    for s in range(EDGES):
        finish_edges(s)
    for slot, n in sums_sent:
        for d in range(1, G):
            stat_copy(slot, n, d).wait_send()
    for move in x_moves:
        move.sent()
    if direct:
        return
    for j in range(TEAM):
        for index, dst in ((0, xu), (4, xh), (31, xd1), (35, xd1e)):
            arrived(dst.at[j], x_r.at[index, j])
    for t in range(T):

        @pl.when(e == t)
        def _():
            for j in range(TEAM):
                for index, dst in ((8, xv), (11, xt), (14, xp), (17, xd5), (21, xd5e), (25, xd4), (28, xd3)):
                    arrived(dst.at[j], x_r.at[index + t, j])

    @pl.when(e == TEAM - 1)
    def _():
        for j in range(TEAM):
            arrived(xd5.at[j], x_r.at[20, j])
            arrived(xd5e.at[j], x_r.at[24, j])


def tables(M, G, H, W):
    pix = H * W
    cm = np.zeros((pix, pix), np.float32)
    spread = np.zeros((pix, 128), np.float32)
    pool = np.zeros((128, pix), np.float32)
    edge = np.zeros((64, 128), np.float32)
    wide = W // 2
    own = pix // 4
    for i in range(H):
        for j in range(W):
            q = j * H + i
            cm[q, i * W + j] = 1
            w = (i // 2) * wide + j // 2
            spread[q, w] = 1
            pool[w, q] = 0.25
            if i >= H - 2:
                pool[own + j // 2, q] = 0.25
            if i < 2:
                pool[own + 16 + j // 2, q] = 0.25
    for j in range(W):
        edge[32 - W + j, own + j // 2] = 1
        edge[32 + j, own + 16 + j // 2] = 1
    return [jnp.asarray(v, half) for v in (cm, cm.T, spread, edge, pool)]


def gradient_kernel(cfg, *refs):
    M, G, H, W, C, T, n = cfg["M"], cfg["G"], cfg["H"], cfg["W"], cfg["C"], cfg["T"], cfg["n"]
    R = M * G
    pix = H * W
    q4 = C // TEAM
    (msk, xu, xh, xp, xt, xv, xd5, xd5e, xd4, xd3, xd1, xd1e) = refs[:12]
    (gm, g1, gi, gt) = refs[12:16]
    (va, vb, vc, vd, d5, d5e, rb, r1, d1, d1e, d3, pm, p1, pi_, pt, am, a1, ai, at, in_sem, s_sem, r_sem) = refs[16:]
    p = lax.axis_index("pipe")
    r = lax.axis_index("rows")
    e = r % TEAM
    z = r // TEAM
    task = e < T

    loads = {}

    def load(name, src, dst, i):
        loads[name] = pltpu.make_async_copy(src, dst, in_sem.at[i])
        loads[name].start()

    load("d5", xd5, d5, 0)
    load("d5e", xd5e, d5e, 1)
    load("h", xh, va, 2)

    @pl.when(task)
    def _():
        pltpu.make_async_copy(xp, vb, in_sem.at[3]).start()
        pltpu.make_async_copy(xv, vc, in_sem.at[4]).start()
        pltpu.make_async_copy(xt, vd, in_sem.at[5]).start()
        pltpu.make_async_copy(xd3, d3.at[0], in_sem.at[6]).start()
        pltpu.make_async_copy(xd4, d3.at[1], in_sem.at[7]).start()

    bar = pltpu.get_barrier_semaphore()

    def greet(i, _):
        pl.semaphore_signal(bar, inc=1, device_id=(p, lax.rem(r + TEAM * i, R)), device_id_type=MESH)
        return 0

    lax.fori_loop(1, n, greet, 0)

    row_of = lax.broadcasted_iota(jnp.int32, (H, C), 0)
    row_of1 = lax.broadcasted_iota(jnp.int32, (H, q4), 0)

    def column(j):
        return pl.ds(pl.multiple_of(j * H, H), H)

    for j in range(TEAM):
        for a in range(3):
            rb[j, a, 0:H, :] = jnp.zeros((H, C), half)
            rb[j, a, H * (W + 1) : H * (W + 2), :] = jnp.zeros((H, C), half)
            r1[j, a, 0:H, :] = jnp.zeros((H, 3 * q4), half)
            r1[j, a, H * (W - 1) :, :] = jnp.zeros((H, 3 * q4), half)

    loads["d5"].wait()
    loads["d5e"].wait()
    for j in range(TEAM):

        def body(c, carry):
            for u in range(2):
                i = c * 2 + u
                here = pl.ds(pl.multiple_of(H + i * H, H), H)
                v = d5[j, column(i), :].astype(f32)
                rb[j, 1, here, :] = v.astype(half)
                rb[j, 0, here, :] = (jnp.where(row_of == 0, d5e[j, 0, i], pltpu.roll(v, 1, 0)) * msk[j, 0]).astype(half)
                rb[j, 2, here, :] = (
                    jnp.where(row_of == H - 1, d5e[j, 1, i], pltpu.roll(v, H - 1, 0)) * msk[j, 1]
                ).astype(half)
            return carry

        lax.fori_loop(0, W // 2, body, 0)
    loads["h"].wait()

    @pl.when(task)
    def _():
        pltpu.make_async_copy(xp, vb, in_sem.at[3]).wait()
        pltpu.make_async_copy(xv, vc, in_sem.at[4]).wait()
        pltpu.make_async_copy(xt, vd, in_sem.at[5]).wait()
        pltpu.make_async_copy(xd3, d3.at[0], in_sem.at[6]).wait()
        pltpu.make_async_copy(xd4, d3.at[1], in_sem.at[7]).wait()

    @pl.when(jnp.logical_not(task))
    def _():
        vb[...] = va[...]

    for tap in range(9):
        a, c = 2 - tap // 3, 2 - tap % 3
        acc = None
        for j in range(TEAM):
            term = dot_tn(vb[j], rb[j, a, H * c : H * c + pix, :])
            acc = term if acc is None else acc + term
        pm[tap * C : (tap + 1) * C, :] = acc.astype(half)

    pltpu.make_async_copy(xu, vb, in_sem.at[8]).start()
    pltpu.make_async_copy(xd1, d1, in_sem.at[9]).start()
    pltpu.make_async_copy(xd1e, d1e, in_sem.at[10]).start()

    def group(index, src, mine, rows):
        moves = []
        for d in range(1, n):
            to = lax.rem(z + d, n)
            moves.append(
                pltpu.make_async_remote_copy(
                    src_ref=src.at[pl.ds(pl.multiple_of(to * rows, 16), rows)],
                    dst_ref=mine.at[z],
                    send_sem=s_sem.at[index, d],
                    recv_sem=r_sem.at[index, z],
                    device_id=(p, TEAM * to + e),
                    device_id_type=MESH,
                )
            )
        return moves

    rows_m, rows_i, rows_t = 9 * C // n, 2 * C // n, C // n
    pl.semaphore_wait(bar, n - 1)
    main = group(0, pm, am, rows_m)
    for move in main:
        move.start()

    @pl.when(task)
    def _():
        for part, value in ((0, va), (1, vc)):
            acc = None
            for j in range(TEAM):
                term = dot_tn(value[j], d3[0, j])
                acc = term if acc is None else acc + term
            pi_[part * C : (part + 1) * C, :] = acc.astype(half)
        acc = None
        for j in range(TEAM):
            term = dot_tn(vd[j], d3[1, j])
            acc = term if acc is None else acc + term
        pt[...] = acc.astype(half)
        for move in group(1, pi_, ai, rows_i) + group(2, pt, at, rows_t):
            move.start()

    pltpu.make_async_copy(xu, vb, in_sem.at[8]).wait()
    pltpu.make_async_copy(xd1, d1, in_sem.at[9]).wait()
    pltpu.make_async_copy(xd1e, d1e, in_sem.at[10]).wait()
    for j in range(TEAM):

        def body1(i, carry):
            v = d1[j, column(i), :].astype(f32)
            three = (
                (jnp.where(row_of1 == 0, d1e[j, 0, i], pltpu.roll(v, 1, 0)) * msk[j, 0][:, 0:q4]).astype(half),
                v.astype(half),
                (jnp.where(row_of1 == H - 1, d1e[j, 1, i], pltpu.roll(v, H - 1, 0)) * msk[j, 1][:, 0:q4]).astype(half),
            )
            for a in range(3):
                r1[j, a, column(i), q4 : 2 * q4] = three[a]
            return carry

        lax.fori_loop(0, W, body1, 0)
        for a in range(3):
            r1[j, a, H : W * H, 0:q4] = r1[j, a, 0 : (W - 1) * H, q4 : 2 * q4]
            r1[j, a, 0 : (W - 1) * H, 2 * q4 : 3 * q4] = r1[j, a, H : W * H, q4 : 2 * q4]
    for a in range(3):
        acc = None
        for j in range(TEAM):
            term = dot_tn(vb[j], r1[j, 2 - a])
            acc = term if acc is None else acc + term
        for c in range(3):
            p1[(3 * a + c) * C : (3 * a + c + 1) * C, :] = acc[:, (2 - c) * q4 : (3 - c) * q4].astype(half)
    one = group(3, p1, a1, rows_m)
    for move in one:
        move.start()

    def reduce(index, src, mine, rows, dst):
        for d in range(1, n):
            s = lax.rem(z + d, n)
            arrived(mine.at[s], r_sem.at[index, s])
        mine[z] = src[pl.ds(pl.multiple_of(z * rows, 16), rows), :]
        acc = mine[0].astype(f32)
        for s in range(1, n):
            acc = acc + mine[s].astype(f32)
        dst[...] = acc.astype(dst.dtype)

    reduce(0, pm, am, rows_m, gm)

    @pl.when(task)
    def _():
        reduce(1, pi_, ai, rows_i, gi)
        reduce(2, pt, at, rows_t, gt)

    @pl.when(jnp.logical_not(task))
    def _():
        gi[...] = jnp.zeros(gi.shape, gi.dtype)
        gt[...] = jnp.zeros(gt.shape, gt.dtype)

    reduce(3, p1, a1, rows_m, g1)
    for move in main + one:
        move.wait_send()

    @pl.when(task)
    def _():
        for move in group(1, pi_, ai, rows_i) + group(2, pt, at, rows_t):
            move.wait_send()


def per_device(cfg, section_in, image_start, pool_choice, conv_shared, task_in, task_mid, task_conv, bn_gain, bn_bias):
    M, G, H, W, C, T, n = cfg["M"], cfg["G"], cfg["H"], cfg["W"], cfg["C"], cfg["T"], cfg["n"]
    R = M * G
    pix = H * W
    part = pix // M
    rows_total = H * G
    norms = 2 + 3 * T
    CW = C * (1 + T)
    p = lax.axis_index("pipe")
    r = lax.axis_index("rows")
    b, m = r // M, r % M
    sec = section_in[0].reshape(M, part, CW)
    hp = pool_choice.shape[1]
    place = jnp.arange(4, dtype=jnp.int32).reshape(2, 1, 2)
    picked = pool_choice[:, :, None, :, None] == place[None, None]
    sel = jnp.broadcast_to(picked.reshape(M, part, 1), (M, part, 128)).astype(half)

    ones = jnp.ones((M, 1), jnp.int32)
    padded = jnp.concatenate([ones, image_start[:, 1:], ones], 1)
    links = 1.0 - lax.dynamic_slice_in_dim(padded, b * H, H + 1, 1).astype(f32)
    both = jnp.stack([links[:, :-1], links[:, 1:]], 1)
    team_masks = jnp.broadcast_to(both[..., None], (M, 2, H, C))

    cm, cm_t, spread, edge, pool = tables(M, G, H, W)
    sds = jax.ShapeDtypeStruct
    exchange = [
        sds((TEAM, pix, C), half),
        sds((TEAM, pix, C), half),
        sds((TEAM, pix, C), half),
        sds((TEAM, pix, C), half),
        sds((TEAM, pix, C), half),
        sds((TEAM, pix, C), half),
        sds((TEAM, 2, W, 1, C), f32),
        sds((TEAM, pix, C), half),
        sds((TEAM, pix, C), half),
        sds((TEAM, pix, C // TEAM), half),
        sds((TEAM, 2, W, 1, C // TEAM), f32),
    ]
    direct = C % (16 * R) == 0
    parts = R if direct else n
    rows_m, rows_i, rows_t = 9 * C // parts, 2 * C // parts, C // parts
    q4 = C // TEAM
    shares, share_scratch = [], []
    dma = pltpu.SemaphoreType.DMA
    if direct:
        shares = [
            sds((TEAM, rows_m, C), f32),
            sds((rows_m, C), f32),
            sds((T * rows_i, C), f32),
            sds((T * rows_t, C), f32),
            sds((TEAM, n, rows_m, C), half),
            sds((TEAM, n, rows_m, q4), half),
            sds((T, n, rows_i, C), half),
            sds((T, n, rows_t, C), half),
        ]
        share_scratch = [
            pltpu.VMEM((TEAM * pix, C), half),
            pltpu.VMEM((TEAM, 2, W, 1, C), f32),
            pltpu.VMEM((TEAM, 2, W, 1, q4), f32),
            dma((25, max(n, TEAM))),
            dma((4, R)),
            dma((4, R)),
            dma((TEAM + 3,)),
        ]
    vm = pltpu.VMEM
    win = pix // 4 + 32
    outs = pl.pallas_call(
        functools.partial(section_kernel, dict(cfg, direct=direct)),
        name="sections",
        out_shape=[sds((M, part, CW), half), sds((2 * norms, C), f32)] + exchange + shares,
        in_specs=[ANY, ANY] + [VMEM] * 8 + [ANY] * 4,
        out_specs=[ANY, VMEM] + [ANY] * (len(exchange) + len(shares)),
        scratch_shapes=[
            vm((2, 9 * C, C), half),
            vm((T, 2 * C, C), half),
            vm((T, C, C), half),
            vm((T, 9 * C, C), half),
            vm((pix, CW), half),
            vm((2, pix, CW), half),
            vm((pix, 128), half),
            vm((pix, 128), half),
            vm((2, 32, C), half),
            vm((2, 32, 128), half),
            vm((2, W, 1, C), f32),
            vm((win, CW), half),
            vm((win, CW), half),
            vm((3, pix + 2 * H, C), half),
            vm((norms, pix, C), f32),
            vm((EDGES, 2, W, 1, C), f32),
            vm((EDGES, 2, W, 1, C), f32),
            vm((2 * norms, 2, C), f32),
            vm((G, 2 * norms, 2, C), f32),
            vm((pix, C), half),
            vm((pix, C), half),
            vm((W, 2, C), f32),
            vm((T, pix, C), half),
            vm((T, pix, C), half),
            vm((pix, CW), half),
            vm((T, pix, C), f32),
            vm((pix, C), f32),
            vm((T, pix, C), half),
            vm((T, 2, W, 1, C), f32),
            vm((pix, C), half),
            vm((2, W, 1, C), f32),
            vm((T, pix, C), half),
            vm((T, pix, C), half),
            vm((TEAM, pix, C // TEAM), half),
            vm((TEAM, 2, W, 1, C // TEAM), f32),
            vm((2 * norms, C), f32),
            vm((M, 2 * norms, C), f32),
            pltpu.SemaphoreType.REGULAR,
            dma((4 + T,)),
            dma((7, M)),
            dma((5, M)),
            dma((EDGES, 2)),
            dma((EDGES, 2)),
            dma((2 * norms, G)),
            dma((2 * norms, G)),
            dma((3,)),
            dma((3,)),
            dma((2, M)),
            dma((2, M)),
            dma((M,)),
            dma((M,)),
            dma((39,)),
            dma((39, TEAM)),
        ]
        + share_scratch,
        compiler_params=pltpu.CompilerParams(
            collective_id=0, has_side_effects=True, vmem_limit_bytes=63 * 2**20
        ),
    )(sec, sel, team_masks, cm, cm_t, spread, edge, pool, bn_gain[0], bn_bias[0], conv_shared[0], task_in[0], task_mid[0], task_conv[0])
    result, bn_grads = outs[:2]

    result = result.reshape(1, M, part // W, W, CW)
    if direct:
        gm, g1, gi, gt = outs[-8:-4]
        return (
            result,
            jnp.stack([g1, gm[T]]).reshape(1, 2, -1),
            gi.reshape(1, T, -1),
            gt.reshape(1, T, -1),
            gm[:T].reshape(1, T, -1),
            bn_grads[None, :norms],
            bn_grads[None, norms:],
        )
    shapes = [sds((rows_m, C), half), sds((rows_m, q4), half), sds((rows_i, C), half), sds((rows_t, C), half)]
    slots = [(n, rows_m, C), (n, rows_m, q4), (n, rows_i, C), (n, rows_t, C)]
    grads = pl.pallas_call(
        functools.partial(gradient_kernel, cfg),
        name="kernel_gradients",
        out_shape=shapes,
        in_specs=[VMEM] + [ANY] * 11,
        out_specs=[VMEM] * 4,
        scratch_shapes=[
            vm((TEAM, pix, C), half),
            vm((TEAM, pix, C), half),
            vm((TEAM, pix, C), half),
            vm((TEAM, pix, C), half),
            vm((TEAM, pix, C), half),
            vm((TEAM, 2, W, 1, C), f32),
            vm((TEAM, 3, pix + 2 * H, C), half),
            vm((TEAM, 3, pix, 3 * q4), half),
            vm((TEAM, pix, q4), half),
            vm((TEAM, 2, W, 1, q4), f32),
            vm((2, TEAM, pix, C), half),
            vm((9 * C, C), half),
            vm((9 * C, q4), half),
            vm((2 * C, C), half),
            vm((C, C), half),
            vm(slots[0], half),
            vm(slots[1], half),
            vm(slots[2], half),
            vm(slots[3], half),
            dma((11,)),
            dma((4, R)),
            dma((4, R)),
        ],
        compiler_params=pltpu.CompilerParams(
            collective_id=1, has_side_effects=True, vmem_limit_bytes=60 * 2**20
        ),
    )(team_masks, *outs[2:])

    gm, g1, gi, gt = grads
    pieces = [
        gm.reshape(TEAM, -1),
        g1.reshape(TEAM, -1),
        gi.reshape(TEAM, -1),
        gt.reshape(TEAM, -1),
    ]
    packed = jnp.concatenate(pieces, 1)
    teams = [[TEAM * i + j for j in range(TEAM)] for i in range(R // TEAM)]
    swapped = lax.all_to_all(packed, "rows", 0, 0, axis_index_groups=teams, tiled=False).astype(f32)
    sizes = [v.shape[1] for v in pieces]
    o = [0, sizes[0], sizes[0] + sizes[1], sizes[0] + sizes[1] + sizes[2], sum(sizes)]
    mains = swapped[:, o[0] : o[1]]
    firsts = swapped[:, o[1] : o[2]].reshape(TEAM, -1, q4).transpose(1, 0, 2).reshape(-1)
    conv_grad = jnp.stack([firsts, mains[T]])
    return (
        result,
        conv_grad[None],
        swapped[:T, o[2] : o[3]][None],
        swapped[:T, o[3] : o[4]][None],
        mains[:T][None],
        bn_grads[None, :norms],
        bn_grads[None, norms:],
    )


def solution(mesh):
    in_specs = (
        P("pipe", None, "rows", None, None),
        P(),
        P(None, "rows", None),
        P("pipe", None, None, None),
        P("pipe", None, None, None),
        P("pipe", None, None, None),
        P("pipe", None, None, None),
        P("pipe", None, None),
        P("pipe", None, None),
    )
    out_specs = (
        P("pipe", None, "rows", None, None),
        P("pipe", None, "rows"),
        P("pipe", None, "rows"),
        P("pipe", None, "rows"),
        P("pipe", None, "rows"),
        P("pipe", None, None),
        P("pipe", None, None),
    )
    bands = mesh.shape["rows"]

    def step(section_in, image_start, pool_choice, conv_shared, task_in, task_mid, task_conv, bn_gain, bn_bias):
        M = section_in.shape[1]
        G = bands // M
        cfg = dict(
            M=M,
            G=G,
            H=section_in.shape[2] // G,
            W=section_in.shape[3],
            C=conv_shared.shape[3],
            T=task_in.shape[1],
            n=bands // TEAM,
            to_all=frozenset(range(0, 8)) | frozenset(range(31, 39)),
        )
        return jax.shard_map(
            functools.partial(per_device, cfg), mesh=mesh, in_specs=in_specs, out_specs=out_specs, check_vma=False
        )(section_in, image_start, pool_choice, conv_shared, task_in, task_mid, task_conv, bn_gain, bn_bias)

    return step
```

```python
import functools

import jax
import jax.numpy as jnp
import numpy as np
from jax import lax
from jax.experimental import pallas as pl
from jax.experimental.pallas import tpu as pltpu
from jax.sharding import PartitionSpec as P

MESH = pl.DeviceIdType.MESH
half = jnp.bfloat16
f32 = jnp.float32
epsilon = 1e-05
TEAM = 4

ANY = pl.BlockSpec(memory_space=pl.ANY)
VMEM = pl.BlockSpec(memory_space=pltpu.VMEM)


def sigmoid(x):
    return 0.5 * jnp.tanh(0.5 * x) + 0.5


def dot(a, b):
    return jnp.dot(a, b, preferred_element_type=f32)


def dot_nt(a, b):
    return lax.dot_general(a, b, (((1,), (1,)), ((), ())), preferred_element_type=f32)


def dot_tn(a, b):
    return lax.dot_general(a, b, (((0,), (0,)), ((), ())), preferred_element_type=f32)


class Remote:
    def __init__(self, src, dst, send, recv, to):
        self.src, self.dst, self.send, self.recv, self.to = src, dst, send, recv, to
        self.local = to == lax.axis_index("rows")

    def remote(self):
        return pltpu.make_async_remote_copy(
            src_ref=self.src,
            dst_ref=self.dst,
            send_sem=self.send,
            recv_sem=self.recv,
            device_id=(lax.axis_index("pipe"), self.to),
            device_id_type=MESH,
        )

    def start(self):
        @pl.when(self.local)
        def _():
            pltpu.make_async_copy(self.src, self.dst, self.recv).start()

        @pl.when(jnp.logical_not(self.local))
        def _():
            self.remote().start()

    def sent(self):
        @pl.when(jnp.logical_not(self.local))
        def _():
            self.remote().wait_send()


def arrived(dst, sem):
    pltpu.make_async_copy(dst, dst, sem).wait()


EDGES = 13


def section_kernel(cfg, *refs):
    M, G, H, W, C, T = cfg["M"], cfg["G"], cfg["H"], cfg["W"], cfg["C"], cfg["T"]
    R = M * G
    pix = H * W
    part = pix // M
    count = float(pix * G)
    norms = 2 + 3 * T
    direct = cfg["direct"]
    (sec, sel, msks, perm, perm_t, spread, spread_edge, pool, gain, bias, wc, wi, wm, wt) = refs[:14]
    (out, bng, xu, xh, xp, xt, xv, xd5, xd5e, xd4, xd3, xd1, xd1e) = refs[14:27]
    refs = refs[27:]
    if direct:
        (gm, g1, gi, gt) = refs[:4]
        flows_in = refs[4:8]
        ends = refs[8:12]
        (d4, d5e, d1e, l_sem, fl_s, fl_r, fl_l, sh_s, sh_r, o_sem) = refs[-10:]
        refs = refs[12:-10]
    (
        kc, ki, km, kt, rin, field, selin, chosen, uh, selh, uedge, px, ps, rb, ys, esend, erecv, ssend, srecv,
        h1, h2, h2e, t1, pr, res, dz, dh, dy5, dy5e, dy2, dy2e, dy4, dy3, dy1, dy1e, bn, bnr,
        go, w_sem, in_s, in_r, ed_s, ed_r, st_s, st_r, pp_s, pp_r, out_s, out_r, bn_s, bn_r, x_s, x_r,
    ) = refs
    p = lax.axis_index("pipe")
    r = lax.axis_index("rows")
    b, m = r // M, r % M
    e, e0 = m, r - m
    first, last = b == 0, b == G - 1
    CW = C * (1 + T)

    loads = {}

    def load(name, src, dst, i):
        loads[name] = pltpu.make_async_copy(src, dst, w_sem.at[i])
        loads[name].start()

    load("c0", wc.at[0], kc.at[0], 0)
    load("i", wi, ki, 1)
    load("c1", wc.at[1], kc.at[1], 2)
    load("m", wm, km, 3)
    for t in range(T):
        load("t%d" % t, wt.at[t], kt.at[t], 4 + t)

    zero_col = jnp.zeros((H, C), half)
    for a in range(3):
        rb[a, 0:H, :] = zero_col
        rb[a, H * (W + 1) : H * (W + 2), :] = zero_col
    px[pix // 4 :, :] = jnp.zeros((px.shape[0] - pix // 4, CW), half)

    @pl.when(first)
    def _():
        for s in range(EDGES):
            erecv[s, 0] = jnp.zeros((W, 1, C), f32)
        uh[0] = jnp.zeros((32, C), half)
        selh[0] = jnp.zeros((32, 128), half)

    @pl.when(last)
    def _():
        for s in range(EDGES):
            erecv[s, 1] = jnp.zeros((W, 1, C), f32)
        uh[1] = jnp.zeros((32, C), half)
        selh[1] = jnp.zeros((32, 128), half)

    bar = pltpu.get_barrier_semaphore()

    def hello(side, row):
        pl.semaphore_signal(bar, inc=1, device_id=(side, row), device_id_type=MESH)

    for d in range(1, M):
        hello(p, e0 + lax.rem(m + d, M))
    for d in range(1, G):
        hello(p, M * lax.rem(b + d, G) + m)
    hello(1 - p, r)
    tops = jnp.logical_and(m == M - 1, jnp.logical_not(last))
    bottoms = jnp.logical_and(m == 0, jnp.logical_not(first))

    @pl.when(jnp.logical_not(first))
    def _():
        hello(1 - p, r - M)
        hello(p, e0 - 1)

    @pl.when(jnp.logical_not(last))
    def _():
        hello(1 - p, r + M)
        hello(p, e0 + M)

    @pl.when(tops)
    def _():
        for j in range(M):
            hello(p, e0 + M + j)

    @pl.when(bottoms)
    def _():
        for j in range(M):
            hello(p, e0 - M + j)

    below_me, above_me = 1 - (b + 1) // G, (b + G - 1) // G
    top_member, bottom_member = (m + 1) // M, 1 - (m + M - 1) // M
    pl.semaphore_wait(
        bar, M + G - 1 + 2 * (below_me + above_me) + M * (top_member * below_me + bottom_member * above_me)
    )

    mine = pl.ds(pl.multiple_of(part * m, 16), part)
    field_moves, rest_moves, sel_moves, edge_moves = [], [], [], ([], [])
    for d in range(M):
        j = lax.rem(m + d, M)
        to = e0 + j
        field_moves.append(Remote(sec.at[j, :, 0:C], rin.at[mine, 0:C], in_s.at[0, d], in_r.at[0, m], to))
        sel_moves.append(Remote(sel.at[j], selin.at[mine], in_s.at[2, d], in_r.at[2, m], to))
        rest_moves.append(Remote(sec.at[j, :, C:CW], rin.at[mine, C:CW], in_s.at[1, d], in_r.at[1, m], to))
    for j in range(M):
        to = e0 + j
        edge_moves[0].append(
            Remote(sec.at[j, pl.ds(part - 32, 32), 0:C], uh.at[0], in_s.at[3, j], in_r.at[3, 0], to + M)
        )
        edge_moves[0].append(Remote(sel.at[j, pl.ds(part - 32, 32)], selh.at[0], in_s.at[4, j], in_r.at[3, 1], to + M))
        edge_moves[1].append(Remote(sec.at[j, pl.ds(0, 32), 0:C], uh.at[1], in_s.at[5, j], in_r.at[4, 0], to - M))
        edge_moves[1].append(Remote(sel.at[j, pl.ds(0, 32)], selh.at[1], in_s.at[6, j], in_r.at[4, 1], to - M))

    def start_field():
        for move in field_moves:
            move.start()
        for move in rest_moves:
            move.start()

    @pl.when(tops)
    def _():
        for move in edge_moves[0]:
            move.start()

    @pl.when(bottoms)
    def _():
        for move in edge_moves[1]:
            move.start()

    @pl.when(p == 0)
    def _():
        start_field()

    for move in sel_moves:
        move.start()

    row_of = lax.broadcasted_iota(jnp.int32, (H, C), 0)
    at_top, at_bottom = row_of == 0, row_of == H - 1

    def column(j):
        return pl.ds(pl.multiple_of(j * H, H), H)

    def over_columns(body, start=0, step=2):
        def several(c, carry):
            for u in range(step):
                carry = body(c * step + u, carry)
            return carry

        return lax.fori_loop(0, W // step, several, start)

    def build(j, value, above, below, up, down):
        here = pl.ds(pl.multiple_of(H + j * H, H), H)
        rb[1, here, :] = value.astype(half)
        rb[0, here, :] = (jnp.where(at_top, above, pltpu.roll(value, 1, 0)) * up).astype(half)
        rb[2, here, :] = (jnp.where(at_bottom, below, pltpu.roll(value, H - 1, 0)) * down).astype(half)

    def conv(kernel):
        total = None
        for tap in range(9):
            a, c = tap // 3, tap % 3
            term = dot(rb[a, H * c : H * c + pix, :], kernel[tap * C : (tap + 1) * C, :])
            total = term if total is None else total + term
        return total

    def conv_t(kernel):
        total = None
        for tap in range(9):
            a, c = tap // 3, tap % 3
            term = dot_nt(rb[a, H * c : H * c + pix, :], kernel[(8 - tap) * C : (9 - tap) * C, :])
            total = term if total is None else total + term
        return total

    def folded(total):
        return jnp.sum(total, 0, keepdims=True)

    def fold(x):
        return jnp.sum(x.reshape(H // 8, 8, C), 0)

    zero8 = jnp.zeros((8, C), f32)

    def edge_copy(slot, side):
        to = r - M if side == 0 else r + M
        return pltpu.make_async_remote_copy(
            src_ref=esend.at[slot, side],
            dst_ref=erecv.at[slot, 1 - side],
            send_sem=ed_s.at[slot, side],
            recv_sem=ed_r.at[slot, 1 - side],
            device_id=(p, to),
            device_id_type=MESH,
        )

    def send_edges(slot):
        @pl.when(jnp.logical_not(first))
        def _():
            edge_copy(slot, 0).start()

        @pl.when(jnp.logical_not(last))
        def _():
            edge_copy(slot, 1).start()

    def get_edges(slot):
        @pl.when(jnp.logical_not(first))
        def _():
            arrived(erecv.at[slot, 0], ed_r.at[slot, 0])

        @pl.when(jnp.logical_not(last))
        def _():
            arrived(erecv.at[slot, 1], ed_r.at[slot, 1])

    def finish_edges(slot):
        @pl.when(jnp.logical_not(first))
        def _():
            edge_copy(slot, 0).wait_send()

        @pl.when(jnp.logical_not(last))
        def _():
            edge_copy(slot, 1).wait_send()

    def stat_copy(slot, n, d):
        to = M * lax.rem(b + d, G) + m
        return pltpu.make_async_remote_copy(
            src_ref=ssend.at[pl.ds(slot, n)],
            dst_ref=srecv.at[b, pl.ds(slot, n)],
            send_sem=st_s.at[slot, d],
            recv_sem=st_r.at[slot, b],
            device_id=(p, to),
            device_id_type=MESH,
        )

    def send_sums(slot, n):
        srecv[b, slot : slot + n] = ssend[slot : slot + n]
        for d in range(1, G):
            stat_copy(slot, n, d).start()

    sums_sent = []

    def get_sums(slot, n):
        sums_sent.append((slot, n))
        for d in range(1, G):
            s = lax.rem(b + d, G)
            arrived(srecv.at[s, pl.ds(slot, n)], st_r.at[slot, s])

    def total(slot):
        acc = srecv[0, slot]
        for g in range(1, G):
            acc = acc + srecv[g, slot]
        return acc

    def put_sums(slot, s, q):
        ssend[slot] = jnp.concatenate([folded(s), folded(q)], 0)

    x_moves = []
    kept = []

    def post(index, src, dst, target, keep=False):
        move = Remote(src, dst.at[e], x_s.at[index], x_r.at[index - (target if index in cfg["to_all"] else 0), e], e0 + target)
        x_moves.append(move)
        if not keep:
            move.start()
        else:
            kept.append(move)

            @pl.when(p == 0)
            def _():
                move.start()

    def send_kept():
        for move in kept:
            move.start()


    def moments(k, slot, edge=None):
        def body(j, carry):
            s, q = carry
            y = ys[k, column(j), :]
            if edge is not None:
                esend[edge, 0, j] = y[0:1]
                esend[edge, 1, j] = y[H - 1 : H]
            return s + fold(y), q + fold(y * y)

        s, q = over_columns(body, (zero8, zero8))
        put_sums(slot, s, q)

    norm = {}

    def norm_rows(k, slot):
        acc = total(slot)
        mean = acc[0:1] / count
        rs = lax.rsqrt(acc[1:2] / count - mean * mean + epsilon)
        scale = gain[k : k + 1, :] * rs
        norm[k] = (mean, rs, scale, bias[k : k + 1, :])

    def normed(k, y):
        mean, rs, scale, shift = norm[k]
        return (y - mean) * scale + shift

    def silu(x):
        return x * sigmoid(x)

    def silu_slope(x):
        s = sigmoid(x)
        return s * (1.0 + x * (1.0 - s))

    def pair(slot, j):
        return jnp.concatenate([erecv[slot, 0, j], erecv[slot, 1, j]], 0)

    nt = 2 + 3 * T
    F3, F4, F5 = 2, 2 + T, 2 + 2 * T

    def wait_field(kind, buffer):
        for k in range(M):
            arrived(buffer(k), in_r.at[kind, k])

    @pl.when(jnp.logical_not(first))
    def _():
        arrived(uh.at[0], in_r.at[3, 0])
        arrived(selh.at[0], in_r.at[3, 1])

    @pl.when(jnp.logical_not(last))
    def _():
        arrived(uh.at[1], in_r.at[4, 0])
        arrived(selh.at[1], in_r.at[4, 1])

    def start_of_field():
        wait_field(0, lambda k: rin.at[pl.ds(part * k, part), 0:C])
        field[p, :, 0:C] = dot(perm[...], rin[:, 0:C]).astype(half)

    def rest_of_field():
        wait_field(1, lambda k: rin.at[pl.ds(part * k, part), C:CW])
        for t in range(T):
            cols = slice((t + 1) * C, (t + 2) * C)
            field[p, :, cols] = dot(perm[...], rin[:, cols]).astype(half)

    @pl.when(p == 0)
    def _():
        start_of_field()

    wait_field(2, lambda k: selin.at[pl.ds(part * k, part)])
    chosen[...] = spread[...] * dot(perm[...], selin[...]).astype(half)

    def halo_copies():
        return (
            pltpu.make_async_remote_copy(
                src_ref=ps.at[pl.ds(pix // 4, 16), 0:C], dst_ref=px.at[pl.ds(pix // 4, 16), 0:C],
                send_sem=pp_s.at[1], recv_sem=pp_r.at[1], device_id=(1 - p, r + M), device_id_type=MESH),
            pltpu.make_async_remote_copy(
                src_ref=ps.at[pl.ds(pix // 4 + 16, 16), 0:C], dst_ref=px.at[pl.ds(pix // 4 + 16, 16), 0:C],
                send_sem=pp_s.at[2], recv_sem=pp_r.at[2], device_id=(1 - p, M * (b - 1) + m), device_id_type=MESH),
        )

    def pool_copy():
        return pltpu.make_async_remote_copy(
            src_ref=ps.at[pl.ds(0, pix // 4)], dst_ref=px.at[pl.ds(0, pix // 4)],
            send_sem=pp_s.at[0], recv_sem=pp_r.at[0], device_id=(1 - p, r), device_id_type=MESH)

    @pl.when(p == 1)
    def _():
        pl.semaphore_wait(go, 1)
        start_field()
        start_of_field()
        rest_of_field()
        arrived(px.at[pl.ds(0, pix // 4)], pp_r.at[0])

        @pl.when(jnp.logical_not(first))
        def _():
            arrived(px.at[pl.ds(pix // 4, 16), 0:C], pp_r.at[1])

        @pl.when(jnp.logical_not(last))
        def _():
            arrived(px.at[pl.ds(pix // 4 + 16, 16), 0:C], pp_r.at[2])

        for t in range(1 + T):
            cols = slice(t * C, (t + 1) * C)
            field[0, :, cols] = dot(chosen[...], px[:, cols]).astype(half)
        edges = spread_edge[...] * jnp.concatenate([selh[0], selh[1]], 0)
        both = dot(edges, px[:, 0:C]).astype(half)
        uh[0] = both[0:32]
        uh[1] = both[32:64]

    above = uh[0].astype(f32)
    below = uh[1].astype(f32)
    for j in range(W):
        uedge[0, j] = above[32 - W + j : 33 - W + j]
        uedge[1, j] = below[j : j + 1]

    up = msks[m, 0]
    down = msks[m, 1]

    def body_u(j, carry):
        build(j, field[0, column(j), 0:C].astype(f32), uedge[0, j], uedge[1, j], up, down)
        return carry

    over_columns(body_u)
    loads["c0"].wait()
    ys[0] = conv(kc.at[0])
    moments(0, 0, 0)
    send_sums(0, 1)
    send_edges(0)

    @pl.when(p == 0)
    def _():
        rest_of_field()
        pl.semaphore_signal(go, inc=1, device_id=(1 - p, r), device_id_type=MESH)

    for q in range(TEAM):
        post(q, field.at[0, :, 0:C], xu, q)
    for t in range(T):
        post(8 + t, field.at[0, :, (t + 1) * C : (t + 2) * C], xv, t, True)
    get_sums(0, 1)
    get_edges(0)
    norm_rows(0, 0)

    def body_h1(j, carry):
        value = silu(normed(0, ys[0, column(j), :]))
        side = silu(normed(0, pair(0, j)))
        h1[column(j), :] = value.astype(half)
        build(j, value, side[0:1], side[1:2], up, down)
        return carry

    over_columns(body_h1)
    for q in range(TEAM):
        post(4 + q, h1, xh, q)

    loads["i"].wait()
    for t in range(T):
        k = 2 + 3 * t
        ys[k] = dot(h1[...], ki[t, 0:C, :]) + dot(field[0, :, (t + 1) * C : (t + 2) * C], ki[t, C : 2 * C, :])
        moments(k, F3 + t)
    send_sums(F3, T)
    loads["c1"].wait()
    ys[1] = conv(kc.at[1])
    moments(1, 1, 1)
    send_sums(1, 1)
    send_edges(1)

    get_sums(F3, T)
    loads["m"].wait()
    for t in range(T):
        k = 2 + 3 * t
        norm_rows(k, F3 + t)

        def body_t1(j, carry):
            t1[t, column(j), :] = silu(normed(k, ys[k, column(j), :])).astype(half)
            return carry

        over_columns(body_t1)
        post(11 + t, t1.at[t], xt, t, True)
        ys[k + 1] = dot(t1[t], km[t])
        moments(k + 1, F4 + t, 2 + t)
    send_sums(F4, T)
    for t in range(T):
        send_edges(2 + t)

    get_sums(1, 1)
    get_edges(1)
    norm_rows(1, 1)

    def body_h2(j, carry):
        value = silu(normed(1, ys[1, column(j), :])).astype(half)
        h2[column(j), :] = value
        res[column(j), 0:C] = value
        side = silu(normed(1, pair(1, j))).astype(half).astype(f32)
        h2e[j] = side
        return carry

    over_columns(body_h2)
    get_sums(F4, T)
    for t in range(T):
        k = 3 + 3 * t
        get_edges(2 + t)
        norm_rows(k, F4 + t)

        def body_p(j, carry):
            gate = sigmoid(normed(k, ys[k, column(j), :]))
            value = gate * h2[column(j), :].astype(f32)
            side = sigmoid(normed(k, pair(2 + t, j))) * h2e[j]
            pr[t, column(j), :] = value.astype(half)
            build(j, value, side[0:1], side[1:2], up, down)
            return carry

        over_columns(body_p)
        post(14 + t, pr.at[t], xp, t)
        loads["t%d" % t].wait()
        ys[k + 1] = conv(kt.at[t])
        moments(k + 1, F5 + t, 5 + t)
    send_sums(F5, T)
    for t in range(T):
        send_edges(5 + t)
    get_sums(F5, T)
    for t in range(T):
        k = 4 + 3 * t
        get_edges(5 + t)
        norm_rows(k, F5 + t)

        def body_q(j, carry):
            res[column(j), (t + 1) * C : (t + 2) * C] = silu(normed(k, ys[k, column(j), :])).astype(half)
            return carry

        over_columns(body_q)

    def out_moves(which):
        cols = slice(0, C) if which == 0 else slice(C, CW)
        moves = []
        for d in range(M):
            k = lax.rem(m + d, M)
            rows = pl.ds(pl.multiple_of(part * k, 16), part)
            moves.append(
                Remote(rin.at[rows, cols], out.at[m, :, cols], out_s.at[which, d], out_r.at[which, m], e0 + k)
            )
        return moves

    def send_result(which):
        for t in range(0, 1) if which == 0 else range(1, 1 + T):
            cols = slice(t * C, (t + 1) * C)
            rin[:, cols] = dot(perm_t[...], res[:, cols]).astype(half)
        for move in out_moves(which):
            move.start()

    @pl.when(p == 0)
    def _():
        for t in range(1 + T):
            cols = slice(t * C, (t + 1) * C)
            ps[:, cols] = dot(pool[...], res[:, cols]).astype(half)
        pool_copy().start()

        @pl.when(jnp.logical_not(last))
        def _():
            halo_copies()[0].start()

        @pl.when(jnp.logical_not(first))
        def _():
            halo_copies()[1].start()

        pool_copy().wait_send()

        @pl.when(jnp.logical_not(last))
        def _():
            halo_copies()[0].wait_send()

        @pl.when(jnp.logical_not(first))
        def _():
            halo_copies()[1].wait_send()

        arrived(px.at[pl.ds(0, pix // 4)], pp_r.at[0])
        for t in range(1 + T):
            cols = slice(t * C, (t + 1) * C)
            field[1, :, cols] = (dot(spread[...], px[:, cols]) * 0.25).astype(half)

    @pl.when(p == 1)
    def _():
        send_result(0)
        send_result(1)

    B3, B4, B5 = nt + F3, nt + F4, nt + F5
    back = {}

    def back_rows(k, slot):
        acc = total(slot)
        mean, rs, scale, shift = norm[k]
        slope = -scale * rs * acc[1:2] / count
        back[k] = (scale, slope, -scale * acc[0:1] / count - slope * mean)
        bn[k : k + 1, :] = acc[1:2]
        bn[norms + k : norms + k + 1, :] = acc[0:1]

    def grad_pre(k, dzv, y):
        scale, slope, rest = back[k]
        return scale * dzv + slope * y + rest

    def hat(k, y):
        mean, rs, scale, shift = norm[k]
        return (y - mean) * rs

    for t in range(T):
        k = 4 + 3 * t

        def body_dz5(j, carry):
            s, q = carry
            y = ys[k, column(j), :]
            g = field[1, column(j), (t + 1) * C : (t + 2) * C].astype(f32)
            v = g * silu_slope(normed(k, y))
            dz[t, column(j), :] = v
            esend[8 + t, 0, j] = v[0:1]
            esend[8 + t, 1, j] = v[H - 1 : H]
            return s + fold(v), q + fold(v * hat(k, y))

        s, q = over_columns(body_dz5, (zero8, zero8))
        put_sums(B5 + t, s, q)
    send_sums(B5, T)
    for t in range(T):
        send_edges(8 + t)
    get_sums(B5, T)

    for t in range(T):
        k = 4 + 3 * t
        get_edges(8 + t)
        back_rows(k, B5 + t)

        def body_dy5(j, carry):
            v = grad_pre(k, dz[t, column(j), :], ys[k, column(j), :])
            side = grad_pre(k, pair(8 + t, j), pair(5 + t, j))
            dy5[t, column(j), :] = v.astype(half)
            dy5e[t, 0, j] = side[0:1]
            dy5e[t, 1, j] = side[1:2]
            build(j, v, side[0:1], side[1:2], up, down)
            return carry

        over_columns(body_dy5)
        post(17 + t, dy5.at[t], xd5, t)
        post(21 + t, dy5e.at[t], xd5e, t)
        ys[k] = conv_t(kt.at[t])

        def body_dz4(j, carry):
            s, q = carry
            dp = ys[k, column(j), :]
            y = ys[k - 1, column(j), :]
            gate = sigmoid(normed(k - 1, y))
            dgate = dp * h2[column(j), :].astype(f32)
            base = field[1, column(j), 0:C].astype(f32) if t == 0 else dh[column(j), :]
            dh[column(j), :] = base + dp * gate
            v = dgate * gate * (1.0 - gate)
            ys[k, column(j), :] = v
            return s + fold(v), q + fold(v * hat(k - 1, y))

        s, q = over_columns(body_dz4, (zero8, zero8))
        put_sums(B4 + t, s, q)
    send_sums(B4, T)

    @pl.when(p == 1)
    def _():
        send_kept()

    def body_dz2(j, carry):
        s, q = carry
        y = ys[1, column(j), :]
        v = dh[column(j), :] * silu_slope(normed(1, y))
        dh[column(j), :] = v
        esend[11, 0, j] = v[0:1]
        esend[11, 1, j] = v[H - 1 : H]
        return s + fold(v), q + fold(v * hat(1, y))

    s, q = over_columns(body_dz2, (zero8, zero8))
    put_sums(nt + 1, s, q)
    send_sums(nt + 1, 1)
    send_edges(11)

    get_sums(B4, T)
    for t in range(T):
        k = 3 + 3 * t
        back_rows(k, B4 + t)

        def body_dy4(j, carry):
            dy4[t, column(j), :] = grad_pre(k, ys[k + 1, column(j), :], ys[k, column(j), :]).astype(half)
            return carry

        over_columns(body_dy4)
        post(25 + t, dy4.at[t], xd4, t)
        dz[t] = dot_nt(dy4[t], km[t])

        def body_dz3(j, carry):
            s, q = carry
            y = ys[k - 1, column(j), :]
            v = dz[t, column(j), :] * silu_slope(normed(k - 1, y))
            dz[t, column(j), :] = v
            return s + fold(v), q + fold(v * hat(k - 1, y))

        s, q = over_columns(body_dz3, (zero8, zero8))
        put_sums(B3 + t, s, q)
    send_sums(B3, T)

    get_sums(nt + 1, 1)
    get_edges(11)
    back_rows(1, nt + 1)

    def body_dy2(j, carry):
        v = grad_pre(1, dh[column(j), :], ys[1, column(j), :])
        side = grad_pre(1, pair(11, j), pair(1, j))
        dy2[column(j), :] = v.astype(half)
        dy2e[0, j] = side[0:1]
        dy2e[1, j] = side[1:2]
        build(j, v, side[0:1], side[1:2], up, down)
        return carry

    over_columns(body_dy2)
    post(20, dy2, xd5, TEAM - 1)
    post(24, dy2e, xd5e, TEAM - 1)

    dh[...] = conv_t(kc.at[1])

    get_sums(B3, T)
    for t in range(T):
        k = 2 + 3 * t
        back_rows(k, B3 + t)

        def body_dy3(j, carry):
            dy3[t, column(j), :] = grad_pre(k, dz[t, column(j), :], ys[k, column(j), :]).astype(half)
            return carry

        over_columns(body_dy3)
        post(28 + t, dy3.at[t], xd3, t)
        dh[...] += dot_nt(dy3[t], ki[t, 0:C, :])
        res[:, (t + 1) * C : (t + 2) * C] = dot_nt(dy3[t], ki[t, C : 2 * C, :]).astype(half)

    @pl.when(p == 0)
    def _():
        send_result(1)

    def body_dz1(j, carry):
        s, q = carry
        y = ys[0, column(j), :]
        v = dh[column(j), :] * silu_slope(normed(0, y))
        dh[column(j), :] = v
        esend[12, 0, j] = v[0:1]
        esend[12, 1, j] = v[H - 1 : H]
        return s + fold(v), q + fold(v * hat(0, y))

    s, q = over_columns(body_dz1, (zero8, zero8))
    put_sums(nt, s, q)
    send_sums(nt, 1)
    send_edges(12)
    get_sums(nt, 1)
    get_edges(12)
    back_rows(0, nt)

    def bn_moves():
        return [Remote(bn, bnr.at[m], bn_s.at[d], bn_r.at[m], e0 + lax.rem(m + d, M)) for d in range(M)]

    for move in bn_moves():
        move.start()

    quarter = C // TEAM

    def body_dy1(j, carry):
        v = grad_pre(0, dh[column(j), :], ys[0, column(j), :])
        side = grad_pre(0, pair(12, j), pair(0, j))
        low = v.astype(half)
        for o in range(TEAM):
            cols = slice(o * quarter, (o + 1) * quarter)
            dy1[o, column(j), :] = low[:, cols]
            dy1e[o, 0, j] = side[0:1, cols]
            dy1e[o, 1, j] = side[1:2, cols]
        build(j, v, side[0:1], side[1:2], up, down)
        return carry

    over_columns(body_dy1)
    for o in range(TEAM):
        post(31 + o, dy1.at[o], xd1, o)
        post(35 + o, dy1e.at[o], xd1e, o)
    res[:, 0:C] = conv_t(kc.at[0]).astype(half)

    @pl.when(p == 1)
    def _():
        for t in range(1 + T):
            cols = slice(t * C, (t + 1) * C)
            ps[0 : pix // 4, cols] = dot_tn(chosen[...], res[:, cols])[0 : pix // 4].astype(half)
        pool_copy().start()
        pool_copy().wait_send()

    @pl.when(p == 0)
    def _():
        send_result(0)

    if direct:
        z, n = b, R // TEAM
        q4 = quarter
        all_rows = TEAM * pix
        wide = pix + 2 * H
        task = e < T
        vb, va, vc = (kt.at[2, i * all_rows : (i + 1) * all_rows, :] for i in range(3))
        vd, d5, d3 = (kc.at[0, i * all_rows : (i + 1) * all_rows, :] for i in range(3))
        pm, p1, pi_, pt = kt.at[0], kc.at[0, :, 0:q4], ki.at[0], km.at[0]
        d1 = kt.at[1, 0:all_rows, 3 * q4 : 4 * q4]
        rows_m, rows_i, rows_t = 9 * C // R, 2 * C // R, C // R

        def band(ref, j):
            return ref.at[j * pix : (j + 1) * pix]

        def fetch(index, src, j, dst, sem):
            arrived(src.at[j], sem)
            copy = pltpu.make_async_copy(src.at[j], dst, l_sem.at[index, j])
            copy.start()
            return copy

        def rows_shifted(j, a, lo):
            if j < TEAM - 1:
                start = (3 * j + a) * wide + lo
                return kc.at[1, start : start + pix, :]
            return rb.at[a, lo : lo + pix, :]

        for j in range(TEAM - 1):
            for a in range(3):
                start = (3 * j + a) * wide
                kc[1, start : start + H, :] = zero_col
                kc[1, start + H + pix : start + wide, :] = zero_col
        got = {}
        for j in range(TEAM):
            got["d5", j] = fetch(0, xd5, j, band(d5, j), x_r.at[17 + e, j])
            got["d5e", j] = fetch(1, xd5e, j, d5e.at[j], x_r.at[21 + e, j])

        @pl.when(task)
        def _():
            for j in range(TEAM):
                fetch(3, xp, j, band(vb, j), x_r.at[14 + e, j])

        @pl.when(jnp.logical_not(task))
        def _():
            for j in range(TEAM):
                fetch(3, xh, j, band(vb, j), x_r.at[4, j])

        for j in range(TEAM):
            got["d5", j].wait()
            got["d5e", j].wait()

            def body_r(i, carry):
                v = kc[0, pl.ds(pl.multiple_of(all_rows + j * pix + i * H, H), H), :].astype(f32)
                three = (
                    (jnp.where(at_top, d5e[j, 0, i], pltpu.roll(v, 1, 0)) * msks[j, 0]).astype(half),
                    v.astype(half),
                    (jnp.where(at_bottom, d5e[j, 1, i], pltpu.roll(v, H - 1, 0)) * msks[j, 1]).astype(half),
                )
                for a in range(3):
                    if j < TEAM - 1:
                        here = pl.ds(pl.multiple_of((3 * j + a) * wide + H + i * H, H), H)
                        kc[1, here, :] = three[a]
                    else:
                        rb[a, pl.ds(pl.multiple_of(H + i * H, H), H), :] = three[a]
                return carry

            over_columns(body_r)
        for j in range(TEAM):
            pltpu.make_async_copy(xp.at[j], band(vb, j), l_sem.at[3, j]).wait()

        for tap in range(9):
            a, c = 2 - tap // 3, 2 - tap % 3
            acc = None
            for j in range(TEAM):
                term = dot_tn(band(vb, j)[...], rows_shifted(j, a, H * c)[...])
                acc = term if acc is None else acc + term
            pm[tap * C : (tap + 1) * C, :] = acc.astype(half)

        partial = (pm, pi_, pt, p1)
        share = (rows_m, rows_i, rows_t, rows_m)
        pieces = (TEAM, 1, 1, 1)
        width = (C, C, C, q4)

        def flow(g, zd, s, way):
            rows = TEAM * share[g] // pieces[g]
            return pltpu.make_async_remote_copy(
                src_ref=partial[g].at[pl.ds(pl.multiple_of((zd * pieces[g] + s) * rows, 16), rows)],
                dst_ref=flows_in[g].at[way, zd, pl.ds(pl.multiple_of(s * rows, 16), rows)],
                send_sem=fl_s.at[way, g, zd, s],
                recv_sem=fl_r.at[way, g, zd, s],
                device_id=(p, r + TEAM * (1 - 2 * way)),
                device_id_type=MESH,
            )

        def incoming(g, zd, s, way, lane):
            rows = TEAM * share[g] // pieces[g]
            src = flows_in[g].at[way, zd, pl.ds(pl.multiple_of(s * rows, 16), rows)]
            dst = kc.at[1, lane * TEAM * rows_m : lane * TEAM * rows_m + rows, 0 : width[g]]
            return src, dst, fl_r.at[way, g, zd, s], fl_l.at[lane]

        def take(g, zd, s, way, lane):
            src, dst, sem, local = incoming(g, zd, s, way, lane)
            arrived(src, sem)
            pltpu.make_async_copy(src, dst, local).start()

        def taken(g, zd, s, way, lane):
            src, dst, sem, local = incoming(g, zd, s, way, lane)
            pltpu.make_async_copy(src, dst, local).wait()
            return dst[...].astype(f32)

        def flow_start(g):
            @pl.when(z == 0)
            def _():
                for zd in range(n - 1, 0, -1):
                    for s in range(pieces[g]):
                        flow(g, zd, s, 0).start()

            @pl.when(z == n - 1)
            def _():
                for zd in range(n - 1):
                    for s in range(pieces[g]):
                        flow(g, zd, s, 1).start()

        def flow_mid(groups):
            upper = (2 * z) // n

            @pl.when(jnp.logical_and(z > 0, z < n - 1))
            def _():
                for phase in range(2):
                    way = lax.rem(phase + upper, 2)
                    for g in groups:
                        rows = TEAM * share[g] // pieces[g]

                        def body_flow(i, carry):
                            k, s = i // pieces[g], i % pieces[g]
                            zd = (1 - way) * (n - 1 - k) + way * k

                            @pl.when((1 - 2 * way) * (zd - z) > 0)
                            def _():
                                take(g, zd, s, way, 0)
                                here = partial[g].at[pl.ds(pl.multiple_of((zd * pieces[g] + s) * rows, 16), rows)]
                                here[...] = (here[...].astype(f32) + taken(g, zd, s, way, 0)).astype(half)
                                flow(g, zd, s, way).start()

                            return carry

                        lax.fori_loop(0, (n - 1) * pieces[g], body_flow, 0)

        def share_moves(g):
            moves = []
            for d in range(TEAM):
                q = lax.rem(e + d, TEAM)
                start = pl.multiple_of((z * TEAM + q) * share[g], 16)
                moves.append(
                    Remote(partial[g].at[pl.ds(start, share[g])], ends[g].at[e], sh_s.at[g, d], sh_r.at[g, e], e0 + q)
                )
            return moves

        def flow_final(g):
            rows = TEAM * share[g] // pieces[g]
            for s in range(pieces[g]):

                @pl.when(z > 0)
                def _():
                    take(g, z, s, 0, 0)

                @pl.when(z < n - 1)
                def _():
                    take(g, z, s, 1, 1)

                here = partial[g].at[pl.ds(pl.multiple_of(z * TEAM * share[g] + s * rows, 16), rows)]

                @pl.when(jnp.logical_and(z > 0, z < n - 1))
                def _():
                    here[...] = (here[...].astype(f32) + taken(g, z, s, 0, 0) + taken(g, z, s, 1, 1)).astype(half)

                @pl.when(z == 0)
                def _():
                    here[...] = (here[...].astype(f32) + taken(g, z, s, 1, 1)).astype(half)

                @pl.when(z == n - 1)
                def _():
                    here[...] = (here[...].astype(f32) + taken(g, z, s, 0, 0)).astype(half)

            for move in share_moves(g):
                move.start()

        def flow_sent(g):
            for way in range(2):
                for zd in range(n):
                    on = z < zd if way == 0 else z > zd

                    @pl.when(on)
                    def _():
                        for s in range(pieces[g]):
                            flow(g, zd, s, way).wait_send()

            for move in share_moves(g):
                move.sent()

        flow_start(0)

        flow_mid((0,))
        flow_final(0)

        first_u = []
        for j in range(TEAM):
            first_u.append(fetch(4, xu, j, band(vb, j), x_r.at[0, j]))

        @pl.when(task)
        def _():
            copies = []
            for j in range(TEAM):
                copies.append(fetch(2, xh, j, band(va, j), x_r.at[4, j]))
                copies.append(fetch(5, xv, j, band(vc, j), x_r.at[8 + e, j]))
                copies.append(fetch(6, xt, j, band(vd, j), x_r.at[11 + e, j]))
                copies.append(fetch(7, xd4, j, band(d4, j), x_r.at[25 + e, j]))
                copies.append(fetch(8, xd3, j, band(d3, j), x_r.at[28 + e, j]))
            for copy in copies:
                copy.wait()
            pi_[0:C, :] = dot_tn(va[...], d3[...]).astype(half)
            pi_[C : 2 * C, :] = dot_tn(vc[...], d3[...]).astype(half)
            pt[...] = dot_tn(vd[...], d4[...]).astype(half)
            flow_start(1)
            flow_start(2)

        for j in range(TEAM):
            got["d1", j] = fetch(9, xd1, j, band(d1, j), x_r.at[31, j])
            got["d1e", j] = fetch(10, xd1e, j, d1e.at[j], x_r.at[35, j])
        row_of1 = lax.broadcasted_iota(jnp.int32, (H, q4), 0)

        def near(j, a, lo, size, cols):
            start = (3 * j + a) * pix + lo
            return kt.at[1, start : start + size, cols * q4 : (cols + 1) * q4]

        for j in range(TEAM):
            got["d1", j].wait()
            got["d1e", j].wait()

        for j in range(TEAM):

            def body_r1(i, carry):
                v = kt[1, pl.ds(pl.multiple_of(j * pix + i * H, H), H), 3 * q4 : 4 * q4].astype(f32)
                three = (
                    (jnp.where(row_of1 == 0, d1e[j, 0, i], pltpu.roll(v, 1, 0)) * msks[j, 0][:, 0:q4]).astype(half),
                    v.astype(half),
                    (jnp.where(row_of1 == H - 1, d1e[j, 1, i], pltpu.roll(v, H - 1, 0)) * msks[j, 1][:, 0:q4]).astype(
                        half
                    ),
                )
                for a in range(3):
                    kt[1, pl.ds(pl.multiple_of((3 * j + a) * pix + i * H, H), H), q4 : 2 * q4] = three[a]
                return carry

            over_columns(body_r1)
            for a in range(3):
                near(j, a, 0, H, 0)[...] = jnp.zeros((H, q4), half)
                near(j, a, H, pix - H, 0)[...] = near(j, a, 0, pix - H, 1)[...]
                near(j, a, 0, pix - H, 2)[...] = near(j, a, H, pix - H, 1)[...]
                near(j, a, pix - H, H, 2)[...] = jnp.zeros((H, q4), half)
        for copy in first_u:
            copy.wait()
        for a in range(3):
            acc = None
            for j in range(TEAM):
                start = (3 * j + 2 - a) * pix
                term = dot_tn(band(vb, j)[...], kt[1, start : start + pix, 0 : 3 * q4])
                acc = term if acc is None else acc + term
            for c in range(3):
                kc[0, (3 * a + c) * C : (3 * a + c + 1) * C, 0:q4] = acc[:, (2 - c) * q4 : (3 - c) * q4].astype(half)
        flow_start(3)

        @pl.when(task)
        def _():
            flow_mid((1, 2, 3))

        @pl.when(jnp.logical_not(task))
        def _():
            flow_mid((3,))

        @pl.when(task)
        def _():
            flow_final(1)
            flow_final(2)

        flow_final(3)

        stores = []

        def store(src, dst, i):
            copy = pltpu.make_async_copy(src, dst, o_sem.at[i])
            copy.start()
            stores.append(copy)

        def last_of(g, members, buffer, base):
            copies = []
            for q in range(members):
                arrived(ends[g].at[q], sh_r.at[g, q])
                copy = pltpu.make_async_copy(
                    ends[g].at[q], buffer.at[q * share[g] : (q + 1) * share[g]], l_sem.at[base, q]
                )
                copy.start()
                copies.append(copy)
            for copy in copies:
                copy.wait()

        def piece(buffer, g, q):
            return buffer[q * share[g] : (q + 1) * share[g], :].astype(f32)

        final_m, final_1 = kc.at[1, 2 * TEAM * rows_m : 3 * TEAM * rows_m, :], kt.at[2, :, 0:q4]
        last_of(0, TEAM, final_m, 11)
        for q in range(TEAM):
            ys[q, 0:rows_m, :] = piece(final_m, 0, q)
            store(ys.at[q, 0:rows_m, :], gm.at[q], q)
        last_of(1, T, ki.at[1], 12)
        last_of(2, T, km.at[1], 13)
        for q in range(T):
            ys[TEAM + 1, q * rows_i : (q + 1) * rows_i, :] = piece(ki.at[1], 1, q)
            ys[TEAM + 2, q * rows_t : (q + 1) * rows_t, :] = piece(km.at[1], 2, q)
        store(ys.at[TEAM + 1, 0 : T * rows_i, :], gi, TEAM)
        store(ys.at[TEAM + 2, 0 : T * rows_t, :], gt, TEAM + 1)
        last_of(3, TEAM, final_1, 14)
        for q in range(TEAM):
            ys[TEAM, 0:rows_m, q * q4 : (q + 1) * q4] = piece(final_1, 3, q)
        store(ys.at[TEAM, 0:rows_m, :], g1, TEAM + 2)
        flow_sent(0)

        @pl.when(task)
        def _():
            flow_sent(1)
            flow_sent(2)

        flow_sent(3)
        for copy in stores:
            copy.wait()

    for k in range(M):
        arrived(bnr.at[k], bn_r.at[k])
    acc = bnr[0]
    for k in range(1, M):
        acc = acc + bnr[k]
    bng[...] = acc
    for k in range(M):
        arrived(out.at[k, :, 0:C], out_r.at[0, k])
        arrived(out.at[k, :, C:CW], out_r.at[1, k])
    for move in out_moves(0) + out_moves(1) + bn_moves() + field_moves + rest_moves + sel_moves:
        move.sent()

    @pl.when(tops)
    def _():
        for move in edge_moves[0]:
            move.sent()

    @pl.when(bottoms)
    def _():
        for move in edge_moves[1]:
            move.sent()

    for s in range(EDGES):
        finish_edges(s)
    for slot, n in sums_sent:
        for d in range(1, G):
            stat_copy(slot, n, d).wait_send()
    for move in x_moves:
        move.sent()
    if direct:
        return
    for j in range(TEAM):
        for index, dst in ((0, xu), (4, xh), (31, xd1), (35, xd1e)):
            arrived(dst.at[j], x_r.at[index, j])
    for t in range(T):

        @pl.when(e == t)
        def _():
            for j in range(TEAM):
                for index, dst in ((8, xv), (11, xt), (14, xp), (17, xd5), (21, xd5e), (25, xd4), (28, xd3)):
                    arrived(dst.at[j], x_r.at[index + t, j])

    @pl.when(e == TEAM - 1)
    def _():
        for j in range(TEAM):
            arrived(xd5.at[j], x_r.at[20, j])
            arrived(xd5e.at[j], x_r.at[24, j])


def tables(M, G, H, W):
    pix = H * W
    cm = np.zeros((pix, pix), np.float32)
    spread = np.zeros((pix, 128), np.float32)
    pool = np.zeros((128, pix), np.float32)
    edge = np.zeros((64, 128), np.float32)
    wide = W // 2
    own = pix // 4
    for i in range(H):
        for j in range(W):
            q = j * H + i
            cm[q, i * W + j] = 1
            w = (i // 2) * wide + j // 2
            spread[q, w] = 1
            pool[w, q] = 0.25
            if i >= H - 2:
                pool[own + j // 2, q] = 0.25
            if i < 2:
                pool[own + 16 + j // 2, q] = 0.25
    for j in range(W):
        edge[32 - W + j, own + j // 2] = 1
        edge[32 + j, own + 16 + j // 2] = 1
    return [jnp.asarray(v, half) for v in (cm, cm.T, spread, edge, pool)]


def gradient_kernel(cfg, *refs):
    M, G, H, W, C, T, n = cfg["M"], cfg["G"], cfg["H"], cfg["W"], cfg["C"], cfg["T"], cfg["n"]
    R = M * G
    pix = H * W
    q4 = C // TEAM
    (msk, xu, xh, xp, xt, xv, xd5, xd5e, xd4, xd3, xd1, xd1e) = refs[:12]
    (gm, g1, gi, gt) = refs[12:16]
    (va, vb, vc, vd, d5, d5e, rb, r1, d1, d1e, d3, pm, p1, pi_, pt, am, a1, ai, at, in_sem, s_sem, r_sem) = refs[16:]
    p = lax.axis_index("pipe")
    r = lax.axis_index("rows")
    e = r % TEAM
    z = r // TEAM
    task = e < T

    loads = {}

    def load(name, src, dst, i):
        loads[name] = pltpu.make_async_copy(src, dst, in_sem.at[i])
        loads[name].start()

    load("d5", xd5, d5, 0)
    load("d5e", xd5e, d5e, 1)
    load("h", xh, va, 2)

    @pl.when(task)
    def _():
        pltpu.make_async_copy(xp, vb, in_sem.at[3]).start()
        pltpu.make_async_copy(xv, vc, in_sem.at[4]).start()
        pltpu.make_async_copy(xt, vd, in_sem.at[5]).start()
        pltpu.make_async_copy(xd3, d3.at[0], in_sem.at[6]).start()
        pltpu.make_async_copy(xd4, d3.at[1], in_sem.at[7]).start()

    bar = pltpu.get_barrier_semaphore()

    def greet(i, _):
        pl.semaphore_signal(bar, inc=1, device_id=(p, lax.rem(r + TEAM * i, R)), device_id_type=MESH)
        return 0

    lax.fori_loop(1, n, greet, 0)

    row_of = lax.broadcasted_iota(jnp.int32, (H, C), 0)
    row_of1 = lax.broadcasted_iota(jnp.int32, (H, q4), 0)

    def column(j):
        return pl.ds(pl.multiple_of(j * H, H), H)

    for j in range(TEAM):
        for a in range(3):
            rb[j, a, 0:H, :] = jnp.zeros((H, C), half)
            rb[j, a, H * (W + 1) : H * (W + 2), :] = jnp.zeros((H, C), half)
            r1[j, a, 0:H, :] = jnp.zeros((H, 3 * q4), half)
            r1[j, a, H * (W - 1) :, :] = jnp.zeros((H, 3 * q4), half)

    loads["d5"].wait()
    loads["d5e"].wait()
    for j in range(TEAM):

        def body(c, carry):
            for u in range(2):
                i = c * 2 + u
                here = pl.ds(pl.multiple_of(H + i * H, H), H)
                v = d5[j, column(i), :].astype(f32)
                rb[j, 1, here, :] = v.astype(half)
                rb[j, 0, here, :] = (jnp.where(row_of == 0, d5e[j, 0, i], pltpu.roll(v, 1, 0)) * msk[j, 0]).astype(half)
                rb[j, 2, here, :] = (
                    jnp.where(row_of == H - 1, d5e[j, 1, i], pltpu.roll(v, H - 1, 0)) * msk[j, 1]
                ).astype(half)
            return carry

        lax.fori_loop(0, W // 2, body, 0)
    loads["h"].wait()

    @pl.when(task)
    def _():
        pltpu.make_async_copy(xp, vb, in_sem.at[3]).wait()
        pltpu.make_async_copy(xv, vc, in_sem.at[4]).wait()
        pltpu.make_async_copy(xt, vd, in_sem.at[5]).wait()
        pltpu.make_async_copy(xd3, d3.at[0], in_sem.at[6]).wait()
        pltpu.make_async_copy(xd4, d3.at[1], in_sem.at[7]).wait()

    @pl.when(jnp.logical_not(task))
    def _():
        vb[...] = va[...]

    for tap in range(9):
        a, c = 2 - tap // 3, 2 - tap % 3
        acc = None
        for j in range(TEAM):
            term = dot_tn(vb[j], rb[j, a, H * c : H * c + pix, :])
            acc = term if acc is None else acc + term
        pm[tap * C : (tap + 1) * C, :] = acc.astype(half)

    pltpu.make_async_copy(xu, vb, in_sem.at[8]).start()
    pltpu.make_async_copy(xd1, d1, in_sem.at[9]).start()
    pltpu.make_async_copy(xd1e, d1e, in_sem.at[10]).start()

    def group(index, src, mine, rows):
        moves = []
        for d in range(1, n):
            to = lax.rem(z + d, n)
            moves.append(
                pltpu.make_async_remote_copy(
                    src_ref=src.at[pl.ds(pl.multiple_of(to * rows, 16), rows)],
                    dst_ref=mine.at[z],
                    send_sem=s_sem.at[index, d],
                    recv_sem=r_sem.at[index, z],
                    device_id=(p, TEAM * to + e),
                    device_id_type=MESH,
                )
            )
        return moves

    rows_m, rows_i, rows_t = 9 * C // n, 2 * C // n, C // n
    pl.semaphore_wait(bar, n - 1)
    main = group(0, pm, am, rows_m)
    for move in main:
        move.start()

    @pl.when(task)
    def _():
        for part, value in ((0, va), (1, vc)):
            acc = None
            for j in range(TEAM):
                term = dot_tn(value[j], d3[0, j])
                acc = term if acc is None else acc + term
            pi_[part * C : (part + 1) * C, :] = acc.astype(half)
        acc = None
        for j in range(TEAM):
            term = dot_tn(vd[j], d3[1, j])
            acc = term if acc is None else acc + term
        pt[...] = acc.astype(half)
        for move in group(1, pi_, ai, rows_i) + group(2, pt, at, rows_t):
            move.start()

    pltpu.make_async_copy(xu, vb, in_sem.at[8]).wait()
    pltpu.make_async_copy(xd1, d1, in_sem.at[9]).wait()
    pltpu.make_async_copy(xd1e, d1e, in_sem.at[10]).wait()
    for j in range(TEAM):

        def body1(i, carry):
            v = d1[j, column(i), :].astype(f32)
            three = (
                (jnp.where(row_of1 == 0, d1e[j, 0, i], pltpu.roll(v, 1, 0)) * msk[j, 0][:, 0:q4]).astype(half),
                v.astype(half),
                (jnp.where(row_of1 == H - 1, d1e[j, 1, i], pltpu.roll(v, H - 1, 0)) * msk[j, 1][:, 0:q4]).astype(half),
            )
            for a in range(3):
                r1[j, a, column(i), q4 : 2 * q4] = three[a]
            return carry

        lax.fori_loop(0, W, body1, 0)
        for a in range(3):
            r1[j, a, H : W * H, 0:q4] = r1[j, a, 0 : (W - 1) * H, q4 : 2 * q4]
            r1[j, a, 0 : (W - 1) * H, 2 * q4 : 3 * q4] = r1[j, a, H : W * H, q4 : 2 * q4]
    for a in range(3):
        acc = None
        for j in range(TEAM):
            term = dot_tn(vb[j], r1[j, 2 - a])
            acc = term if acc is None else acc + term
        for c in range(3):
            p1[(3 * a + c) * C : (3 * a + c + 1) * C, :] = acc[:, (2 - c) * q4 : (3 - c) * q4].astype(half)
    one = group(3, p1, a1, rows_m)
    for move in one:
        move.start()

    def reduce(index, src, mine, rows, dst):
        for d in range(1, n):
            s = lax.rem(z + d, n)
            arrived(mine.at[s], r_sem.at[index, s])
        mine[z] = src[pl.ds(pl.multiple_of(z * rows, 16), rows), :]
        acc = mine[0].astype(f32)
        for s in range(1, n):
            acc = acc + mine[s].astype(f32)
        dst[...] = acc.astype(dst.dtype)

    reduce(0, pm, am, rows_m, gm)

    @pl.when(task)
    def _():
        reduce(1, pi_, ai, rows_i, gi)
        reduce(2, pt, at, rows_t, gt)

    @pl.when(jnp.logical_not(task))
    def _():
        gi[...] = jnp.zeros(gi.shape, gi.dtype)
        gt[...] = jnp.zeros(gt.shape, gt.dtype)

    reduce(3, p1, a1, rows_m, g1)
    for move in main + one:
        move.wait_send()

    @pl.when(task)
    def _():
        for move in group(1, pi_, ai, rows_i) + group(2, pt, at, rows_t):
            move.wait_send()


def per_device(cfg, section_in, image_start, pool_choice, conv_shared, task_in, task_mid, task_conv, bn_gain, bn_bias):
    M, G, H, W, C, T, n = cfg["M"], cfg["G"], cfg["H"], cfg["W"], cfg["C"], cfg["T"], cfg["n"]
    R = M * G
    pix = H * W
    part = pix // M
    rows_total = H * G
    norms = 2 + 3 * T
    CW = C * (1 + T)
    p = lax.axis_index("pipe")
    r = lax.axis_index("rows")
    b, m = r // M, r % M
    sec = section_in[0].reshape(M, part, CW)
    hp = pool_choice.shape[1]
    place = jnp.arange(4, dtype=jnp.int32).reshape(2, 1, 2)
    picked = pool_choice[:, :, None, :, None] == place[None, None]
    sel = jnp.broadcast_to(picked.reshape(M, part, 1), (M, part, 128)).astype(half)

    ones = jnp.ones((M, 1), jnp.int32)
    padded = jnp.concatenate([ones, image_start[:, 1:], ones], 1)
    links = 1.0 - lax.dynamic_slice_in_dim(padded, b * H, H + 1, 1).astype(f32)
    both = jnp.stack([links[:, :-1], links[:, 1:]], 1)
    team_masks = jnp.broadcast_to(both[..., None], (M, 2, H, C))

    cm, cm_t, spread, edge, pool = tables(M, G, H, W)
    sds = jax.ShapeDtypeStruct
    exchange = [
        sds((TEAM, pix, C), half),
        sds((TEAM, pix, C), half),
        sds((TEAM, pix, C), half),
        sds((TEAM, pix, C), half),
        sds((TEAM, pix, C), half),
        sds((TEAM, pix, C), half),
        sds((TEAM, 2, W, 1, C), f32),
        sds((TEAM, pix, C), half),
        sds((TEAM, pix, C), half),
        sds((TEAM, pix, C // TEAM), half),
        sds((TEAM, 2, W, 1, C // TEAM), f32),
    ]
    direct = C % (16 * R) == 0
    parts = R if direct else n
    rows_m, rows_i, rows_t = 9 * C // parts, 2 * C // parts, C // parts
    q4 = C // TEAM
    shares, share_scratch = [], []
    dma = pltpu.SemaphoreType.DMA
    if direct:
        shares = [
            sds((TEAM, rows_m, C), f32),
            sds((rows_m, C), f32),
            sds((T * rows_i, C), f32),
            sds((T * rows_t, C), f32),
            sds((2, n, TEAM * rows_m, C), half),
            sds((2, n, TEAM * rows_i, C), half),
            sds((2, n, TEAM * rows_t, C), half),
            sds((2, n, TEAM * rows_m, q4), half),
            sds((TEAM, rows_m, C), half),
            sds((T, rows_i, C), half),
            sds((T, rows_t, C), half),
            sds((TEAM, rows_m, q4), half),
        ]
        share_scratch = [
            pltpu.VMEM((TEAM * pix, C), half),
            pltpu.VMEM((TEAM, 2, W, 1, C), f32),
            pltpu.VMEM((TEAM, 2, W, 1, q4), f32),
            dma((15, TEAM)),
            dma((2, 4, n, TEAM)),
            dma((2, 4, n, TEAM)),
            dma((2,)),
            dma((4, TEAM)),
            dma((4, TEAM)),
            dma((TEAM + 3,)),
        ]
    vm = pltpu.VMEM
    win = pix // 4 + 32
    outs = pl.pallas_call(
        functools.partial(section_kernel, dict(cfg, direct=direct)),
        name="sections",
        out_shape=[sds((M, part, CW), half), sds((2 * norms, C), f32)] + exchange + shares,
        in_specs=[ANY, ANY] + [VMEM] * 8 + [ANY] * 4,
        out_specs=[ANY, VMEM] + [ANY] * (len(exchange) + len(shares)),
        scratch_shapes=[
            vm((2, 9 * C, C), half),
            vm((T, 2 * C, C), half),
            vm((T, C, C), half),
            vm((T, 9 * C, C), half),
            vm((pix, CW), half),
            vm((2, pix, CW), half),
            vm((pix, 128), half),
            vm((pix, 128), half),
            vm((2, 32, C), half),
            vm((2, 32, 128), half),
            vm((2, W, 1, C), f32),
            vm((win, CW), half),
            vm((win, CW), half),
            vm((3, pix + 2 * H, C), half),
            vm((norms, pix, C), f32),
            vm((EDGES, 2, W, 1, C), f32),
            vm((EDGES, 2, W, 1, C), f32),
            vm((2 * norms, 2, C), f32),
            vm((G, 2 * norms, 2, C), f32),
            vm((pix, C), half),
            vm((pix, C), half),
            vm((W, 2, C), f32),
            vm((T, pix, C), half),
            vm((T, pix, C), half),
            vm((pix, CW), half),
            vm((T, pix, C), f32),
            vm((pix, C), f32),
            vm((T, pix, C), half),
            vm((T, 2, W, 1, C), f32),
            vm((pix, C), half),
            vm((2, W, 1, C), f32),
            vm((T, pix, C), half),
            vm((T, pix, C), half),
            vm((TEAM, pix, C // TEAM), half),
            vm((TEAM, 2, W, 1, C // TEAM), f32),
            vm((2 * norms, C), f32),
            vm((M, 2 * norms, C), f32),
            pltpu.SemaphoreType.REGULAR,
            dma((4 + T,)),
            dma((7, M)),
            dma((5, M)),
            dma((EDGES, 2)),
            dma((EDGES, 2)),
            dma((2 * norms, G)),
            dma((2 * norms, G)),
            dma((3,)),
            dma((3,)),
            dma((2, M)),
            dma((2, M)),
            dma((M,)),
            dma((M,)),
            dma((39,)),
            dma((39, TEAM)),
        ]
        + share_scratch,
        compiler_params=pltpu.CompilerParams(
            collective_id=0, has_side_effects=True, vmem_limit_bytes=63 * 2**20
        ),
    )(sec, sel, team_masks, cm, cm_t, spread, edge, pool, bn_gain[0], bn_bias[0], conv_shared[0], task_in[0], task_mid[0], task_conv[0])
    result, bn_grads = outs[:2]

    result = result.reshape(1, M, part // W, W, CW)
    if direct:
        gm, g1, gi, gt = outs[-12:-8]
        return (
            result,
            jnp.stack([g1, gm[T]]).reshape(1, 2, -1),
            gi.reshape(1, T, -1),
            gt.reshape(1, T, -1),
            gm[:T].reshape(1, T, -1),
            bn_grads[None, :norms],
            bn_grads[None, norms:],
        )
    shapes = [sds((rows_m, C), half), sds((rows_m, q4), half), sds((rows_i, C), half), sds((rows_t, C), half)]
    slots = [(n, rows_m, C), (n, rows_m, q4), (n, rows_i, C), (n, rows_t, C)]
    grads = pl.pallas_call(
        functools.partial(gradient_kernel, cfg),
        name="kernel_gradients",
        out_shape=shapes,
        in_specs=[VMEM] + [ANY] * 11,
        out_specs=[VMEM] * 4,
        scratch_shapes=[
            vm((TEAM, pix, C), half),
            vm((TEAM, pix, C), half),
            vm((TEAM, pix, C), half),
            vm((TEAM, pix, C), half),
            vm((TEAM, pix, C), half),
            vm((TEAM, 2, W, 1, C), f32),
            vm((TEAM, 3, pix + 2 * H, C), half),
            vm((TEAM, 3, pix, 3 * q4), half),
            vm((TEAM, pix, q4), half),
            vm((TEAM, 2, W, 1, q4), f32),
            vm((2, TEAM, pix, C), half),
            vm((9 * C, C), half),
            vm((9 * C, q4), half),
            vm((2 * C, C), half),
            vm((C, C), half),
            vm(slots[0], half),
            vm(slots[1], half),
            vm(slots[2], half),
            vm(slots[3], half),
            dma((11,)),
            dma((4, R)),
            dma((4, R)),
        ],
        compiler_params=pltpu.CompilerParams(
            collective_id=1, has_side_effects=True, vmem_limit_bytes=60 * 2**20
        ),
    )(team_masks, *outs[2:])

    gm, g1, gi, gt = grads
    pieces = [
        gm.reshape(TEAM, -1),
        g1.reshape(TEAM, -1),
        gi.reshape(TEAM, -1),
        gt.reshape(TEAM, -1),
    ]
    packed = jnp.concatenate(pieces, 1)
    teams = [[TEAM * i + j for j in range(TEAM)] for i in range(R // TEAM)]
    swapped = lax.all_to_all(packed, "rows", 0, 0, axis_index_groups=teams, tiled=False).astype(f32)
    sizes = [v.shape[1] for v in pieces]
    o = [0, sizes[0], sizes[0] + sizes[1], sizes[0] + sizes[1] + sizes[2], sum(sizes)]
    mains = swapped[:, o[0] : o[1]]
    firsts = swapped[:, o[1] : o[2]].reshape(TEAM, -1, q4).transpose(1, 0, 2).reshape(-1)
    conv_grad = jnp.stack([firsts, mains[T]])
    return (
        result,
        conv_grad[None],
        swapped[:T, o[2] : o[3]][None],
        swapped[:T, o[3] : o[4]][None],
        mains[:T][None],
        bn_grads[None, :norms],
        bn_grads[None, norms:],
    )


def solution(mesh):
    in_specs = (
        P("pipe", None, "rows", None, None),
        P(),
        P(None, "rows", None),
        P("pipe", None, None, None),
        P("pipe", None, None, None),
        P("pipe", None, None, None),
        P("pipe", None, None, None),
        P("pipe", None, None),
        P("pipe", None, None),
    )
    out_specs = (
        P("pipe", None, "rows", None, None),
        P("pipe", None, "rows"),
        P("pipe", None, "rows"),
        P("pipe", None, "rows"),
        P("pipe", None, "rows"),
        P("pipe", None, None),
        P("pipe", None, None),
    )
    bands = mesh.shape["rows"]

    def step(section_in, image_start, pool_choice, conv_shared, task_in, task_mid, task_conv, bn_gain, bn_bias):
        M = section_in.shape[1]
        G = bands // M
        cfg = dict(
            M=M,
            G=G,
            H=section_in.shape[2] // G,
            W=section_in.shape[3],
            C=conv_shared.shape[3],
            T=task_in.shape[1],
            n=bands // TEAM,
            to_all=frozenset(range(0, 8)) | frozenset(range(31, 39)),
        )
        return jax.shard_map(
            functools.partial(per_device, cfg), mesh=mesh, in_specs=in_specs, out_specs=out_specs, check_vma=False
        )(section_in, image_start, pool_choice, conv_shared, task_in, task_mid, task_conv, bn_gain, bn_bias)

    return step
```

```python
import functools

import jax
import jax.numpy as jnp
import numpy as np
from jax import lax
from jax.experimental import pallas as pl
from jax.experimental.pallas import tpu as pltpu
from jax.sharding import PartitionSpec as P

MESH = pl.DeviceIdType.MESH
half = jnp.bfloat16
f32 = jnp.float32
epsilon = 1e-05
TEAM = 4

ANY = pl.BlockSpec(memory_space=pl.ANY)
VMEM = pl.BlockSpec(memory_space=pltpu.VMEM)


def sigmoid(x):
    return 0.5 * jnp.tanh(0.5 * x) + 0.5


def dot(a, b):
    return jnp.dot(a, b, preferred_element_type=f32)


def dot_nt(a, b):
    return lax.dot_general(a, b, (((1,), (1,)), ((), ())), preferred_element_type=f32)


def dot_tn(a, b):
    return lax.dot_general(a, b, (((0,), (0,)), ((), ())), preferred_element_type=f32)


class Remote:
    def __init__(self, src, dst, send, recv, to):
        self.src, self.dst, self.send, self.recv, self.to = src, dst, send, recv, to
        self.local = to == lax.axis_index("rows")

    def remote(self):
        return pltpu.make_async_remote_copy(
            src_ref=self.src,
            dst_ref=self.dst,
            send_sem=self.send,
            recv_sem=self.recv,
            device_id=(lax.axis_index("pipe"), self.to),
            device_id_type=MESH,
        )

    def start(self):
        @pl.when(self.local)
        def _():
            pltpu.make_async_copy(self.src, self.dst, self.recv).start()

        @pl.when(jnp.logical_not(self.local))
        def _():
            self.remote().start()

    def sent(self):
        @pl.when(jnp.logical_not(self.local))
        def _():
            self.remote().wait_send()


def arrived(dst, sem):
    pltpu.make_async_copy(dst, dst, sem).wait()


EDGES = 13


def section_kernel(cfg, *refs):
    M, G, H, W, C, T = cfg["M"], cfg["G"], cfg["H"], cfg["W"], cfg["C"], cfg["T"]
    R = M * G
    pix = H * W
    part = pix // M
    count = float(pix * G)
    norms = 2 + 3 * T
    direct = cfg["direct"]
    (sec, sel, msks, perm, perm_t, spread, spread_edge, pool, gain, bias, wc, wi, wm, wt) = refs[:14]
    (out, bng, xu, xh, xp, xt, xv, xd5, xd5e, xd4, xd3, xd1, xd1e) = refs[14:27]
    refs = refs[27:]
    if direct:
        (gm, g1, gi, gt) = refs[:4]
        flows_in = refs[4:8]
        ends = refs[8:12]
        (d4, d5e, d1e, l_sem, fl_s, fl_r, fl_l, sh_s, sh_r, o_sem) = refs[-10:]
        refs = refs[12:-10]
    (
        kc, ki, km, kt, rin, field, selin, chosen, uh, selh, uedge, px, ps, rb, ys, esend, erecv, ssend, srecv,
        h1, h2, h2e, t1, pr, res, dz, dh, dy5, dy5e, dy2, dy2e, dy4, dy3, dy1, dy1e, bn, bnr,
        go, w_sem, in_s, in_r, ed_s, ed_r, st_s, st_r, pp_s, pp_r, out_s, out_r, bn_s, bn_r, x_s, x_r,
    ) = refs
    p = lax.axis_index("pipe")
    r = lax.axis_index("rows")
    b, m = r // M, r % M
    e, e0 = m, r - m
    first, last = b == 0, b == G - 1
    CW = C * (1 + T)

    loads = {}

    def load(name, src, dst, i):
        loads[name] = pltpu.make_async_copy(src, dst, w_sem.at[i])
        loads[name].start()

    load("c0", wc.at[0], kc.at[0], 0)
    load("i", wi, ki, 1)
    load("c1", wc.at[1], kc.at[1], 2)
    load("m", wm, km, 3)
    for t in range(T):
        load("t%d" % t, wt.at[t], kt.at[t], 4 + t)

    zero_col = jnp.zeros((H, C), half)
    for a in range(3):
        rb[a, 0:H, :] = zero_col
        rb[a, H * (W + 1) : H * (W + 2), :] = zero_col
    px[pix // 4 :, :] = jnp.zeros((px.shape[0] - pix // 4, CW), half)

    @pl.when(first)
    def _():
        for s in range(EDGES):
            erecv[s, 0] = jnp.zeros((W, 1, C), f32)
        uh[0] = jnp.zeros((32, C), half)
        selh[0] = jnp.zeros((32, 128), half)

    @pl.when(last)
    def _():
        for s in range(EDGES):
            erecv[s, 1] = jnp.zeros((W, 1, C), f32)
        uh[1] = jnp.zeros((32, C), half)
        selh[1] = jnp.zeros((32, 128), half)

    bar = pltpu.get_barrier_semaphore()

    def hello(side, row):
        pl.semaphore_signal(bar, inc=1, device_id=(side, row), device_id_type=MESH)

    for d in range(1, M):
        hello(p, e0 + lax.rem(m + d, M))
    for d in range(1, G):
        hello(p, M * lax.rem(b + d, G) + m)
    hello(1 - p, r)
    tops = jnp.logical_and(m == M - 1, jnp.logical_not(last))
    bottoms = jnp.logical_and(m == 0, jnp.logical_not(first))

    @pl.when(jnp.logical_not(first))
    def _():
        hello(1 - p, r - M)
        hello(p, e0 - 1)

    @pl.when(jnp.logical_not(last))
    def _():
        hello(1 - p, r + M)
        hello(p, e0 + M)

    @pl.when(tops)
    def _():
        for j in range(M):
            hello(p, e0 + M + j)

    @pl.when(bottoms)
    def _():
        for j in range(M):
            hello(p, e0 - M + j)

    below_me, above_me = 1 - (b + 1) // G, (b + G - 1) // G
    top_member, bottom_member = (m + 1) // M, 1 - (m + M - 1) // M
    pl.semaphore_wait(
        bar, M + G - 1 + 2 * (below_me + above_me) + M * (top_member * below_me + bottom_member * above_me)
    )

    mine = pl.ds(pl.multiple_of(part * m, 16), part)
    field_moves, rest_moves, sel_moves, edge_moves = [], [], [], ([], [])
    for d in range(M):
        j = lax.rem(m + d, M)
        to = e0 + j
        field_moves.append(Remote(sec.at[j, :, 0:C], rin.at[mine, 0:C], in_s.at[0, d], in_r.at[0, m], to))
        sel_moves.append(Remote(sel.at[j], selin.at[mine], in_s.at[2, d], in_r.at[2, m], to))
        rest_moves.append(Remote(sec.at[j, :, C:CW], rin.at[mine, C:CW], in_s.at[1, d], in_r.at[1, m], to))
    for j in range(M):
        to = e0 + j
        edge_moves[0].append(
            Remote(sec.at[j, pl.ds(part - 32, 32), 0:C], uh.at[0], in_s.at[3, j], in_r.at[3, 0], to + M)
        )
        edge_moves[0].append(Remote(sel.at[j, pl.ds(part - 32, 32)], selh.at[0], in_s.at[4, j], in_r.at[3, 1], to + M))
        edge_moves[1].append(Remote(sec.at[j, pl.ds(0, 32), 0:C], uh.at[1], in_s.at[5, j], in_r.at[4, 0], to - M))
        edge_moves[1].append(Remote(sel.at[j, pl.ds(0, 32)], selh.at[1], in_s.at[6, j], in_r.at[4, 1], to - M))

    def start_field():
        for move in field_moves:
            move.start()
        for move in rest_moves:
            move.start()

    @pl.when(tops)
    def _():
        for move in edge_moves[0]:
            move.start()

    @pl.when(bottoms)
    def _():
        for move in edge_moves[1]:
            move.start()

    @pl.when(p == 0)
    def _():
        start_field()

    for move in sel_moves:
        move.start()

    row_of = lax.broadcasted_iota(jnp.int32, (H, C), 0)
    at_top, at_bottom = row_of == 0, row_of == H - 1

    def column(j):
        return pl.ds(pl.multiple_of(j * H, H), H)

    def over_columns(body, start=0, step=2):
        def several(c, carry):
            for u in range(step):
                carry = body(c * step + u, carry)
            return carry

        return lax.fori_loop(0, W // step, several, start)

    def build(j, value, above, below, up, down):
        here = pl.ds(pl.multiple_of(H + j * H, H), H)
        rb[1, here, :] = value.astype(half)
        rb[0, here, :] = (jnp.where(at_top, above, pltpu.roll(value, 1, 0)) * up).astype(half)
        rb[2, here, :] = (jnp.where(at_bottom, below, pltpu.roll(value, H - 1, 0)) * down).astype(half)

    def conv(kernel):
        total = None
        for tap in range(9):
            a, c = tap // 3, tap % 3
            term = dot(rb[a, H * c : H * c + pix, :], kernel[tap * C : (tap + 1) * C, :])
            total = term if total is None else total + term
        return total

    def conv_t(kernel):
        total = None
        for tap in range(9):
            a, c = tap // 3, tap % 3
            term = dot_nt(rb[a, H * c : H * c + pix, :], kernel[(8 - tap) * C : (9 - tap) * C, :])
            total = term if total is None else total + term
        return total

    def folded(total):
        return jnp.sum(total, 0, keepdims=True)

    def fold(x):
        return jnp.sum(x.reshape(H // 8, 8, C), 0)

    zero8 = jnp.zeros((8, C), f32)

    def edge_copy(slot, side):
        to = r - M if side == 0 else r + M
        return pltpu.make_async_remote_copy(
            src_ref=esend.at[slot, side],
            dst_ref=erecv.at[slot, 1 - side],
            send_sem=ed_s.at[slot, side],
            recv_sem=ed_r.at[slot, 1 - side],
            device_id=(p, to),
            device_id_type=MESH,
        )

    def send_edges(slot):
        @pl.when(jnp.logical_not(first))
        def _():
            edge_copy(slot, 0).start()

        @pl.when(jnp.logical_not(last))
        def _():
            edge_copy(slot, 1).start()

    def get_edges(slot):
        @pl.when(jnp.logical_not(first))
        def _():
            arrived(erecv.at[slot, 0], ed_r.at[slot, 0])

        @pl.when(jnp.logical_not(last))
        def _():
            arrived(erecv.at[slot, 1], ed_r.at[slot, 1])

    def finish_edges(slot):
        @pl.when(jnp.logical_not(first))
        def _():
            edge_copy(slot, 0).wait_send()

        @pl.when(jnp.logical_not(last))
        def _():
            edge_copy(slot, 1).wait_send()

    def stat_copy(slot, n, d):
        to = M * lax.rem(b + d, G) + m
        return pltpu.make_async_remote_copy(
            src_ref=ssend.at[pl.ds(slot, n)],
            dst_ref=srecv.at[b, pl.ds(slot, n)],
            send_sem=st_s.at[slot, d],
            recv_sem=st_r.at[slot, b],
            device_id=(p, to),
            device_id_type=MESH,
        )

    def send_sums(slot, n):
        srecv[b, slot : slot + n] = ssend[slot : slot + n]
        for d in range(1, G):
            stat_copy(slot, n, d).start()

    sums_sent = []

    def get_sums(slot, n):
        sums_sent.append((slot, n))
        for d in range(1, G):
            s = lax.rem(b + d, G)
            arrived(srecv.at[s, pl.ds(slot, n)], st_r.at[slot, s])

    def total(slot):
        acc = srecv[0, slot]
        for g in range(1, G):
            acc = acc + srecv[g, slot]
        return acc

    def put_sums(slot, s, q):
        ssend[slot] = jnp.concatenate([folded(s), folded(q)], 0)

    x_moves = []
    kept = []

    def post(index, src, dst, target, keep=False):
        move = Remote(src, dst.at[e], x_s.at[index], x_r.at[index - (target if index in cfg["to_all"] else 0), e], e0 + target)
        x_moves.append(move)
        if not keep:
            move.start()
        else:
            kept.append(move)

            @pl.when(p == 0)
            def _():
                move.start()

    def send_kept():
        for move in kept:
            move.start()


    def moments(k, slot, edge=None):
        def body(j, carry):
            s, q = carry
            y = ys[k, column(j), :]
            if edge is not None:
                esend[edge, 0, j] = y[0:1]
                esend[edge, 1, j] = y[H - 1 : H]
            return s + fold(y), q + fold(y * y)

        s, q = over_columns(body, (zero8, zero8))
        put_sums(slot, s, q)

    norm = {}

    def norm_rows(k, slot):
        acc = total(slot)
        mean = acc[0:1] / count
        rs = lax.rsqrt(acc[1:2] / count - mean * mean + epsilon)
        scale = gain[k : k + 1, :] * rs
        norm[k] = (mean, rs, scale, bias[k : k + 1, :])

    def normed(k, y):
        mean, rs, scale, shift = norm[k]
        return (y - mean) * scale + shift

    def silu(x):
        return x * sigmoid(x)

    def silu_slope(x):
        s = sigmoid(x)
        return s * (1.0 + x * (1.0 - s))

    def pair(slot, j):
        return jnp.concatenate([erecv[slot, 0, j], erecv[slot, 1, j]], 0)

    nt = 2 + 3 * T
    F3, F4, F5 = 2, 2 + T, 2 + 2 * T

    def wait_field(kind, buffer):
        for k in range(M):
            arrived(buffer(k), in_r.at[kind, k])

    @pl.when(jnp.logical_not(first))
    def _():
        arrived(uh.at[0], in_r.at[3, 0])

    @pl.when(jnp.logical_not(last))
    def _():
        arrived(uh.at[1], in_r.at[4, 0])

    def start_of_field():
        wait_field(0, lambda k: rin.at[pl.ds(part * k, part), 0:C])
        field[p, :, 0:C] = dot(perm[...], rin[:, 0:C]).astype(half)

    def rest_of_field():
        wait_field(1, lambda k: rin.at[pl.ds(part * k, part), C:CW])
        for t in range(T):
            cols = slice((t + 1) * C, (t + 2) * C)
            field[p, :, cols] = dot(perm[...], rin[:, cols]).astype(half)

    @pl.when(p == 0)
    def _():
        start_of_field()

    def wait_selection():
        wait_field(2, lambda k: selin.at[pl.ds(part * k, part)])

        @pl.when(jnp.logical_not(first))
        def _():
            arrived(selh.at[0], in_r.at[3, 1])

        @pl.when(jnp.logical_not(last))
        def _():
            arrived(selh.at[1], in_r.at[4, 1])

    def halo_copies():
        return (
            pltpu.make_async_remote_copy(
                src_ref=ps.at[pl.ds(pix // 4, 16), 0:C], dst_ref=px.at[pl.ds(pix // 4, 16), 0:C],
                send_sem=pp_s.at[1], recv_sem=pp_r.at[1], device_id=(1 - p, r + M), device_id_type=MESH),
            pltpu.make_async_remote_copy(
                src_ref=ps.at[pl.ds(pix // 4 + 16, 16), 0:C], dst_ref=px.at[pl.ds(pix // 4 + 16, 16), 0:C],
                send_sem=pp_s.at[2], recv_sem=pp_r.at[2], device_id=(1 - p, M * (b - 1) + m), device_id_type=MESH),
        )

    def pool_copy():
        return pltpu.make_async_remote_copy(
            src_ref=ps.at[pl.ds(0, pix // 4)], dst_ref=px.at[pl.ds(0, pix // 4)],
            send_sem=pp_s.at[0], recv_sem=pp_r.at[0], device_id=(1 - p, r), device_id_type=MESH)

    @pl.when(p == 1)
    def _():
        wait_selection()
        chosen[...] = spread[...] * dot(perm[...], selin[...]).astype(half)
        pl.semaphore_wait(go, 1)
        start_field()
        start_of_field()
        rest_of_field()
        arrived(px.at[pl.ds(0, pix // 4)], pp_r.at[0])

        @pl.when(jnp.logical_not(first))
        def _():
            arrived(px.at[pl.ds(pix // 4, 16), 0:C], pp_r.at[1])

        @pl.when(jnp.logical_not(last))
        def _():
            arrived(px.at[pl.ds(pix // 4 + 16, 16), 0:C], pp_r.at[2])

        for t in range(1 + T):
            cols = slice(t * C, (t + 1) * C)
            field[0, :, cols] = dot(chosen[...], px[:, cols]).astype(half)
        edges = spread_edge[...] * jnp.concatenate([selh[0], selh[1]], 0)
        both = dot(edges, px[:, 0:C]).astype(half)
        uh[0] = both[0:32]
        uh[1] = both[32:64]

    above = uh[0].astype(f32)
    below = uh[1].astype(f32)
    for j in range(W):
        uedge[0, j] = above[32 - W + j : 33 - W + j]
        uedge[1, j] = below[j : j + 1]

    up = msks[m, 0]
    down = msks[m, 1]

    def body_u(j, carry):
        build(j, field[0, column(j), 0:C].astype(f32), uedge[0, j], uedge[1, j], up, down)
        return carry

    over_columns(body_u)
    loads["c0"].wait()
    ys[0] = conv(kc.at[0])
    moments(0, 0, 0)
    send_sums(0, 1)
    send_edges(0)

    @pl.when(p == 0)
    def _():
        rest_of_field()
        pl.semaphore_signal(go, inc=1, device_id=(1 - p, r), device_id_type=MESH)

    for q in range(TEAM):
        post(q, field.at[0, :, 0:C], xu, q, True)
    for t in range(T):
        post(8 + t, field.at[0, :, (t + 1) * C : (t + 2) * C], xv, t, True)
    get_sums(0, 1)
    get_edges(0)
    norm_rows(0, 0)

    def body_h1(j, carry):
        value = silu(normed(0, ys[0, column(j), :]))
        side = silu(normed(0, pair(0, j)))
        h1[column(j), :] = value.astype(half)
        build(j, value, side[0:1], side[1:2], up, down)
        return carry

    over_columns(body_h1)
    for q in range(TEAM):
        post(4 + q, h1, xh, q, q < T)

    loads["i"].wait()
    for t in range(T):
        k = 2 + 3 * t
        ys[k] = dot(h1[...], ki[t, 0:C, :]) + dot(field[0, :, (t + 1) * C : (t + 2) * C], ki[t, C : 2 * C, :])
        moments(k, F3 + t)
    send_sums(F3, T)
    loads["c1"].wait()
    ys[1] = conv(kc.at[1])
    moments(1, 1, 1)
    send_sums(1, 1)
    send_edges(1)

    get_sums(F3, T)
    loads["m"].wait()
    for t in range(T):
        k = 2 + 3 * t
        norm_rows(k, F3 + t)

        def body_t1(j, carry):
            t1[t, column(j), :] = silu(normed(k, ys[k, column(j), :])).astype(half)
            return carry

        over_columns(body_t1)
        post(11 + t, t1.at[t], xt, t, True)
        ys[k + 1] = dot(t1[t], km[t])
        moments(k + 1, F4 + t, 2 + t)
        send_sums(F4 + t, 1)
        send_edges(2 + t)

    get_sums(1, 1)
    get_edges(1)
    norm_rows(1, 1)

    def body_h2(j, carry):
        value = silu(normed(1, ys[1, column(j), :])).astype(half)
        h2[column(j), :] = value
        res[column(j), 0:C] = value
        side = silu(normed(1, pair(1, j))).astype(half).astype(f32)
        h2e[j] = side
        return carry

    over_columns(body_h2)
    for t in range(T):
        k = 3 + 3 * t
        get_sums(F4 + t, 1)
        get_edges(2 + t)
        norm_rows(k, F4 + t)

        def body_p(j, carry):
            gate = sigmoid(normed(k, ys[k, column(j), :]))
            value = gate * h2[column(j), :].astype(f32)
            side = sigmoid(normed(k, pair(2 + t, j))) * h2e[j]
            pr[t, column(j), :] = value.astype(half)
            build(j, value, side[0:1], side[1:2], up, down)
            return carry

        over_columns(body_p)
        post(14 + t, pr.at[t], xp, t)
        loads["t%d" % t].wait()
        ys[k + 1] = conv(kt.at[t])
        moments(k + 1, F5 + t, 5 + t)
        send_sums(F5 + t, 1)
        send_edges(5 + t)
    for t in range(T):
        k = 4 + 3 * t
        get_sums(F5 + t, 1)
        get_edges(5 + t)
        norm_rows(k, F5 + t)

        def body_q(j, carry):
            res[column(j), (t + 1) * C : (t + 2) * C] = silu(normed(k, ys[k, column(j), :])).astype(half)
            return carry

        over_columns(body_q)

    def out_moves(which):
        cols = slice(0, C) if which == 0 else slice(C, CW)
        moves = []
        for d in range(M):
            k = lax.rem(m + d, M)
            rows = pl.ds(pl.multiple_of(part * k, 16), part)
            moves.append(
                Remote(rin.at[rows, cols], out.at[m, :, cols], out_s.at[which, d], out_r.at[which, m], e0 + k)
            )
        return moves

    def stage_result(which):
        for t in range(0, 1) if which == 0 else range(1, 1 + T):
            cols = slice(t * C, (t + 1) * C)
            rin[:, cols] = dot(perm_t[...], res[:, cols]).astype(half)

    def start_result(which):
        for move in out_moves(which):
            move.start()

    @pl.when(p == 0)
    def _():
        for t in range(1 + T):
            cols = slice(t * C, (t + 1) * C)
            ps[:, cols] = dot(pool[...], res[:, cols]).astype(half)
        pool_copy().start()

        @pl.when(jnp.logical_not(last))
        def _():
            halo_copies()[0].start()

        @pl.when(jnp.logical_not(first))
        def _():
            halo_copies()[1].start()

        pool_copy().wait_send()

        @pl.when(jnp.logical_not(last))
        def _():
            halo_copies()[0].wait_send()

        @pl.when(jnp.logical_not(first))
        def _():
            halo_copies()[1].wait_send()

        arrived(px.at[pl.ds(0, pix // 4)], pp_r.at[0])
        for t in range(1 + T):
            cols = slice(t * C, (t + 1) * C)
            field[1, :, cols] = (dot(spread[...], px[:, cols]) * 0.25).astype(half)

    @pl.when(p == 1)
    def _():
        stage_result(0)
        stage_result(1)

    B3, B4, B5 = nt + F3, nt + F4, nt + F5
    back = {}

    def back_rows(k, slot):
        acc = total(slot)
        mean, rs, scale, shift = norm[k]
        slope = -scale * rs * acc[1:2] / count
        back[k] = (scale, slope, -scale * acc[0:1] / count - slope * mean)
        bn[k : k + 1, :] = acc[1:2]
        bn[norms + k : norms + k + 1, :] = acc[0:1]

    def grad_pre(k, dzv, y):
        scale, slope, rest = back[k]
        return scale * dzv + slope * y + rest

    def hat(k, y):
        mean, rs, scale, shift = norm[k]
        return (y - mean) * rs

    for t in range(T):
        k = 4 + 3 * t

        def body_dz5(j, carry):
            s, q = carry
            y = ys[k, column(j), :]
            g = field[1, column(j), (t + 1) * C : (t + 2) * C].astype(f32)
            v = g * silu_slope(normed(k, y))
            dz[t, column(j), :] = v
            esend[8 + t, 0, j] = v[0:1]
            esend[8 + t, 1, j] = v[H - 1 : H]
            return s + fold(v), q + fold(v * hat(k, y))

        s, q = over_columns(body_dz5, (zero8, zero8))
        put_sums(B5 + t, s, q)
        send_sums(B5 + t, 1)
        send_edges(8 + t)

    for t in range(T):
        k = 4 + 3 * t
        get_sums(B5 + t, 1)
        get_edges(8 + t)
        back_rows(k, B5 + t)

        def body_dy5(j, carry):
            v = grad_pre(k, dz[t, column(j), :], ys[k, column(j), :])
            side = grad_pre(k, pair(8 + t, j), pair(5 + t, j))
            dy5[t, column(j), :] = v.astype(half)
            dy5e[t, 0, j] = side[0:1]
            dy5e[t, 1, j] = side[1:2]
            build(j, v, side[0:1], side[1:2], up, down)
            return carry

        over_columns(body_dy5)
        post(17 + t, dy5.at[t], xd5, t)
        post(21 + t, dy5e.at[t], xd5e, t)
        ys[k] = conv_t(kt.at[t])

        def body_dz4(j, carry):
            s, q = carry
            dp = ys[k, column(j), :]
            y = ys[k - 1, column(j), :]
            gate = sigmoid(normed(k - 1, y))
            dgate = dp * h2[column(j), :].astype(f32)
            base = field[1, column(j), 0:C].astype(f32) if t == 0 else dh[column(j), :]
            dh[column(j), :] = base + dp * gate
            v = dgate * gate * (1.0 - gate)
            ys[k, column(j), :] = v
            return s + fold(v), q + fold(v * hat(k - 1, y))

        s, q = over_columns(body_dz4, (zero8, zero8))
        put_sums(B4 + t, s, q)
        send_sums(B4 + t, 1)

    def body_dz2(j, carry):
        s, q = carry
        y = ys[1, column(j), :]
        v = dh[column(j), :] * silu_slope(normed(1, y))
        dh[column(j), :] = v
        esend[11, 0, j] = v[0:1]
        esend[11, 1, j] = v[H - 1 : H]
        return s + fold(v), q + fold(v * hat(1, y))

    s, q = over_columns(body_dz2, (zero8, zero8))
    put_sums(nt + 1, s, q)
    send_sums(nt + 1, 1)
    send_edges(11)

    for t in range(T):
        k = 3 + 3 * t
        get_sums(B4 + t, 1)
        back_rows(k, B4 + t)

        def body_dy4(j, carry):
            dy4[t, column(j), :] = grad_pre(k, ys[k + 1, column(j), :], ys[k, column(j), :]).astype(half)
            return carry

        over_columns(body_dy4)
        post(25 + t, dy4.at[t], xd4, t)
        dz[t] = dot_nt(dy4[t], km[t])

        def body_dz3(j, carry):
            s, q = carry
            y = ys[k - 1, column(j), :]
            v = dz[t, column(j), :] * silu_slope(normed(k - 1, y))
            dz[t, column(j), :] = v
            return s + fold(v), q + fold(v * hat(k - 1, y))

        s, q = over_columns(body_dz3, (zero8, zero8))
        put_sums(B3 + t, s, q)
    send_sums(B3, T)

    get_sums(nt + 1, 1)
    get_edges(11)
    back_rows(1, nt + 1)

    def body_dy2(j, carry):
        v = grad_pre(1, dh[column(j), :], ys[1, column(j), :])
        side = grad_pre(1, pair(11, j), pair(1, j))
        dy2[column(j), :] = v.astype(half)
        dy2e[0, j] = side[0:1]
        dy2e[1, j] = side[1:2]
        build(j, v, side[0:1], side[1:2], up, down)
        return carry

    over_columns(body_dy2)
    post(20, dy2, xd5, TEAM - 1)
    post(24, dy2e, xd5e, TEAM - 1)

    @pl.when(p == 1)
    def _():
        send_kept()


    dh[...] = conv_t(kc.at[1])

    get_sums(B3, T)
    for t in range(T):
        k = 2 + 3 * t
        back_rows(k, B3 + t)

        def body_dy3(j, carry):
            dy3[t, column(j), :] = grad_pre(k, dz[t, column(j), :], ys[k, column(j), :]).astype(half)
            return carry

        over_columns(body_dy3)
        post(28 + t, dy3.at[t], xd3, t)
        dh[...] += dot_nt(dy3[t], ki[t, 0:C, :])
        res[:, (t + 1) * C : (t + 2) * C] = dot_nt(dy3[t], ki[t, C : 2 * C, :]).astype(half)

    @pl.when(p == 0)
    def _():
        stage_result(1)
        start_result(1)

    def body_dz1(j, carry):
        s, q = carry
        y = ys[0, column(j), :]
        v = dh[column(j), :] * silu_slope(normed(0, y))
        dh[column(j), :] = v
        esend[12, 0, j] = v[0:1]
        esend[12, 1, j] = v[H - 1 : H]
        return s + fold(v), q + fold(v * hat(0, y))

    s, q = over_columns(body_dz1, (zero8, zero8))
    put_sums(nt, s, q)
    send_sums(nt, 1)
    send_edges(12)
    get_sums(nt, 1)
    get_edges(12)
    back_rows(0, nt)

    def bn_moves():
        return [Remote(bn, bnr.at[m], bn_s.at[d], bn_r.at[m], e0 + lax.rem(m + d, M)) for d in range(M)]

    for move in bn_moves():
        move.start()

    quarter = C // TEAM

    def body_dy1(j, carry):
        v = grad_pre(0, dh[column(j), :], ys[0, column(j), :])
        side = grad_pre(0, pair(12, j), pair(0, j))
        low = v.astype(half)
        for o in range(TEAM):
            cols = slice(o * quarter, (o + 1) * quarter)
            dy1[o, column(j), :] = low[:, cols]
            dy1e[o, 0, j] = side[0:1, cols]
            dy1e[o, 1, j] = side[1:2, cols]
        build(j, v, side[0:1], side[1:2], up, down)
        return carry

    over_columns(body_dy1)
    for o in range(TEAM):
        post(31 + o, dy1.at[o], xd1, o)
        post(35 + o, dy1e.at[o], xd1e, o)
    res[:, 0:C] = conv_t(kc.at[0]).astype(half)

    @pl.when(p == 1)
    def _():
        for t in range(1 + T):
            cols = slice(t * C, (t + 1) * C)
            ps[0 : pix // 4, cols] = dot_tn(chosen[...], res[:, cols])[0 : pix // 4].astype(half)
        pool_copy().start()
        start_result(0)
        start_result(1)
        pool_copy().wait_send()

    @pl.when(p == 0)
    def _():
        stage_result(0)
        start_result(0)

    def finish_sends():
        for move in field_moves + rest_moves + sel_moves:
            move.sent()

        @pl.when(tops)
        def _():
            for move in edge_moves[0]:
                move.sent()

        @pl.when(bottoms)
        def _():
            for move in edge_moves[1]:
                move.sent()

        for s in range(EDGES):
            finish_edges(s)
        for slot, n in sums_sent:
            for d in range(1, G):
                stat_copy(slot, n, d).wait_send()

        @pl.when(p == 0)
        def _():
            wait_selection()

    if not direct:
        finish_sends()
    if direct:
        z, n = b, R // TEAM
        q4 = quarter
        all_rows = TEAM * pix
        wide = pix + 2 * H
        task = e < T
        vb, va, vc = (kt.at[2, i * all_rows : (i + 1) * all_rows, :] for i in range(3))
        vd, d5, d3 = (kc.at[0, i * all_rows : (i + 1) * all_rows, :] for i in range(3))
        pm, p1, pi_, pt = kt.at[0], kc.at[0, :, 0:q4], ki.at[0], km.at[0]
        d1 = kt.at[1, 0:all_rows, 3 * q4 : 4 * q4]
        rows_m, rows_i, rows_t = 9 * C // R, 2 * C // R, C // R

        def band(ref, j):
            return ref.at[j * pix : (j + 1) * pix]

        def fetch(index, src, j, dst, sem):
            arrived(src.at[j], sem)
            copy = pltpu.make_async_copy(src.at[j], dst, l_sem.at[index, j])
            copy.start()
            return copy

        def rows_shifted(j, a, lo):
            if j < TEAM - 1:
                start = (3 * j + a) * wide + lo
                return kc.at[1, start : start + pix, :]
            return rb.at[a, lo : lo + pix, :]

        for j in range(TEAM - 1):
            for a in range(3):
                start = (3 * j + a) * wide
                kc[1, start : start + H, :] = zero_col
                kc[1, start + H + pix : start + wide, :] = zero_col
        got = {}
        for j in range(TEAM):
            got["d5", j] = fetch(0, xd5, j, band(d5, j), x_r.at[17 + e, j])
            got["d5e", j] = fetch(1, xd5e, j, d5e.at[j], x_r.at[21 + e, j])

        @pl.when(task)
        def _():
            for j in range(TEAM):
                fetch(3, xp, j, band(vb, j), x_r.at[14 + e, j])

        @pl.when(jnp.logical_not(task))
        def _():
            for j in range(TEAM):
                fetch(3, xh, j, band(vb, j), x_r.at[4, j])

        for j in range(TEAM):
            got["d5", j].wait()
            got["d5e", j].wait()

            def body_r(i, carry):
                v = kc[0, pl.ds(pl.multiple_of(all_rows + j * pix + i * H, H), H), :].astype(f32)
                three = (
                    (jnp.where(at_top, d5e[j, 0, i], pltpu.roll(v, 1, 0)) * msks[j, 0]).astype(half),
                    v.astype(half),
                    (jnp.where(at_bottom, d5e[j, 1, i], pltpu.roll(v, H - 1, 0)) * msks[j, 1]).astype(half),
                )
                for a in range(3):
                    if j < TEAM - 1:
                        here = pl.ds(pl.multiple_of((3 * j + a) * wide + H + i * H, H), H)
                        kc[1, here, :] = three[a]
                    else:
                        rb[a, pl.ds(pl.multiple_of(H + i * H, H), H), :] = three[a]
                return carry

            over_columns(body_r)
        for j in range(TEAM):
            pltpu.make_async_copy(xp.at[j], band(vb, j), l_sem.at[3, j]).wait()

        for tap in range(9):
            a, c = 2 - tap // 3, 2 - tap % 3
            acc = None
            for j in range(TEAM):
                term = dot_tn(band(vb, j)[...], rows_shifted(j, a, H * c)[...])
                acc = term if acc is None else acc + term
            pm[tap * C : (tap + 1) * C, :] = acc.astype(half)

        partial = (pm, pi_, pt, p1)
        share = (rows_m, rows_i, rows_t, rows_m)
        pieces = (TEAM, 1, 1, 1)
        width = (C, C, C, q4)

        def flow(g, zd, s, way):
            rows = TEAM * share[g] // pieces[g]
            return pltpu.make_async_remote_copy(
                src_ref=partial[g].at[pl.ds(pl.multiple_of((zd * pieces[g] + s) * rows, 16), rows)],
                dst_ref=flows_in[g].at[way, zd, pl.ds(pl.multiple_of(s * rows, 16), rows)],
                send_sem=fl_s.at[way, g, zd, s],
                recv_sem=fl_r.at[way, g, zd, s],
                device_id=(p, r + TEAM * (1 - 2 * way)),
                device_id_type=MESH,
            )

        def incoming(g, zd, s, way, lane):
            rows = TEAM * share[g] // pieces[g]
            src = flows_in[g].at[way, zd, pl.ds(pl.multiple_of(s * rows, 16), rows)]
            dst = kc.at[1, lane * TEAM * rows_m : lane * TEAM * rows_m + rows, 0 : width[g]]
            return src, dst, fl_r.at[way, g, zd, s], fl_l.at[lane]

        def take(g, zd, s, way, lane):
            src, dst, sem, local = incoming(g, zd, s, way, lane)
            arrived(src, sem)
            pltpu.make_async_copy(src, dst, local).start()

        def taken(g, zd, s, way, lane):
            src, dst, sem, local = incoming(g, zd, s, way, lane)
            pltpu.make_async_copy(src, dst, local).wait()
            return dst[...].astype(f32)

        def flow_start(g):
            @pl.when(z == 0)
            def _():
                for zd in range(n - 1, 0, -1):
                    for s in range(pieces[g]):
                        flow(g, zd, s, 0).start()

            @pl.when(z == n - 1)
            def _():
                for zd in range(n - 1):
                    for s in range(pieces[g]):
                        flow(g, zd, s, 1).start()

        def flow_mid(groups):
            upper = (2 * z) // n

            @pl.when(jnp.logical_and(z > 0, z < n - 1))
            def _():
                for phase in range(2):
                    way = lax.rem(phase + upper, 2)
                    for g in groups:
                        rows = TEAM * share[g] // pieces[g]

                        def body_flow(i, carry):
                            k, s = i // pieces[g], i % pieces[g]
                            zd = (1 - way) * (n - 1 - k) + way * k

                            @pl.when((1 - 2 * way) * (zd - z) > 0)
                            def _():
                                take(g, zd, s, way, 0)
                                here = partial[g].at[pl.ds(pl.multiple_of((zd * pieces[g] + s) * rows, 16), rows)]
                                here[...] = (here[...].astype(f32) + taken(g, zd, s, way, 0)).astype(half)
                                flow(g, zd, s, way).start()

                            return carry

                        lax.fori_loop(0, (n - 1) * pieces[g], body_flow, 0)

        def share_moves(g):
            moves = []
            for d in range(TEAM):
                q = lax.rem(e + d, TEAM)
                start = pl.multiple_of((z * TEAM + q) * share[g], 16)
                moves.append(
                    Remote(partial[g].at[pl.ds(start, share[g])], ends[g].at[e], sh_s.at[g, d], sh_r.at[g, e], e0 + q)
                )
            return moves

        def flow_final(g):
            rows = TEAM * share[g] // pieces[g]
            for s in range(pieces[g]):

                @pl.when(z > 0)
                def _():
                    take(g, z, s, 0, 0)

                @pl.when(z < n - 1)
                def _():
                    take(g, z, s, 1, 1)

                here = partial[g].at[pl.ds(pl.multiple_of(z * TEAM * share[g] + s * rows, 16), rows)]

                @pl.when(jnp.logical_and(z > 0, z < n - 1))
                def _():
                    here[...] = (here[...].astype(f32) + taken(g, z, s, 0, 0) + taken(g, z, s, 1, 1)).astype(half)

                @pl.when(z == 0)
                def _():
                    here[...] = (here[...].astype(f32) + taken(g, z, s, 1, 1)).astype(half)

                @pl.when(z == n - 1)
                def _():
                    here[...] = (here[...].astype(f32) + taken(g, z, s, 0, 0)).astype(half)

            for move in share_moves(g):
                move.start()

        def flow_sent(g):
            for way in range(2):
                for zd in range(n):
                    on = z < zd if way == 0 else z > zd

                    @pl.when(on)
                    def _():
                        for s in range(pieces[g]):
                            flow(g, zd, s, way).wait_send()

            for move in share_moves(g):
                move.sent()

        flow_start(0)

        finish_sends()
        flow_mid((0,))

        first_u = []
        for j in range(TEAM):
            first_u.append(fetch(4, xu, j, band(vb, j), x_r.at[0, j]))

        @pl.when(task)
        def _():
            copies = []
            for j in range(TEAM):
                copies.append(fetch(2, xh, j, band(va, j), x_r.at[4, j]))
                copies.append(fetch(5, xv, j, band(vc, j), x_r.at[8 + e, j]))
                copies.append(fetch(6, xt, j, band(vd, j), x_r.at[11 + e, j]))
                copies.append(fetch(7, xd4, j, band(d4, j), x_r.at[25 + e, j]))
                copies.append(fetch(8, xd3, j, band(d3, j), x_r.at[28 + e, j]))
            for copy in copies:
                copy.wait()
            pi_[0:C, :] = dot_tn(va[...], d3[...]).astype(half)
            pi_[C : 2 * C, :] = dot_tn(vc[...], d3[...]).astype(half)
            pt[...] = dot_tn(vd[...], d4[...]).astype(half)
            flow_start(1)
            flow_start(2)

        for j in range(TEAM):
            got["d1", j] = fetch(9, xd1, j, band(d1, j), x_r.at[31, j])
            got["d1e", j] = fetch(10, xd1e, j, d1e.at[j], x_r.at[35, j])
        row_of1 = lax.broadcasted_iota(jnp.int32, (H, q4), 0)

        def near(j, a, lo, size, cols):
            start = (3 * j + a) * pix + lo
            return kt.at[1, start : start + size, cols * q4 : (cols + 1) * q4]

        for j in range(TEAM):
            got["d1", j].wait()
            got["d1e", j].wait()

        for j in range(TEAM):

            def body_r1(i, carry):
                v = kt[1, pl.ds(pl.multiple_of(j * pix + i * H, H), H), 3 * q4 : 4 * q4].astype(f32)
                three = (
                    (jnp.where(row_of1 == 0, d1e[j, 0, i], pltpu.roll(v, 1, 0)) * msks[j, 0][:, 0:q4]).astype(half),
                    v.astype(half),
                    (jnp.where(row_of1 == H - 1, d1e[j, 1, i], pltpu.roll(v, H - 1, 0)) * msks[j, 1][:, 0:q4]).astype(
                        half
                    ),
                )
                for a in range(3):
                    kt[1, pl.ds(pl.multiple_of((3 * j + a) * pix + i * H, H), H), q4 : 2 * q4] = three[a]
                return carry

            over_columns(body_r1)
            for a in range(3):
                near(j, a, 0, H, 0)[...] = jnp.zeros((H, q4), half)
                near(j, a, H, pix - H, 0)[...] = near(j, a, 0, pix - H, 1)[...]
                near(j, a, 0, pix - H, 2)[...] = near(j, a, H, pix - H, 1)[...]
                near(j, a, pix - H, H, 2)[...] = jnp.zeros((H, q4), half)
        for copy in first_u:
            copy.wait()
        for a in range(3):
            acc = None
            for j in range(TEAM):
                start = (3 * j + 2 - a) * pix
                term = dot_tn(band(vb, j)[...], kt[1, start : start + pix, 0 : 3 * q4])
                acc = term if acc is None else acc + term
            for c in range(3):
                kc[0, (3 * a + c) * C : (3 * a + c + 1) * C, 0:q4] = acc[:, (2 - c) * q4 : (3 - c) * q4].astype(half)
        flow_start(3)

        flow_final(0)

        @pl.when(task)
        def _():
            flow_mid((1, 2, 3))

        @pl.when(jnp.logical_not(task))
        def _():
            flow_mid((3,))

        @pl.when(task)
        def _():
            flow_final(1)
            flow_final(2)

        flow_final(3)

        stores = []

        def store(src, dst, i):
            copy = pltpu.make_async_copy(src, dst, o_sem.at[i])
            copy.start()
            stores.append(copy)

        def last_of(g, members, buffer, base):
            copies = []
            for q in range(members):
                arrived(ends[g].at[q], sh_r.at[g, q])
                copy = pltpu.make_async_copy(
                    ends[g].at[q], buffer.at[q * share[g] : (q + 1) * share[g]], l_sem.at[base, q]
                )
                copy.start()
                copies.append(copy)
            for copy in copies:
                copy.wait()

        def piece(buffer, g, q):
            return buffer[q * share[g] : (q + 1) * share[g], :].astype(f32)

        final_m, final_1 = kc.at[1, 2 * TEAM * rows_m : 3 * TEAM * rows_m, :], kt.at[2, :, 0:q4]
        last_of(0, TEAM, final_m, 11)
        for q in range(TEAM):
            ys[q, 0:rows_m, :] = piece(final_m, 0, q)
            store(ys.at[q, 0:rows_m, :], gm.at[q], q)
        last_of(1, T, ki.at[1], 12)
        last_of(2, T, km.at[1], 13)
        for q in range(T):
            ys[TEAM + 1, q * rows_i : (q + 1) * rows_i, :] = piece(ki.at[1], 1, q)
            ys[TEAM + 2, q * rows_t : (q + 1) * rows_t, :] = piece(km.at[1], 2, q)
        store(ys.at[TEAM + 1, 0 : T * rows_i, :], gi, TEAM)
        store(ys.at[TEAM + 2, 0 : T * rows_t, :], gt, TEAM + 1)
        last_of(3, TEAM, final_1, 14)
        for q in range(TEAM):
            ys[TEAM, 0:rows_m, q * q4 : (q + 1) * q4] = piece(final_1, 3, q)
        store(ys.at[TEAM, 0:rows_m, :], g1, TEAM + 2)
        flow_sent(0)

        @pl.when(task)
        def _():
            flow_sent(1)
            flow_sent(2)

        flow_sent(3)
        for copy in stores:
            copy.wait()

    for k in range(M):
        arrived(bnr.at[k], bn_r.at[k])
    acc = bnr[0]
    for k in range(1, M):
        acc = acc + bnr[k]
    bng[...] = acc
    for k in range(M):
        arrived(out.at[k, :, 0:C], out_r.at[0, k])
        arrived(out.at[k, :, C:CW], out_r.at[1, k])
    for move in out_moves(0) + out_moves(1) + bn_moves():
        move.sent()
    for move in x_moves:
        move.sent()
    if direct:
        return
    for j in range(TEAM):
        for index, dst in ((0, xu), (4, xh), (31, xd1), (35, xd1e)):
            arrived(dst.at[j], x_r.at[index, j])
    for t in range(T):

        @pl.when(e == t)
        def _():
            for j in range(TEAM):
                for index, dst in ((8, xv), (11, xt), (14, xp), (17, xd5), (21, xd5e), (25, xd4), (28, xd3)):
                    arrived(dst.at[j], x_r.at[index + t, j])

    @pl.when(e == TEAM - 1)
    def _():
        for j in range(TEAM):
            arrived(xd5.at[j], x_r.at[20, j])
            arrived(xd5e.at[j], x_r.at[24, j])


def tables(M, G, H, W):
    pix = H * W
    cm = np.zeros((pix, pix), np.float32)
    spread = np.zeros((pix, 128), np.float32)
    pool = np.zeros((128, pix), np.float32)
    edge = np.zeros((64, 128), np.float32)
    wide = W // 2
    own = pix // 4
    for i in range(H):
        for j in range(W):
            q = j * H + i
            cm[q, i * W + j] = 1
            w = (i // 2) * wide + j // 2
            spread[q, w] = 1
            pool[w, q] = 0.25
            if i >= H - 2:
                pool[own + j // 2, q] = 0.25
            if i < 2:
                pool[own + 16 + j // 2, q] = 0.25
    for j in range(W):
        edge[32 - W + j, own + j // 2] = 1
        edge[32 + j, own + 16 + j // 2] = 1
    return [jnp.asarray(v, half) for v in (cm, cm.T, spread, edge, pool)]


def gradient_kernel(cfg, *refs):
    M, G, H, W, C, T, n = cfg["M"], cfg["G"], cfg["H"], cfg["W"], cfg["C"], cfg["T"], cfg["n"]
    R = M * G
    pix = H * W
    q4 = C // TEAM
    (msk, xu, xh, xp, xt, xv, xd5, xd5e, xd4, xd3, xd1, xd1e) = refs[:12]
    (gm, g1, gi, gt) = refs[12:16]
    (va, vb, vc, vd, d5, d5e, rb, r1, d1, d1e, d3, pm, p1, pi_, pt, am, a1, ai, at, in_sem, s_sem, r_sem) = refs[16:]
    p = lax.axis_index("pipe")
    r = lax.axis_index("rows")
    e = r % TEAM
    z = r // TEAM
    task = e < T

    loads = {}

    def load(name, src, dst, i):
        loads[name] = pltpu.make_async_copy(src, dst, in_sem.at[i])
        loads[name].start()

    load("d5", xd5, d5, 0)
    load("d5e", xd5e, d5e, 1)
    load("h", xh, va, 2)

    @pl.when(task)
    def _():
        pltpu.make_async_copy(xp, vb, in_sem.at[3]).start()
        pltpu.make_async_copy(xv, vc, in_sem.at[4]).start()
        pltpu.make_async_copy(xt, vd, in_sem.at[5]).start()
        pltpu.make_async_copy(xd3, d3.at[0], in_sem.at[6]).start()
        pltpu.make_async_copy(xd4, d3.at[1], in_sem.at[7]).start()

    bar = pltpu.get_barrier_semaphore()

    def greet(i, _):
        pl.semaphore_signal(bar, inc=1, device_id=(p, lax.rem(r + TEAM * i, R)), device_id_type=MESH)
        return 0

    lax.fori_loop(1, n, greet, 0)

    row_of = lax.broadcasted_iota(jnp.int32, (H, C), 0)
    row_of1 = lax.broadcasted_iota(jnp.int32, (H, q4), 0)

    def column(j):
        return pl.ds(pl.multiple_of(j * H, H), H)

    for j in range(TEAM):
        for a in range(3):
            rb[j, a, 0:H, :] = jnp.zeros((H, C), half)
            rb[j, a, H * (W + 1) : H * (W + 2), :] = jnp.zeros((H, C), half)
            r1[j, a, 0:H, :] = jnp.zeros((H, 3 * q4), half)
            r1[j, a, H * (W - 1) :, :] = jnp.zeros((H, 3 * q4), half)

    loads["d5"].wait()
    loads["d5e"].wait()
    for j in range(TEAM):

        def body(c, carry):
            for u in range(2):
                i = c * 2 + u
                here = pl.ds(pl.multiple_of(H + i * H, H), H)
                v = d5[j, column(i), :].astype(f32)
                rb[j, 1, here, :] = v.astype(half)
                rb[j, 0, here, :] = (jnp.where(row_of == 0, d5e[j, 0, i], pltpu.roll(v, 1, 0)) * msk[j, 0]).astype(half)
                rb[j, 2, here, :] = (
                    jnp.where(row_of == H - 1, d5e[j, 1, i], pltpu.roll(v, H - 1, 0)) * msk[j, 1]
                ).astype(half)
            return carry

        lax.fori_loop(0, W // 2, body, 0)
    loads["h"].wait()

    @pl.when(task)
    def _():
        pltpu.make_async_copy(xp, vb, in_sem.at[3]).wait()
        pltpu.make_async_copy(xv, vc, in_sem.at[4]).wait()
        pltpu.make_async_copy(xt, vd, in_sem.at[5]).wait()
        pltpu.make_async_copy(xd3, d3.at[0], in_sem.at[6]).wait()
        pltpu.make_async_copy(xd4, d3.at[1], in_sem.at[7]).wait()

    @pl.when(jnp.logical_not(task))
    def _():
        vb[...] = va[...]

    for tap in range(9):
        a, c = 2 - tap // 3, 2 - tap % 3
        acc = None
        for j in range(TEAM):
            term = dot_tn(vb[j], rb[j, a, H * c : H * c + pix, :])
            acc = term if acc is None else acc + term
        pm[tap * C : (tap + 1) * C, :] = acc.astype(half)

    pltpu.make_async_copy(xu, vb, in_sem.at[8]).start()
    pltpu.make_async_copy(xd1, d1, in_sem.at[9]).start()
    pltpu.make_async_copy(xd1e, d1e, in_sem.at[10]).start()

    def group(index, src, mine, rows):
        moves = []
        for d in range(1, n):
            to = lax.rem(z + d, n)
            moves.append(
                pltpu.make_async_remote_copy(
                    src_ref=src.at[pl.ds(pl.multiple_of(to * rows, 16), rows)],
                    dst_ref=mine.at[z],
                    send_sem=s_sem.at[index, d],
                    recv_sem=r_sem.at[index, z],
                    device_id=(p, TEAM * to + e),
                    device_id_type=MESH,
                )
            )
        return moves

    rows_m, rows_i, rows_t = 9 * C // n, 2 * C // n, C // n
    pl.semaphore_wait(bar, n - 1)
    main = group(0, pm, am, rows_m)
    for move in main:
        move.start()

    @pl.when(task)
    def _():
        for part, value in ((0, va), (1, vc)):
            acc = None
            for j in range(TEAM):
                term = dot_tn(value[j], d3[0, j])
                acc = term if acc is None else acc + term
            pi_[part * C : (part + 1) * C, :] = acc.astype(half)
        acc = None
        for j in range(TEAM):
            term = dot_tn(vd[j], d3[1, j])
            acc = term if acc is None else acc + term
        pt[...] = acc.astype(half)
        for move in group(1, pi_, ai, rows_i) + group(2, pt, at, rows_t):
            move.start()

    pltpu.make_async_copy(xu, vb, in_sem.at[8]).wait()
    pltpu.make_async_copy(xd1, d1, in_sem.at[9]).wait()
    pltpu.make_async_copy(xd1e, d1e, in_sem.at[10]).wait()
    for j in range(TEAM):

        def body1(i, carry):
            v = d1[j, column(i), :].astype(f32)
            three = (
                (jnp.where(row_of1 == 0, d1e[j, 0, i], pltpu.roll(v, 1, 0)) * msk[j, 0][:, 0:q4]).astype(half),
                v.astype(half),
                (jnp.where(row_of1 == H - 1, d1e[j, 1, i], pltpu.roll(v, H - 1, 0)) * msk[j, 1][:, 0:q4]).astype(half),
            )
            for a in range(3):
                r1[j, a, column(i), q4 : 2 * q4] = three[a]
            return carry

        lax.fori_loop(0, W, body1, 0)
        for a in range(3):
            r1[j, a, H : W * H, 0:q4] = r1[j, a, 0 : (W - 1) * H, q4 : 2 * q4]
            r1[j, a, 0 : (W - 1) * H, 2 * q4 : 3 * q4] = r1[j, a, H : W * H, q4 : 2 * q4]
    for a in range(3):
        acc = None
        for j in range(TEAM):
            term = dot_tn(vb[j], r1[j, 2 - a])
            acc = term if acc is None else acc + term
        for c in range(3):
            p1[(3 * a + c) * C : (3 * a + c + 1) * C, :] = acc[:, (2 - c) * q4 : (3 - c) * q4].astype(half)
    one = group(3, p1, a1, rows_m)
    for move in one:
        move.start()

    def reduce(index, src, mine, rows, dst):
        for d in range(1, n):
            s = lax.rem(z + d, n)
            arrived(mine.at[s], r_sem.at[index, s])
        mine[z] = src[pl.ds(pl.multiple_of(z * rows, 16), rows), :]
        acc = mine[0].astype(f32)
        for s in range(1, n):
            acc = acc + mine[s].astype(f32)
        dst[...] = acc.astype(dst.dtype)

    reduce(0, pm, am, rows_m, gm)

    @pl.when(task)
    def _():
        reduce(1, pi_, ai, rows_i, gi)
        reduce(2, pt, at, rows_t, gt)

    @pl.when(jnp.logical_not(task))
    def _():
        gi[...] = jnp.zeros(gi.shape, gi.dtype)
        gt[...] = jnp.zeros(gt.shape, gt.dtype)

    reduce(3, p1, a1, rows_m, g1)
    for move in main + one:
        move.wait_send()

    @pl.when(task)
    def _():
        for move in group(1, pi_, ai, rows_i) + group(2, pt, at, rows_t):
            move.wait_send()


def per_device(cfg, section_in, image_start, pool_choice, conv_shared, task_in, task_mid, task_conv, bn_gain, bn_bias):
    M, G, H, W, C, T, n = cfg["M"], cfg["G"], cfg["H"], cfg["W"], cfg["C"], cfg["T"], cfg["n"]
    R = M * G
    pix = H * W
    part = pix // M
    rows_total = H * G
    norms = 2 + 3 * T
    CW = C * (1 + T)
    p = lax.axis_index("pipe")
    r = lax.axis_index("rows")
    b, m = r // M, r % M
    sec = section_in[0].reshape(M, part, CW)
    hp = pool_choice.shape[1]
    place = jnp.arange(4, dtype=jnp.int32).reshape(2, 1, 2)
    picked = pool_choice[:, :, None, :, None] == place[None, None]
    sel = jnp.broadcast_to(picked.reshape(M, part, 1), (M, part, 128)).astype(half)

    ones = jnp.ones((M, 1), jnp.int32)
    padded = jnp.concatenate([ones, image_start[:, 1:], ones], 1)
    links = 1.0 - lax.dynamic_slice_in_dim(padded, b * H, H + 1, 1).astype(f32)
    both = jnp.stack([links[:, :-1], links[:, 1:]], 1)
    team_masks = jnp.broadcast_to(both[..., None], (M, 2, H, C))

    cm, cm_t, spread, edge, pool = tables(M, G, H, W)
    sds = jax.ShapeDtypeStruct
    exchange = [
        sds((TEAM, pix, C), half),
        sds((TEAM, pix, C), half),
        sds((TEAM, pix, C), half),
        sds((TEAM, pix, C), half),
        sds((TEAM, pix, C), half),
        sds((TEAM, pix, C), half),
        sds((TEAM, 2, W, 1, C), f32),
        sds((TEAM, pix, C), half),
        sds((TEAM, pix, C), half),
        sds((TEAM, pix, C // TEAM), half),
        sds((TEAM, 2, W, 1, C // TEAM), f32),
    ]
    direct = C % (16 * R) == 0
    parts = R if direct else n
    rows_m, rows_i, rows_t = 9 * C // parts, 2 * C // parts, C // parts
    q4 = C // TEAM
    shares, share_scratch = [], []
    dma = pltpu.SemaphoreType.DMA
    if direct:
        shares = [
            sds((TEAM, rows_m, C), f32),
            sds((rows_m, C), f32),
            sds((T * rows_i, C), f32),
            sds((T * rows_t, C), f32),
            sds((2, n, TEAM * rows_m, C), half),
            sds((2, n, TEAM * rows_i, C), half),
            sds((2, n, TEAM * rows_t, C), half),
            sds((2, n, TEAM * rows_m, q4), half),
            sds((TEAM, rows_m, C), half),
            sds((T, rows_i, C), half),
            sds((T, rows_t, C), half),
            sds((TEAM, rows_m, q4), half),
        ]
        share_scratch = [
            pltpu.VMEM((TEAM * pix, C), half),
            pltpu.VMEM((TEAM, 2, W, 1, C), f32),
            pltpu.VMEM((TEAM, 2, W, 1, q4), f32),
            dma((15, TEAM)),
            dma((2, 4, n, TEAM)),
            dma((2, 4, n, TEAM)),
            dma((2,)),
            dma((4, TEAM)),
            dma((4, TEAM)),
            dma((TEAM + 3,)),
        ]
    vm = pltpu.VMEM
    win = pix // 4 + 32
    outs = pl.pallas_call(
        functools.partial(section_kernel, dict(cfg, direct=direct)),
        name="sections",
        out_shape=[sds((M, part, CW), half), sds((2 * norms, C), f32)] + exchange + shares,
        in_specs=[ANY, ANY] + [VMEM] * 8 + [ANY] * 4,
        out_specs=[ANY, VMEM] + [ANY] * (len(exchange) + len(shares)),
        scratch_shapes=[
            vm((2, 9 * C, C), half),
            vm((T, 2 * C, C), half),
            vm((T, C, C), half),
            vm((T, 9 * C, C), half),
            vm((pix, CW), half),
            vm((2, pix, CW), half),
            vm((pix, 128), half),
            vm((pix, 128), half),
            vm((2, 32, C), half),
            vm((2, 32, 128), half),
            vm((2, W, 1, C), f32),
            vm((win, CW), half),
            vm((win, CW), half),
            vm((3, pix + 2 * H, C), half),
            vm((norms, pix, C), f32),
            vm((EDGES, 2, W, 1, C), f32),
            vm((EDGES, 2, W, 1, C), f32),
            vm((2 * norms, 2, C), f32),
            vm((G, 2 * norms, 2, C), f32),
            vm((pix, C), half),
            vm((pix, C), half),
            vm((W, 2, C), f32),
            vm((T, pix, C), half),
            vm((T, pix, C), half),
            vm((pix, CW), half),
            vm((T, pix, C), f32),
            vm((pix, C), f32),
            vm((T, pix, C), half),
            vm((T, 2, W, 1, C), f32),
            vm((pix, C), half),
            vm((2, W, 1, C), f32),
            vm((T, pix, C), half),
            vm((T, pix, C), half),
            vm((TEAM, pix, C // TEAM), half),
            vm((TEAM, 2, W, 1, C // TEAM), f32),
            vm((2 * norms, C), f32),
            vm((M, 2 * norms, C), f32),
            pltpu.SemaphoreType.REGULAR,
            dma((4 + T,)),
            dma((7, M)),
            dma((5, M)),
            dma((EDGES, 2)),
            dma((EDGES, 2)),
            dma((2 * norms, G)),
            dma((2 * norms, G)),
            dma((3,)),
            dma((3,)),
            dma((2, M)),
            dma((2, M)),
            dma((M,)),
            dma((M,)),
            dma((39,)),
            dma((39, TEAM)),
        ]
        + share_scratch,
        compiler_params=pltpu.CompilerParams(
            collective_id=0, has_side_effects=True, vmem_limit_bytes=63 * 2**20
        ),
    )(sec, sel, team_masks, cm, cm_t, spread, edge, pool, bn_gain[0], bn_bias[0], conv_shared[0], task_in[0], task_mid[0], task_conv[0])
    result, bn_grads = outs[:2]

    result = result.reshape(1, M, part // W, W, CW)
    if direct:
        gm, g1, gi, gt = outs[-12:-8]
        return (
            result,
            jnp.stack([g1, gm[T]]).reshape(1, 2, -1),
            gi.reshape(1, T, -1),
            gt.reshape(1, T, -1),
            gm[:T].reshape(1, T, -1),
            bn_grads[None, :norms],
            bn_grads[None, norms:],
        )
    shapes = [sds((rows_m, C), half), sds((rows_m, q4), half), sds((rows_i, C), half), sds((rows_t, C), half)]
    slots = [(n, rows_m, C), (n, rows_m, q4), (n, rows_i, C), (n, rows_t, C)]
    grads = pl.pallas_call(
        functools.partial(gradient_kernel, cfg),
        name="kernel_gradients",
        out_shape=shapes,
        in_specs=[VMEM] + [ANY] * 11,
        out_specs=[VMEM] * 4,
        scratch_shapes=[
            vm((TEAM, pix, C), half),
            vm((TEAM, pix, C), half),
            vm((TEAM, pix, C), half),
            vm((TEAM, pix, C), half),
            vm((TEAM, pix, C), half),
            vm((TEAM, 2, W, 1, C), f32),
            vm((TEAM, 3, pix + 2 * H, C), half),
            vm((TEAM, 3, pix, 3 * q4), half),
            vm((TEAM, pix, q4), half),
            vm((TEAM, 2, W, 1, q4), f32),
            vm((2, TEAM, pix, C), half),
            vm((9 * C, C), half),
            vm((9 * C, q4), half),
            vm((2 * C, C), half),
            vm((C, C), half),
            vm(slots[0], half),
            vm(slots[1], half),
            vm(slots[2], half),
            vm(slots[3], half),
            dma((11,)),
            dma((4, R)),
            dma((4, R)),
        ],
        compiler_params=pltpu.CompilerParams(
            collective_id=1, has_side_effects=True, vmem_limit_bytes=60 * 2**20
        ),
    )(team_masks, *outs[2:])

    gm, g1, gi, gt = grads
    pieces = [
        gm.reshape(TEAM, -1),
        g1.reshape(TEAM, -1),
        gi.reshape(TEAM, -1),
        gt.reshape(TEAM, -1),
    ]
    packed = jnp.concatenate(pieces, 1)
    teams = [[TEAM * i + j for j in range(TEAM)] for i in range(R // TEAM)]
    swapped = lax.all_to_all(packed, "rows", 0, 0, axis_index_groups=teams, tiled=False).astype(f32)
    sizes = [v.shape[1] for v in pieces]
    o = [0, sizes[0], sizes[0] + sizes[1], sizes[0] + sizes[1] + sizes[2], sum(sizes)]
    mains = swapped[:, o[0] : o[1]]
    firsts = swapped[:, o[1] : o[2]].reshape(TEAM, -1, q4).transpose(1, 0, 2).reshape(-1)
    conv_grad = jnp.stack([firsts, mains[T]])
    return (
        result,
        conv_grad[None],
        swapped[:T, o[2] : o[3]][None],
        swapped[:T, o[3] : o[4]][None],
        mains[:T][None],
        bn_grads[None, :norms],
        bn_grads[None, norms:],
    )


def solution(mesh):
    in_specs = (
        P("pipe", None, "rows", None, None),
        P(),
        P(None, "rows", None),
        P("pipe", None, None, None),
        P("pipe", None, None, None),
        P("pipe", None, None, None),
        P("pipe", None, None, None),
        P("pipe", None, None),
        P("pipe", None, None),
    )
    out_specs = (
        P("pipe", None, "rows", None, None),
        P("pipe", None, "rows"),
        P("pipe", None, "rows"),
        P("pipe", None, "rows"),
        P("pipe", None, "rows"),
        P("pipe", None, None),
        P("pipe", None, None),
    )
    bands = mesh.shape["rows"]

    def step(section_in, image_start, pool_choice, conv_shared, task_in, task_mid, task_conv, bn_gain, bn_bias):
        M = section_in.shape[1]
        G = bands // M
        cfg = dict(
            M=M,
            G=G,
            H=section_in.shape[2] // G,
            W=section_in.shape[3],
            C=conv_shared.shape[3],
            T=task_in.shape[1],
            n=bands // TEAM,
            to_all=frozenset(range(0, 8)) | frozenset(range(31, 39)),
        )
        return jax.shard_map(
            functools.partial(per_device, cfg), mesh=mesh, in_specs=in_specs, out_specs=out_specs, check_vma=False
        )(section_in, image_start, pool_choice, conv_shared, task_in, task_mid, task_conv, bn_gain, bn_bias)

    return step
```

```python
import functools

import jax
import jax.numpy as jnp
import numpy as np
from jax import lax
from jax.experimental import pallas as pl
from jax.experimental.pallas import tpu as pltpu
from jax.sharding import PartitionSpec as P

MESH = pl.DeviceIdType.MESH
half = jnp.bfloat16
f32 = jnp.float32
epsilon = 1e-05
TEAM = 4

ANY = pl.BlockSpec(memory_space=pl.ANY)
VMEM = pl.BlockSpec(memory_space=pltpu.VMEM)


def sigmoid(x):
    return 0.5 * jnp.tanh(0.5 * x) + 0.5


def dot(a, b):
    return jnp.dot(a, b, preferred_element_type=f32)


def dot_nt(a, b):
    return lax.dot_general(a, b, (((1,), (1,)), ((), ())), preferred_element_type=f32)


def dot_tn(a, b):
    return lax.dot_general(a, b, (((0,), (0,)), ((), ())), preferred_element_type=f32)


class Remote:
    def __init__(self, src, dst, send, recv, to):
        self.src, self.dst, self.send, self.recv, self.to = src, dst, send, recv, to
        self.local = to == lax.axis_index("rows")

    def remote(self):
        return pltpu.make_async_remote_copy(
            src_ref=self.src,
            dst_ref=self.dst,
            send_sem=self.send,
            recv_sem=self.recv,
            device_id=(lax.axis_index("pipe"), self.to),
            device_id_type=MESH,
        )

    def start(self):
        @pl.when(self.local)
        def _():
            pltpu.make_async_copy(self.src, self.dst, self.recv).start()

        @pl.when(jnp.logical_not(self.local))
        def _():
            self.remote().start()

    def sent(self):
        @pl.when(jnp.logical_not(self.local))
        def _():
            self.remote().wait_send()


def arrived(dst, sem):
    pltpu.make_async_copy(dst, dst, sem).wait()


EDGES = 13


def section_kernel(cfg, *refs):
    M, G, H, W, C, T = cfg["M"], cfg["G"], cfg["H"], cfg["W"], cfg["C"], cfg["T"]
    R = M * G
    pix = H * W
    part = pix // M
    count = float(pix * G)
    norms = 2 + 3 * T
    direct = cfg["direct"]
    (sec, sel, msks, perm, perm_t, spread, spread_edge, pool, gain, bias, wc, wi, wm, wt) = refs[:14]
    (out, bng, xu, xh, xp, xv, xd5, xd5e, xd4, xd3, xd1, xd1e) = refs[14:26]
    refs = refs[26:]
    if direct:
        (gm, g1, gi, gt) = refs[:4]
        flows_in = refs[4:8]
        ends = refs[8:12]
        (lin, d5e, d1e, l_sem, fl_s, fl_r, fl_l, sh_s, sh_r, o_sem) = refs[-10:]
        refs = refs[12:-10]
    (
        kc, ki, km, kt, rin, field, selin, chosen, uh, selh, uedge, px, ps, rb, ys, esend, erecv, ssend, srecv,
        h1, h2, h2e, t1, pr, res, dz, dh, dy5, dy5e, dy2e, dy3, dy1, dy1e, bn, bnr,
        go, w_sem, in_s, in_r, ed_s, ed_r, st_s, st_r, pp_s, pp_r, out_s, out_r, bn_s, bn_r, x_s, x_r,
    ) = refs
    p = lax.axis_index("pipe")
    r = lax.axis_index("rows")
    b, m = r // M, r % M
    e, e0 = m, r - m
    first, last = b == 0, b == G - 1
    CW = C * (1 + T)

    loads = {}

    def load(name, src, dst, i):
        loads[name] = pltpu.make_async_copy(src, dst, w_sem.at[i])
        loads[name].start()

    load("c0", wc.at[0], kc.at[0], 0)
    load("i", wi, ki, 1)
    load("c1", wc.at[1], kc.at[1], 2)
    load("m", wm, km, 3)
    for t in range(T):
        load("t%d" % t, wt.at[t], kt.at[t], 4 + t)

    zero_col = jnp.zeros((H, C), half)
    for a in range(3):
        rb[a, 0:H, :] = zero_col
        rb[a, H * (W + 1) : H * (W + 2), :] = zero_col
    px[pix // 4 :, :] = jnp.zeros((px.shape[0] - pix // 4, CW), half)

    @pl.when(first)
    def _():
        for s in range(EDGES):
            erecv[s, 0] = jnp.zeros((W, 1, C), f32)
        uh[0] = jnp.zeros((32, C), half)
        selh[0] = jnp.zeros((32, 128), half)

    @pl.when(last)
    def _():
        for s in range(EDGES):
            erecv[s, 1] = jnp.zeros((W, 1, C), f32)
        uh[1] = jnp.zeros((32, C), half)
        selh[1] = jnp.zeros((32, 128), half)

    bar = pltpu.get_barrier_semaphore()

    def hello(side, row):
        pl.semaphore_signal(bar, inc=1, device_id=(side, row), device_id_type=MESH)

    for d in range(1, M):
        hello(p, e0 + lax.rem(m + d, M))
    for d in range(1, G):
        hello(p, M * lax.rem(b + d, G) + m)
    hello(1 - p, r)
    tops = jnp.logical_and(m == M - 1, jnp.logical_not(last))
    bottoms = jnp.logical_and(m == 0, jnp.logical_not(first))

    @pl.when(jnp.logical_not(first))
    def _():
        hello(1 - p, r - M)
        hello(p, e0 - 1)

    @pl.when(jnp.logical_not(last))
    def _():
        hello(1 - p, r + M)
        hello(p, e0 + M)

    @pl.when(tops)
    def _():
        for j in range(M):
            hello(p, e0 + M + j)

    @pl.when(bottoms)
    def _():
        for j in range(M):
            hello(p, e0 - M + j)

    below_me, above_me = 1 - (b + 1) // G, (b + G - 1) // G
    top_member, bottom_member = (m + 1) // M, 1 - (m + M - 1) // M
    pl.semaphore_wait(
        bar, M + G - 1 + 2 * (below_me + above_me) + M * (top_member * below_me + bottom_member * above_me)
    )

    mine = pl.ds(pl.multiple_of(part * m, 16), part)
    field_moves, rest_moves, sel_moves, edge_moves = [], [], [], ([], [])
    for d in range(M):
        j = lax.rem(m + d, M)
        to = e0 + j
        field_moves.append(Remote(sec.at[j, :, 0:C], rin.at[mine, 0:C], in_s.at[0, d], in_r.at[0, m], to))
        sel_moves.append(Remote(sel.at[j], selin.at[mine], in_s.at[2, d], in_r.at[2, m], to))
        rest_moves.append(Remote(sec.at[j, :, C:CW], rin.at[mine, C:CW], in_s.at[1, d], in_r.at[1, m], to))
    for j in range(M):
        to = e0 + j
        edge_moves[0].append(
            Remote(sec.at[j, pl.ds(part - 32, 32), 0:C], uh.at[0], in_s.at[3, j], in_r.at[3, 0], to + M)
        )
        edge_moves[0].append(Remote(sel.at[j, pl.ds(part - 32, 32)], selh.at[0], in_s.at[4, j], in_r.at[3, 1], to + M))
        edge_moves[1].append(Remote(sec.at[j, pl.ds(0, 32), 0:C], uh.at[1], in_s.at[5, j], in_r.at[4, 0], to - M))
        edge_moves[1].append(Remote(sel.at[j, pl.ds(0, 32)], selh.at[1], in_s.at[6, j], in_r.at[4, 1], to - M))

    def start_field():
        for move in field_moves:
            move.start()
        for move in rest_moves:
            move.start()

    @pl.when(tops)
    def _():
        for move in edge_moves[0]:
            move.start()

    @pl.when(bottoms)
    def _():
        for move in edge_moves[1]:
            move.start()

    @pl.when(p == 0)
    def _():
        start_field()

    for move in sel_moves:
        move.start()

    row_of = lax.broadcasted_iota(jnp.int32, (H, C), 0)
    at_top, at_bottom = row_of == 0, row_of == H - 1

    def column(j):
        return pl.ds(pl.multiple_of(j * H, H), H)

    def over_columns(body, start=0, step=2):
        def several(c, carry):
            for u in range(step):
                carry = body(c * step + u, carry)
            return carry

        return lax.fori_loop(0, W // step, several, start)

    def build(j, value, above, below, up, down):
        here = pl.ds(pl.multiple_of(H + j * H, H), H)
        rb[1, here, :] = value.astype(half)
        rb[0, here, :] = (jnp.where(at_top, above, pltpu.roll(value, 1, 0)) * up).astype(half)
        rb[2, here, :] = (jnp.where(at_bottom, below, pltpu.roll(value, H - 1, 0)) * down).astype(half)

    def conv(kernel):
        total = None
        for tap in range(9):
            a, c = tap // 3, tap % 3
            term = dot(rb[a, H * c : H * c + pix, :], kernel[tap * C : (tap + 1) * C, :])
            total = term if total is None else total + term
        return total

    def conv_t(kernel):
        total = None
        for tap in range(9):
            a, c = tap // 3, tap % 3
            term = dot_nt(rb[a, H * c : H * c + pix, :], kernel[(8 - tap) * C : (9 - tap) * C, :])
            total = term if total is None else total + term
        return total

    def folded(total):
        return jnp.sum(total, 0, keepdims=True)

    def fold(x):
        return jnp.sum(x.reshape(H // 8, 8, C), 0)

    zero8 = jnp.zeros((8, C), f32)

    def edge_copy(slot, side):
        to = r - M if side == 0 else r + M
        return pltpu.make_async_remote_copy(
            src_ref=esend.at[slot, side],
            dst_ref=erecv.at[slot, 1 - side],
            send_sem=ed_s.at[slot, side],
            recv_sem=ed_r.at[slot, 1 - side],
            device_id=(p, to),
            device_id_type=MESH,
        )

    def send_edges(slot):
        @pl.when(jnp.logical_not(first))
        def _():
            edge_copy(slot, 0).start()

        @pl.when(jnp.logical_not(last))
        def _():
            edge_copy(slot, 1).start()

    def get_edges(slot):
        @pl.when(jnp.logical_not(first))
        def _():
            arrived(erecv.at[slot, 0], ed_r.at[slot, 0])

        @pl.when(jnp.logical_not(last))
        def _():
            arrived(erecv.at[slot, 1], ed_r.at[slot, 1])

    def finish_edges(slot):
        @pl.when(jnp.logical_not(first))
        def _():
            edge_copy(slot, 0).wait_send()

        @pl.when(jnp.logical_not(last))
        def _():
            edge_copy(slot, 1).wait_send()

    def stat_copy(slot, n, d):
        to = M * lax.rem(b + d, G) + m
        return pltpu.make_async_remote_copy(
            src_ref=ssend.at[pl.ds(slot, n)],
            dst_ref=srecv.at[b, pl.ds(slot, n)],
            send_sem=st_s.at[slot, d],
            recv_sem=st_r.at[slot, b],
            device_id=(p, to),
            device_id_type=MESH,
        )

    def send_sums(slot, n):
        srecv[b, slot : slot + n] = ssend[slot : slot + n]
        for d in range(1, G):
            stat_copy(slot, n, d).start()

    sums_sent = []

    def get_sums(slot, n):
        sums_sent.append((slot, n))
        for d in range(1, G):
            s = lax.rem(b + d, G)
            arrived(srecv.at[s, pl.ds(slot, n)], st_r.at[slot, s])

    def total(slot):
        acc = srecv[0, slot]
        for g in range(1, G):
            acc = acc + srecv[g, slot]
        return acc

    def put_sums(slot, s, q):
        ssend[slot] = jnp.concatenate([folded(s), folded(q)], 0)

    x_moves = []
    kept = []

    def post(index, src, dst, target, keep=False):
        move = Remote(src, dst.at[e], x_s.at[index], x_r.at[index - (target if index in cfg["to_all"] else 0), e], e0 + target)
        x_moves.append(move)
        if not keep:
            move.start()
        else:
            kept.append(move)

            @pl.when(p == 0)
            def _():
                move.start()

    def send_kept():
        for move in kept:
            move.start()


    def moments(k, slot, edge=None):
        def body(j, carry):
            s, q = carry
            y = ys[k, column(j), :]
            if edge is not None:
                esend[edge, 0, j] = y[0:1]
                esend[edge, 1, j] = y[H - 1 : H]
            return s + fold(y), q + fold(y * y)

        s, q = over_columns(body, (zero8, zero8))
        put_sums(slot, s, q)

    norm = {}

    def norm_rows(k, slot):
        acc = total(slot)
        mean = acc[0:1] / count
        rs = lax.rsqrt(acc[1:2] / count - mean * mean + epsilon)
        scale = gain[k : k + 1, :] * rs
        norm[k] = (mean, rs, scale, bias[k : k + 1, :])

    def normed(k, y):
        mean, rs, scale, shift = norm[k]
        return (y - mean) * scale + shift

    def silu(x):
        return x * sigmoid(x)

    def silu_slope(x):
        s = sigmoid(x)
        return s * (1.0 + x * (1.0 - s))

    def pair(slot, j):
        return jnp.concatenate([erecv[slot, 0, j], erecv[slot, 1, j]], 0)

    nt = 2 + 3 * T
    F3, F4, F5 = 2, 2 + T, 2 + 2 * T

    def wait_field(kind, buffer):
        for k in range(M):
            arrived(buffer(k), in_r.at[kind, k])

    @pl.when(jnp.logical_not(first))
    def _():
        arrived(uh.at[0], in_r.at[3, 0])

    @pl.when(jnp.logical_not(last))
    def _():
        arrived(uh.at[1], in_r.at[4, 0])

    def start_of_field():
        wait_field(0, lambda k: rin.at[pl.ds(part * k, part), 0:C])
        field[p, :, 0:C] = dot(perm[...], rin[:, 0:C]).astype(half)

    def rest_of_field():
        wait_field(1, lambda k: rin.at[pl.ds(part * k, part), C:CW])
        for t in range(T):
            cols = slice((t + 1) * C, (t + 2) * C)
            field[p, :, cols] = dot(perm[...], rin[:, cols]).astype(half)

    @pl.when(p == 0)
    def _():
        start_of_field()

    def wait_selection():
        wait_field(2, lambda k: selin.at[pl.ds(part * k, part)])

        @pl.when(jnp.logical_not(first))
        def _():
            arrived(selh.at[0], in_r.at[3, 1])

        @pl.when(jnp.logical_not(last))
        def _():
            arrived(selh.at[1], in_r.at[4, 1])

    def halo_copies():
        return (
            pltpu.make_async_remote_copy(
                src_ref=ps.at[pl.ds(pix // 4, 16), 0:C], dst_ref=px.at[pl.ds(pix // 4, 16), 0:C],
                send_sem=pp_s.at[1], recv_sem=pp_r.at[1], device_id=(1 - p, r + M), device_id_type=MESH),
            pltpu.make_async_remote_copy(
                src_ref=ps.at[pl.ds(pix // 4 + 16, 16), 0:C], dst_ref=px.at[pl.ds(pix // 4 + 16, 16), 0:C],
                send_sem=pp_s.at[2], recv_sem=pp_r.at[2], device_id=(1 - p, M * (b - 1) + m), device_id_type=MESH),
        )

    def pool_copy():
        return pltpu.make_async_remote_copy(
            src_ref=ps.at[pl.ds(0, pix // 4)], dst_ref=px.at[pl.ds(0, pix // 4)],
            send_sem=pp_s.at[0], recv_sem=pp_r.at[0], device_id=(1 - p, r), device_id_type=MESH)

    @pl.when(p == 1)
    def _():
        wait_selection()
        chosen[...] = spread[...] * dot(perm[...], selin[...]).astype(half)
        pl.semaphore_wait(go, 1)
        start_field()
        start_of_field()
        rest_of_field()
        arrived(px.at[pl.ds(0, pix // 4)], pp_r.at[0])

        @pl.when(jnp.logical_not(first))
        def _():
            arrived(px.at[pl.ds(pix // 4, 16), 0:C], pp_r.at[1])

        @pl.when(jnp.logical_not(last))
        def _():
            arrived(px.at[pl.ds(pix // 4 + 16, 16), 0:C], pp_r.at[2])

        for t in range(1 + T):
            cols = slice(t * C, (t + 1) * C)
            field[0, :, cols] = dot(chosen[...], px[:, cols]).astype(half)
        edges = spread_edge[...] * jnp.concatenate([selh[0], selh[1]], 0)
        both = dot(edges, px[:, 0:C]).astype(half)
        uh[0] = both[0:32]
        uh[1] = both[32:64]

    above = uh[0].astype(f32)
    below = uh[1].astype(f32)
    for j in range(W):
        uedge[0, j] = above[32 - W + j : 33 - W + j]
        uedge[1, j] = below[j : j + 1]

    up = msks[m, 0]
    down = msks[m, 1]

    def body_u(j, carry):
        build(j, field[0, column(j), 0:C].astype(f32), uedge[0, j], uedge[1, j], up, down)
        return carry

    over_columns(body_u)
    loads["c0"].wait()
    ys[0] = conv(kc.at[0])
    moments(0, 0, 0)
    send_sums(0, 1)
    send_edges(0)

    @pl.when(p == 0)
    def _():
        rest_of_field()
        pl.semaphore_signal(go, inc=1, device_id=(1 - p, r), device_id_type=MESH)

    for q in range(TEAM):
        post(q, field.at[0, :, 0:C], xu, q, True)
    for t in range(T):
        post(8 + t, field.at[0, :, (t + 1) * C : (t + 2) * C], xv, t, True)
    get_sums(0, 1)
    get_edges(0)
    norm_rows(0, 0)

    def body_h1(j, carry):
        value = silu(normed(0, ys[0, column(j), :]))
        side = silu(normed(0, pair(0, j)))
        h1[column(j), :] = value.astype(half)
        build(j, value, side[0:1], side[1:2], up, down)
        return carry

    over_columns(body_h1)
    for q in range(TEAM):
        post(4 + q, h1, xh, q, q < T)

    loads["i"].wait()
    for t in range(T):
        k = 2 + 3 * t
        ys[k] = dot(h1[...], ki[t, 0:C, :]) + dot(field[0, :, (t + 1) * C : (t + 2) * C], ki[t, C : 2 * C, :])
        moments(k, F3 + t)
    send_sums(F3, T)
    loads["c1"].wait()
    ys[1] = conv(kc.at[1])
    moments(1, 1, 1)
    send_sums(1, 1)
    send_edges(1)

    get_sums(F3, T)
    loads["m"].wait()
    for t in range(T):
        k = 2 + 3 * t
        norm_rows(k, F3 + t)

        def body_t1(j, carry):
            t1[t, column(j), :] = silu(normed(k, ys[k, column(j), :])).astype(half)
            return carry

        over_columns(body_t1)
        ys[k + 1] = dot(t1[t], km[t])
        moments(k + 1, F4 + t, 2 + t)
        send_sums(F4 + t, 1)
        send_edges(2 + t)

    get_sums(1, 1)
    get_edges(1)
    norm_rows(1, 1)

    def body_h2(j, carry):
        value = silu(normed(1, ys[1, column(j), :])).astype(half)
        h2[column(j), :] = value
        res[column(j), 0:C] = value
        side = silu(normed(1, pair(1, j))).astype(half).astype(f32)
        h2e[j] = side
        return carry

    over_columns(body_h2)
    for t in range(T):
        k = 3 + 3 * t
        get_sums(F4 + t, 1)
        get_edges(2 + t)
        norm_rows(k, F4 + t)

        def body_p(j, carry):
            gate = sigmoid(normed(k, ys[k, column(j), :]))
            value = gate * h2[column(j), :].astype(f32)
            side = sigmoid(normed(k, pair(2 + t, j))) * h2e[j]
            pr[t, column(j), :] = value.astype(half)
            build(j, value, side[0:1], side[1:2], up, down)
            return carry

        over_columns(body_p)
        post(14 + t, pr.at[t], xp, t)
        loads["t%d" % t].wait()
        ys[k + 1] = conv(kt.at[t])
        moments(k + 1, F5 + t, 5 + t)
        send_sums(F5 + t, 1)
        send_edges(5 + t)
    for t in range(T):
        k = 4 + 3 * t
        get_sums(F5 + t, 1)
        get_edges(5 + t)
        norm_rows(k, F5 + t)

        def body_q(j, carry):
            res[column(j), (t + 1) * C : (t + 2) * C] = silu(normed(k, ys[k, column(j), :])).astype(half)
            return carry

        over_columns(body_q)

    def out_moves(which):
        cols = slice(0, C) if which == 0 else slice(C, CW)
        moves = []
        for d in range(M):
            k = lax.rem(m + d, M)
            rows = pl.ds(pl.multiple_of(part * k, 16), part)
            moves.append(
                Remote(rin.at[rows, cols], out.at[m, :, cols], out_s.at[which, d], out_r.at[which, m], e0 + k)
            )
        return moves

    def stage_result(which):
        for t in range(0, 1) if which == 0 else range(1, 1 + T):
            cols = slice(t * C, (t + 1) * C)
            rin[:, cols] = dot(perm_t[...], res[:, cols]).astype(half)

    def start_result(which):
        for move in out_moves(which):
            move.start()

    @pl.when(p == 0)
    def _():
        for t in range(1 + T):
            cols = slice(t * C, (t + 1) * C)
            ps[:, cols] = dot(pool[...], res[:, cols]).astype(half)
        pool_copy().start()

        @pl.when(jnp.logical_not(last))
        def _():
            halo_copies()[0].start()

        @pl.when(jnp.logical_not(first))
        def _():
            halo_copies()[1].start()

        pool_copy().wait_send()

        @pl.when(jnp.logical_not(last))
        def _():
            halo_copies()[0].wait_send()

        @pl.when(jnp.logical_not(first))
        def _():
            halo_copies()[1].wait_send()

        arrived(px.at[pl.ds(0, pix // 4)], pp_r.at[0])
        for t in range(1 + T):
            cols = slice(t * C, (t + 1) * C)
            field[1, :, cols] = (dot(spread[...], px[:, cols]) * 0.25).astype(half)

    @pl.when(p == 1)
    def _():
        stage_result(0)
        stage_result(1)

    B3, B4, B5 = nt + F3, nt + F4, nt + F5
    back = {}

    def back_rows(k, slot):
        acc = total(slot)
        mean, rs, scale, shift = norm[k]
        slope = -scale * rs * acc[1:2] / count
        back[k] = (scale, slope, -scale * acc[0:1] / count - slope * mean)
        bn[k : k + 1, :] = acc[1:2]
        bn[norms + k : norms + k + 1, :] = acc[0:1]

    def grad_pre(k, dzv, y):
        scale, slope, rest = back[k]
        return scale * dzv + slope * y + rest

    def hat(k, y):
        mean, rs, scale, shift = norm[k]
        return (y - mean) * rs

    for t in range(T):
        k = 4 + 3 * t

        def body_dz5(j, carry):
            s, q = carry
            y = ys[k, column(j), :]
            g = field[1, column(j), (t + 1) * C : (t + 2) * C].astype(f32)
            v = g * silu_slope(normed(k, y))
            dz[t, column(j), :] = v
            esend[8 + t, 0, j] = v[0:1]
            esend[8 + t, 1, j] = v[H - 1 : H]
            return s + fold(v), q + fold(v * hat(k, y))

        s, q = over_columns(body_dz5, (zero8, zero8))
        put_sums(B5 + t, s, q)
        send_sums(B5 + t, 1)
        send_edges(8 + t)

    for t in range(T):
        k = 4 + 3 * t
        get_sums(B5 + t, 1)
        get_edges(8 + t)
        back_rows(k, B5 + t)

        def body_dy5(j, carry):
            v = grad_pre(k, dz[t, column(j), :], ys[k, column(j), :])
            side = grad_pre(k, pair(8 + t, j), pair(5 + t, j))
            dy5[t, column(j), :] = v.astype(half)
            dy5e[t, 0, j] = side[0:1]
            dy5e[t, 1, j] = side[1:2]
            build(j, v, side[0:1], side[1:2], up, down)
            return carry

        over_columns(body_dy5)
        post(17 + t, dy5.at[t], xd5, t)
        post(21 + t, dy5e.at[t], xd5e, t)
        ys[k] = conv_t(kt.at[t])

        def body_dz4(j, carry):
            s, q = carry
            dp = ys[k, column(j), :]
            y = ys[k - 1, column(j), :]
            gate = sigmoid(normed(k - 1, y))
            dgate = dp * h2[column(j), :].astype(f32)
            base = field[1, column(j), 0:C].astype(f32) if t == 0 else dh[column(j), :]
            dh[column(j), :] = base + dp * gate
            v = dgate * gate * (1.0 - gate)
            ys[k, column(j), :] = v
            return s + fold(v), q + fold(v * hat(k - 1, y))

        s, q = over_columns(body_dz4, (zero8, zero8))
        put_sums(B4 + t, s, q)
        send_sums(B4 + t, 1)

    def body_dz2(j, carry):
        s, q = carry
        y = ys[1, column(j), :]
        v = dh[column(j), :] * silu_slope(normed(1, y))
        dh[column(j), :] = v
        esend[11, 0, j] = v[0:1]
        esend[11, 1, j] = v[H - 1 : H]
        return s + fold(v), q + fold(v * hat(1, y))

    s, q = over_columns(body_dz2, (zero8, zero8))
    put_sums(nt + 1, s, q)
    send_sums(nt + 1, 1)
    send_edges(11)

    dy4 = [field.at[1, :, t * C : (t + 1) * C] for t in range(T)]
    dy2 = field.at[1, :, T * C : (T + 1) * C]
    mid = km
    for t in range(T):
        k = 3 + 3 * t
        get_sums(B4 + t, 1)
        back_rows(k, B4 + t)

        def body_dy4(j, carry):
            dy4[t][column(j), :] = grad_pre(k, ys[k + 1, column(j), :], ys[k, column(j), :]).astype(half)
            return carry

        over_columns(body_dy4)
        dz[t] = dot_nt(dy4[t][...], km[t])

        def body_dz3(j, carry):
            s, q = carry
            y = ys[k - 1, column(j), :]
            v = dz[t, column(j), :] * silu_slope(normed(k - 1, y))
            dz[t, column(j), :] = v
            return s + fold(v), q + fold(v * hat(k - 1, y))

        s, q = over_columns(body_dz3, (zero8, zero8))
        put_sums(B3 + t, s, q)
    send_sums(B3, T)

    get_sums(nt + 1, 1)
    get_edges(11)
    back_rows(1, nt + 1)

    def body_dy2(j, carry):
        v = grad_pre(1, dh[column(j), :], ys[1, column(j), :])
        side = grad_pre(1, pair(11, j), pair(1, j))
        dy2[column(j), :] = v.astype(half)
        dy2e[0, j] = side[0:1]
        dy2e[1, j] = side[1:2]
        build(j, v, side[0:1], side[1:2], up, down)
        return carry

    over_columns(body_dy2)
    post(20, dy2, xd5, TEAM - 1)
    post(24, dy2e, xd5e, TEAM - 1)

    @pl.when(p == 1)
    def _():
        send_kept()


    dh[...] = conv_t(kc.at[1])

    get_sums(B3, T)
    for t in range(T):
        k = 2 + 3 * t
        back_rows(k, B3 + t)

        def body_dy3(j, carry):
            dy3[t, column(j), :] = grad_pre(k, dz[t, column(j), :], ys[k, column(j), :]).astype(half)
            return carry

        over_columns(body_dy3)
        post(28 + t, dy3.at[t], xd3, t)
        dh[...] += dot_nt(dy3[t], ki[t, 0:C, :])
        res[:, (t + 1) * C : (t + 2) * C] = dot_nt(dy3[t], ki[t, C : 2 * C, :]).astype(half)

    @pl.when(p == 0)
    def _():
        stage_result(1)
        start_result(1)

    def body_dz1(j, carry):
        s, q = carry
        y = ys[0, column(j), :]
        v = dh[column(j), :] * silu_slope(normed(0, y))
        dh[column(j), :] = v
        esend[12, 0, j] = v[0:1]
        esend[12, 1, j] = v[H - 1 : H]
        return s + fold(v), q + fold(v * hat(0, y))

    s, q = over_columns(body_dz1, (zero8, zero8))
    put_sums(nt, s, q)
    send_sums(nt, 1)
    send_edges(12)
    for t in range(T):
        mid[t] = dot_tn(t1[t], dy4[t][...]).astype(half)
        post(25 + t, mid.at[t], xd4, t)
    get_sums(nt, 1)
    get_edges(12)
    back_rows(0, nt)

    def bn_moves():
        return [Remote(bn, bnr.at[m], bn_s.at[d], bn_r.at[m], e0 + lax.rem(m + d, M)) for d in range(M)]

    for move in bn_moves():
        move.start()

    quarter = C // TEAM

    def body_dy1(j, carry):
        v = grad_pre(0, dh[column(j), :], ys[0, column(j), :])
        side = grad_pre(0, pair(12, j), pair(0, j))
        low = v.astype(half)
        for o in range(TEAM):
            cols = slice(o * quarter, (o + 1) * quarter)
            dy1[o, column(j), :] = low[:, cols]
            dy1e[o, 0, j] = side[0:1, cols]
            dy1e[o, 1, j] = side[1:2, cols]
        build(j, v, side[0:1], side[1:2], up, down)
        return carry

    over_columns(body_dy1)
    for o in range(TEAM):
        post(31 + o, dy1.at[o], xd1, o)
        post(35 + o, dy1e.at[o], xd1e, o)
    res[:, 0:C] = conv_t(kc.at[0]).astype(half)

    @pl.when(p == 1)
    def _():
        for t in range(1 + T):
            cols = slice(t * C, (t + 1) * C)
            ps[0 : pix // 4, cols] = dot_tn(chosen[...], res[:, cols])[0 : pix // 4].astype(half)
        pool_copy().start()
        start_result(0)
        start_result(1)
        pool_copy().wait_send()

    @pl.when(p == 0)
    def _():
        stage_result(0)
        start_result(0)

    def finish_sends():
        for move in field_moves + rest_moves + sel_moves:
            move.sent()

        @pl.when(tops)
        def _():
            for move in edge_moves[0]:
                move.sent()

        @pl.when(bottoms)
        def _():
            for move in edge_moves[1]:
                move.sent()

        for s in range(EDGES):
            finish_edges(s)
        for slot, n in sums_sent:
            for d in range(1, G):
                stat_copy(slot, n, d).wait_send()

        @pl.when(p == 0)
        def _():
            wait_selection()

    if not direct:
        finish_sends()
    if direct:
        z, n = b, R // TEAM
        q4 = quarter
        all_rows = TEAM * pix
        wide = pix + 2 * H
        task = e < T
        vb, va, vc = (kt.at[2, i * all_rows : (i + 1) * all_rows, :] for i in range(3))
        _, d5, d3 = (kc.at[0, i * all_rows : (i + 1) * all_rows, :] for i in range(3))
        pm, p1, pi_, pt = kt.at[0], kc.at[0, :, 0:q4], ki.at[0], ki.at[T - 1, 0:C]
        d1 = kt.at[1, 0:all_rows, 3 * q4 : 4 * q4]
        rows_m, rows_i, rows_t = 9 * C // R, 2 * C // R, C // R

        def band(ref, j):
            return ref.at[j * pix : (j + 1) * pix]

        def fetch(index, src, j, dst, sem):
            arrived(src.at[j], sem)
            copy = pltpu.make_async_copy(src.at[j], dst, l_sem.at[index, j])
            copy.start()
            return copy

        def rows_shifted(j, a, lo):
            if j < TEAM - 1:
                start = (3 * j + a) * wide + lo
                return kc.at[1, start : start + pix, :]
            return rb.at[a, lo : lo + pix, :]

        for j in range(TEAM - 1):
            for a in range(3):
                start = (3 * j + a) * wide
                kc[1, start : start + H, :] = zero_col
                kc[1, start + H + pix : start + wide, :] = zero_col
        got = {}
        for j in range(TEAM):
            got["d5", j] = fetch(0, xd5, j, band(d5, j), x_r.at[17 + e, j])
            got["d5e", j] = fetch(1, xd5e, j, d5e.at[j], x_r.at[21 + e, j])

        @pl.when(task)
        def _():
            for j in range(TEAM):
                fetch(3, xp, j, band(vb, j), x_r.at[14 + e, j])

        @pl.when(jnp.logical_not(task))
        def _():
            for j in range(TEAM):
                fetch(3, xh, j, band(vb, j), x_r.at[4, j])

        for j in range(TEAM):
            got["d5", j].wait()
            got["d5e", j].wait()

            def body_r(i, carry):
                v = kc[0, pl.ds(pl.multiple_of(all_rows + j * pix + i * H, H), H), :].astype(f32)
                three = (
                    (jnp.where(at_top, d5e[j, 0, i], pltpu.roll(v, 1, 0)) * msks[j, 0]).astype(half),
                    v.astype(half),
                    (jnp.where(at_bottom, d5e[j, 1, i], pltpu.roll(v, H - 1, 0)) * msks[j, 1]).astype(half),
                )
                for a in range(3):
                    if j < TEAM - 1:
                        here = pl.ds(pl.multiple_of((3 * j + a) * wide + H + i * H, H), H)
                        kc[1, here, :] = three[a]
                    else:
                        rb[a, pl.ds(pl.multiple_of(H + i * H, H), H), :] = three[a]
                return carry

            over_columns(body_r)
        for j in range(TEAM):
            pltpu.make_async_copy(xp.at[j], band(vb, j), l_sem.at[3, j]).wait()

        for tap in range(9):
            a, c = 2 - tap // 3, 2 - tap % 3
            acc = None
            for j in range(TEAM):
                term = dot_tn(band(vb, j)[...], rows_shifted(j, a, H * c)[...])
                acc = term if acc is None else acc + term
            pm[tap * C : (tap + 1) * C, :] = acc.astype(half)

        partial = (pm, pi_, pt, p1)
        share = (rows_m, rows_i, rows_t, rows_m)
        pieces = (TEAM, 1, 1, 1)
        width = (C, C, C, q4)

        def flow(g, zd, s, way):
            rows = TEAM * share[g] // pieces[g]
            return pltpu.make_async_remote_copy(
                src_ref=partial[g].at[pl.ds(pl.multiple_of((zd * pieces[g] + s) * rows, 16), rows)],
                dst_ref=flows_in[g].at[way, zd, pl.ds(pl.multiple_of(s * rows, 16), rows)],
                send_sem=fl_s.at[way, g, zd, s],
                recv_sem=fl_r.at[way, g, zd, s],
                device_id=(p, r + TEAM * (1 - 2 * way)),
                device_id_type=MESH,
            )

        def incoming(g, zd, s, way, lane):
            rows = TEAM * share[g] // pieces[g]
            src = flows_in[g].at[way, zd, pl.ds(pl.multiple_of(s * rows, 16), rows)]
            dst = kc.at[1, lane * TEAM * rows_m : lane * TEAM * rows_m + rows, 0 : width[g]]
            return src, dst, fl_r.at[way, g, zd, s], fl_l.at[lane]

        def take(g, zd, s, way, lane):
            src, dst, sem, local = incoming(g, zd, s, way, lane)
            arrived(src, sem)
            pltpu.make_async_copy(src, dst, local).start()

        def taken(g, zd, s, way, lane):
            src, dst, sem, local = incoming(g, zd, s, way, lane)
            pltpu.make_async_copy(src, dst, local).wait()
            return dst[...].astype(f32)

        def flow_start(g):
            @pl.when(z == 0)
            def _():
                for zd in range(n - 1, 0, -1):
                    for s in range(pieces[g]):
                        flow(g, zd, s, 0).start()

            @pl.when(z == n - 1)
            def _():
                for zd in range(n - 1):
                    for s in range(pieces[g]):
                        flow(g, zd, s, 1).start()

        def flow_mid(groups):
            upper = (2 * z) // n

            @pl.when(jnp.logical_and(z > 0, z < n - 1))
            def _():
                for phase in range(2):
                    way = lax.rem(phase + upper, 2)
                    for g in groups:
                        rows = TEAM * share[g] // pieces[g]

                        def body_flow(i, carry):
                            k, s = i // pieces[g], i % pieces[g]
                            zd = (1 - way) * (n - 1 - k) + way * k

                            @pl.when((1 - 2 * way) * (zd - z) > 0)
                            def _():
                                take(g, zd, s, way, 0)
                                here = partial[g].at[pl.ds(pl.multiple_of((zd * pieces[g] + s) * rows, 16), rows)]
                                here[...] = (here[...].astype(f32) + taken(g, zd, s, way, 0)).astype(half)
                                flow(g, zd, s, way).start()

                            return carry

                        lax.fori_loop(0, (n - 1) * pieces[g], body_flow, 0)

        def share_moves(g):
            moves = []
            for d in range(TEAM):
                q = lax.rem(e + d, TEAM)
                start = pl.multiple_of((z * TEAM + q) * share[g], 16)
                moves.append(
                    Remote(partial[g].at[pl.ds(start, share[g])], ends[g].at[e], sh_s.at[g, d], sh_r.at[g, e], e0 + q)
                )
            return moves

        def flow_final(g):
            rows = TEAM * share[g] // pieces[g]
            for s in range(pieces[g]):

                @pl.when(z > 0)
                def _():
                    take(g, z, s, 0, 0)

                @pl.when(z < n - 1)
                def _():
                    take(g, z, s, 1, 1)

                here = partial[g].at[pl.ds(pl.multiple_of(z * TEAM * share[g] + s * rows, 16), rows)]

                @pl.when(jnp.logical_and(z > 0, z < n - 1))
                def _():
                    here[...] = (here[...].astype(f32) + taken(g, z, s, 0, 0) + taken(g, z, s, 1, 1)).astype(half)

                @pl.when(z == 0)
                def _():
                    here[...] = (here[...].astype(f32) + taken(g, z, s, 1, 1)).astype(half)

                @pl.when(z == n - 1)
                def _():
                    here[...] = (here[...].astype(f32) + taken(g, z, s, 0, 0)).astype(half)

            for move in share_moves(g):
                move.start()

        def flow_sent(g):
            for way in range(2):
                for zd in range(n):
                    on = z < zd if way == 0 else z > zd

                    @pl.when(on)
                    def _():
                        for s in range(pieces[g]):
                            flow(g, zd, s, way).wait_send()

            for move in share_moves(g):
                move.sent()

        flow_start(0)

        finish_sends()
        flow_mid((0,))

        first_u = []
        for j in range(TEAM):
            first_u.append(fetch(4, xu, j, band(vb, j), x_r.at[0, j]))

        @pl.when(task)
        def _():
            copies = []
            for j in range(TEAM):
                copies.append(fetch(2, xh, j, band(va, j), x_r.at[4, j]))
                copies.append(fetch(5, xv, j, band(vc, j), x_r.at[8 + e, j]))
                copies.append(fetch(6, xd4, j, kc.at[0, j * C : (j + 1) * C, :], x_r.at[25 + e, j]))
                copies.append(fetch(8, xd3, j, band(d3, j), x_r.at[28 + e, j]))
            for copy in copies:
                copy.wait()
            pi_[0:C, :] = dot_tn(va[...], d3[...]).astype(half)
            pi_[C : 2 * C, :] = dot_tn(vc[...], d3[...]).astype(half)
            acc = kc[0, 0:C, :].astype(f32)
            for j in range(1, TEAM):
                acc = acc + kc[0, j * C : (j + 1) * C, :].astype(f32)
            pt[...] = acc.astype(half)
            flow_start(1)
            flow_start(2)

        for j in range(TEAM):
            got["d1", j] = fetch(9, xd1, j, band(d1, j), x_r.at[31, j])
            got["d1e", j] = fetch(10, xd1e, j, d1e.at[j], x_r.at[35, j])
        row_of1 = lax.broadcasted_iota(jnp.int32, (H, q4), 0)

        def near(j, a, lo, size, cols):
            start = (3 * j + a) * pix + lo
            return kt.at[1, start : start + size, cols * q4 : (cols + 1) * q4]

        for j in range(TEAM):
            got["d1", j].wait()
            got["d1e", j].wait()

        for j in range(TEAM):

            def body_r1(i, carry):
                v = kt[1, pl.ds(pl.multiple_of(j * pix + i * H, H), H), 3 * q4 : 4 * q4].astype(f32)
                three = (
                    (jnp.where(row_of1 == 0, d1e[j, 0, i], pltpu.roll(v, 1, 0)) * msks[j, 0][:, 0:q4]).astype(half),
                    v.astype(half),
                    (jnp.where(row_of1 == H - 1, d1e[j, 1, i], pltpu.roll(v, H - 1, 0)) * msks[j, 1][:, 0:q4]).astype(
                        half
                    ),
                )
                for a in range(3):
                    kt[1, pl.ds(pl.multiple_of((3 * j + a) * pix + i * H, H), H), q4 : 2 * q4] = three[a]
                return carry

            over_columns(body_r1)
            for a in range(3):
                near(j, a, 0, H, 0)[...] = jnp.zeros((H, q4), half)
                near(j, a, H, pix - H, 0)[...] = near(j, a, 0, pix - H, 1)[...]
                near(j, a, 0, pix - H, 2)[...] = near(j, a, H, pix - H, 1)[...]
                near(j, a, pix - H, H, 2)[...] = jnp.zeros((H, q4), half)
        for copy in first_u:
            copy.wait()
        for a in range(3):
            acc = None
            for j in range(TEAM):
                start = (3 * j + 2 - a) * pix
                term = dot_tn(band(vb, j)[...], kt[1, start : start + pix, 0 : 3 * q4])
                acc = term if acc is None else acc + term
            for c in range(3):
                kc[0, (3 * a + c) * C : (3 * a + c + 1) * C, 0:q4] = acc[:, (2 - c) * q4 : (3 - c) * q4].astype(half)
        flow_start(3)

        flow_final(0)

        @pl.when(task)
        def _():
            flow_mid((1, 2, 3))

        @pl.when(jnp.logical_not(task))
        def _():
            flow_mid((3,))

        @pl.when(task)
        def _():
            flow_final(1)
            flow_final(2)

        flow_final(3)

        stores = []

        def store(start, rows, dst, i):
            copy = pltpu.make_async_copy(lin.at[start : start + rows], dst, o_sem.at[i])
            copy.start()
            stores.append(copy)
            return copy

        lanes = C // 128
        lin_m, lin_i, lin_t = rows_m * lanes, rows_i * lanes, rows_t * lanes
        pair_at = 2 * lin_m

        def flatten(value, start, rows, lane, step=1):
            for k in range(value.shape[1] // 128):
                lin[pl.ds(start + step * (lane + k), rows, stride=step * lanes), :] = value[:, 128 * k : 128 * (k + 1)]

        def last_of(g, members, buffer, base):
            copies = []
            for q in range(members):
                arrived(ends[g].at[q], sh_r.at[g, q])
                copy = pltpu.make_async_copy(
                    ends[g].at[q], buffer.at[q * share[g] : (q + 1) * share[g]], l_sem.at[base, q]
                )
                copy.start()
                copies.append(copy)
            for copy in copies:
                copy.wait()

        def piece(buffer, g, q):
            return buffer[q * share[g] : (q + 1) * share[g], :].astype(f32)

        final_m, final_1 = kc.at[1, 2 * TEAM * rows_m : 3 * TEAM * rows_m, :], kt.at[2, :, 0:q4]
        last_of(0, TEAM, final_m, 11)
        for q in range(T):
            if q >= 2:
                stores[q - 2].wait()
            flatten(piece(final_m, 0, q), q % 2 * lin_m, rows_m, 0)
            store(q % 2 * lin_m, lin_m, gm.at[q * lin_m : (q + 1) * lin_m], q)
        flatten(piece(final_m, 0, T), pair_at + 1, rows_m, 0, 2)
        for copy in stores[max(0, T - 2) :]:
            copy.wait()
        del stores[:]
        last_of(1, T, ki.at[1], 12)
        for q in range(T):
            flatten(piece(ki.at[1], 1, q), q * lin_i, rows_i, 0)
        store(0, T * lin_i, gi, T)
        last_of(2, T, ki.at[T - 1, C : 2 * C], 13)
        for q in range(T):
            flatten(piece(ki.at[T - 1, C : 2 * C], 2, q), T * lin_i + q * lin_t, rows_t, 0)
        store(T * lin_i, T * lin_t, gt, T + 1)
        last_of(3, TEAM, final_1, 14)
        for q in range(TEAM):
            flatten(piece(final_1, 3, q), pair_at, rows_m, q * q4 // 128, 2)
        store(pair_at, 2 * lin_m, g1, T + 2)
        flow_sent(0)

        @pl.when(task)
        def _():
            flow_sent(1)
            flow_sent(2)

        flow_sent(3)
        for copy in stores:
            copy.wait()

    for k in range(M):
        arrived(bnr.at[k], bn_r.at[k])
    acc = bnr[0]
    for k in range(1, M):
        acc = acc + bnr[k]
    bng[...] = acc
    for k in range(M):
        arrived(out.at[k, :, 0:C], out_r.at[0, k])
        arrived(out.at[k, :, C:CW], out_r.at[1, k])
    for move in out_moves(0) + out_moves(1) + bn_moves():
        move.sent()
    for move in x_moves:
        move.sent()
    if direct:
        return
    for j in range(TEAM):
        for index, dst in ((0, xu), (4, xh), (31, xd1), (35, xd1e)):
            arrived(dst.at[j], x_r.at[index, j])
    for t in range(T):

        @pl.when(e == t)
        def _():
            for j in range(TEAM):
                for index, dst in ((8, xv), (14, xp), (17, xd5), (21, xd5e), (25, xd4), (28, xd3)):
                    arrived(dst.at[j], x_r.at[index + t, j])

    @pl.when(e == TEAM - 1)
    def _():
        for j in range(TEAM):
            arrived(xd5.at[j], x_r.at[20, j])
            arrived(xd5e.at[j], x_r.at[24, j])


def tables(M, G, H, W):
    pix = H * W
    cm = np.zeros((pix, pix), np.float32)
    spread = np.zeros((pix, 128), np.float32)
    pool = np.zeros((128, pix), np.float32)
    edge = np.zeros((64, 128), np.float32)
    wide = W // 2
    own = pix // 4
    for i in range(H):
        for j in range(W):
            q = j * H + i
            cm[q, i * W + j] = 1
            w = (i // 2) * wide + j // 2
            spread[q, w] = 1
            pool[w, q] = 0.25
            if i >= H - 2:
                pool[own + j // 2, q] = 0.25
            if i < 2:
                pool[own + 16 + j // 2, q] = 0.25
    for j in range(W):
        edge[32 - W + j, own + j // 2] = 1
        edge[32 + j, own + 16 + j // 2] = 1
    return [jnp.asarray(v, half) for v in (cm, cm.T, spread, edge, pool)]


def gradient_kernel(cfg, *refs):
    M, G, H, W, C, T, n = cfg["M"], cfg["G"], cfg["H"], cfg["W"], cfg["C"], cfg["T"], cfg["n"]
    R = M * G
    pix = H * W
    q4 = C // TEAM
    (msk, xu, xh, xp, xv, xd5, xd5e, xd4, xd3, xd1, xd1e) = refs[:11]
    (gm, g1, gi, gt) = refs[11:15]
    (va, vb, vc, d5, d5e, rb, r1, d1, d1e, d3, d4, pm, p1, pi_, pt, am, a1, ai, at, in_sem, s_sem, r_sem) = refs[15:]
    p = lax.axis_index("pipe")
    r = lax.axis_index("rows")
    e = r % TEAM
    z = r // TEAM
    task = e < T

    loads = {}

    def load(name, src, dst, i):
        loads[name] = pltpu.make_async_copy(src, dst, in_sem.at[i])
        loads[name].start()

    load("d5", xd5, d5, 0)
    load("d5e", xd5e, d5e, 1)
    load("h", xh, va, 2)

    @pl.when(task)
    def _():
        pltpu.make_async_copy(xp, vb, in_sem.at[3]).start()
        pltpu.make_async_copy(xv, vc, in_sem.at[4]).start()
        pltpu.make_async_copy(xd3, d3, in_sem.at[6]).start()
        pltpu.make_async_copy(xd4, d4, in_sem.at[7]).start()

    bar = pltpu.get_barrier_semaphore()

    def greet(i, _):
        pl.semaphore_signal(bar, inc=1, device_id=(p, lax.rem(r + TEAM * i, R)), device_id_type=MESH)
        return 0

    lax.fori_loop(1, n, greet, 0)

    row_of = lax.broadcasted_iota(jnp.int32, (H, C), 0)
    row_of1 = lax.broadcasted_iota(jnp.int32, (H, q4), 0)

    def column(j):
        return pl.ds(pl.multiple_of(j * H, H), H)

    for j in range(TEAM):
        for a in range(3):
            rb[j, a, 0:H, :] = jnp.zeros((H, C), half)
            rb[j, a, H * (W + 1) : H * (W + 2), :] = jnp.zeros((H, C), half)
            r1[j, a, 0:H, :] = jnp.zeros((H, 3 * q4), half)
            r1[j, a, H * (W - 1) :, :] = jnp.zeros((H, 3 * q4), half)

    loads["d5"].wait()
    loads["d5e"].wait()
    for j in range(TEAM):

        def body(c, carry):
            for u in range(2):
                i = c * 2 + u
                here = pl.ds(pl.multiple_of(H + i * H, H), H)
                v = d5[j, column(i), :].astype(f32)
                rb[j, 1, here, :] = v.astype(half)
                rb[j, 0, here, :] = (jnp.where(row_of == 0, d5e[j, 0, i], pltpu.roll(v, 1, 0)) * msk[j, 0]).astype(half)
                rb[j, 2, here, :] = (
                    jnp.where(row_of == H - 1, d5e[j, 1, i], pltpu.roll(v, H - 1, 0)) * msk[j, 1]
                ).astype(half)
            return carry

        lax.fori_loop(0, W // 2, body, 0)
    loads["h"].wait()

    @pl.when(task)
    def _():
        pltpu.make_async_copy(xp, vb, in_sem.at[3]).wait()
        pltpu.make_async_copy(xv, vc, in_sem.at[4]).wait()
        pltpu.make_async_copy(xd3, d3, in_sem.at[6]).wait()
        pltpu.make_async_copy(xd4, d4, in_sem.at[7]).wait()

    @pl.when(jnp.logical_not(task))
    def _():
        vb[...] = va[...]

    for tap in range(9):
        a, c = 2 - tap // 3, 2 - tap % 3
        acc = None
        for j in range(TEAM):
            term = dot_tn(vb[j], rb[j, a, H * c : H * c + pix, :])
            acc = term if acc is None else acc + term
        pm[tap * C : (tap + 1) * C, :] = acc.astype(half)

    pltpu.make_async_copy(xu, vb, in_sem.at[8]).start()
    pltpu.make_async_copy(xd1, d1, in_sem.at[9]).start()
    pltpu.make_async_copy(xd1e, d1e, in_sem.at[10]).start()

    def group(index, src, mine, rows):
        moves = []
        for d in range(1, n):
            to = lax.rem(z + d, n)
            moves.append(
                pltpu.make_async_remote_copy(
                    src_ref=src.at[pl.ds(pl.multiple_of(to * rows, 16), rows)],
                    dst_ref=mine.at[z],
                    send_sem=s_sem.at[index, d],
                    recv_sem=r_sem.at[index, z],
                    device_id=(p, TEAM * to + e),
                    device_id_type=MESH,
                )
            )
        return moves

    rows_m, rows_i, rows_t = 9 * C // n, 2 * C // n, C // n
    pl.semaphore_wait(bar, n - 1)
    main = group(0, pm, am, rows_m)
    for move in main:
        move.start()

    @pl.when(task)
    def _():
        for part, value in ((0, va), (1, vc)):
            acc = None
            for j in range(TEAM):
                term = dot_tn(value[j], d3[j])
                acc = term if acc is None else acc + term
            pi_[part * C : (part + 1) * C, :] = acc.astype(half)
        acc = d4[0].astype(f32)
        for j in range(1, TEAM):
            acc = acc + d4[j].astype(f32)
        pt[...] = acc.astype(half)
        for move in group(1, pi_, ai, rows_i) + group(2, pt, at, rows_t):
            move.start()

    pltpu.make_async_copy(xu, vb, in_sem.at[8]).wait()
    pltpu.make_async_copy(xd1, d1, in_sem.at[9]).wait()
    pltpu.make_async_copy(xd1e, d1e, in_sem.at[10]).wait()
    for j in range(TEAM):

        def body1(i, carry):
            v = d1[j, column(i), :].astype(f32)
            three = (
                (jnp.where(row_of1 == 0, d1e[j, 0, i], pltpu.roll(v, 1, 0)) * msk[j, 0][:, 0:q4]).astype(half),
                v.astype(half),
                (jnp.where(row_of1 == H - 1, d1e[j, 1, i], pltpu.roll(v, H - 1, 0)) * msk[j, 1][:, 0:q4]).astype(half),
            )
            for a in range(3):
                r1[j, a, column(i), q4 : 2 * q4] = three[a]
            return carry

        lax.fori_loop(0, W, body1, 0)
        for a in range(3):
            r1[j, a, H : W * H, 0:q4] = r1[j, a, 0 : (W - 1) * H, q4 : 2 * q4]
            r1[j, a, 0 : (W - 1) * H, 2 * q4 : 3 * q4] = r1[j, a, H : W * H, q4 : 2 * q4]
    for a in range(3):
        acc = None
        for j in range(TEAM):
            term = dot_tn(vb[j], r1[j, 2 - a])
            acc = term if acc is None else acc + term
        for c in range(3):
            p1[(3 * a + c) * C : (3 * a + c + 1) * C, :] = acc[:, (2 - c) * q4 : (3 - c) * q4].astype(half)
    one = group(3, p1, a1, rows_m)
    for move in one:
        move.start()

    def reduce(index, src, mine, rows, dst):
        for d in range(1, n):
            s = lax.rem(z + d, n)
            arrived(mine.at[s], r_sem.at[index, s])
        mine[z] = src[pl.ds(pl.multiple_of(z * rows, 16), rows), :]
        acc = mine[0].astype(f32)
        for s in range(1, n):
            acc = acc + mine[s].astype(f32)
        dst[...] = acc.astype(dst.dtype)

    reduce(0, pm, am, rows_m, gm)

    @pl.when(task)
    def _():
        reduce(1, pi_, ai, rows_i, gi)
        reduce(2, pt, at, rows_t, gt)

    @pl.when(jnp.logical_not(task))
    def _():
        gi[...] = jnp.zeros(gi.shape, gi.dtype)
        gt[...] = jnp.zeros(gt.shape, gt.dtype)

    reduce(3, p1, a1, rows_m, g1)
    for move in main + one:
        move.wait_send()

    @pl.when(task)
    def _():
        for move in group(1, pi_, ai, rows_i) + group(2, pt, at, rows_t):
            move.wait_send()


def per_device(cfg, section_in, image_start, pool_choice, conv_shared, task_in, task_mid, task_conv, bn_gain, bn_bias):
    M, G, H, W, C, T, n = cfg["M"], cfg["G"], cfg["H"], cfg["W"], cfg["C"], cfg["T"], cfg["n"]
    R = M * G
    pix = H * W
    part = pix // M
    rows_total = H * G
    norms = 2 + 3 * T
    CW = C * (1 + T)
    p = lax.axis_index("pipe")
    r = lax.axis_index("rows")
    b, m = r // M, r % M
    sec = section_in[0].reshape(M, part, CW)
    hp = pool_choice.shape[1]
    place = jnp.arange(4, dtype=jnp.int32).reshape(2, 1, 2)
    picked = pool_choice[:, :, None, :, None] == place[None, None]
    sel = jnp.broadcast_to(picked.reshape(M, part, 1), (M, part, 128)).astype(half)

    ones = jnp.ones((M, 1), jnp.int32)
    padded = jnp.concatenate([ones, image_start[:, 1:], ones], 1)
    links = 1.0 - lax.dynamic_slice_in_dim(padded, b * H, H + 1, 1).astype(f32)
    both = jnp.stack([links[:, :-1], links[:, 1:]], 1)
    team_masks = jnp.broadcast_to(both[..., None], (M, 2, H, C))

    cm, cm_t, spread, edge, pool = tables(M, G, H, W)
    sds = jax.ShapeDtypeStruct
    exchange = [
        sds((TEAM, pix, C), half),
        sds((TEAM, pix, C), half),
        sds((TEAM, pix, C), half),
        sds((TEAM, pix, C), half),
        sds((TEAM, pix, C), half),
        sds((TEAM, 2, W, 1, C), f32),
        sds((TEAM, C, C), half),
        sds((TEAM, pix, C), half),
        sds((TEAM, pix, C // TEAM), half),
        sds((TEAM, 2, W, 1, C // TEAM), f32),
    ]
    direct = C % (16 * R) == 0
    parts = R if direct else n
    rows_m, rows_i, rows_t = 9 * C // parts, 2 * C // parts, C // parts
    q4 = C // TEAM
    shares, share_scratch = [], []
    dma = pltpu.SemaphoreType.DMA
    if direct:
        shares = [
            sds((T * rows_m * C // 128, 128), f32),
            sds((2 * rows_m * C // 128, 128), f32),
            sds((T * rows_i * C // 128, 128), f32),
            sds((T * rows_t * C // 128, 128), f32),
            sds((2, n, TEAM * rows_m, C), half),
            sds((2, n, TEAM * rows_i, C), half),
            sds((2, n, TEAM * rows_t, C), half),
            sds((2, n, TEAM * rows_m, q4), half),
            sds((TEAM, rows_m, C), half),
            sds((T, rows_i, C), half),
            sds((T, rows_t, C), half),
            sds((TEAM, rows_m, q4), half),
        ]
        share_scratch = [
            pltpu.VMEM((4 * rows_m * C // 128, 128), f32),
            pltpu.VMEM((TEAM, 2, W, 1, C), f32),
            pltpu.VMEM((TEAM, 2, W, 1, q4), f32),
            dma((15, TEAM)),
            dma((2, 4, n, TEAM)),
            dma((2, 4, n, TEAM)),
            dma((2,)),
            dma((4, TEAM)),
            dma((4, TEAM)),
            dma((TEAM + 3,)),
        ]
    vm = pltpu.VMEM
    win = pix // 4 + 32
    outs = pl.pallas_call(
        functools.partial(section_kernel, dict(cfg, direct=direct)),
        name="sections",
        out_shape=[sds((M, part, CW), half), sds((2 * norms, C), f32)] + exchange + shares,
        in_specs=[ANY, ANY] + [VMEM] * 8 + [ANY] * 4,
        out_specs=[ANY, VMEM] + [ANY] * (len(exchange) + len(shares)),
        scratch_shapes=[
            vm((2, 9 * C, C), half),
            vm((T, 2 * C, C), half),
            vm((T, C, C), half),
            vm((T, 9 * C, C), half),
            vm((pix, CW), half),
            vm((2, pix, CW), half),
            vm((pix, 128), half),
            vm((pix, 128), half),
            vm((2, 32, C), half),
            vm((2, 32, 128), half),
            vm((2, W, 1, C), f32),
            vm((win, CW), half),
            vm((win, CW), half),
            vm((3, pix + 2 * H, C), half),
            vm((norms, pix, C), f32),
            vm((EDGES, 2, W, 1, C), f32),
            vm((EDGES, 2, W, 1, C), f32),
            vm((2 * norms, 2, C), f32),
            vm((G, 2 * norms, 2, C), f32),
            vm((pix, C), half),
            vm((pix, C), half),
            vm((W, 2, C), f32),
            vm((T, pix, C), half),
            vm((T, pix, C), half),
            vm((pix, CW), half),
            vm((T, pix, C), f32),
            vm((pix, C), f32),
            vm((T, pix, C), half),
            vm((T, 2, W, 1, C), f32),
            vm((2, W, 1, C), f32),
            vm((T, pix, C), half),
            vm((TEAM, pix, C // TEAM), half),
            vm((TEAM, 2, W, 1, C // TEAM), f32),
            vm((2 * norms, C), f32),
            vm((M, 2 * norms, C), f32),
            pltpu.SemaphoreType.REGULAR,
            dma((4 + T,)),
            dma((7, M)),
            dma((5, M)),
            dma((EDGES, 2)),
            dma((EDGES, 2)),
            dma((2 * norms, G)),
            dma((2 * norms, G)),
            dma((3,)),
            dma((3,)),
            dma((2, M)),
            dma((2, M)),
            dma((M,)),
            dma((M,)),
            dma((39,)),
            dma((39, TEAM)),
        ]
        + share_scratch,
        compiler_params=pltpu.CompilerParams(
            collective_id=0, has_side_effects=True, vmem_limit_bytes=63 * 2**20
        ),
    )(sec, sel, team_masks, cm, cm_t, spread, edge, pool, bn_gain[0], bn_bias[0], conv_shared[0], task_in[0], task_mid[0], task_conv[0])
    result, bn_grads = outs[:2]

    result = result.reshape(1, M, part // W, W, CW)
    if direct:
        gm, g1, gi, gt = outs[-12:-8]
        return (
            result,
            g1.reshape(-1, 2, 128).transpose(1, 0, 2).reshape(1, 2, -1),
            gi.reshape(1, T, -1),
            gt.reshape(1, T, -1),
            gm.reshape(1, T, -1),
            bn_grads[None, :norms],
            bn_grads[None, norms:],
        )
    shapes = [sds((rows_m, C), half), sds((rows_m, q4), half), sds((rows_i, C), half), sds((rows_t, C), half)]
    slots = [(n, rows_m, C), (n, rows_m, q4), (n, rows_i, C), (n, rows_t, C)]
    grads = pl.pallas_call(
        functools.partial(gradient_kernel, cfg),
        name="kernel_gradients",
        out_shape=shapes,
        in_specs=[VMEM] + [ANY] * 10,
        out_specs=[VMEM] * 4,
        scratch_shapes=[
            vm((TEAM, pix, C), half),
            vm((TEAM, pix, C), half),
            vm((TEAM, pix, C), half),
            vm((TEAM, pix, C), half),
            vm((TEAM, 2, W, 1, C), f32),
            vm((TEAM, 3, pix + 2 * H, C), half),
            vm((TEAM, 3, pix, 3 * q4), half),
            vm((TEAM, pix, q4), half),
            vm((TEAM, 2, W, 1, q4), f32),
            vm((TEAM, pix, C), half),
            vm((TEAM, C, C), half),
            vm((9 * C, C), half),
            vm((9 * C, q4), half),
            vm((2 * C, C), half),
            vm((C, C), half),
            vm(slots[0], half),
            vm(slots[1], half),
            vm(slots[2], half),
            vm(slots[3], half),
            dma((11,)),
            dma((4, R)),
            dma((4, R)),
        ],
        compiler_params=pltpu.CompilerParams(
            collective_id=1, has_side_effects=True, vmem_limit_bytes=60 * 2**20
        ),
    )(team_masks, *outs[2:])

    gm, g1, gi, gt = grads
    pieces = [
        gm.reshape(TEAM, -1),
        g1.reshape(TEAM, -1),
        gi.reshape(TEAM, -1),
        gt.reshape(TEAM, -1),
    ]
    packed = jnp.concatenate(pieces, 1)
    teams = [[TEAM * i + j for j in range(TEAM)] for i in range(R // TEAM)]
    swapped = lax.all_to_all(packed, "rows", 0, 0, axis_index_groups=teams, tiled=False).astype(f32)
    sizes = [v.shape[1] for v in pieces]
    o = [0, sizes[0], sizes[0] + sizes[1], sizes[0] + sizes[1] + sizes[2], sum(sizes)]
    mains = swapped[:, o[0] : o[1]]
    firsts = swapped[:, o[1] : o[2]].reshape(TEAM, -1, q4).transpose(1, 0, 2).reshape(-1)
    conv_grad = jnp.stack([firsts, mains[T]])
    return (
        result,
        conv_grad[None],
        swapped[:T, o[2] : o[3]][None],
        swapped[:T, o[3] : o[4]][None],
        mains[:T][None],
        bn_grads[None, :norms],
        bn_grads[None, norms:],
    )


def solution(mesh):
    in_specs = (
        P("pipe", None, "rows", None, None),
        P(),
        P(None, "rows", None),
        P("pipe", None, None, None),
        P("pipe", None, None, None),
        P("pipe", None, None, None),
        P("pipe", None, None, None),
        P("pipe", None, None),
        P("pipe", None, None),
    )
    out_specs = (
        P("pipe", None, "rows", None, None),
        P("pipe", None, "rows"),
        P("pipe", None, "rows"),
        P("pipe", None, "rows"),
        P("pipe", None, "rows"),
        P("pipe", None, None),
        P("pipe", None, None),
    )
    bands = mesh.shape["rows"]

    def step(section_in, image_start, pool_choice, conv_shared, task_in, task_mid, task_conv, bn_gain, bn_bias):
        M = section_in.shape[1]
        G = bands // M
        cfg = dict(
            M=M,
            G=G,
            H=section_in.shape[2] // G,
            W=section_in.shape[3],
            C=conv_shared.shape[3],
            T=task_in.shape[1],
            n=bands // TEAM,
            to_all=frozenset(range(0, 8)) | frozenset(range(31, 39)),
        )
        return jax.shard_map(
            functools.partial(per_device, cfg), mesh=mesh, in_specs=in_specs, out_specs=out_specs, check_vma=False
        )(section_in, image_start, pool_choice, conv_shared, task_in, task_mid, task_conv, bn_gain, bn_bias)

    return step
```

```python
import functools

import jax
import jax.numpy as jnp
import numpy as np
from jax import lax
from jax.experimental import pallas as pl
from jax.experimental.pallas import tpu as pltpu
from jax.sharding import PartitionSpec as P

MESH = pl.DeviceIdType.MESH
half = jnp.bfloat16
f32 = jnp.float32
epsilon = 1e-05
TEAM = 4

ANY = pl.BlockSpec(memory_space=pl.ANY)
VMEM = pl.BlockSpec(memory_space=pltpu.VMEM)


def sigmoid(x):
    return 0.5 * jnp.tanh(0.5 * x) + 0.5


def dot(a, b):
    return jnp.dot(a, b, preferred_element_type=f32)


def dot_nt(a, b):
    return lax.dot_general(a, b, (((1,), (1,)), ((), ())), preferred_element_type=f32)


def dot_tn(a, b):
    return lax.dot_general(a, b, (((0,), (0,)), ((), ())), preferred_element_type=f32)


class Remote:
    def __init__(self, src, dst, send, recv, to):
        self.src, self.dst, self.send, self.recv, self.to = src, dst, send, recv, to
        self.local = to == lax.axis_index("rows")

    def remote(self):
        return pltpu.make_async_remote_copy(
            src_ref=self.src,
            dst_ref=self.dst,
            send_sem=self.send,
            recv_sem=self.recv,
            device_id=(lax.axis_index("pipe"), self.to),
            device_id_type=MESH,
        )

    def start(self):
        @pl.when(self.local)
        def _():
            pltpu.make_async_copy(self.src, self.dst, self.recv).start()

        @pl.when(jnp.logical_not(self.local))
        def _():
            self.remote().start()

    def sent(self):
        @pl.when(jnp.logical_not(self.local))
        def _():
            self.remote().wait_send()


def arrived(dst, sem):
    pltpu.make_async_copy(dst, dst, sem).wait()


EDGES = 13


def section_kernel(cfg, *refs):
    M, G, H, W, C, T = cfg["M"], cfg["G"], cfg["H"], cfg["W"], cfg["C"], cfg["T"]
    R = M * G
    pix = H * W
    part = pix // M
    count = float(pix * G)
    norms = 2 + 3 * T
    direct = cfg["direct"]
    (sec, sel, msks, perm, perm_t, spread, spread_edge, pool, gain, bias, wc, wi, wm, wt) = refs[:14]
    (out, bng, xu, xh, xp, xv, xd5, xd5e, xd4, xd3, xd1, xd1e) = refs[14:26]
    refs = refs[26:]
    if direct:
        (gm, g1, gi, gt) = refs[:4]
        flows_in = refs[4:8]
        ends = refs[8:12]
        (lin, d5e, d1e, l_sem, fl_s, fl_r, fl_l, sh_s, sh_r, o_sem) = refs[-10:]
        refs = refs[12:-10]
    (
        kc, ki, km, kt, rin, field, selin, chosen, uh, selh, uedge, px, ps, rb, ys, esend, erecv, ssend, srecv,
        h1, h2, h2e, t1, pr, res, dz, dh, dy5, dy5e, dy2e, dy3, dy1, dy1e, bn, bnr,
        go, w_sem, in_s, in_r, ed_s, ed_r, st_s, st_r, pp_s, pp_r, out_s, out_r, bn_s, bn_r, x_s, x_r,
    ) = refs
    p = lax.axis_index("pipe")
    r = lax.axis_index("rows")
    b, m = r // M, r % M
    e, e0 = m, r - m
    first, last = b == 0, b == G - 1
    CW = C * (1 + T)

    loads = {}

    def load(name, src, dst, i):
        loads[name] = pltpu.make_async_copy(src, dst, w_sem.at[i])
        loads[name].start()

    load("c0", wc.at[0], kc.at[0], 0)
    load("i", wi, ki, 1)
    load("c1", wc.at[1], kc.at[1], 2)
    load("m", wm, km, 3)
    for t in range(T):
        load("t%d" % t, wt.at[t], kt.at[t], 4 + t)

    zero_col = jnp.zeros((H, C), half)
    for a in range(3):
        rb[a, 0:H, :] = zero_col
        rb[a, H * (W + 1) : H * (W + 2), :] = zero_col
    px[pix // 4 :, :] = jnp.zeros((px.shape[0] - pix // 4, CW), half)

    @pl.when(first)
    def _():
        for s in range(EDGES):
            erecv[s, 0] = jnp.zeros((W, 1, C), f32)
        uh[0] = jnp.zeros((32, C), half)
        selh[0] = jnp.zeros((32, 128), half)

    @pl.when(last)
    def _():
        for s in range(EDGES):
            erecv[s, 1] = jnp.zeros((W, 1, C), f32)
        uh[1] = jnp.zeros((32, C), half)
        selh[1] = jnp.zeros((32, 128), half)

    bar = pltpu.get_barrier_semaphore()

    def hello(side, row):
        pl.semaphore_signal(bar, inc=1, device_id=(side, row), device_id_type=MESH)

    for d in range(1, M):
        hello(p, e0 + lax.rem(m + d, M))
    for d in range(1, G):
        hello(p, M * lax.rem(b + d, G) + m)
    hello(1 - p, r)
    tops = jnp.logical_and(m == M - 1, jnp.logical_not(last))
    bottoms = jnp.logical_and(m == 0, jnp.logical_not(first))

    @pl.when(jnp.logical_not(first))
    def _():
        hello(1 - p, r - M)
        hello(p, e0 - 1)

    @pl.when(jnp.logical_not(last))
    def _():
        hello(1 - p, r + M)
        hello(p, e0 + M)

    @pl.when(tops)
    def _():
        for j in range(M):
            hello(p, e0 + M + j)

    @pl.when(bottoms)
    def _():
        for j in range(M):
            hello(p, e0 - M + j)

    below_me, above_me = 1 - (b + 1) // G, (b + G - 1) // G
    top_member, bottom_member = (m + 1) // M, 1 - (m + M - 1) // M
    pl.semaphore_wait(
        bar, M + G - 1 + 2 * (below_me + above_me) + M * (top_member * below_me + bottom_member * above_me)
    )

    mine = pl.ds(pl.multiple_of(part * m, 16), part)
    field_moves, rest_moves, sel_moves, edge_moves = [], [], [], ([], [])
    for d in range(M):
        j = lax.rem(m + d, M)
        to = e0 + j
        field_moves.append(Remote(sec.at[j, :, 0:C], rin.at[mine, 0:C], in_s.at[0, d], in_r.at[0, m], to))
        sel_moves.append(Remote(sel.at[j], selin.at[mine], in_s.at[2, d], in_r.at[2, m], to))
        rest_moves.append(Remote(sec.at[j, :, C:CW], rin.at[mine, C:CW], in_s.at[1, d], in_r.at[1, m], to))
    for j in range(M):
        to = e0 + j
        edge_moves[0].append(
            Remote(sec.at[j, pl.ds(part - 32, 32), 0:C], uh.at[0], in_s.at[3, j], in_r.at[3, 0], to + M)
        )
        edge_moves[0].append(Remote(sel.at[j, pl.ds(part - 32, 32)], selh.at[0], in_s.at[4, j], in_r.at[3, 1], to + M))
        edge_moves[1].append(Remote(sec.at[j, pl.ds(0, 32), 0:C], uh.at[1], in_s.at[5, j], in_r.at[4, 0], to - M))
        edge_moves[1].append(Remote(sel.at[j, pl.ds(0, 32)], selh.at[1], in_s.at[6, j], in_r.at[4, 1], to - M))

    def start_field():
        for move in field_moves:
            move.start()
        for move in rest_moves:
            move.start()

    @pl.when(tops)
    def _():
        for move in edge_moves[0]:
            move.start()

    @pl.when(bottoms)
    def _():
        for move in edge_moves[1]:
            move.start()

    @pl.when(p == 0)
    def _():
        start_field()

    for move in sel_moves:
        move.start()

    row_of = lax.broadcasted_iota(jnp.int32, (H, C), 0)
    at_top, at_bottom = row_of == 0, row_of == H - 1

    def column(j):
        return pl.ds(pl.multiple_of(j * H, H), H)

    def over_columns(body, start=0, step=2):
        def several(c, carry):
            for u in range(step):
                carry = body(c * step + u, carry)
            return carry

        return lax.fori_loop(0, W // step, several, start)

    def build(j, value, above, below, up, down):
        here = pl.ds(pl.multiple_of(H + j * H, H), H)
        rb[1, here, :] = value.astype(half)
        rb[0, here, :] = (jnp.where(at_top, above, pltpu.roll(value, 1, 0)) * up).astype(half)
        rb[2, here, :] = (jnp.where(at_bottom, below, pltpu.roll(value, H - 1, 0)) * down).astype(half)

    def conv(kernel):
        total = None
        for tap in range(9):
            a, c = tap // 3, tap % 3
            term = dot(rb[a, H * c : H * c + pix, :], kernel[tap * C : (tap + 1) * C, :])
            total = term if total is None else total + term
        return total

    def conv_t(kernel):
        total = None
        for tap in range(9):
            a, c = tap // 3, tap % 3
            term = dot_nt(rb[a, H * c : H * c + pix, :], kernel[(8 - tap) * C : (9 - tap) * C, :])
            total = term if total is None else total + term
        return total

    def folded(total):
        return jnp.sum(total, 0, keepdims=True)

    def fold(x):
        return jnp.sum(x.reshape(H // 8, 8, C), 0)

    zero8 = jnp.zeros((8, C), f32)

    def edge_copy(slot, side):
        to = r - M if side == 0 else r + M
        return pltpu.make_async_remote_copy(
            src_ref=esend.at[slot, side],
            dst_ref=erecv.at[slot, 1 - side],
            send_sem=ed_s.at[slot, side],
            recv_sem=ed_r.at[slot, 1 - side],
            device_id=(p, to),
            device_id_type=MESH,
        )

    def send_edges(slot):
        @pl.when(jnp.logical_not(first))
        def _():
            edge_copy(slot, 0).start()

        @pl.when(jnp.logical_not(last))
        def _():
            edge_copy(slot, 1).start()

    def get_edges(slot):
        @pl.when(jnp.logical_not(first))
        def _():
            arrived(erecv.at[slot, 0], ed_r.at[slot, 0])

        @pl.when(jnp.logical_not(last))
        def _():
            arrived(erecv.at[slot, 1], ed_r.at[slot, 1])

    def finish_edges(slot):
        @pl.when(jnp.logical_not(first))
        def _():
            edge_copy(slot, 0).wait_send()

        @pl.when(jnp.logical_not(last))
        def _():
            edge_copy(slot, 1).wait_send()

    def stat_copy(slot, n, d):
        to = M * lax.rem(b + d, G) + m
        return pltpu.make_async_remote_copy(
            src_ref=ssend.at[pl.ds(slot, n)],
            dst_ref=srecv.at[b, pl.ds(slot, n)],
            send_sem=st_s.at[slot, d],
            recv_sem=st_r.at[slot, b],
            device_id=(p, to),
            device_id_type=MESH,
        )

    def send_sums(slot, n):
        srecv[b, slot : slot + n] = ssend[slot : slot + n]
        for d in range(1, G):
            stat_copy(slot, n, d).start()

    sums_sent = []

    def get_sums(slot, n):
        sums_sent.append((slot, n))
        for d in range(1, G):
            s = lax.rem(b + d, G)
            arrived(srecv.at[s, pl.ds(slot, n)], st_r.at[slot, s])

    def total(slot):
        acc = srecv[0, slot]
        for g in range(1, G):
            acc = acc + srecv[g, slot]
        return acc

    def put_sums(slot, s, q):
        ssend[slot] = jnp.concatenate([folded(s), folded(q)], 0)

    x_moves = []
    kept = []

    def post(index, src, dst, target, keep=False):
        move = Remote(src, dst.at[e], x_s.at[index], x_r.at[index - (target if index in cfg["to_all"] else 0), e], e0 + target)
        x_moves.append(move)
        if not keep:
            move.start()
        else:
            kept.append(move)

            @pl.when(p == 0)
            def _():
                move.start()

    def send_kept():
        for move in kept:
            move.start()


    def moments(k, slot, edge=None):
        def body(j, carry):
            s, q = carry
            y = ys[k, column(j), :]
            if edge is not None:
                esend[edge, 0, j] = y[0:1]
                esend[edge, 1, j] = y[H - 1 : H]
            return s + fold(y), q + fold(y * y)

        s, q = over_columns(body, (zero8, zero8))
        put_sums(slot, s, q)

    norm = {}

    def norm_rows(k, slot):
        acc = total(slot)
        mean = acc[0:1] / count
        rs = lax.rsqrt(acc[1:2] / count - mean * mean + epsilon)
        scale = gain[k : k + 1, :] * rs
        norm[k] = (mean, rs, scale, bias[k : k + 1, :])

    def normed(k, y):
        mean, rs, scale, shift = norm[k]
        return (y - mean) * scale + shift

    def silu(x):
        return x * sigmoid(x)

    def silu_slope(x):
        s = sigmoid(x)
        return s * (1.0 + x * (1.0 - s))

    def pair(slot, j):
        return jnp.concatenate([erecv[slot, 0, j], erecv[slot, 1, j]], 0)

    nt = 2 + 3 * T
    F3, F4, F5 = 2, 2 + T, 2 + 2 * T

    def wait_field(kind, buffer):
        for k in range(M):
            arrived(buffer(k), in_r.at[kind, k])

    @pl.when(jnp.logical_not(first))
    def _():
        arrived(uh.at[0], in_r.at[3, 0])

    @pl.when(jnp.logical_not(last))
    def _():
        arrived(uh.at[1], in_r.at[4, 0])

    def start_of_field():
        wait_field(0, lambda k: rin.at[pl.ds(part * k, part), 0:C])
        field[p, :, 0:C] = dot(perm[...], rin[:, 0:C]).astype(half)

    def rest_of_field():
        wait_field(1, lambda k: rin.at[pl.ds(part * k, part), C:CW])
        for t in range(T):
            cols = slice((t + 1) * C, (t + 2) * C)
            field[p, :, cols] = dot(perm[...], rin[:, cols]).astype(half)

    @pl.when(p == 0)
    def _():
        start_of_field()

    def wait_selection():
        wait_field(2, lambda k: selin.at[pl.ds(part * k, part)])

        @pl.when(jnp.logical_not(first))
        def _():
            arrived(selh.at[0], in_r.at[3, 1])

        @pl.when(jnp.logical_not(last))
        def _():
            arrived(selh.at[1], in_r.at[4, 1])

    def halo_copies():
        return (
            pltpu.make_async_remote_copy(
                src_ref=ps.at[pl.ds(pix // 4, 16), 0:C], dst_ref=px.at[pl.ds(pix // 4, 16), 0:C],
                send_sem=pp_s.at[1], recv_sem=pp_r.at[1], device_id=(1 - p, r + M), device_id_type=MESH),
            pltpu.make_async_remote_copy(
                src_ref=ps.at[pl.ds(pix // 4 + 16, 16), 0:C], dst_ref=px.at[pl.ds(pix // 4 + 16, 16), 0:C],
                send_sem=pp_s.at[2], recv_sem=pp_r.at[2], device_id=(1 - p, M * (b - 1) + m), device_id_type=MESH),
        )

    def pool_copy():
        return pltpu.make_async_remote_copy(
            src_ref=ps.at[pl.ds(0, pix // 4)], dst_ref=px.at[pl.ds(0, pix // 4)],
            send_sem=pp_s.at[0], recv_sem=pp_r.at[0], device_id=(1 - p, r), device_id_type=MESH)

    @pl.when(p == 1)
    def _():
        wait_selection()
        chosen[...] = spread[...] * dot(perm[...], selin[...]).astype(half)
        pl.semaphore_wait(go, 1)
        start_field()
        start_of_field()
        rest_of_field()
        arrived(px.at[pl.ds(0, pix // 4)], pp_r.at[0])

        @pl.when(jnp.logical_not(first))
        def _():
            arrived(px.at[pl.ds(pix // 4, 16), 0:C], pp_r.at[1])

        @pl.when(jnp.logical_not(last))
        def _():
            arrived(px.at[pl.ds(pix // 4 + 16, 16), 0:C], pp_r.at[2])

        for t in range(1 + T):
            cols = slice(t * C, (t + 1) * C)
            field[0, :, cols] = dot(chosen[...], px[:, cols]).astype(half)
        edges = spread_edge[...] * jnp.concatenate([selh[0], selh[1]], 0)
        both = dot(edges, px[:, 0:C]).astype(half)
        uh[0] = both[0:32]
        uh[1] = both[32:64]

    above = uh[0].astype(f32)
    below = uh[1].astype(f32)
    for j in range(W):
        uedge[0, j] = above[32 - W + j : 33 - W + j]
        uedge[1, j] = below[j : j + 1]

    up = msks[m, 0]
    down = msks[m, 1]

    def body_u(j, carry):
        build(j, field[0, column(j), 0:C].astype(f32), uedge[0, j], uedge[1, j], up, down)
        return carry

    over_columns(body_u)
    loads["c0"].wait()
    ys[0] = conv(kc.at[0])
    moments(0, 0, 0)
    send_sums(0, 1)
    send_edges(0)

    @pl.when(p == 0)
    def _():
        rest_of_field()
        pl.semaphore_signal(go, inc=1, device_id=(1 - p, r), device_id_type=MESH)

    for q in range(TEAM):
        post(q, field.at[0, :, 0:C], xu, q, True)
    for t in range(T):
        post(8 + t, field.at[0, :, (t + 1) * C : (t + 2) * C], xv, t, True)
    get_sums(0, 1)
    get_edges(0)
    norm_rows(0, 0)

    def body_h1(j, carry):
        value = silu(normed(0, ys[0, column(j), :]))
        side = silu(normed(0, pair(0, j)))
        h1[column(j), :] = value.astype(half)
        build(j, value, side[0:1], side[1:2], up, down)
        return carry

    over_columns(body_h1)
    for q in range(TEAM):
        post(4 + q, h1, xh, q, q < T)

    loads["i"].wait()
    for t in range(T):
        k = 2 + 3 * t
        ys[k] = dot(h1[...], ki[t, 0:C, :]) + dot(field[0, :, (t + 1) * C : (t + 2) * C], ki[t, C : 2 * C, :])
        moments(k, F3 + t)
    send_sums(F3, T)
    loads["c1"].wait()
    ys[1] = conv(kc.at[1])
    moments(1, 1, 1)
    send_sums(1, 1)
    send_edges(1)

    get_sums(F3, T)
    loads["m"].wait()
    for t in range(T):
        k = 2 + 3 * t
        norm_rows(k, F3 + t)

        def body_t1(j, carry):
            t1[t, column(j), :] = silu(normed(k, ys[k, column(j), :])).astype(half)
            return carry

        over_columns(body_t1)
        ys[k + 1] = dot(t1[t], km[t])
        moments(k + 1, F4 + t, 2 + t)
        send_sums(F4 + t, 1)
        send_edges(2 + t)

    get_sums(1, 1)
    get_edges(1)
    norm_rows(1, 1)

    def body_h2(j, carry):
        value = silu(normed(1, ys[1, column(j), :])).astype(half)
        h2[column(j), :] = value
        res[column(j), 0:C] = value
        side = silu(normed(1, pair(1, j))).astype(half).astype(f32)
        h2e[j] = side
        return carry

    over_columns(body_h2)
    for t in range(T):
        k = 3 + 3 * t
        get_sums(F4 + t, 1)
        get_edges(2 + t)
        norm_rows(k, F4 + t)

        def body_p(j, carry):
            gate = sigmoid(normed(k, ys[k, column(j), :]))
            value = gate * h2[column(j), :].astype(f32)
            side = sigmoid(normed(k, pair(2 + t, j))) * h2e[j]
            pr[t, column(j), :] = value.astype(half)
            build(j, value, side[0:1], side[1:2], up, down)
            return carry

        over_columns(body_p)
        post(14 + t, pr.at[t], xp, t)
        loads["t%d" % t].wait()
        ys[k + 1] = conv(kt.at[t])
        moments(k + 1, F5 + t, 5 + t)
        send_sums(F5 + t, 1)
        send_edges(5 + t)
    for t in range(T):
        k = 4 + 3 * t
        get_sums(F5 + t, 1)
        get_edges(5 + t)
        norm_rows(k, F5 + t)

        def body_q(j, carry):
            res[column(j), (t + 1) * C : (t + 2) * C] = silu(normed(k, ys[k, column(j), :])).astype(half)
            return carry

        over_columns(body_q)

    def out_moves(which):
        cols = slice(0, C) if which == 0 else slice(C, CW)
        moves = []
        for d in range(M):
            k = lax.rem(m + d, M)
            rows = pl.ds(pl.multiple_of(part * k, 16), part)
            moves.append(
                Remote(rin.at[rows, cols], out.at[m, :, cols], out_s.at[which, d], out_r.at[which, m], e0 + k)
            )
        return moves

    def stage_result(which):
        for t in range(0, 1) if which == 0 else range(1, 1 + T):
            cols = slice(t * C, (t + 1) * C)
            rin[:, cols] = dot(perm_t[...], res[:, cols]).astype(half)

    def start_result(which):
        for move in out_moves(which):
            move.start()

    @pl.when(p == 0)
    def _():
        for t in range(1 + T):
            cols = slice(t * C, (t + 1) * C)
            ps[:, cols] = dot(pool[...], res[:, cols]).astype(half)
        pool_copy().start()

        @pl.when(jnp.logical_not(last))
        def _():
            halo_copies()[0].start()

        @pl.when(jnp.logical_not(first))
        def _():
            halo_copies()[1].start()

        pool_copy().wait_send()

        @pl.when(jnp.logical_not(last))
        def _():
            halo_copies()[0].wait_send()

        @pl.when(jnp.logical_not(first))
        def _():
            halo_copies()[1].wait_send()

        arrived(px.at[pl.ds(0, pix // 4)], pp_r.at[0])
        for t in range(1 + T):
            cols = slice(t * C, (t + 1) * C)
            field[1, :, cols] = (dot(spread[...], px[:, cols]) * 0.25).astype(half)

    @pl.when(p == 1)
    def _():
        stage_result(0)
        stage_result(1)

    B3, B4, B5 = nt + F3, nt + F4, nt + F5
    back = {}

    def back_rows(k, slot):
        acc = total(slot)
        mean, rs, scale, shift = norm[k]
        slope = -scale * rs * acc[1:2] / count
        back[k] = (scale, slope, -scale * acc[0:1] / count - slope * mean)
        bn[k : k + 1, :] = acc[1:2]
        bn[norms + k : norms + k + 1, :] = acc[0:1]

    def grad_pre(k, dzv, y):
        scale, slope, rest = back[k]
        return scale * dzv + slope * y + rest

    def hat(k, y):
        mean, rs, scale, shift = norm[k]
        return (y - mean) * rs

    for t in range(T):
        k = 4 + 3 * t

        def body_dz5(j, carry):
            s, q = carry
            y = ys[k, column(j), :]
            g = field[1, column(j), (t + 1) * C : (t + 2) * C].astype(f32)
            v = g * silu_slope(normed(k, y))
            dz[t, column(j), :] = v
            esend[8 + t, 0, j] = v[0:1]
            esend[8 + t, 1, j] = v[H - 1 : H]
            return s + fold(v), q + fold(v * hat(k, y))

        s, q = over_columns(body_dz5, (zero8, zero8))
        put_sums(B5 + t, s, q)
        send_sums(B5 + t, 1)
        send_edges(8 + t)

    for t in range(T):
        k = 4 + 3 * t
        get_sums(B5 + t, 1)
        get_edges(8 + t)
        back_rows(k, B5 + t)

        def body_dy5(j, carry):
            v = grad_pre(k, dz[t, column(j), :], ys[k, column(j), :])
            side = grad_pre(k, pair(8 + t, j), pair(5 + t, j))
            dy5[t, column(j), :] = v.astype(half)
            dy5e[t, 0, j] = side[0:1]
            dy5e[t, 1, j] = side[1:2]
            build(j, v, side[0:1], side[1:2], up, down)
            return carry

        over_columns(body_dy5)
        post(17 + t, dy5.at[t], xd5, t)
        post(21 + t, dy5e.at[t], xd5e, t)
        ys[k] = conv_t(kt.at[t])

        def body_dz4(j, carry):
            s, q = carry
            dp = ys[k, column(j), :]
            y = ys[k - 1, column(j), :]
            gate = sigmoid(normed(k - 1, y))
            dgate = dp * h2[column(j), :].astype(f32)
            base = field[1, column(j), 0:C].astype(f32) if t == 0 else dh[column(j), :]
            dh[column(j), :] = base + dp * gate
            v = dgate * gate * (1.0 - gate)
            ys[k, column(j), :] = v
            return s + fold(v), q + fold(v * hat(k - 1, y))

        s, q = over_columns(body_dz4, (zero8, zero8))
        put_sums(B4 + t, s, q)
        send_sums(B4 + t, 1)

    def body_dz2(j, carry):
        s, q = carry
        y = ys[1, column(j), :]
        v = dh[column(j), :] * silu_slope(normed(1, y))
        dh[column(j), :] = v
        esend[11, 0, j] = v[0:1]
        esend[11, 1, j] = v[H - 1 : H]
        return s + fold(v), q + fold(v * hat(1, y))

    s, q = over_columns(body_dz2, (zero8, zero8))
    put_sums(nt + 1, s, q)
    send_sums(nt + 1, 1)
    send_edges(11)

    dy4 = [field.at[1, :, t * C : (t + 1) * C] for t in range(T)]
    dy2 = field.at[1, :, T * C : (T + 1) * C]
    mid = km
    for t in range(T):
        k = 3 + 3 * t
        get_sums(B4 + t, 1)
        back_rows(k, B4 + t)

        def body_dy4(j, carry):
            dy4[t][column(j), :] = grad_pre(k, ys[k + 1, column(j), :], ys[k, column(j), :]).astype(half)
            return carry

        over_columns(body_dy4)
        dz[t] = dot_nt(dy4[t][...], km[t])

        def body_dz3(j, carry):
            s, q = carry
            y = ys[k - 1, column(j), :]
            v = dz[t, column(j), :] * silu_slope(normed(k - 1, y))
            dz[t, column(j), :] = v
            return s + fold(v), q + fold(v * hat(k - 1, y))

        s, q = over_columns(body_dz3, (zero8, zero8))
        put_sums(B3 + t, s, q)
    send_sums(B3, T)

    get_sums(nt + 1, 1)
    get_edges(11)
    back_rows(1, nt + 1)

    def body_dy2(j, carry):
        v = grad_pre(1, dh[column(j), :], ys[1, column(j), :])
        side = grad_pre(1, pair(11, j), pair(1, j))
        dy2[column(j), :] = v.astype(half)
        dy2e[0, j] = side[0:1]
        dy2e[1, j] = side[1:2]
        build(j, v, side[0:1], side[1:2], up, down)
        return carry

    over_columns(body_dy2)
    post(20, dy2, xd5, TEAM - 1)
    post(24, dy2e, xd5e, TEAM - 1)


    dh[...] = conv_t(kc.at[1])

    get_sums(B3, T)
    for t in range(T):
        k = 2 + 3 * t
        back_rows(k, B3 + t)

        def body_dy3(j, carry):
            dy3[t, column(j), :] = grad_pre(k, dz[t, column(j), :], ys[k, column(j), :]).astype(half)
            return carry

        over_columns(body_dy3)
        post(28 + t, dy3.at[t], xd3, t)
        dh[...] += dot_nt(dy3[t], ki[t, 0:C, :])
        res[:, (t + 1) * C : (t + 2) * C] = dot_nt(dy3[t], ki[t, C : 2 * C, :]).astype(half)

    @pl.when(p == 0)
    def _():
        stage_result(1)

    def body_dz1(j, carry):
        s, q = carry
        y = ys[0, column(j), :]
        v = dh[column(j), :] * silu_slope(normed(0, y))
        dh[column(j), :] = v
        esend[12, 0, j] = v[0:1]
        esend[12, 1, j] = v[H - 1 : H]
        return s + fold(v), q + fold(v * hat(0, y))

    s, q = over_columns(body_dz1, (zero8, zero8))
    put_sums(nt, s, q)
    send_sums(nt, 1)
    send_edges(12)
    for t in range(T):
        mid[t] = dot_tn(t1[t], dy4[t][...]).astype(half)
        post(25 + t, mid.at[t], xd4, t)
    get_sums(nt, 1)
    get_edges(12)
    back_rows(0, nt)

    def bn_moves():
        return [Remote(bn, bnr.at[m], bn_s.at[d], bn_r.at[m], e0 + lax.rem(m + d, M)) for d in range(M)]

    for move in bn_moves():
        move.start()

    quarter = C // TEAM

    def body_dy1(j, carry):
        v = grad_pre(0, dh[column(j), :], ys[0, column(j), :])
        side = grad_pre(0, pair(12, j), pair(0, j))
        low = v.astype(half)
        for o in range(TEAM):
            cols = slice(o * quarter, (o + 1) * quarter)
            dy1[o, column(j), :] = low[:, cols]
            dy1e[o, 0, j] = side[0:1, cols]
            dy1e[o, 1, j] = side[1:2, cols]
        build(j, v, side[0:1], side[1:2], up, down)
        return carry

    over_columns(body_dy1)
    for o in range(TEAM):
        post(31 + o, dy1.at[o], xd1, o)
        post(35 + o, dy1e.at[o], xd1e, o)
    res[:, 0:C] = conv_t(kc.at[0]).astype(half)

    @pl.when(p == 1)
    def _():
        for t in range(1 + T):
            cols = slice(t * C, (t + 1) * C)
            ps[0 : pix // 4, cols] = dot_tn(chosen[...], res[:, cols])[0 : pix // 4].astype(half)
        pool_copy().start()
        pool_copy().wait_send()

    @pl.when(p == 0)
    def _():
        stage_result(0)

    def finish_sends():
        for move in field_moves + rest_moves + sel_moves:
            move.sent()

        @pl.when(tops)
        def _():
            for move in edge_moves[0]:
                move.sent()

        @pl.when(bottoms)
        def _():
            for move in edge_moves[1]:
                move.sent()

        for s in range(EDGES):
            finish_edges(s)
        for slot, n in sums_sent:
            for d in range(1, G):
                stat_copy(slot, n, d).wait_send()

        @pl.when(p == 0)
        def _():
            wait_selection()

    if not direct:

        @pl.when(p == 1)
        def _():
            send_kept()

        start_result(1)
        start_result(0)
        finish_sends()
    if direct:
        z, n = b, R // TEAM
        q4 = quarter
        all_rows = TEAM * pix
        wide = pix + 2 * H
        task = e < T
        vb, va, vc = (kt.at[2, i * all_rows : (i + 1) * all_rows, :] for i in range(3))
        _, d5, d3 = (kc.at[0, i * all_rows : (i + 1) * all_rows, :] for i in range(3))
        pm, p1, pi_, pt = kt.at[0], kc.at[0, :, 0:q4], ki.at[0], ki.at[T - 1, 0:C]
        d1 = kt.at[1, 0:all_rows, 3 * q4 : 4 * q4]
        rows_m, rows_i, rows_t = 9 * C // R, 2 * C // R, C // R

        def band(ref, j):
            return ref.at[j * pix : (j + 1) * pix]

        def fetch(index, src, j, dst, sem):
            arrived(src.at[j], sem)
            copy = pltpu.make_async_copy(src.at[j], dst, l_sem.at[index, j])
            copy.start()
            return copy

        def rows_shifted(j, a, lo):
            if j < TEAM - 1:
                start = (3 * j + a) * wide + lo
                return kc.at[1, start : start + pix, :]
            return rb.at[a, lo : lo + pix, :]

        for j in range(TEAM - 1):
            for a in range(3):
                start = (3 * j + a) * wide
                kc[1, start : start + H, :] = zero_col
                kc[1, start + H + pix : start + wide, :] = zero_col
        got = {}
        for j in range(TEAM):
            got["d5", j] = fetch(0, xd5, j, band(d5, j), x_r.at[17 + e, j])
            got["d5e", j] = fetch(1, xd5e, j, d5e.at[j], x_r.at[21 + e, j])

        @pl.when(task)
        def _():
            for j in range(TEAM):
                fetch(3, xp, j, band(vb, j), x_r.at[14 + e, j])

        @pl.when(jnp.logical_not(task))
        def _():
            for j in range(TEAM):
                fetch(3, xh, j, band(vb, j), x_r.at[4, j])

        for j in range(TEAM):
            got["d5", j].wait()
            got["d5e", j].wait()

            def body_r(i, carry):
                v = kc[0, pl.ds(pl.multiple_of(all_rows + j * pix + i * H, H), H), :].astype(f32)
                three = (
                    (jnp.where(at_top, d5e[j, 0, i], pltpu.roll(v, 1, 0)) * msks[j, 0]).astype(half),
                    v.astype(half),
                    (jnp.where(at_bottom, d5e[j, 1, i], pltpu.roll(v, H - 1, 0)) * msks[j, 1]).astype(half),
                )
                for a in range(3):
                    if j < TEAM - 1:
                        here = pl.ds(pl.multiple_of((3 * j + a) * wide + H + i * H, H), H)
                        kc[1, here, :] = three[a]
                    else:
                        rb[a, pl.ds(pl.multiple_of(H + i * H, H), H), :] = three[a]
                return carry

            over_columns(body_r)
        for j in range(TEAM):
            pltpu.make_async_copy(xp.at[j], band(vb, j), l_sem.at[3, j]).wait()

        for tap in range(9):
            a, c = 2 - tap // 3, 2 - tap % 3
            acc = None
            for j in range(TEAM):
                term = dot_tn(band(vb, j)[...], rows_shifted(j, a, H * c)[...])
                acc = term if acc is None else acc + term
            pm[tap * C : (tap + 1) * C, :] = acc.astype(half)

        partial = (pm, pi_, pt, p1)
        share = (rows_m, rows_i, rows_t, rows_m)
        pieces = (TEAM, 1, 1, 1)
        width = (C, C, C, q4)

        def flow(g, zd, s, way):
            rows = TEAM * share[g] // pieces[g]
            return pltpu.make_async_remote_copy(
                src_ref=partial[g].at[pl.ds(pl.multiple_of((zd * pieces[g] + s) * rows, 16), rows)],
                dst_ref=flows_in[g].at[way, zd, pl.ds(pl.multiple_of(s * rows, 16), rows)],
                send_sem=fl_s.at[way, g, zd, s],
                recv_sem=fl_r.at[way, g, zd, s],
                device_id=(p, r + TEAM * (1 - 2 * way)),
                device_id_type=MESH,
            )

        def incoming(g, zd, s, way, lane):
            rows = TEAM * share[g] // pieces[g]
            src = flows_in[g].at[way, zd, pl.ds(pl.multiple_of(s * rows, 16), rows)]
            dst = kc.at[1, lane * TEAM * rows_m : lane * TEAM * rows_m + rows, 0 : width[g]]
            return src, dst, fl_r.at[way, g, zd, s], fl_l.at[lane]

        def take(g, zd, s, way, lane):
            src, dst, sem, local = incoming(g, zd, s, way, lane)
            arrived(src, sem)
            pltpu.make_async_copy(src, dst, local).start()

        def taken(g, zd, s, way, lane):
            src, dst, sem, local = incoming(g, zd, s, way, lane)
            pltpu.make_async_copy(src, dst, local).wait()
            return dst[...].astype(f32)

        def flow_start(g):
            @pl.when(z == 0)
            def _():
                for zd in range(n - 1, 0, -1):
                    for s in range(pieces[g]):
                        flow(g, zd, s, 0).start()

            @pl.when(z == n - 1)
            def _():
                for zd in range(n - 1):
                    for s in range(pieces[g]):
                        flow(g, zd, s, 1).start()

        def flow_mid(groups):
            upper = (2 * z) // n

            @pl.when(jnp.logical_and(z > 0, z < n - 1))
            def _():
                for phase in range(2):
                    way = lax.rem(phase + upper, 2)
                    for g in groups:
                        rows = TEAM * share[g] // pieces[g]

                        def body_flow(i, carry):
                            k, s = i // pieces[g], i % pieces[g]
                            zd = (1 - way) * (n - 1 - k) + way * k

                            @pl.when((1 - 2 * way) * (zd - z) > 0)
                            def _():
                                take(g, zd, s, way, 0)
                                here = partial[g].at[pl.ds(pl.multiple_of((zd * pieces[g] + s) * rows, 16), rows)]
                                here[...] = (here[...].astype(f32) + taken(g, zd, s, way, 0)).astype(half)
                                flow(g, zd, s, way).start()

                            return carry

                        lax.fori_loop(0, (n - 1) * pieces[g], body_flow, 0)

        def share_moves(g):
            moves = []
            for d in range(TEAM):
                q = lax.rem(e + d, TEAM)
                start = pl.multiple_of((z * TEAM + q) * share[g], 16)
                moves.append(
                    Remote(partial[g].at[pl.ds(start, share[g])], ends[g].at[e], sh_s.at[g, d], sh_r.at[g, e], e0 + q)
                )
            return moves

        def flow_final(g):
            rows = TEAM * share[g] // pieces[g]
            for s in range(pieces[g]):

                @pl.when(z > 0)
                def _():
                    take(g, z, s, 0, 0)

                @pl.when(z < n - 1)
                def _():
                    take(g, z, s, 1, 1)

                here = partial[g].at[pl.ds(pl.multiple_of(z * TEAM * share[g] + s * rows, 16), rows)]

                @pl.when(jnp.logical_and(z > 0, z < n - 1))
                def _():
                    here[...] = (here[...].astype(f32) + taken(g, z, s, 0, 0) + taken(g, z, s, 1, 1)).astype(half)

                @pl.when(z == 0)
                def _():
                    here[...] = (here[...].astype(f32) + taken(g, z, s, 1, 1)).astype(half)

                @pl.when(z == n - 1)
                def _():
                    here[...] = (here[...].astype(f32) + taken(g, z, s, 0, 0)).astype(half)

            for move in share_moves(g):
                move.start()

        def flow_sent(g):
            for way in range(2):
                for zd in range(n):
                    on = z < zd if way == 0 else z > zd

                    @pl.when(on)
                    def _():
                        for s in range(pieces[g]):
                            flow(g, zd, s, way).wait_send()

            for move in share_moves(g):
                move.sent()

        flow_start(0)

        @pl.when(p == 1)
        def _():
            send_kept()

        finish_sends()
        flow_mid((0,))

        first_u = []
        for j in range(TEAM):
            first_u.append(fetch(4, xu, j, band(vb, j), x_r.at[0, j]))

        @pl.when(task)
        def _():
            copies = []
            for j in range(TEAM):
                copies.append(fetch(2, xh, j, band(va, j), x_r.at[4, j]))
                copies.append(fetch(5, xv, j, band(vc, j), x_r.at[8 + e, j]))
                copies.append(fetch(6, xd4, j, kc.at[0, j * C : (j + 1) * C, :], x_r.at[25 + e, j]))
                copies.append(fetch(8, xd3, j, band(d3, j), x_r.at[28 + e, j]))
            for copy in copies:
                copy.wait()
            pi_[0:C, :] = dot_tn(va[...], d3[...]).astype(half)
            pi_[C : 2 * C, :] = dot_tn(vc[...], d3[...]).astype(half)
            acc = kc[0, 0:C, :].astype(f32)
            for j in range(1, TEAM):
                acc = acc + kc[0, j * C : (j + 1) * C, :].astype(f32)
            pt[...] = acc.astype(half)
            flow_start(1)
            flow_start(2)

        for j in range(TEAM):
            got["d1", j] = fetch(9, xd1, j, band(d1, j), x_r.at[31, j])
            got["d1e", j] = fetch(10, xd1e, j, d1e.at[j], x_r.at[35, j])
        row_of1 = lax.broadcasted_iota(jnp.int32, (H, q4), 0)

        def near(j, a, lo, size, cols):
            start = (3 * j + a) * pix + lo
            return kt.at[1, start : start + size, cols * q4 : (cols + 1) * q4]

        for j in range(TEAM):
            got["d1", j].wait()
            got["d1e", j].wait()

        for j in range(TEAM):

            def body_r1(i, carry):
                v = kt[1, pl.ds(pl.multiple_of(j * pix + i * H, H), H), 3 * q4 : 4 * q4].astype(f32)
                three = (
                    (jnp.where(row_of1 == 0, d1e[j, 0, i], pltpu.roll(v, 1, 0)) * msks[j, 0][:, 0:q4]).astype(half),
                    v.astype(half),
                    (jnp.where(row_of1 == H - 1, d1e[j, 1, i], pltpu.roll(v, H - 1, 0)) * msks[j, 1][:, 0:q4]).astype(
                        half
                    ),
                )
                for a in range(3):
                    kt[1, pl.ds(pl.multiple_of((3 * j + a) * pix + i * H, H), H), q4 : 2 * q4] = three[a]
                return carry

            over_columns(body_r1)
            for a in range(3):
                near(j, a, 0, H, 0)[...] = jnp.zeros((H, q4), half)
                near(j, a, H, pix - H, 0)[...] = near(j, a, 0, pix - H, 1)[...]
                near(j, a, 0, pix - H, 2)[...] = near(j, a, H, pix - H, 1)[...]
                near(j, a, pix - H, H, 2)[...] = jnp.zeros((H, q4), half)
        for copy in first_u:
            copy.wait()
        for a in range(3):
            acc = None
            for j in range(TEAM):
                start = (3 * j + 2 - a) * pix
                term = dot_tn(band(vb, j)[...], kt[1, start : start + pix, 0 : 3 * q4])
                acc = term if acc is None else acc + term
            for c in range(3):
                kc[0, (3 * a + c) * C : (3 * a + c + 1) * C, 0:q4] = acc[:, (2 - c) * q4 : (3 - c) * q4].astype(half)
        flow_start(3)

        flow_final(0)
        start_result(1)
        start_result(0)

        @pl.when(task)
        def _():
            flow_mid((1, 2, 3))

        @pl.when(jnp.logical_not(task))
        def _():
            flow_mid((3,))

        @pl.when(task)
        def _():
            flow_final(1)
            flow_final(2)

        flow_final(3)

        stores = []

        def store(start, rows, dst, i):
            copy = pltpu.make_async_copy(lin.at[start : start + rows], dst, o_sem.at[i])
            copy.start()
            stores.append(copy)
            return copy

        lanes = C // 128
        lin_m, lin_i, lin_t = rows_m * lanes, rows_i * lanes, rows_t * lanes
        pair_at = 2 * lin_m

        def flatten(value, start, rows, lane, step=1):
            for k in range(value.shape[1] // 128):
                lin[pl.ds(start + step * (lane + k), rows, stride=step * lanes), :] = value[:, 128 * k : 128 * (k + 1)]

        def last_of(g, members, buffer, base):
            copies = []
            for q in range(members):
                arrived(ends[g].at[q], sh_r.at[g, q])
                copy = pltpu.make_async_copy(
                    ends[g].at[q], buffer.at[q * share[g] : (q + 1) * share[g]], l_sem.at[base, q]
                )
                copy.start()
                copies.append(copy)
            for copy in copies:
                copy.wait()

        def piece(buffer, g, q):
            return buffer[q * share[g] : (q + 1) * share[g], :].astype(f32)

        final_m, final_1 = kc.at[1, 2 * TEAM * rows_m : 3 * TEAM * rows_m, :], kt.at[2, :, 0:q4]
        last_of(0, TEAM, final_m, 11)
        for q in range(T):
            if q >= 2:
                stores[q - 2].wait()
            flatten(piece(final_m, 0, q), q % 2 * lin_m, rows_m, 0)
            store(q % 2 * lin_m, lin_m, gm.at[q * lin_m : (q + 1) * lin_m], q)
        flatten(piece(final_m, 0, T), pair_at + 1, rows_m, 0, 2)
        for copy in stores[max(0, T - 2) :]:
            copy.wait()
        del stores[:]
        last_of(1, T, ki.at[1], 12)
        for q in range(T):
            flatten(piece(ki.at[1], 1, q), q * lin_i, rows_i, 0)
        store(0, T * lin_i, gi, T)
        last_of(2, T, ki.at[T - 1, C : 2 * C], 13)
        for q in range(T):
            flatten(piece(ki.at[T - 1, C : 2 * C], 2, q), T * lin_i + q * lin_t, rows_t, 0)
        store(T * lin_i, T * lin_t, gt, T + 1)
        last_of(3, TEAM, final_1, 14)
        for q in range(TEAM):
            flatten(piece(final_1, 3, q), pair_at, rows_m, q * q4 // 128, 2)
        store(pair_at, 2 * lin_m, g1, T + 2)
        flow_sent(0)

        @pl.when(task)
        def _():
            flow_sent(1)
            flow_sent(2)

        flow_sent(3)
        for copy in stores:
            copy.wait()

    for k in range(M):
        arrived(bnr.at[k], bn_r.at[k])
    acc = bnr[0]
    for k in range(1, M):
        acc = acc + bnr[k]
    bng[...] = acc
    for k in range(M):
        arrived(out.at[k, :, 0:C], out_r.at[0, k])
        arrived(out.at[k, :, C:CW], out_r.at[1, k])
    for move in out_moves(0) + out_moves(1) + bn_moves():
        move.sent()
    for move in x_moves:
        move.sent()
    if direct:
        return
    for j in range(TEAM):
        for index, dst in ((0, xu), (4, xh), (31, xd1), (35, xd1e)):
            arrived(dst.at[j], x_r.at[index, j])
    for t in range(T):

        @pl.when(e == t)
        def _():
            for j in range(TEAM):
                for index, dst in ((8, xv), (14, xp), (17, xd5), (21, xd5e), (25, xd4), (28, xd3)):
                    arrived(dst.at[j], x_r.at[index + t, j])

    @pl.when(e == TEAM - 1)
    def _():
        for j in range(TEAM):
            arrived(xd5.at[j], x_r.at[20, j])
            arrived(xd5e.at[j], x_r.at[24, j])


def tables(M, G, H, W):
    pix = H * W
    cm = np.zeros((pix, pix), np.float32)
    spread = np.zeros((pix, 128), np.float32)
    pool = np.zeros((128, pix), np.float32)
    edge = np.zeros((64, 128), np.float32)
    wide = W // 2
    own = pix // 4
    for i in range(H):
        for j in range(W):
            q = j * H + i
            cm[q, i * W + j] = 1
            w = (i // 2) * wide + j // 2
            spread[q, w] = 1
            pool[w, q] = 0.25
            if i >= H - 2:
                pool[own + j // 2, q] = 0.25
            if i < 2:
                pool[own + 16 + j // 2, q] = 0.25
    for j in range(W):
        edge[32 - W + j, own + j // 2] = 1
        edge[32 + j, own + 16 + j // 2] = 1
    return [jnp.asarray(v, half) for v in (cm, cm.T, spread, edge, pool)]


def gradient_kernel(cfg, *refs):
    M, G, H, W, C, T, n = cfg["M"], cfg["G"], cfg["H"], cfg["W"], cfg["C"], cfg["T"], cfg["n"]
    R = M * G
    pix = H * W
    q4 = C // TEAM
    (msk, xu, xh, xp, xv, xd5, xd5e, xd4, xd3, xd1, xd1e) = refs[:11]
    (gm, g1, gi, gt) = refs[11:15]
    (va, vb, vc, d5, d5e, rb, r1, d1, d1e, d3, d4, pm, p1, pi_, pt, am, a1, ai, at, in_sem, s_sem, r_sem) = refs[15:]
    p = lax.axis_index("pipe")
    r = lax.axis_index("rows")
    e = r % TEAM
    z = r // TEAM
    task = e < T

    loads = {}

    def load(name, src, dst, i):
        loads[name] = pltpu.make_async_copy(src, dst, in_sem.at[i])
        loads[name].start()

    load("d5", xd5, d5, 0)
    load("d5e", xd5e, d5e, 1)
    load("h", xh, va, 2)

    @pl.when(task)
    def _():
        pltpu.make_async_copy(xp, vb, in_sem.at[3]).start()
        pltpu.make_async_copy(xv, vc, in_sem.at[4]).start()
        pltpu.make_async_copy(xd3, d3, in_sem.at[6]).start()
        pltpu.make_async_copy(xd4, d4, in_sem.at[7]).start()

    bar = pltpu.get_barrier_semaphore()

    def greet(i, _):
        pl.semaphore_signal(bar, inc=1, device_id=(p, lax.rem(r + TEAM * i, R)), device_id_type=MESH)
        return 0

    lax.fori_loop(1, n, greet, 0)

    row_of = lax.broadcasted_iota(jnp.int32, (H, C), 0)
    row_of1 = lax.broadcasted_iota(jnp.int32, (H, q4), 0)

    def column(j):
        return pl.ds(pl.multiple_of(j * H, H), H)

    for j in range(TEAM):
        for a in range(3):
            rb[j, a, 0:H, :] = jnp.zeros((H, C), half)
            rb[j, a, H * (W + 1) : H * (W + 2), :] = jnp.zeros((H, C), half)
            r1[j, a, 0:H, :] = jnp.zeros((H, 3 * q4), half)
            r1[j, a, H * (W - 1) :, :] = jnp.zeros((H, 3 * q4), half)

    loads["d5"].wait()
    loads["d5e"].wait()
    for j in range(TEAM):

        def body(c, carry):
            for u in range(2):
                i = c * 2 + u
                here = pl.ds(pl.multiple_of(H + i * H, H), H)
                v = d5[j, column(i), :].astype(f32)
                rb[j, 1, here, :] = v.astype(half)
                rb[j, 0, here, :] = (jnp.where(row_of == 0, d5e[j, 0, i], pltpu.roll(v, 1, 0)) * msk[j, 0]).astype(half)
                rb[j, 2, here, :] = (
                    jnp.where(row_of == H - 1, d5e[j, 1, i], pltpu.roll(v, H - 1, 0)) * msk[j, 1]
                ).astype(half)
            return carry

        lax.fori_loop(0, W // 2, body, 0)
    loads["h"].wait()

    @pl.when(task)
    def _():
        pltpu.make_async_copy(xp, vb, in_sem.at[3]).wait()
        pltpu.make_async_copy(xv, vc, in_sem.at[4]).wait()
        pltpu.make_async_copy(xd3, d3, in_sem.at[6]).wait()
        pltpu.make_async_copy(xd4, d4, in_sem.at[7]).wait()

    @pl.when(jnp.logical_not(task))
    def _():
        vb[...] = va[...]

    for tap in range(9):
        a, c = 2 - tap // 3, 2 - tap % 3
        acc = None
        for j in range(TEAM):
            term = dot_tn(vb[j], rb[j, a, H * c : H * c + pix, :])
            acc = term if acc is None else acc + term
        pm[tap * C : (tap + 1) * C, :] = acc.astype(half)

    pltpu.make_async_copy(xu, vb, in_sem.at[8]).start()
    pltpu.make_async_copy(xd1, d1, in_sem.at[9]).start()
    pltpu.make_async_copy(xd1e, d1e, in_sem.at[10]).start()

    def group(index, src, mine, rows):
        moves = []
        for d in range(1, n):
            to = lax.rem(z + d, n)
            moves.append(
                pltpu.make_async_remote_copy(
                    src_ref=src.at[pl.ds(pl.multiple_of(to * rows, 16), rows)],
                    dst_ref=mine.at[z],
                    send_sem=s_sem.at[index, d],
                    recv_sem=r_sem.at[index, z],
                    device_id=(p, TEAM * to + e),
                    device_id_type=MESH,
                )
            )
        return moves

    rows_m, rows_i, rows_t = 9 * C // n, 2 * C // n, C // n
    pl.semaphore_wait(bar, n - 1)
    main = group(0, pm, am, rows_m)
    for move in main:
        move.start()

    @pl.when(task)
    def _():
        for part, value in ((0, va), (1, vc)):
            acc = None
            for j in range(TEAM):
                term = dot_tn(value[j], d3[j])
                acc = term if acc is None else acc + term
            pi_[part * C : (part + 1) * C, :] = acc.astype(half)
        acc = d4[0].astype(f32)
        for j in range(1, TEAM):
            acc = acc + d4[j].astype(f32)
        pt[...] = acc.astype(half)
        for move in group(1, pi_, ai, rows_i) + group(2, pt, at, rows_t):
            move.start()

    pltpu.make_async_copy(xu, vb, in_sem.at[8]).wait()
    pltpu.make_async_copy(xd1, d1, in_sem.at[9]).wait()
    pltpu.make_async_copy(xd1e, d1e, in_sem.at[10]).wait()
    for j in range(TEAM):

        def body1(i, carry):
            v = d1[j, column(i), :].astype(f32)
            three = (
                (jnp.where(row_of1 == 0, d1e[j, 0, i], pltpu.roll(v, 1, 0)) * msk[j, 0][:, 0:q4]).astype(half),
                v.astype(half),
                (jnp.where(row_of1 == H - 1, d1e[j, 1, i], pltpu.roll(v, H - 1, 0)) * msk[j, 1][:, 0:q4]).astype(half),
            )
            for a in range(3):
                r1[j, a, column(i), q4 : 2 * q4] = three[a]
            return carry

        lax.fori_loop(0, W, body1, 0)
        for a in range(3):
            r1[j, a, H : W * H, 0:q4] = r1[j, a, 0 : (W - 1) * H, q4 : 2 * q4]
            r1[j, a, 0 : (W - 1) * H, 2 * q4 : 3 * q4] = r1[j, a, H : W * H, q4 : 2 * q4]
    for a in range(3):
        acc = None
        for j in range(TEAM):
            term = dot_tn(vb[j], r1[j, 2 - a])
            acc = term if acc is None else acc + term
        for c in range(3):
            p1[(3 * a + c) * C : (3 * a + c + 1) * C, :] = acc[:, (2 - c) * q4 : (3 - c) * q4].astype(half)
    one = group(3, p1, a1, rows_m)
    for move in one:
        move.start()

    def reduce(index, src, mine, rows, dst):
        for d in range(1, n):
            s = lax.rem(z + d, n)
            arrived(mine.at[s], r_sem.at[index, s])
        mine[z] = src[pl.ds(pl.multiple_of(z * rows, 16), rows), :]
        acc = mine[0].astype(f32)
        for s in range(1, n):
            acc = acc + mine[s].astype(f32)
        dst[...] = acc.astype(dst.dtype)

    reduce(0, pm, am, rows_m, gm)

    @pl.when(task)
    def _():
        reduce(1, pi_, ai, rows_i, gi)
        reduce(2, pt, at, rows_t, gt)

    @pl.when(jnp.logical_not(task))
    def _():
        gi[...] = jnp.zeros(gi.shape, gi.dtype)
        gt[...] = jnp.zeros(gt.shape, gt.dtype)

    reduce(3, p1, a1, rows_m, g1)
    for move in main + one:
        move.wait_send()

    @pl.when(task)
    def _():
        for move in group(1, pi_, ai, rows_i) + group(2, pt, at, rows_t):
            move.wait_send()


def per_device(cfg, section_in, image_start, pool_choice, conv_shared, task_in, task_mid, task_conv, bn_gain, bn_bias):
    M, G, H, W, C, T, n = cfg["M"], cfg["G"], cfg["H"], cfg["W"], cfg["C"], cfg["T"], cfg["n"]
    R = M * G
    pix = H * W
    part = pix // M
    rows_total = H * G
    norms = 2 + 3 * T
    CW = C * (1 + T)
    p = lax.axis_index("pipe")
    r = lax.axis_index("rows")
    b, m = r // M, r % M
    sec = section_in[0].reshape(M, part, CW)
    hp = pool_choice.shape[1]
    place = jnp.arange(4, dtype=jnp.int32).reshape(2, 1, 2)
    picked = pool_choice[:, :, None, :, None] == place[None, None]
    sel = jnp.broadcast_to(picked.reshape(M, part, 1), (M, part, 128)).astype(half)

    ones = jnp.ones((M, 1), jnp.int32)
    padded = jnp.concatenate([ones, image_start[:, 1:], ones], 1)
    links = 1.0 - lax.dynamic_slice_in_dim(padded, b * H, H + 1, 1).astype(f32)
    both = jnp.stack([links[:, :-1], links[:, 1:]], 1)
    team_masks = jnp.broadcast_to(both[..., None], (M, 2, H, C))

    cm, cm_t, spread, edge, pool = tables(M, G, H, W)
    sds = jax.ShapeDtypeStruct
    exchange = [
        sds((TEAM, pix, C), half),
        sds((TEAM, pix, C), half),
        sds((TEAM, pix, C), half),
        sds((TEAM, pix, C), half),
        sds((TEAM, pix, C), half),
        sds((TEAM, 2, W, 1, C), f32),
        sds((TEAM, C, C), half),
        sds((TEAM, pix, C), half),
        sds((TEAM, pix, C // TEAM), half),
        sds((TEAM, 2, W, 1, C // TEAM), f32),
    ]
    direct = C % (16 * R) == 0
    parts = R if direct else n
    rows_m, rows_i, rows_t = 9 * C // parts, 2 * C // parts, C // parts
    q4 = C // TEAM
    shares, share_scratch = [], []
    dma = pltpu.SemaphoreType.DMA
    if direct:
        shares = [
            sds((T * rows_m * C // 128, 128), f32),
            sds((2 * rows_m * C // 128, 128), f32),
            sds((T * rows_i * C // 128, 128), f32),
            sds((T * rows_t * C // 128, 128), f32),
            sds((2, n, TEAM * rows_m, C), half),
            sds((2, n, TEAM * rows_i, C), half),
            sds((2, n, TEAM * rows_t, C), half),
            sds((2, n, TEAM * rows_m, q4), half),
            sds((TEAM, rows_m, C), half),
            sds((T, rows_i, C), half),
            sds((T, rows_t, C), half),
            sds((TEAM, rows_m, q4), half),
        ]
        share_scratch = [
            pltpu.VMEM((4 * rows_m * C // 128, 128), f32),
            pltpu.VMEM((TEAM, 2, W, 1, C), f32),
            pltpu.VMEM((TEAM, 2, W, 1, q4), f32),
            dma((15, TEAM)),
            dma((2, 4, n, TEAM)),
            dma((2, 4, n, TEAM)),
            dma((2,)),
            dma((4, TEAM)),
            dma((4, TEAM)),
            dma((TEAM + 3,)),
        ]
    vm = pltpu.VMEM
    win = pix // 4 + 32
    outs = pl.pallas_call(
        functools.partial(section_kernel, dict(cfg, direct=direct)),
        name="sections",
        out_shape=[sds((M, part, CW), half), sds((2 * norms, C), f32)] + exchange + shares,
        in_specs=[ANY, ANY] + [VMEM] * 8 + [ANY] * 4,
        out_specs=[ANY, VMEM] + [ANY] * (len(exchange) + len(shares)),
        scratch_shapes=[
            vm((2, 9 * C, C), half),
            vm((T, 2 * C, C), half),
            vm((T, C, C), half),
            vm((T, 9 * C, C), half),
            vm((pix, CW), half),
            vm((2, pix, CW), half),
            vm((pix, 128), half),
            vm((pix, 128), half),
            vm((2, 32, C), half),
            vm((2, 32, 128), half),
            vm((2, W, 1, C), f32),
            vm((win, CW), half),
            vm((win, CW), half),
            vm((3, pix + 2 * H, C), half),
            vm((norms, pix, C), f32),
            vm((EDGES, 2, W, 1, C), f32),
            vm((EDGES, 2, W, 1, C), f32),
            vm((2 * norms, 2, C), f32),
            vm((G, 2 * norms, 2, C), f32),
            vm((pix, C), half),
            vm((pix, C), half),
            vm((W, 2, C), f32),
            vm((T, pix, C), half),
            vm((T, pix, C), half),
            vm((pix, CW), half),
            vm((T, pix, C), f32),
            vm((pix, C), f32),
            vm((T, pix, C), half),
            vm((T, 2, W, 1, C), f32),
            vm((2, W, 1, C), f32),
            vm((T, pix, C), half),
            vm((TEAM, pix, C // TEAM), half),
            vm((TEAM, 2, W, 1, C // TEAM), f32),
            vm((2 * norms, C), f32),
            vm((M, 2 * norms, C), f32),
            pltpu.SemaphoreType.REGULAR,
            dma((4 + T,)),
            dma((7, M)),
            dma((5, M)),
            dma((EDGES, 2)),
            dma((EDGES, 2)),
            dma((2 * norms, G)),
            dma((2 * norms, G)),
            dma((3,)),
            dma((3,)),
            dma((2, M)),
            dma((2, M)),
            dma((M,)),
            dma((M,)),
            dma((39,)),
            dma((39, TEAM)),
        ]
        + share_scratch,
        compiler_params=pltpu.CompilerParams(
            collective_id=0, has_side_effects=True, vmem_limit_bytes=63 * 2**20
        ),
    )(sec, sel, team_masks, cm, cm_t, spread, edge, pool, bn_gain[0], bn_bias[0], conv_shared[0], task_in[0], task_mid[0], task_conv[0])
    result, bn_grads = outs[:2]

    result = result.reshape(1, M, part // W, W, CW)
    if direct:
        gm, g1, gi, gt = outs[-12:-8]
        return (
            result,
            g1.reshape(-1, 2, 128).transpose(1, 0, 2).reshape(1, 2, -1),
            gi.reshape(1, T, -1),
            gt.reshape(1, T, -1),
            gm.reshape(1, T, -1),
            bn_grads[None, :norms],
            bn_grads[None, norms:],
        )
    shapes = [sds((rows_m, C), half), sds((rows_m, q4), half), sds((rows_i, C), half), sds((rows_t, C), half)]
    slots = [(n, rows_m, C), (n, rows_m, q4), (n, rows_i, C), (n, rows_t, C)]
    grads = pl.pallas_call(
        functools.partial(gradient_kernel, cfg),
        name="kernel_gradients",
        out_shape=shapes,
        in_specs=[VMEM] + [ANY] * 10,
        out_specs=[VMEM] * 4,
        scratch_shapes=[
            vm((TEAM, pix, C), half),
            vm((TEAM, pix, C), half),
            vm((TEAM, pix, C), half),
            vm((TEAM, pix, C), half),
            vm((TEAM, 2, W, 1, C), f32),
            vm((TEAM, 3, pix + 2 * H, C), half),
            vm((TEAM, 3, pix, 3 * q4), half),
            vm((TEAM, pix, q4), half),
            vm((TEAM, 2, W, 1, q4), f32),
            vm((TEAM, pix, C), half),
            vm((TEAM, C, C), half),
            vm((9 * C, C), half),
            vm((9 * C, q4), half),
            vm((2 * C, C), half),
            vm((C, C), half),
            vm(slots[0], half),
            vm(slots[1], half),
            vm(slots[2], half),
            vm(slots[3], half),
            dma((11,)),
            dma((4, R)),
            dma((4, R)),
        ],
        compiler_params=pltpu.CompilerParams(
            collective_id=1, has_side_effects=True, vmem_limit_bytes=60 * 2**20
        ),
    )(team_masks, *outs[2:])

    gm, g1, gi, gt = grads
    pieces = [
        gm.reshape(TEAM, -1),
        g1.reshape(TEAM, -1),
        gi.reshape(TEAM, -1),
        gt.reshape(TEAM, -1),
    ]
    packed = jnp.concatenate(pieces, 1)
    teams = [[TEAM * i + j for j in range(TEAM)] for i in range(R // TEAM)]
    swapped = lax.all_to_all(packed, "rows", 0, 0, axis_index_groups=teams, tiled=False).astype(f32)
    sizes = [v.shape[1] for v in pieces]
    o = [0, sizes[0], sizes[0] + sizes[1], sizes[0] + sizes[1] + sizes[2], sum(sizes)]
    mains = swapped[:, o[0] : o[1]]
    firsts = swapped[:, o[1] : o[2]].reshape(TEAM, -1, q4).transpose(1, 0, 2).reshape(-1)
    conv_grad = jnp.stack([firsts, mains[T]])
    return (
        result,
        conv_grad[None],
        swapped[:T, o[2] : o[3]][None],
        swapped[:T, o[3] : o[4]][None],
        mains[:T][None],
        bn_grads[None, :norms],
        bn_grads[None, norms:],
    )


def solution(mesh):
    in_specs = (
        P("pipe", None, "rows", None, None),
        P(),
        P(None, "rows", None),
        P("pipe", None, None, None),
        P("pipe", None, None, None),
        P("pipe", None, None, None),
        P("pipe", None, None, None),
        P("pipe", None, None),
        P("pipe", None, None),
    )
    out_specs = (
        P("pipe", None, "rows", None, None),
        P("pipe", None, "rows"),
        P("pipe", None, "rows"),
        P("pipe", None, "rows"),
        P("pipe", None, "rows"),
        P("pipe", None, None),
        P("pipe", None, None),
    )
    bands = mesh.shape["rows"]

    def step(section_in, image_start, pool_choice, conv_shared, task_in, task_mid, task_conv, bn_gain, bn_bias):
        M = section_in.shape[1]
        G = bands // M
        cfg = dict(
            M=M,
            G=G,
            H=section_in.shape[2] // G,
            W=section_in.shape[3],
            C=conv_shared.shape[3],
            T=task_in.shape[1],
            n=bands // TEAM,
            to_all=frozenset(range(0, 8)) | frozenset(range(31, 39)),
        )
        return jax.shard_map(
            functools.partial(per_device, cfg), mesh=mesh, in_specs=in_specs, out_specs=out_specs, check_vma=False
        )(section_in, image_start, pool_choice, conv_shared, task_in, task_mid, task_conv, bn_gain, bn_bias)

    return step
```

```python
import functools

import jax
import jax.numpy as jnp
import numpy as np
from jax import lax
from jax.experimental import pallas as pl
from jax.experimental.pallas import tpu as pltpu
from jax.sharding import PartitionSpec as P

MESH = pl.DeviceIdType.MESH
half = jnp.bfloat16
f32 = jnp.float32
epsilon = 1e-05
TEAM = 4

ANY = pl.BlockSpec(memory_space=pl.ANY)
VMEM = pl.BlockSpec(memory_space=pltpu.VMEM)


def sigmoid(x):
    return 0.5 * jnp.tanh(0.5 * x) + 0.5


def dot(a, b):
    return jnp.dot(a, b, preferred_element_type=f32)


def dot_nt(a, b):
    return lax.dot_general(a, b, (((1,), (1,)), ((), ())), preferred_element_type=f32)


def dot_tn(a, b):
    return lax.dot_general(a, b, (((0,), (0,)), ((), ())), preferred_element_type=f32)


class Remote:
    def __init__(self, src, dst, send, recv, to):
        self.src, self.dst, self.send, self.recv, self.to = src, dst, send, recv, to
        self.local = to == lax.axis_index("rows")

    def remote(self):
        return pltpu.make_async_remote_copy(
            src_ref=self.src,
            dst_ref=self.dst,
            send_sem=self.send,
            recv_sem=self.recv,
            device_id=(lax.axis_index("pipe"), self.to),
            device_id_type=MESH,
        )

    def start(self):
        @pl.when(self.local)
        def _():
            pltpu.make_async_copy(self.src, self.dst, self.recv).start()

        @pl.when(jnp.logical_not(self.local))
        def _():
            self.remote().start()

    def sent(self):
        @pl.when(jnp.logical_not(self.local))
        def _():
            self.remote().wait_send()


def arrived(dst, sem):
    pltpu.make_async_copy(dst, dst, sem).wait()


EDGES = 13


def section_kernel(cfg, *refs):
    M, G, H, W, C, T = cfg["M"], cfg["G"], cfg["H"], cfg["W"], cfg["C"], cfg["T"]
    R = M * G
    pix = H * W
    part = pix // M
    count = float(pix * G)
    norms = 2 + 3 * T
    direct = cfg["direct"]
    (sec, sel, msks, perm, perm_t, spread, spread_edge, pool, gain, bias, wc, wi, wm, wt) = refs[:14]
    (out, bng, bnb, xu, xh, xp, xv, xd5, xd5e, xd4, xd3, xd1, xd1e) = refs[14:27]
    refs = refs[27:]
    if direct:
        (gm, g1, gi, gt) = refs[:4]
        flows_in = refs[4:8]
        ends = refs[8:12]
        (lin, d5e, d1e, l_sem, fl_s, fl_r, fl_l, sh_s, sh_r, o_sem) = refs[-10:]
        refs = refs[12:-10]
    (
        kc, ki, km, kt, rin, field, selin, chosen, uh, selh, uedge, px, ps, rb, ys, esend, erecv, ssend, srecv,
        h1, h2, h2e, t1, pr, res, dz, dh, dy5, dy5e, dy2e, dy3, dy1, dy1e, bn, bnr,
        go, w_sem, in_s, in_r, ed_s, ed_r, st_s, st_r, pp_s, pp_r, out_s, out_r, bn_s, bn_r, x_s, x_r,
    ) = refs
    p = lax.axis_index("pipe")
    r = lax.axis_index("rows")
    b, m = r // M, r % M
    e, e0 = m, r - m
    first, last = b == 0, b == G - 1
    CW = C * (1 + T)

    px[pix // 4 :, :] = jnp.zeros((px.shape[0] - pix // 4, CW), half)

    bar = pltpu.get_barrier_semaphore()

    def hello(side, row):
        pl.semaphore_signal(bar, inc=1, device_id=(side, row), device_id_type=MESH)

    for d in range(1, M):
        hello(p, e0 + lax.rem(m + d, M))
    for d in range(1, G):
        hello(p, M * lax.rem(b + d, G) + m)
    hello(1 - p, r)
    tops = jnp.logical_and(m == M - 1, jnp.logical_not(last))
    bottoms = jnp.logical_and(m == 0, jnp.logical_not(first))

    @pl.when(jnp.logical_not(first))
    def _():
        hello(1 - p, r - M)
        hello(p, e0 - 1)

    @pl.when(jnp.logical_not(last))
    def _():
        hello(1 - p, r + M)
        hello(p, e0 + M)

    @pl.when(tops)
    def _():
        for j in range(M):
            hello(p, e0 + M + j)

    @pl.when(bottoms)
    def _():
        for j in range(M):
            hello(p, e0 - M + j)

    loads = {}

    def load(name, src, dst, i):
        loads[name] = pltpu.make_async_copy(src, dst, w_sem.at[i])
        loads[name].start()

    load("c0", wc.at[0], kc.at[0], 0)
    load("i", wi, ki, 1)
    load("c1", wc.at[1], kc.at[1], 2)
    load("m", wm, km, 3)
    for t in range(T):
        load("t%d" % t, wt.at[t], kt.at[t], 4 + t)

    zero_col = jnp.zeros((H, C), half)
    for a in range(3):
        rb[a, 0:H, :] = zero_col
        rb[a, H * (W + 1) : H * (W + 2), :] = zero_col

    @pl.when(first)
    def _():
        for s in range(EDGES):
            erecv[s, 0] = jnp.zeros((W, 1, C), f32)
        uh[0] = jnp.zeros((32, C), half)
        selh[0] = jnp.zeros((32, 128), half)

    @pl.when(last)
    def _():
        for s in range(EDGES):
            erecv[s, 1] = jnp.zeros((W, 1, C), f32)
        uh[1] = jnp.zeros((32, C), half)
        selh[1] = jnp.zeros((32, 128), half)

    below_me, above_me = 1 - (b + 1) // G, (b + G - 1) // G
    top_member, bottom_member = (m + 1) // M, 1 - (m + M - 1) // M
    pl.semaphore_wait(
        bar, M + G - 1 + 2 * (below_me + above_me) + M * (top_member * below_me + bottom_member * above_me)
    )

    mine = pl.ds(pl.multiple_of(part * m, 16), part)
    field_moves, rest_moves, sel_moves, edge_moves = [], [], [], ([], [])
    for d in range(M):
        j = lax.rem(m + d, M)
        to = e0 + j
        field_moves.append(Remote(sec.at[j, :, 0:C], rin.at[mine, 0:C], in_s.at[0, d], in_r.at[0, m], to))
        sel_moves.append(Remote(sel.at[j], selin.at[mine], in_s.at[2, d], in_r.at[2, m], to))
        rest_moves.append(Remote(sec.at[j, :, C:CW], rin.at[mine, C:CW], in_s.at[1, d], in_r.at[1, m], to))
    for j in range(M):
        to = e0 + j
        edge_moves[0].append(
            Remote(sec.at[j, pl.ds(part - 32, 32), 0:C], uh.at[0], in_s.at[3, j], in_r.at[3, 0], to + M)
        )
        edge_moves[0].append(Remote(sel.at[j, pl.ds(part - 32, 32)], selh.at[0], in_s.at[4, j], in_r.at[3, 1], to + M))
        edge_moves[1].append(Remote(sec.at[j, pl.ds(0, 32), 0:C], uh.at[1], in_s.at[5, j], in_r.at[4, 0], to - M))
        edge_moves[1].append(Remote(sel.at[j, pl.ds(0, 32)], selh.at[1], in_s.at[6, j], in_r.at[4, 1], to - M))

    def start_field():
        for move in field_moves:
            move.start()
        for move in rest_moves:
            move.start()

    @pl.when(tops)
    def _():
        for move in edge_moves[0]:
            move.start()

    @pl.when(bottoms)
    def _():
        for move in edge_moves[1]:
            move.start()

    @pl.when(p == 0)
    def _():
        start_field()

    for move in sel_moves:
        move.start()

    row_of = lax.broadcasted_iota(jnp.int32, (H, C), 0)
    at_top, at_bottom = row_of == 0, row_of == H - 1

    def column(j):
        return pl.ds(pl.multiple_of(j * H, H), H)

    def over_columns(body, start=0, step=2):
        def several(c, carry):
            for u in range(step):
                carry = body(c * step + u, carry)
            return carry

        return lax.fori_loop(0, W // step, several, start)

    def build(j, value, above, below, up, down):
        here = pl.ds(pl.multiple_of(H + j * H, H), H)
        rb[1, here, :] = value.astype(half)
        rb[0, here, :] = (jnp.where(at_top, above, pltpu.roll(value, 1, 0)) * up).astype(half)
        rb[2, here, :] = (jnp.where(at_bottom, below, pltpu.roll(value, H - 1, 0)) * down).astype(half)

    def conv(kernel):
        total = None
        for tap in range(9):
            a, c = tap // 3, tap % 3
            term = dot(rb[a, H * c : H * c + pix, :], kernel[tap * C : (tap + 1) * C, :])
            total = term if total is None else total + term
        return total

    def conv_t(kernel):
        total = None
        for tap in range(9):
            a, c = tap // 3, tap % 3
            term = dot_nt(rb[a, H * c : H * c + pix, :], kernel[(8 - tap) * C : (9 - tap) * C, :])
            total = term if total is None else total + term
        return total

    def folded(total):
        return jnp.sum(total, 0, keepdims=True)

    def fold(x):
        return jnp.sum(x.reshape(H // 8, 8, C), 0)

    zero8 = jnp.zeros((8, C), f32)

    def edge_copy(slot, side):
        to = r - M if side == 0 else r + M
        return pltpu.make_async_remote_copy(
            src_ref=esend.at[slot, side],
            dst_ref=erecv.at[slot, 1 - side],
            send_sem=ed_s.at[slot, side],
            recv_sem=ed_r.at[slot, 1 - side],
            device_id=(p, to),
            device_id_type=MESH,
        )

    def send_edges(slot):
        @pl.when(jnp.logical_not(first))
        def _():
            edge_copy(slot, 0).start()

        @pl.when(jnp.logical_not(last))
        def _():
            edge_copy(slot, 1).start()

    def get_edges(slot):
        @pl.when(jnp.logical_not(first))
        def _():
            arrived(erecv.at[slot, 0], ed_r.at[slot, 0])

        @pl.when(jnp.logical_not(last))
        def _():
            arrived(erecv.at[slot, 1], ed_r.at[slot, 1])

    def finish_edges(slot):
        @pl.when(jnp.logical_not(first))
        def _():
            edge_copy(slot, 0).wait_send()

        @pl.when(jnp.logical_not(last))
        def _():
            edge_copy(slot, 1).wait_send()

    def stat_copy(slot, n, d):
        to = M * lax.rem(b + d, G) + m
        return pltpu.make_async_remote_copy(
            src_ref=ssend.at[pl.ds(slot, n)],
            dst_ref=srecv.at[b, pl.ds(slot, n)],
            send_sem=st_s.at[slot, d],
            recv_sem=st_r.at[slot, b],
            device_id=(p, to),
            device_id_type=MESH,
        )

    def send_sums(slot, n):
        srecv[b, slot : slot + n] = ssend[slot : slot + n]
        for d in range(1, G):
            stat_copy(slot, n, d).start()

    sums_sent = []

    def get_sums(slot, n):
        sums_sent.append((slot, n))
        for d in range(1, G):
            s = lax.rem(b + d, G)
            arrived(srecv.at[s, pl.ds(slot, n)], st_r.at[slot, s])

    def total(slot):
        acc = srecv[0, slot]
        for g in range(1, G):
            acc = acc + srecv[g, slot]
        return acc

    def put_sums(slot, s, q):
        ssend[slot] = jnp.concatenate([folded(s), folded(q)], 0)

    x_moves = []
    kept = []

    def post(index, src, dst, target, keep=False):
        move = Remote(src, dst.at[e], x_s.at[index], x_r.at[index - (target if index in cfg["to_all"] else 0), e], e0 + target)
        x_moves.append(move)
        if not keep:
            move.start()
        else:
            kept.append(move)

            @pl.when(p == 0)
            def _():
                move.start()

    def send_kept():
        for move in kept:
            move.start()


    def moments(k, slot, edge=None):
        def body(j, carry):
            s, q = carry
            y = ys[k, column(j), :]
            if edge is not None:
                esend[edge, 0, j] = y[0:1]
                esend[edge, 1, j] = y[H - 1 : H]
            return s + fold(y), q + fold(y * y)

        s, q = over_columns(body, (zero8, zero8))
        put_sums(slot, s, q)

    norm = {}

    def norm_rows(k, slot):
        acc = total(slot)
        mean = acc[0:1] / count
        rs = lax.rsqrt(acc[1:2] / count - mean * mean + epsilon)
        scale = gain[k] * rs
        norm[k] = (mean, rs, scale, bias[k])

    def normed(k, y):
        mean, rs, scale, shift = norm[k]
        return (y - mean) * scale + shift

    def silu(x):
        return x * sigmoid(x)

    def silu_slope(x):
        s = sigmoid(x)
        return s * (1.0 + x * (1.0 - s))

    def pair(slot, j):
        return jnp.concatenate([erecv[slot, 0, j], erecv[slot, 1, j]], 0)

    nt = 2 + 3 * T
    F3, F4, F5 = 2, 2 + T, 2 + 2 * T

    def wait_field(kind, buffer):
        for k in range(M):
            arrived(buffer(k), in_r.at[kind, k])

    @pl.when(jnp.logical_not(first))
    def _():
        arrived(uh.at[0], in_r.at[3, 0])

    @pl.when(jnp.logical_not(last))
    def _():
        arrived(uh.at[1], in_r.at[4, 0])

    def start_of_field():
        wait_field(0, lambda k: rin.at[pl.ds(part * k, part), 0:C])
        field[p, :, 0:C] = dot(perm[...], rin[:, 0:C]).astype(half)

    def rest_of_field():
        wait_field(1, lambda k: rin.at[pl.ds(part * k, part), C:CW])
        for t in range(T):
            cols = slice((t + 1) * C, (t + 2) * C)
            field[p, :, cols] = dot(perm[...], rin[:, cols]).astype(half)

    @pl.when(p == 0)
    def _():
        start_of_field()

    def wait_selection():
        wait_field(2, lambda k: selin.at[pl.ds(part * k, part)])

        @pl.when(jnp.logical_not(first))
        def _():
            arrived(selh.at[0], in_r.at[3, 1])

        @pl.when(jnp.logical_not(last))
        def _():
            arrived(selh.at[1], in_r.at[4, 1])

    def halo_copies():
        return (
            pltpu.make_async_remote_copy(
                src_ref=ps.at[pl.ds(pix // 4, 16), 0:C], dst_ref=px.at[pl.ds(pix // 4, 16), 0:C],
                send_sem=pp_s.at[1], recv_sem=pp_r.at[1], device_id=(1 - p, r + M), device_id_type=MESH),
            pltpu.make_async_remote_copy(
                src_ref=ps.at[pl.ds(pix // 4 + 16, 16), 0:C], dst_ref=px.at[pl.ds(pix // 4 + 16, 16), 0:C],
                send_sem=pp_s.at[2], recv_sem=pp_r.at[2], device_id=(1 - p, M * (b - 1) + m), device_id_type=MESH),
        )

    def pool_copy():
        return pltpu.make_async_remote_copy(
            src_ref=ps.at[pl.ds(0, pix // 4)], dst_ref=px.at[pl.ds(0, pix // 4)],
            send_sem=pp_s.at[0], recv_sem=pp_r.at[0], device_id=(1 - p, r), device_id_type=MESH)

    @pl.when(p == 1)
    def _():
        wait_selection()
        chosen[...] = spread[...] * dot(perm[...], selin[...]).astype(half)
        pl.semaphore_wait(go, 1)
        start_field()
        start_of_field()
        rest_of_field()
        arrived(px.at[pl.ds(0, pix // 4)], pp_r.at[0])

        @pl.when(jnp.logical_not(first))
        def _():
            arrived(px.at[pl.ds(pix // 4, 16), 0:C], pp_r.at[1])

        @pl.when(jnp.logical_not(last))
        def _():
            arrived(px.at[pl.ds(pix // 4 + 16, 16), 0:C], pp_r.at[2])

        for t in range(1 + T):
            cols = slice(t * C, (t + 1) * C)
            field[0, :, cols] = dot(chosen[...], px[:, cols]).astype(half)
        edges = spread_edge[...] * jnp.concatenate([selh[0], selh[1]], 0)
        both = dot(edges, px[:, 0:C]).astype(half)
        uh[0] = both[0:32]
        uh[1] = both[32:64]

    above = uh[0].astype(f32)
    below = uh[1].astype(f32)
    for j in range(W):
        uedge[0, j] = above[32 - W + j : 33 - W + j]
        uedge[1, j] = below[j : j + 1]

    up = msks[m, 0]
    down = msks[m, 1]

    def body_u(j, carry):
        build(j, field[0, column(j), 0:C].astype(f32), uedge[0, j], uedge[1, j], up, down)
        return carry

    over_columns(body_u)
    loads["c0"].wait()
    ys[0] = conv(kc.at[0])
    moments(0, 0, 0)
    send_sums(0, 1)
    send_edges(0)

    @pl.when(p == 0)
    def _():
        rest_of_field()
        pl.semaphore_signal(go, inc=1, device_id=(1 - p, r), device_id_type=MESH)

    for q in range(TEAM):
        post(q, field.at[0, :, 0:C], xu, q, True)
    for t in range(T):
        post(8 + t, field.at[0, :, (t + 1) * C : (t + 2) * C], xv, t, True)
    get_sums(0, 1)
    get_edges(0)
    norm_rows(0, 0)

    def body_h1(j, carry):
        value = silu(normed(0, ys[0, column(j), :]))
        side = silu(normed(0, pair(0, j)))
        h1[column(j), :] = value.astype(half)
        build(j, value, side[0:1], side[1:2], up, down)
        return carry

    over_columns(body_h1)
    for q in range(TEAM):
        post(4 + q, h1, xh, q, q < T)

    loads["i"].wait()
    for t in range(T):
        k = 2 + 3 * t
        ys[k] = dot(h1[...], ki[t, 0:C, :]) + dot(field[0, :, (t + 1) * C : (t + 2) * C], ki[t, C : 2 * C, :])
        moments(k, F3 + t)
    send_sums(F3, T)
    loads["c1"].wait()
    ys[1] = conv(kc.at[1])
    moments(1, 1, 1)
    send_sums(1, 1)
    send_edges(1)

    get_sums(F3, T)
    loads["m"].wait()
    for t in range(T):
        k = 2 + 3 * t
        norm_rows(k, F3 + t)

        def body_t1(j, carry):
            t1[t, column(j), :] = silu(normed(k, ys[k, column(j), :])).astype(half)
            return carry

        over_columns(body_t1)
        ys[k + 1] = dot(t1[t], km[t])
        moments(k + 1, F4 + t, 2 + t)
        send_sums(F4 + t, 1)
        send_edges(2 + t)

    get_sums(1, 1)
    get_edges(1)
    norm_rows(1, 1)

    def body_h2(j, carry):
        value = silu(normed(1, ys[1, column(j), :])).astype(half)
        h2[column(j), :] = value
        res[column(j), 0:C] = value
        side = silu(normed(1, pair(1, j))).astype(half).astype(f32)
        h2e[j] = side
        return carry

    over_columns(body_h2)
    for t in range(T):
        k = 3 + 3 * t
        get_sums(F4 + t, 1)
        get_edges(2 + t)
        norm_rows(k, F4 + t)

        def body_p(j, carry):
            gate = sigmoid(normed(k, ys[k, column(j), :]))
            value = gate * h2[column(j), :].astype(f32)
            side = sigmoid(normed(k, pair(2 + t, j))) * h2e[j]
            pr[t, column(j), :] = value.astype(half)
            build(j, value, side[0:1], side[1:2], up, down)
            return carry

        over_columns(body_p)
        post(14 + t, pr.at[t], xp, t)
        loads["t%d" % t].wait()
        ys[k + 1] = conv(kt.at[t])
        moments(k + 1, F5 + t, 5 + t)
        send_sums(F5 + t, 1)
        send_edges(5 + t)
    for t in range(T):
        k = 4 + 3 * t
        get_sums(F5 + t, 1)
        get_edges(5 + t)
        norm_rows(k, F5 + t)

        def body_q(j, carry):
            res[column(j), (t + 1) * C : (t + 2) * C] = silu(normed(k, ys[k, column(j), :])).astype(half)
            return carry

        over_columns(body_q)

    def out_moves(which):
        cols = slice(0, C) if which == 0 else slice(C, CW)
        moves = []
        for d in range(M):
            k = lax.rem(m + d, M)
            rows = pl.ds(pl.multiple_of(part * k, 16), part)
            moves.append(
                Remote(rin.at[rows, cols], out.at[m, :, cols], out_s.at[which, d], out_r.at[which, m], e0 + k)
            )
        return moves

    def stage_result(which):
        for t in range(0, 1) if which == 0 else range(1, 1 + T):
            cols = slice(t * C, (t + 1) * C)
            rin[:, cols] = dot(perm_t[...], res[:, cols]).astype(half)

    def start_result(which):
        for move in out_moves(which):
            move.start()

    @pl.when(p == 0)
    def _():
        for t in range(1 + T):
            cols = slice(t * C, (t + 1) * C)
            ps[:, cols] = dot(pool[...], res[:, cols]).astype(half)
        pool_copy().start()

        @pl.when(jnp.logical_not(last))
        def _():
            halo_copies()[0].start()

        @pl.when(jnp.logical_not(first))
        def _():
            halo_copies()[1].start()

        pool_copy().wait_send()

        @pl.when(jnp.logical_not(last))
        def _():
            halo_copies()[0].wait_send()

        @pl.when(jnp.logical_not(first))
        def _():
            halo_copies()[1].wait_send()

        arrived(px.at[pl.ds(0, pix // 4)], pp_r.at[0])
        for t in range(1 + T):
            cols = slice(t * C, (t + 1) * C)
            field[1, :, cols] = (dot(spread[...], px[:, cols]) * 0.25).astype(half)

    @pl.when(p == 1)
    def _():
        stage_result(0)
        stage_result(1)

    B3, B4, B5 = nt + F3, nt + F4, nt + F5
    back = {}

    def back_rows(k, slot):
        acc = total(slot)
        mean, rs, scale, shift = norm[k]
        slope = -scale * rs * acc[1:2] / count
        back[k] = (scale, slope, -scale * acc[0:1] / count - slope * mean)
        bn[k : k + 1, :] = acc[1:2]
        bn[norms + k : norms + k + 1, :] = acc[0:1]

    def grad_pre(k, dzv, y):
        scale, slope, rest = back[k]
        return scale * dzv + slope * y + rest

    def hat(k, y):
        mean, rs, scale, shift = norm[k]
        return (y - mean) * rs

    for t in range(T):
        k = 4 + 3 * t

        def body_dz5(j, carry):
            s, q = carry
            y = ys[k, column(j), :]
            g = field[1, column(j), (t + 1) * C : (t + 2) * C].astype(f32)
            v = g * silu_slope(normed(k, y))
            dz[t, column(j), :] = v
            esend[8 + t, 0, j] = v[0:1]
            esend[8 + t, 1, j] = v[H - 1 : H]
            return s + fold(v), q + fold(v * hat(k, y))

        s, q = over_columns(body_dz5, (zero8, zero8))
        put_sums(B5 + t, s, q)
        send_sums(B5 + t, 1)
        send_edges(8 + t)

    for t in range(T):
        k = 4 + 3 * t
        get_sums(B5 + t, 1)
        get_edges(8 + t)
        back_rows(k, B5 + t)

        def body_dy5(j, carry):
            v = grad_pre(k, dz[t, column(j), :], ys[k, column(j), :])
            side = grad_pre(k, pair(8 + t, j), pair(5 + t, j))
            dy5[t, column(j), :] = v.astype(half)
            dy5e[t, 0, j] = side[0:1]
            dy5e[t, 1, j] = side[1:2]
            build(j, v, side[0:1], side[1:2], up, down)
            return carry

        over_columns(body_dy5)
        post(17 + t, dy5.at[t], xd5, t)
        post(21 + t, dy5e.at[t], xd5e, t)
        ys[k] = conv_t(kt.at[t])

        def body_dz4(j, carry):
            s, q = carry
            dp = ys[k, column(j), :]
            y = ys[k - 1, column(j), :]
            gate = sigmoid(normed(k - 1, y))
            dgate = dp * h2[column(j), :].astype(f32)
            base = field[1, column(j), 0:C].astype(f32) if t == 0 else dh[column(j), :]
            dh[column(j), :] = base + dp * gate
            v = dgate * gate * (1.0 - gate)
            ys[k, column(j), :] = v
            return s + fold(v), q + fold(v * hat(k - 1, y))

        s, q = over_columns(body_dz4, (zero8, zero8))
        put_sums(B4 + t, s, q)
        send_sums(B4 + t, 1)

    def body_dz2(j, carry):
        s, q = carry
        y = ys[1, column(j), :]
        v = dh[column(j), :] * silu_slope(normed(1, y))
        dh[column(j), :] = v
        esend[11, 0, j] = v[0:1]
        esend[11, 1, j] = v[H - 1 : H]
        return s + fold(v), q + fold(v * hat(1, y))

    s, q = over_columns(body_dz2, (zero8, zero8))
    put_sums(nt + 1, s, q)
    send_sums(nt + 1, 1)
    send_edges(11)

    dy4 = [field.at[1, :, t * C : (t + 1) * C] for t in range(T)]
    dy2 = field.at[1, :, T * C : (T + 1) * C]
    mid = km
    for t in range(T):
        k = 3 + 3 * t
        get_sums(B4 + t, 1)
        back_rows(k, B4 + t)

        def body_dy4(j, carry):
            dy4[t][column(j), :] = grad_pre(k, ys[k + 1, column(j), :], ys[k, column(j), :]).astype(half)
            return carry

        over_columns(body_dy4)
        dz[t] = dot_nt(dy4[t][...], km[t])

        def body_dz3(j, carry):
            s, q = carry
            y = ys[k - 1, column(j), :]
            v = dz[t, column(j), :] * silu_slope(normed(k - 1, y))
            dz[t, column(j), :] = v
            return s + fold(v), q + fold(v * hat(k - 1, y))

        s, q = over_columns(body_dz3, (zero8, zero8))
        put_sums(B3 + t, s, q)
    send_sums(B3, T)

    get_sums(nt + 1, 1)
    get_edges(11)
    back_rows(1, nt + 1)

    def body_dy2(j, carry):
        v = grad_pre(1, dh[column(j), :], ys[1, column(j), :])
        side = grad_pre(1, pair(11, j), pair(1, j))
        dy2[column(j), :] = v.astype(half)
        dy2e[0, j] = side[0:1]
        dy2e[1, j] = side[1:2]
        build(j, v, side[0:1], side[1:2], up, down)
        return carry

    over_columns(body_dy2)
    post(20, dy2, xd5, TEAM - 1)
    post(24, dy2e, xd5e, TEAM - 1)


    dh[...] = conv_t(kc.at[1])

    get_sums(B3, T)
    for t in range(T):
        k = 2 + 3 * t
        back_rows(k, B3 + t)

        def body_dy3(j, carry):
            dy3[t, column(j), :] = grad_pre(k, dz[t, column(j), :], ys[k, column(j), :]).astype(half)
            return carry

        over_columns(body_dy3)
        post(28 + t, dy3.at[t], xd3, t)
        dh[...] += dot_nt(dy3[t], ki[t, 0:C, :])
        res[:, (t + 1) * C : (t + 2) * C] = dot_nt(dy3[t], ki[t, C : 2 * C, :]).astype(half)

    @pl.when(p == 0)
    def _():
        stage_result(1)

    def body_dz1(j, carry):
        s, q = carry
        y = ys[0, column(j), :]
        v = dh[column(j), :] * silu_slope(normed(0, y))
        dh[column(j), :] = v
        esend[12, 0, j] = v[0:1]
        esend[12, 1, j] = v[H - 1 : H]
        return s + fold(v), q + fold(v * hat(0, y))

    s, q = over_columns(body_dz1, (zero8, zero8))
    put_sums(nt, s, q)
    send_sums(nt, 1)
    send_edges(12)
    for t in range(T):
        mid[t] = dot_tn(t1[t], dy4[t][...]).astype(half)
        post(25 + t, mid.at[t], xd4, t)
    get_sums(nt, 1)
    get_edges(12)
    back_rows(0, nt)

    def bn_moves():
        return [Remote(bn, bnr.at[m], bn_s.at[d], bn_r.at[m], e0 + lax.rem(m + d, M)) for d in range(M)]

    for move in bn_moves():
        move.start()

    quarter = C // TEAM

    def body_dy1(j, carry):
        v = grad_pre(0, dh[column(j), :], ys[0, column(j), :])
        side = grad_pre(0, pair(12, j), pair(0, j))
        low = v.astype(half)
        for o in range(TEAM):
            cols = slice(o * quarter, (o + 1) * quarter)
            dy1[o, column(j), :] = low[:, cols]
            dy1e[o, 0, j] = side[0:1, cols]
            dy1e[o, 1, j] = side[1:2, cols]
        build(j, v, side[0:1], side[1:2], up, down)
        return carry

    over_columns(body_dy1)
    for o in range(TEAM):
        post(31 + o, dy1.at[o], xd1, o)
        post(35 + o, dy1e.at[o], xd1e, o)
    res[:, 0:C] = conv_t(kc.at[0]).astype(half)

    @pl.when(p == 1)
    def _():
        for t in range(1 + T):
            cols = slice(t * C, (t + 1) * C)
            ps[0 : pix // 4, cols] = dot_tn(chosen[...], res[:, cols])[0 : pix // 4].astype(half)
        pool_copy().start()
        pool_copy().wait_send()

    @pl.when(p == 0)
    def _():
        stage_result(0)

    def finish_sends():
        for move in field_moves + rest_moves + sel_moves:
            move.sent()

        @pl.when(tops)
        def _():
            for move in edge_moves[0]:
                move.sent()

        @pl.when(bottoms)
        def _():
            for move in edge_moves[1]:
                move.sent()

        for s in range(EDGES):
            finish_edges(s)
        for slot, n in sums_sent:
            for d in range(1, G):
                stat_copy(slot, n, d).wait_send()

        @pl.when(p == 0)
        def _():
            wait_selection()

    if not direct:

        @pl.when(p == 1)
        def _():
            send_kept()

        start_result(1)
        start_result(0)
        finish_sends()
    if direct:
        z, n = b, R // TEAM
        q4 = quarter
        all_rows = TEAM * pix
        wide = pix + 2 * H
        task = e < T
        vb, va, vc = (kt.at[2, i * all_rows : (i + 1) * all_rows, :] for i in range(3))
        _, d5, d3 = (kc.at[0, i * all_rows : (i + 1) * all_rows, :] for i in range(3))
        pm, p1, pi_, pt = kt.at[0], kc.at[0, :, 0:q4], ki.at[0], ki.at[T - 1, 0:C]
        d1 = kt.at[1, 0:all_rows, 3 * q4 : 4 * q4]
        rows_m, rows_i, rows_t = 9 * C // R, 2 * C // R, C // R

        def band(ref, j):
            return ref.at[j * pix : (j + 1) * pix]

        def fetch(index, src, j, dst, sem):
            arrived(src.at[j], sem)
            copy = pltpu.make_async_copy(src.at[j], dst, l_sem.at[index, j])
            copy.start()
            return copy

        def rows_shifted(j, a, lo):
            if j < TEAM - 1:
                start = (3 * j + a) * wide + lo
                return kc.at[1, start : start + pix, :]
            return rb.at[a, lo : lo + pix, :]

        for j in range(TEAM - 1):
            for a in range(3):
                start = (3 * j + a) * wide
                kc[1, start : start + H, :] = zero_col
                kc[1, start + H + pix : start + wide, :] = zero_col
        got = {}
        for j in range(TEAM):
            got["d5", j] = fetch(0, xd5, j, band(d5, j), x_r.at[17 + e, j])
            got["d5e", j] = fetch(1, xd5e, j, d5e.at[j], x_r.at[21 + e, j])

        @pl.when(task)
        def _():
            for j in range(TEAM):
                fetch(3, xp, j, band(vb, j), x_r.at[14 + e, j])

        @pl.when(jnp.logical_not(task))
        def _():
            for j in range(TEAM):
                fetch(3, xh, j, band(vb, j), x_r.at[4, j])

        for j in range(TEAM):
            got["d5", j].wait()
            got["d5e", j].wait()

            def body_r(i, carry):
                v = kc[0, pl.ds(pl.multiple_of(all_rows + j * pix + i * H, H), H), :].astype(f32)
                three = (
                    (jnp.where(at_top, d5e[j, 0, i], pltpu.roll(v, 1, 0)) * msks[j, 0]).astype(half),
                    v.astype(half),
                    (jnp.where(at_bottom, d5e[j, 1, i], pltpu.roll(v, H - 1, 0)) * msks[j, 1]).astype(half),
                )
                for a in range(3):
                    if j < TEAM - 1:
                        here = pl.ds(pl.multiple_of((3 * j + a) * wide + H + i * H, H), H)
                        kc[1, here, :] = three[a]
                    else:
                        rb[a, pl.ds(pl.multiple_of(H + i * H, H), H), :] = three[a]
                return carry

            over_columns(body_r)
        for j in range(TEAM):
            pltpu.make_async_copy(xp.at[j], band(vb, j), l_sem.at[3, j]).wait()

        for tap in range(9):
            a, c = 2 - tap // 3, 2 - tap % 3
            acc = None
            for j in range(TEAM):
                term = dot_tn(band(vb, j)[...], rows_shifted(j, a, H * c)[...])
                acc = term if acc is None else acc + term
            pm[tap * C : (tap + 1) * C, :] = acc.astype(half)

        partial = (pm, pi_, pt, p1)
        share = (rows_m, rows_i, rows_t, rows_m)
        pieces = (TEAM, 1, 1, 1)
        width = (C, C, C, q4)

        def flow(g, zd, s, way):
            rows = TEAM * share[g] // pieces[g]
            return pltpu.make_async_remote_copy(
                src_ref=partial[g].at[pl.ds(pl.multiple_of((zd * pieces[g] + s) * rows, 16), rows)],
                dst_ref=flows_in[g].at[way, zd, pl.ds(pl.multiple_of(s * rows, 16), rows)],
                send_sem=fl_s.at[way, g, zd, s],
                recv_sem=fl_r.at[way, g, zd, s],
                device_id=(p, r + TEAM * (1 - 2 * way)),
                device_id_type=MESH,
            )

        def incoming(g, zd, s, way, slot):
            rows = TEAM * share[g] // pieces[g]
            src = flows_in[g].at[way, zd, pl.ds(pl.multiple_of(s * rows, 16), rows)]
            first_row = way * TEAM * rows_m + slot * rows
            dst = kc.at[1, pl.ds(pl.multiple_of(first_row, 16), rows), 0 : width[g]]
            return src, dst, fl_r.at[way, g, zd, s], fl_l.at[way, slot]

        def take(g, zd, s, way, slot):
            src, dst, sem, local = incoming(g, zd, s, way, slot)
            arrived(src, sem)
            pltpu.make_async_copy(src, dst, local).start()

        def taken(g, zd, s, way, slot):
            src, dst, sem, local = incoming(g, zd, s, way, slot)
            pltpu.make_async_copy(src, dst, local).wait()
            return dst[...].astype(f32)

        def flow_start(g):
            @pl.when(z == 0)
            def _():
                for zd in range(n - 1, 0, -1):
                    for s in range(pieces[g]):
                        flow(g, zd, s, 0).start()

            @pl.when(z == n - 1)
            def _():
                for zd in range(n - 1):
                    for s in range(pieces[g]):
                        flow(g, zd, s, 1).start()

        def flow_mid(groups):
            upper = (2 * z) // n

            @pl.when(jnp.logical_and(z > 0, z < n - 1))
            def _():
                for phase in range(2):
                    way = lax.rem(phase + upper, 2)
                    for g in groups:
                        rows = TEAM * share[g] // pieces[g]

                        def body_flow(i, carry):
                            k, s = i // pieces[g], i % pieces[g]
                            zd = (1 - way) * (n - 1 - k) + way * k

                            @pl.when((1 - 2 * way) * (zd - z) > 0)
                            def _():
                                take(g, zd, s, way, 0)
                                here = partial[g].at[pl.ds(pl.multiple_of((zd * pieces[g] + s) * rows, 16), rows)]
                                here[...] = (here[...].astype(f32) + taken(g, zd, s, way, 0)).astype(half)
                                flow(g, zd, s, way).start()

                            return carry

                        lax.fori_loop(0, (n - 1) * pieces[g], body_flow, 0)

        def share_moves(g):
            moves = []
            for d in range(TEAM):
                q = lax.rem(e + d, TEAM)
                start = pl.multiple_of((z * TEAM + q) * share[g], 16)
                moves.append(
                    Remote(partial[g].at[pl.ds(start, share[g])], ends[g].at[e], sh_s.at[g, d], sh_r.at[g, e], e0 + q)
                )
            return moves

        def flow_final(g):
            rows = TEAM * share[g] // pieces[g]
            for s in range(pieces[g]):

                @pl.when(z > 0)
                def _():
                    take(g, z, s, 0, s)

                @pl.when(z < n - 1)
                def _():
                    take(g, z, s, 1, s)

            for s in range(pieces[g]):
                here = partial[g].at[pl.ds(pl.multiple_of(z * TEAM * share[g] + s * rows, 16), rows)]

                @pl.when(jnp.logical_and(z > 0, z < n - 1))
                def _():
                    here[...] = (here[...].astype(f32) + taken(g, z, s, 0, s) + taken(g, z, s, 1, s)).astype(half)

                @pl.when(z == 0)
                def _():
                    here[...] = (here[...].astype(f32) + taken(g, z, s, 1, s)).astype(half)

                @pl.when(z == n - 1)
                def _():
                    here[...] = (here[...].astype(f32) + taken(g, z, s, 0, s)).astype(half)

            for move in share_moves(g):
                move.start()

        def flow_sent(g):
            for way in range(2):
                for zd in range(n):
                    on = z < zd if way == 0 else z > zd

                    @pl.when(on)
                    def _():
                        for s in range(pieces[g]):
                            flow(g, zd, s, way).wait_send()

            for move in share_moves(g):
                move.sent()

        flow_start(0)

        @pl.when(p == 1)
        def _():
            send_kept()

        finish_sends()
        flow_mid((0,))

        first_u = []
        for j in range(TEAM):
            first_u.append(fetch(4, xu, j, band(vb, j), x_r.at[0, j]))

        @pl.when(task)
        def _():
            copies = []
            for j in range(TEAM):
                copies.append(fetch(2, xh, j, band(va, j), x_r.at[4, j]))
                copies.append(fetch(5, xv, j, band(vc, j), x_r.at[8 + e, j]))
                copies.append(fetch(6, xd4, j, kc.at[0, j * C : (j + 1) * C, :], x_r.at[25 + e, j]))
                copies.append(fetch(8, xd3, j, band(d3, j), x_r.at[28 + e, j]))
            for copy in copies:
                copy.wait()
            pi_[0:C, :] = dot_tn(va[...], d3[...]).astype(half)
            pi_[C : 2 * C, :] = dot_tn(vc[...], d3[...]).astype(half)
            acc = kc[0, 0:C, :].astype(f32)
            for j in range(1, TEAM):
                acc = acc + kc[0, j * C : (j + 1) * C, :].astype(f32)
            pt[...] = acc.astype(half)
            flow_start(1)
            flow_start(2)

        for j in range(TEAM):
            got["d1", j] = fetch(9, xd1, j, band(d1, j), x_r.at[31, j])
            got["d1e", j] = fetch(10, xd1e, j, d1e.at[j], x_r.at[35, j])
        row_of1 = lax.broadcasted_iota(jnp.int32, (H, q4), 0)

        def near(j, a, lo, size, cols):
            start = (3 * j + a) * pix + lo
            return kt.at[1, start : start + size, cols * q4 : (cols + 1) * q4]

        for j in range(TEAM):
            got["d1", j].wait()
            got["d1e", j].wait()

        for j in range(TEAM):

            def body_r1(i, carry):
                v = kt[1, pl.ds(pl.multiple_of(j * pix + i * H, H), H), 3 * q4 : 4 * q4].astype(f32)
                three = (
                    (jnp.where(row_of1 == 0, d1e[j, 0, i], pltpu.roll(v, 1, 0)) * msks[j, 0][:, 0:q4]).astype(half),
                    v.astype(half),
                    (jnp.where(row_of1 == H - 1, d1e[j, 1, i], pltpu.roll(v, H - 1, 0)) * msks[j, 1][:, 0:q4]).astype(
                        half
                    ),
                )
                for a in range(3):
                    kt[1, pl.ds(pl.multiple_of((3 * j + a) * pix + i * H, H), H), q4 : 2 * q4] = three[a]
                return carry

            over_columns(body_r1)
            for a in range(3):
                near(j, a, 0, H, 0)[...] = jnp.zeros((H, q4), half)
                near(j, a, H, pix - H, 0)[...] = near(j, a, 0, pix - H, 1)[...]
                near(j, a, 0, pix - H, 2)[...] = near(j, a, H, pix - H, 1)[...]
                near(j, a, pix - H, H, 2)[...] = jnp.zeros((H, q4), half)
        for copy in first_u:
            copy.wait()
        for a in range(3):
            acc = None
            for j in range(TEAM):
                start = (3 * j + 2 - a) * pix
                term = dot_tn(band(vb, j)[...], kt[1, start : start + pix, 0 : 3 * q4])
                acc = term if acc is None else acc + term
            for c in range(3):
                kc[0, (3 * a + c) * C : (3 * a + c + 1) * C, 0:q4] = acc[:, (2 - c) * q4 : (3 - c) * q4].astype(half)
        flow_start(3)

        flow_final(0)
        start_result(1)
        start_result(0)

        @pl.when(task)
        def _():
            flow_mid((1, 2, 3))

        @pl.when(jnp.logical_not(task))
        def _():
            flow_mid((3,))

        stores = []

        def store(start, rows, dst, i):
            copy = pltpu.make_async_copy(lin.at[start : start + rows], dst, o_sem.at[i])
            copy.start()
            stores.append(copy)
            return copy

        lanes = C // 128
        lin_m, lin_i, lin_t = rows_m * lanes, rows_i * lanes, rows_t * lanes
        pair_at = 2 * lin_m

        def flatten(value, start, rows, lane, step=1):
            for k in range(value.shape[1] // 128):
                lin[pl.ds(start + step * (lane + k), rows, stride=step * lanes), :] = value[:, 128 * k : 128 * (k + 1)]

        def last_of(g, members, buffer, base):
            copies = []
            for q in range(members):
                arrived(ends[g].at[q], sh_r.at[g, q])
                copy = pltpu.make_async_copy(
                    ends[g].at[q], buffer.at[q * share[g] : (q + 1) * share[g]], l_sem.at[base, q]
                )
                copy.start()
                copies.append(copy)
            for copy in copies:
                copy.wait()

        def piece(buffer, g, q):
            return buffer[q * share[g] : (q + 1) * share[g], :].astype(f32)

        final_m, final_1 = kc.at[1, 2 * TEAM * rows_m : 3 * TEAM * rows_m, :], kt.at[2, :, 0:q4]
        last_of(0, TEAM, final_m, 11)
        for q in range(T):
            if q >= 2:
                stores[q - 2].wait()
            flatten(piece(final_m, 0, q), q % 2 * lin_m, rows_m, 0)
            store(q % 2 * lin_m, lin_m, gm.at[q * lin_m : (q + 1) * lin_m], q)
        flatten(piece(final_m, 0, T), pair_at + 1, rows_m, 0, 2)
        for copy in stores[max(0, T - 2) :]:
            copy.wait()
        del stores[:]

        @pl.when(task)
        def _():
            flow_final(1)
            flow_final(2)

        flow_final(3)
        last_of(1, T, ki.at[1], 12)
        for q in range(T):
            flatten(piece(ki.at[1], 1, q), q * lin_i, rows_i, 0)
        store(0, T * lin_i, gi, T)
        last_of(2, T, ki.at[T - 1, C : 2 * C], 13)
        for q in range(T):
            flatten(piece(ki.at[T - 1, C : 2 * C], 2, q), T * lin_i + q * lin_t, rows_t, 0)
        store(T * lin_i, T * lin_t, gt, T + 1)
        last_of(3, TEAM, final_1, 14)
        for q in range(TEAM):
            flatten(piece(final_1, 3, q), pair_at, rows_m, q * q4 // 128, 2)
        store(pair_at, 2 * lin_m, g1, T + 2)
        flow_sent(0)

        @pl.when(task)
        def _():
            flow_sent(1)
            flow_sent(2)

        flow_sent(3)
        for copy in stores:
            copy.wait()

    for k in range(M):
        arrived(bnr.at[k], bn_r.at[k])
    acc = bnr[0]
    for k in range(1, M):
        acc = acc + bnr[k]
    for k in range(norms):
        bng[k] = acc[k : k + 1]
        bnb[k] = acc[norms + k : norms + k + 1]
    for k in range(M):
        arrived(out.at[k, :, 0:C], out_r.at[0, k])
        arrived(out.at[k, :, C:CW], out_r.at[1, k])
    for move in out_moves(0) + out_moves(1) + bn_moves():
        move.sent()
    for move in x_moves:
        move.sent()
    if direct:
        return
    for j in range(TEAM):
        for index, dst in ((0, xu), (4, xh), (31, xd1), (35, xd1e)):
            arrived(dst.at[j], x_r.at[index, j])
    for t in range(T):

        @pl.when(e == t)
        def _():
            for j in range(TEAM):
                for index, dst in ((8, xv), (14, xp), (17, xd5), (21, xd5e), (25, xd4), (28, xd3)):
                    arrived(dst.at[j], x_r.at[index + t, j])

    @pl.when(e == TEAM - 1)
    def _():
        for j in range(TEAM):
            arrived(xd5.at[j], x_r.at[20, j])
            arrived(xd5e.at[j], x_r.at[24, j])


def tables(M, G, H, W):
    pix = H * W
    cm = np.zeros((pix, pix), np.float32)
    spread = np.zeros((pix, 128), np.float32)
    pool = np.zeros((128, pix), np.float32)
    edge = np.zeros((64, 128), np.float32)
    wide = W // 2
    own = pix // 4
    for i in range(H):
        for j in range(W):
            q = j * H + i
            cm[q, i * W + j] = 1
            w = (i // 2) * wide + j // 2
            spread[q, w] = 1
            pool[w, q] = 0.25
            if i >= H - 2:
                pool[own + j // 2, q] = 0.25
            if i < 2:
                pool[own + 16 + j // 2, q] = 0.25
    for j in range(W):
        edge[32 - W + j, own + j // 2] = 1
        edge[32 + j, own + 16 + j // 2] = 1
    return [jnp.asarray(v, half) for v in (cm, cm.T, spread, edge, pool)]


def gradient_kernel(cfg, *refs):
    M, G, H, W, C, T, n = cfg["M"], cfg["G"], cfg["H"], cfg["W"], cfg["C"], cfg["T"], cfg["n"]
    R = M * G
    pix = H * W
    q4 = C // TEAM
    (msk, xu, xh, xp, xv, xd5, xd5e, xd4, xd3, xd1, xd1e) = refs[:11]
    (gm, g1, gi, gt) = refs[11:15]
    (va, vb, vc, d5, d5e, rb, r1, d1, d1e, d3, d4, pm, p1, pi_, pt, am, a1, ai, at, in_sem, s_sem, r_sem) = refs[15:]
    p = lax.axis_index("pipe")
    r = lax.axis_index("rows")
    e = r % TEAM
    z = r // TEAM
    task = e < T

    loads = {}

    def load(name, src, dst, i):
        loads[name] = pltpu.make_async_copy(src, dst, in_sem.at[i])
        loads[name].start()

    load("d5", xd5, d5, 0)
    load("d5e", xd5e, d5e, 1)
    load("h", xh, va, 2)

    @pl.when(task)
    def _():
        pltpu.make_async_copy(xp, vb, in_sem.at[3]).start()
        pltpu.make_async_copy(xv, vc, in_sem.at[4]).start()
        pltpu.make_async_copy(xd3, d3, in_sem.at[6]).start()
        pltpu.make_async_copy(xd4, d4, in_sem.at[7]).start()

    bar = pltpu.get_barrier_semaphore()

    def greet(i, _):
        pl.semaphore_signal(bar, inc=1, device_id=(p, lax.rem(r + TEAM * i, R)), device_id_type=MESH)
        return 0

    lax.fori_loop(1, n, greet, 0)

    row_of = lax.broadcasted_iota(jnp.int32, (H, C), 0)
    row_of1 = lax.broadcasted_iota(jnp.int32, (H, q4), 0)

    def column(j):
        return pl.ds(pl.multiple_of(j * H, H), H)

    for j in range(TEAM):
        for a in range(3):
            rb[j, a, 0:H, :] = jnp.zeros((H, C), half)
            rb[j, a, H * (W + 1) : H * (W + 2), :] = jnp.zeros((H, C), half)
            r1[j, a, 0:H, :] = jnp.zeros((H, 3 * q4), half)
            r1[j, a, H * (W - 1) :, :] = jnp.zeros((H, 3 * q4), half)

    loads["d5"].wait()
    loads["d5e"].wait()
    for j in range(TEAM):

        def body(c, carry):
            for u in range(2):
                i = c * 2 + u
                here = pl.ds(pl.multiple_of(H + i * H, H), H)
                v = d5[j, column(i), :].astype(f32)
                rb[j, 1, here, :] = v.astype(half)
                rb[j, 0, here, :] = (jnp.where(row_of == 0, d5e[j, 0, i], pltpu.roll(v, 1, 0)) * msk[j, 0]).astype(half)
                rb[j, 2, here, :] = (
                    jnp.where(row_of == H - 1, d5e[j, 1, i], pltpu.roll(v, H - 1, 0)) * msk[j, 1]
                ).astype(half)
            return carry

        lax.fori_loop(0, W // 2, body, 0)
    loads["h"].wait()

    @pl.when(task)
    def _():
        pltpu.make_async_copy(xp, vb, in_sem.at[3]).wait()
        pltpu.make_async_copy(xv, vc, in_sem.at[4]).wait()
        pltpu.make_async_copy(xd3, d3, in_sem.at[6]).wait()
        pltpu.make_async_copy(xd4, d4, in_sem.at[7]).wait()

    @pl.when(jnp.logical_not(task))
    def _():
        vb[...] = va[...]

    for tap in range(9):
        a, c = 2 - tap // 3, 2 - tap % 3
        acc = None
        for j in range(TEAM):
            term = dot_tn(vb[j], rb[j, a, H * c : H * c + pix, :])
            acc = term if acc is None else acc + term
        pm[tap * C : (tap + 1) * C, :] = acc.astype(half)

    pltpu.make_async_copy(xu, vb, in_sem.at[8]).start()
    pltpu.make_async_copy(xd1, d1, in_sem.at[9]).start()
    pltpu.make_async_copy(xd1e, d1e, in_sem.at[10]).start()

    def group(index, src, mine, rows):
        moves = []
        for d in range(1, n):
            to = lax.rem(z + d, n)
            moves.append(
                pltpu.make_async_remote_copy(
                    src_ref=src.at[pl.ds(pl.multiple_of(to * rows, 16), rows)],
                    dst_ref=mine.at[z],
                    send_sem=s_sem.at[index, d],
                    recv_sem=r_sem.at[index, z],
                    device_id=(p, TEAM * to + e),
                    device_id_type=MESH,
                )
            )
        return moves

    rows_m, rows_i, rows_t = 9 * C // n, 2 * C // n, C // n
    pl.semaphore_wait(bar, n - 1)
    main = group(0, pm, am, rows_m)
    for move in main:
        move.start()

    @pl.when(task)
    def _():
        for part, value in ((0, va), (1, vc)):
            acc = None
            for j in range(TEAM):
                term = dot_tn(value[j], d3[j])
                acc = term if acc is None else acc + term
            pi_[part * C : (part + 1) * C, :] = acc.astype(half)
        acc = d4[0].astype(f32)
        for j in range(1, TEAM):
            acc = acc + d4[j].astype(f32)
        pt[...] = acc.astype(half)
        for move in group(1, pi_, ai, rows_i) + group(2, pt, at, rows_t):
            move.start()

    pltpu.make_async_copy(xu, vb, in_sem.at[8]).wait()
    pltpu.make_async_copy(xd1, d1, in_sem.at[9]).wait()
    pltpu.make_async_copy(xd1e, d1e, in_sem.at[10]).wait()
    for j in range(TEAM):

        def body1(i, carry):
            v = d1[j, column(i), :].astype(f32)
            three = (
                (jnp.where(row_of1 == 0, d1e[j, 0, i], pltpu.roll(v, 1, 0)) * msk[j, 0][:, 0:q4]).astype(half),
                v.astype(half),
                (jnp.where(row_of1 == H - 1, d1e[j, 1, i], pltpu.roll(v, H - 1, 0)) * msk[j, 1][:, 0:q4]).astype(half),
            )
            for a in range(3):
                r1[j, a, column(i), q4 : 2 * q4] = three[a]
            return carry

        lax.fori_loop(0, W, body1, 0)
        for a in range(3):
            r1[j, a, H : W * H, 0:q4] = r1[j, a, 0 : (W - 1) * H, q4 : 2 * q4]
            r1[j, a, 0 : (W - 1) * H, 2 * q4 : 3 * q4] = r1[j, a, H : W * H, q4 : 2 * q4]
    for a in range(3):
        acc = None
        for j in range(TEAM):
            term = dot_tn(vb[j], r1[j, 2 - a])
            acc = term if acc is None else acc + term
        for c in range(3):
            p1[(3 * a + c) * C : (3 * a + c + 1) * C, :] = acc[:, (2 - c) * q4 : (3 - c) * q4].astype(half)
    one = group(3, p1, a1, rows_m)
    for move in one:
        move.start()

    def reduce(index, src, mine, rows, dst):
        for d in range(1, n):
            s = lax.rem(z + d, n)
            arrived(mine.at[s], r_sem.at[index, s])
        mine[z] = src[pl.ds(pl.multiple_of(z * rows, 16), rows), :]
        acc = mine[0].astype(f32)
        for s in range(1, n):
            acc = acc + mine[s].astype(f32)
        dst[...] = acc.astype(dst.dtype)

    reduce(0, pm, am, rows_m, gm)

    @pl.when(task)
    def _():
        reduce(1, pi_, ai, rows_i, gi)
        reduce(2, pt, at, rows_t, gt)

    @pl.when(jnp.logical_not(task))
    def _():
        gi[...] = jnp.zeros(gi.shape, gi.dtype)
        gt[...] = jnp.zeros(gt.shape, gt.dtype)

    reduce(3, p1, a1, rows_m, g1)
    for move in main + one:
        move.wait_send()

    @pl.when(task)
    def _():
        for move in group(1, pi_, ai, rows_i) + group(2, pt, at, rows_t):
            move.wait_send()


def per_device(cfg, section_in, image_start, pool_choice, conv_shared, task_in, task_mid, task_conv, bn_gain, bn_bias):
    M, G, H, W, C, T, n = cfg["M"], cfg["G"], cfg["H"], cfg["W"], cfg["C"], cfg["T"], cfg["n"]
    R = M * G
    pix = H * W
    part = pix // M
    rows_total = H * G
    norms = 2 + 3 * T
    CW = C * (1 + T)
    p = lax.axis_index("pipe")
    r = lax.axis_index("rows")
    b, m = r // M, r % M
    sec = section_in[0].reshape(M, part, CW)
    hp = pool_choice.shape[1]
    place = jnp.arange(4, dtype=jnp.int32).reshape(2, 1, 2)
    picked = pool_choice[:, :, None, :, None] == place[None, None]
    sel = jnp.broadcast_to(picked.reshape(M, part, 1), (M, part, 128)).astype(half)

    ones = jnp.ones((M, 1), jnp.int32)
    padded = jnp.concatenate([ones, image_start[:, 1:], ones], 1)
    links = 1.0 - lax.dynamic_slice_in_dim(padded, b * H, H + 1, 1).astype(f32)
    both = jnp.stack([links[:, :-1], links[:, 1:]], 1)
    team_masks = jnp.broadcast_to(both[..., None], (M, 2, H, C))

    cm, cm_t, spread, edge, pool = tables(M, G, H, W)
    sds = jax.ShapeDtypeStruct
    exchange = [
        sds((TEAM, pix, C), half),
        sds((TEAM, pix, C), half),
        sds((TEAM, pix, C), half),
        sds((TEAM, pix, C), half),
        sds((TEAM, pix, C), half),
        sds((TEAM, 2, W, 1, C), f32),
        sds((TEAM, C, C), half),
        sds((TEAM, pix, C), half),
        sds((TEAM, pix, C // TEAM), half),
        sds((TEAM, 2, W, 1, C // TEAM), f32),
    ]
    direct = C % (16 * R) == 0
    parts = R if direct else n
    rows_m, rows_i, rows_t = 9 * C // parts, 2 * C // parts, C // parts
    q4 = C // TEAM
    shares, share_scratch = [], []
    dma = pltpu.SemaphoreType.DMA
    if direct:
        shares = [
            sds((T * rows_m * C // 128, 128), f32),
            sds((2 * rows_m * C // 128, 128), f32),
            sds((T * rows_i * C // 128, 128), f32),
            sds((T * rows_t * C // 128, 128), f32),
            sds((2, n, TEAM * rows_m, C), half),
            sds((2, n, TEAM * rows_i, C), half),
            sds((2, n, TEAM * rows_t, C), half),
            sds((2, n, TEAM * rows_m, q4), half),
            sds((TEAM, rows_m, C), half),
            sds((T, rows_i, C), half),
            sds((T, rows_t, C), half),
            sds((TEAM, rows_m, q4), half),
        ]
        share_scratch = [
            pltpu.VMEM((4 * rows_m * C // 128, 128), f32),
            pltpu.VMEM((TEAM, 2, W, 1, C), f32),
            pltpu.VMEM((TEAM, 2, W, 1, q4), f32),
            dma((15, TEAM)),
            dma((2, 4, n, TEAM)),
            dma((2, 4, n, TEAM)),
            dma((2, TEAM)),
            dma((4, TEAM)),
            dma((4, TEAM)),
            dma((TEAM + 3,)),
        ]
    vm = pltpu.VMEM
    win = pix // 4 + 32
    outs = pl.pallas_call(
        functools.partial(section_kernel, dict(cfg, direct=direct)),
        name="sections",
        out_shape=[sds((M, part, CW), half), sds((norms, 1, C), f32), sds((norms, 1, C), f32)] + exchange + shares,
        in_specs=[ANY, ANY] + [VMEM] * 8 + [ANY] * 4,
        out_specs=[ANY, VMEM, VMEM] + [ANY] * (len(exchange) + len(shares)),
        scratch_shapes=[
            vm((2, 9 * C, C), half),
            vm((T, 2 * C, C), half),
            vm((T, C, C), half),
            vm((T, 9 * C, C), half),
            vm((pix, CW), half),
            vm((2, pix, CW), half),
            vm((pix, 128), half),
            vm((pix, 128), half),
            vm((2, 32, C), half),
            vm((2, 32, 128), half),
            vm((2, W, 1, C), f32),
            vm((win, CW), half),
            vm((win, CW), half),
            vm((3, pix + 2 * H, C), half),
            vm((norms, pix, C), f32),
            vm((EDGES, 2, W, 1, C), f32),
            vm((EDGES, 2, W, 1, C), f32),
            vm((2 * norms, 2, C), f32),
            vm((G, 2 * norms, 2, C), f32),
            vm((pix, C), half),
            vm((pix, C), half),
            vm((W, 2, C), f32),
            vm((T, pix, C), half),
            vm((T, pix, C), half),
            vm((pix, CW), half),
            vm((T, pix, C), f32),
            vm((pix, C), f32),
            vm((T, pix, C), half),
            vm((T, 2, W, 1, C), f32),
            vm((2, W, 1, C), f32),
            vm((T, pix, C), half),
            vm((TEAM, pix, C // TEAM), half),
            vm((TEAM, 2, W, 1, C // TEAM), f32),
            vm((2 * norms, C), f32),
            vm((M, 2 * norms, C), f32),
            pltpu.SemaphoreType.REGULAR,
            dma((4 + T,)),
            dma((7, M)),
            dma((5, M)),
            dma((EDGES, 2)),
            dma((EDGES, 2)),
            dma((2 * norms, G)),
            dma((2 * norms, G)),
            dma((3,)),
            dma((3,)),
            dma((2, M)),
            dma((2, M)),
            dma((M,)),
            dma((M,)),
            dma((39,)),
            dma((39, TEAM)),
        ]
        + share_scratch,
        compiler_params=pltpu.CompilerParams(
            collective_id=0, has_side_effects=True, vmem_limit_bytes=63 * 2**20
        ),
    )(sec, sel, team_masks, cm, cm_t, spread, edge, pool, bn_gain.reshape(norms, 1, C), bn_bias.reshape(norms, 1, C), conv_shared[0], task_in[0], task_mid[0], task_conv[0])
    result, gain_grad, bias_grad = outs[:3]
    gain_grad, bias_grad = gain_grad.reshape(1, norms, C), bias_grad.reshape(1, norms, C)

    result = result.reshape(1, M, part // W, W, CW)
    if direct:
        gm, g1, gi, gt = outs[-12:-8]
        return (
            result,
            g1.reshape(-1, 2, 128).transpose(1, 0, 2).reshape(1, 2, -1),
            gi.reshape(1, T, -1),
            gt.reshape(1, T, -1),
            gm.reshape(1, T, -1),
            gain_grad,
            bias_grad,
        )
    shapes = [sds((rows_m, C), half), sds((rows_m, q4), half), sds((rows_i, C), half), sds((rows_t, C), half)]
    slots = [(n, rows_m, C), (n, rows_m, q4), (n, rows_i, C), (n, rows_t, C)]
    grads = pl.pallas_call(
        functools.partial(gradient_kernel, cfg),
        name="kernel_gradients",
        out_shape=shapes,
        in_specs=[VMEM] + [ANY] * 10,
        out_specs=[VMEM] * 4,
        scratch_shapes=[
            vm((TEAM, pix, C), half),
            vm((TEAM, pix, C), half),
            vm((TEAM, pix, C), half),
            vm((TEAM, pix, C), half),
            vm((TEAM, 2, W, 1, C), f32),
            vm((TEAM, 3, pix + 2 * H, C), half),
            vm((TEAM, 3, pix, 3 * q4), half),
            vm((TEAM, pix, q4), half),
            vm((TEAM, 2, W, 1, q4), f32),
            vm((TEAM, pix, C), half),
            vm((TEAM, C, C), half),
            vm((9 * C, C), half),
            vm((9 * C, q4), half),
            vm((2 * C, C), half),
            vm((C, C), half),
            vm(slots[0], half),
            vm(slots[1], half),
            vm(slots[2], half),
            vm(slots[3], half),
            dma((11,)),
            dma((4, R)),
            dma((4, R)),
        ],
        compiler_params=pltpu.CompilerParams(
            collective_id=1, has_side_effects=True, vmem_limit_bytes=60 * 2**20
        ),
    )(team_masks, *outs[3:])

    gm, g1, gi, gt = grads
    pieces = [
        gm.reshape(TEAM, -1),
        g1.reshape(TEAM, -1),
        gi.reshape(TEAM, -1),
        gt.reshape(TEAM, -1),
    ]
    packed = jnp.concatenate(pieces, 1)
    teams = [[TEAM * i + j for j in range(TEAM)] for i in range(R // TEAM)]
    swapped = lax.all_to_all(packed, "rows", 0, 0, axis_index_groups=teams, tiled=False).astype(f32)
    sizes = [v.shape[1] for v in pieces]
    o = [0, sizes[0], sizes[0] + sizes[1], sizes[0] + sizes[1] + sizes[2], sum(sizes)]
    mains = swapped[:, o[0] : o[1]]
    firsts = swapped[:, o[1] : o[2]].reshape(TEAM, -1, q4).transpose(1, 0, 2).reshape(-1)
    conv_grad = jnp.stack([firsts, mains[T]])
    return (
        result,
        conv_grad[None],
        swapped[:T, o[2] : o[3]][None],
        swapped[:T, o[3] : o[4]][None],
        mains[:T][None],
        gain_grad,
        bias_grad,
    )


def solution(mesh):
    in_specs = (
        P("pipe", None, "rows", None, None),
        P(),
        P(None, "rows", None),
        P("pipe", None, None, None),
        P("pipe", None, None, None),
        P("pipe", None, None, None),
        P("pipe", None, None, None),
        P("pipe", None, None),
        P("pipe", None, None),
    )
    out_specs = (
        P("pipe", None, "rows", None, None),
        P("pipe", None, "rows"),
        P("pipe", None, "rows"),
        P("pipe", None, "rows"),
        P("pipe", None, "rows"),
        P("pipe", None, None),
        P("pipe", None, None),
    )
    bands = mesh.shape["rows"]

    def step(section_in, image_start, pool_choice, conv_shared, task_in, task_mid, task_conv, bn_gain, bn_bias):
        M = section_in.shape[1]
        G = bands // M
        cfg = dict(
            M=M,
            G=G,
            H=section_in.shape[2] // G,
            W=section_in.shape[3],
            C=conv_shared.shape[3],
            T=task_in.shape[1],
            n=bands // TEAM,
            to_all=frozenset(range(0, 8)) | frozenset(range(31, 39)),
        )
        return jax.shard_map(
            functools.partial(per_device, cfg), mesh=mesh, in_specs=in_specs, out_specs=out_specs, check_vma=False
        )(section_in, image_start, pool_choice, conv_shared, task_in, task_mid, task_conv, bn_gain, bn_bias)

    return step
```
